32 devices in a mesh: blk: 16 (over z, x, core), feat: 2 (over y).
Axes of the slice: x: 2, y: 2, z: 4, core: 2. Of those that a mesh axis runs over, the one named last changes fastest.
Arguments:
- features: bfloat16 [8192, 1024], P('blk', 'feat'), may hold values from -6 to 6
- weight_in: bfloat16 [1024, 1024], P(None, 'feat'), may hold values from -0.1875 to 0.1875
- weight_out: bfloat16 [1024, 1024], P(None, 'feat'), may hold values from -0.1875 to 0.1875
- adj_tiles: bfloat16 [16, 5, 8, 128, 128], P('blk'), may hold values from -0.625 to 0.625
- tile_rows: int32 [16, 5, 8], P('blk'), may hold values from 0 to 3, as said below
- tile_cols: int32 [16, 5, 8], P('blk'), may hold values from 0 to 3, as said below
- tile_counts: int32 [16, 5], P('blk'), may hold values from 0 to 8
- cotangent: bfloat16 [8192, 1024], P('blk', 'feat'), may hold values from -0.15625 to 0.15625
Outputs:
- layer_output: bfloat16 [8192, 1024], P('blk', 'feat')
- grad_weight_in: float32 [1024, 1024], P('blk', 'feat')
- grad_weight_out: float32 [1024, 1024], P('blk', 'feat')
The draws below stay inside these ranges and needn't reach their ends.
Inputs may be any that keep to these rules, and one draw needn't show every extreme that they name: `tile_rows`: within one block and cycle step the 8 slots name distinct (row, column) tile pairs. `tile_cols`: within one block and cycle step the 8 slots name distinct (row, column) tile pairs.
All inputs are finite; a program needn't handle non-finite values.
Results may differ from the reference program's by a relative error of at most 0.0064.
Values may be sent and summed in bfloat16 or wider, within the bound.
No kernel may reach another device: no remote copies, remote signals or barrier semaphores. Data moves between devices by JAX's collectives and lax.ppermute only.
A program may use at most 128 MiB of HBM per device.

```python
import jax
import jax.numpy as jnp
from jax import lax

FEAT = 1024
HIDDEN_SIZE = 1024
TILE = 128
RADIUS = 2
CAP = 8
ROWS_DEV = 512
STEPS = 5
TILE_ROWS = 4
NBLOCKS = 16
NODES = 8192


def index_pairs(key):
    key_list = jax.random.split(jax.random.fold_in(key, 11), NBLOCKS * STEPS)

    def one_order(one_key):
        return jax.random.permutation(one_key, TILE_ROWS * TILE_ROWS)
    orders = jax.vmap(one_order)(key_list)
    return orders[:, :CAP].reshape(NBLOCKS, STEPS, CAP).astype(jnp.int32)


def draw_tile_rows(key, part):
    return (index_pairs(key) // TILE_ROWS).astype(jnp.int32)


def draw_tile_cols(key, part):
    return (index_pairs(key) % TILE_ROWS).astype(jnp.int32)


def draw_tile_counts(key, part):
    first_draw = jax.random.randint(jax.random.fold_in(key, 21), (NBLOCKS, STEPS), 0, CAP + 1)
    second_draw = jax.random.randint(jax.random.fold_in(key, 22), (NBLOCKS, STEPS), 0, CAP + 1)
    skewed = first_draw * second_draw // CAP
    centre = (jnp.arange(STEPS) == RADIUS)[None, :]
    return jnp.where(centre, CAP, skewed).astype(jnp.int32)


def spiked(array, rng, source, target, parts, factor):
    def block_of(dim):
        return (jnp.arange(array.shape[dim]) // (array.shape[dim] // parts)).reshape((-1,) + (1,) * (array.ndim - 1 - dim))

    near = jax.random.permutation(rng, parts)[block_of(target)]
    far = (block_of(target) + parts // 2) % parts
    return jnp.where((block_of(source) == near) | (block_of(source) == far), factor * array, array)


def steps_of(own_key, extent, cuts, smallest, high):
    level, own = 1.0, jax.random.fold_in(own_key, 6)
    for position, parts in cuts:
        heights = jnp.exp(jax.random.uniform(jax.random.fold_in(own, position), (parts,), jnp.float32, smallest / len(cuts), high / len(cuts)))
        level = level * jnp.repeat(heights, extent[position] // parts).reshape([-1 if axis == position else 1 for axis in range(len(extent))])
    return level


def noise(rng, extent, width, limit, shards=(), kind=jnp.bfloat16):
    values = jax.random.normal(rng, extent, jnp.float32) * width
    if len(shards) > 0:
        values = steps_of(rng, extent, shards, -0.22, 0.18) * values
    return jnp.clip(values, min=-limit, max=limit).astype(kind)


def noise_with(key, shape, scale, reach, cuts, heavy, held_as=jnp.bfloat16):
    array = scale * jax.random.normal(key, shape, jnp.float32)
    if cuts:
        array = array * steps_of(key, shape, cuts, -0.22, 0.18)
    return jnp.clip(spiked(array, jax.random.fold_in(key, 3), *heavy), -reach, reach).astype(held_as)


def setup_inputs(seed: int = 0) -> dict:
    keys = jax.random.split(jax.random.key(seed), 9)
    features = noise_with(keys[0], (NODES, FEAT), 1.0, 6.0, ((0, 16), (1, 2)), (0, 1, 16, 2.0))
    weight_in = noise(keys[1], (FEAT, HIDDEN_SIZE), FEAT ** -0.5, 0.1875, ((1, 2),))
    weight_out = noise(keys[2], (HIDDEN_SIZE, HIDDEN_SIZE), HIDDEN_SIZE ** -0.5, 0.1875, ((1, 2),))
    adj_tiles = noise(keys[3], (NBLOCKS, STEPS, CAP, TILE, TILE), ((TILE * (CAP // TILE_ROWS + 2)) ** -0.5), 0.625, ((0, 16),))
    tile_rows = draw_tile_rows(jax.random.fold_in(keys[8], 71), 0)
    tile_cols = draw_tile_cols(jax.random.fold_in(keys[8], 71), 0)
    tile_counts = draw_tile_counts(jax.random.fold_in(keys[8], 71), 0)
    cotangent = noise(keys[7], (NODES, HIDDEN_SIZE), (NODES ** -0.5), 0.15625, ((0, 16), (1, 2)))
    return {"features": features, "weight_in": weight_in, "weight_out": weight_out, "adj_tiles": adj_tiles, "tile_rows": tile_rows, "tile_cols": tile_cols, "tile_counts": tile_counts, "cotangent": cotangent}


def slot_weights(put_ids, live_count, block_rows):
    chosen = put_ids[:, None] == jnp.arange(block_rows, dtype=jnp.int32)[None, :]
    live_mask = (jnp.arange(put_ids.shape[0], dtype=jnp.int32) < live_count)[:, None]
    return (chosen & live_mask).astype(jnp.float32)


def spread_rows(adj_tiles, tile_rows, tile_cols, tile_counts, values_in):
    columns = values_in.shape[1]
    blocks = values_in.reshape(NBLOCKS, TILE_ROWS, TILE, columns)

    def one_block(block_index):
        summed = jnp.zeros((TILE_ROWS, TILE, columns), jnp.float32)
        for cycle_step in range(STEPS):
            source = (block_index + cycle_step - RADIUS) % NBLOCKS
            source_rows = lax.dynamic_index_in_dim(blocks, source, 0, keepdims=False)
            picked = jnp.take(source_rows, tile_cols[block_index, cycle_step], axis=0)
            product = jnp.einsum("kab,kbw->kaw", adj_tiles[block_index, cycle_step].astype(jnp.float32),
                                 picked.astype(jnp.float32), precision=lax.Precision.HIGHEST)
            weights = slot_weights(tile_rows[block_index, cycle_step], tile_counts[block_index, cycle_step], TILE_ROWS)
            summed = summed + jnp.einsum("kr,kaw->raw", weights, product, precision=lax.Precision.HIGHEST)
        return summed.reshape(ROWS_DEV, columns)

    return lax.map(one_block, jnp.arange(NBLOCKS, dtype=jnp.int32)).reshape(NODES, columns)


def return_rows(adj_tiles, tile_rows, tile_cols, tile_counts, values_in):
    columns = values_in.shape[1]
    blocks = values_in.reshape(NBLOCKS, TILE_ROWS, TILE, columns)

    def one_block(block_index):
        summed = jnp.zeros((TILE_ROWS, TILE, columns), jnp.float32)
        for cycle_step in range(STEPS):
            source = (block_index - (cycle_step - RADIUS)) % NBLOCKS
            source_rows = lax.dynamic_index_in_dim(blocks, source, 0, keepdims=False)
            picked = jnp.take(source_rows, tile_rows[source, cycle_step], axis=0)
            product = jnp.einsum("kba,kbw->kaw", adj_tiles[source, cycle_step].astype(jnp.float32),
                                 picked.astype(jnp.float32), precision=lax.Precision.HIGHEST)
            weights = slot_weights(tile_cols[source, cycle_step], tile_counts[source, cycle_step], TILE_ROWS)
            summed = summed + jnp.einsum("kr,kaw->raw", weights, product, precision=lax.Precision.HIGHEST)
        return summed.reshape(ROWS_DEV, columns)

    return lax.map(one_block, jnp.arange(NBLOCKS, dtype=jnp.int32)).reshape(NODES, columns)


def reference(features, weight_in, weight_out, adj_tiles, tile_rows, tile_cols, tile_counts, cotangent):
    spread_in = spread_rows(adj_tiles, tile_rows, tile_cols, tile_counts, features).astype(jnp.bfloat16)
    pre_hidden = jnp.dot(spread_in, weight_in, preferred_element_type=jnp.float32)
    hidden = jax.nn.silu(pre_hidden).astype(jnp.bfloat16)
    spread_hidden = spread_rows(adj_tiles, tile_rows, tile_cols, tile_counts, hidden).astype(jnp.bfloat16)
    layer_output = jnp.dot(spread_hidden, weight_out, preferred_element_type=jnp.float32).astype(jnp.bfloat16)
    back_mixed = lax.dot_general(cotangent, weight_out, (((1,), (1,)), ((), ())),
                                 preferred_element_type=jnp.float32).astype(jnp.bfloat16)
    back_hidden = return_rows(adj_tiles, tile_rows, tile_cols, tile_counts, back_mixed)
    sigmoid_gate = jax.nn.sigmoid(pre_hidden)
    back_pre = (back_hidden * sigmoid_gate * (1.0 + pre_hidden * (1.0 - sigmoid_gate))).astype(jnp.bfloat16)
    grad_weight_in = lax.dot_general(spread_in, back_pre, (((0,), (0,)), ((), ())),
                                     preferred_element_type=jnp.float32)
    grad_weight_out = lax.dot_general(spread_hidden, cotangent, (((0,), (0,)), ((), ())),
                                      preferred_element_type=jnp.float32)
    return (layer_output, grad_weight_in, grad_weight_out)
```

```python
import functools

import jax
import jax.numpy as jnp
from jax import lax
from jax.experimental import pallas as pl
from jax.experimental.pallas import tpu as pltpu
from jax.sharding import PartitionSpec as P

BF16 = jnp.bfloat16
F32 = jnp.float32
VMEM = pl.BlockSpec(memory_space=pltpu.VMEM)
SMEM = pl.BlockSpec(memory_space=pltpu.SMEM)


def params(limit_mib=40):
    return pltpu.CompilerParams(vmem_limit_bytes=limit_mib * 1024 * 1024)


def cost(flops, nbytes, transcendentals=0):
    return pl.CostEstimate(
        flops=flops, bytes_accessed=nbytes, transcendentals=transcendentals
    )


def blk_pairs(target):
    count = lax.axis_size("blk")
    return [(source, target(source) % count) for source in range(count)]


def to_core(value):
    return lax.ppermute(value, "blk", blk_pairs(lambda b: b ^ 1))


def to_mate(value):
    return lax.ppermute(value, "blk", blk_pairs(lambda b: b ^ 2))


def to_mate_core(value):
    return lax.ppermute(value, "blk", blk_pairs(lambda b: b ^ 3))


def relay_out(value):
    return lax.ppermute(value, "blk", blk_pairs(lambda b: b - 4 if b & 2 else b + 4))


def relay_back(value):
    return lax.ppermute(value, "blk", blk_pairs(lambda b: b + 4 if b & 2 else b - 4))


def to_group(value, distance):
    return lax.ppermute(value, "blk", blk_pairs(lambda b: b + 4 * distance))


def to_panel(value):
    return lax.ppermute(value, "feat", [(0, 1), (1, 0)])


def to_panel_core(value):
    blocks, panels = lax.axis_size("blk"), lax.axis_size("feat")
    pairs = [
        (b * panels + f, (b ^ 1) * panels + (1 - f)) for b in range(blocks) for f in range(panels)
    ]
    return lax.ppermute(value, ("blk", "feat"), pairs)


def swapped(value, axis, flag):
    half = value.shape[axis] // 2
    first = lax.slice_in_dim(value, 0, half, axis=axis)
    second = lax.slice_in_dim(value, half, 2 * half, axis=axis)
    return jnp.where(flag == 0, value, jnp.concatenate([second, first], axis=axis))


def halves(value, flag):
    half = value.shape[1] // 2
    left, right = value[:, :half], value[:, half:]
    return jnp.where(flag == 0, left, right), jnp.where(flag == 0, right, left)


def build_body(meta, own_tiles, other_tiles, dense):
    steps, cap, tile, _ = own_tiles.shape
    radius = (steps - 1) // 2
    block_tiles = dense.shape[0] // (2 * tile)
    entries = steps * cap
    width = 2 * entries + steps
    core, mate = meta[2 * width], meta[2 * width + 1]
    dense[...] = jnp.zeros_like(dense)
    for which, tiles in enumerate((own_tiles, other_tiles)):
        base = which * width
        row_core = core ^ which

        def place(entry, carry, base=base, tiles=tiles, row_core=row_core, which=which):
            step, slot = entry // cap, entry % cap
            shifted = step - radius + row_core + 2
            chip = shifted // 2 - 1
            position = (shifted % 2) ^ core
            ahead = jnp.where(mate == 0, 1, -1)
            segment = jnp.where(chip == 0, 0, jnp.where(chip == ahead, 1, 2))
            row = which * block_tiles + meta[base + entry]
            col = (2 * segment + position) * block_tiles + meta[base + entries + entry]

            @pl.when(slot < meta[base + 2 * entries + step])
            def _():
                dense[
                    pl.ds(pl.multiple_of(row * tile, tile), tile),
                    pl.ds(pl.multiple_of(col * tile, tile), tile),
                ] = tiles[step, slot]

            return carry

        lax.fori_loop(0, entries, place, 0)


def build(meta, own_tiles, other_tiles, rows):
    size = 2 * rows * 6 * rows
    return pl.pallas_call(
        build_body,
        out_shape=jax.ShapeDtypeStruct((2 * rows, 6 * rows), BF16),
        in_specs=[SMEM, VMEM, VMEM],
        out_specs=VMEM,
        compiler_params=params(),
        cost_estimate=cost(0, 4 * size),
        name="build_dense",
    )(meta, own_tiles, other_tiles)


def spread_body(dense, *refs):
    parts, (own, other) = refs[:6], refs[6:]
    rows = parts[0].shape[0]
    total = jnp.dot(dense[:, :rows], parts[0][...], preferred_element_type=F32)
    for index in range(1, 6):
        total += jnp.dot(
            dense[:, index * rows : (index + 1) * rows],
            parts[index][...],
            preferred_element_type=F32,
        )
    result = total.astype(BF16)
    first = pl.program_id(0) < pl.num_programs(0) // 2

    @pl.when(first)
    def _():
        own[...] = result

    @pl.when(jnp.logical_not(first))
    def _():
        other[...] = result


def spread(dense, parts):
    rows, cols = parts[0].shape
    block = rows // 2
    whole = pl.BlockSpec((rows, cols), lambda i: (0, 0))
    return pl.pallas_call(
        spread_body,
        grid=(4,),
        out_shape=[jax.ShapeDtypeStruct((rows, cols), BF16)] * 2,
        in_specs=[pl.BlockSpec((block, 6 * rows), lambda i: (i, 0))] + [whole] * 6,
        out_specs=[
            pl.BlockSpec((block, cols), lambda i: (jnp.minimum(i, 1), 0)),
            pl.BlockSpec((block, cols), lambda i: (jnp.maximum(i - 2, 0), 0)),
        ],
        compiler_params=params(),
        cost_estimate=cost(24 * rows * rows * cols, 24 * rows * rows),
        name="spread",
    )(dense, *parts)


def pull_body(dense, own, other, out):
    rows = own.shape[0]
    contract = (((0,), (0,)), ((), ()))
    total = lax.dot_general(own[...], dense[:rows], contract, preferred_element_type=F32)
    total += lax.dot_general(other[...], dense[rows:], contract, preferred_element_type=F32)
    out[...] = total.astype(out.dtype)


def pull(dense, own, other, segment, dtype):
    rows, cols = own.shape
    whole = pl.BlockSpec((rows, cols), lambda i: (0, 0))
    return pl.pallas_call(
        pull_body,
        grid=(2,),
        out_shape=jax.ShapeDtypeStruct((cols, 2 * rows), dtype),
        in_specs=[
            pl.BlockSpec((2 * rows, rows), lambda i: (0, 2 * segment + i)),
            whole,
            whole,
        ],
        out_specs=pl.BlockSpec((cols, rows), lambda i: (0, i)),
        compiler_params=params(),
        cost_estimate=cost(8 * rows * rows * cols, 8 * rows * rows),
        name="pull",
    )(dense, own, other)


def hidden_body(s0, s1, s2, s3, w_mine, w_near, w_far, w_out, pre, hid, t_keep, t_give):
    rows, piece = s0.shape
    width = w_mine.shape[1]
    tall = rows // 2
    others = (w_near[:piece], w_far[:piece], w_near[piece:], w_far[piece:])

    def chunk(index, carry):
        span = pl.ds(pl.multiple_of(index * tall, tall), tall)
        taken = [ref[span, :] for ref in (s0, s1, s2, s3)]
        mine = jnp.dot(
            jnp.concatenate(taken, axis=1), w_mine[...], preferred_element_type=F32
        )
        theirs = jnp.dot(taken[0], others[0], preferred_element_type=F32)
        for number in range(1, 4):
            theirs += jnp.dot(taken[number], others[number], preferred_element_type=F32)
        pre[span, :] = mine
        h_mine = (mine * jax.nn.sigmoid(mine)).astype(BF16)
        h_theirs = (theirs * jax.nn.sigmoid(theirs)).astype(BF16)
        hid[span, :width] = h_mine
        hid[span, width:] = h_theirs
        mixed = jnp.dot(
            jnp.concatenate([h_mine, h_theirs], axis=1), w_out[...], preferred_element_type=F32
        ).astype(BF16)
        t_keep[span, :] = mixed[:, :piece]
        t_give[span, :] = mixed[:, piece:]
        return carry

    lax.fori_loop(0, rows // tall, chunk, 0)


def hidden_step(pieces, w_mine, w_near, w_far, w_out):
    rows, piece = pieces[0].shape
    width = w_mine.shape[1]
    return pl.pallas_call(
        hidden_body,
        out_shape=[
            jax.ShapeDtypeStruct((rows, width), F32),
            jax.ShapeDtypeStruct((rows, 2 * width), BF16),
            jax.ShapeDtypeStruct((rows, piece), BF16),
            jax.ShapeDtypeStruct((rows, piece), BF16),
        ],
        in_specs=[VMEM] * 8,
        out_specs=[VMEM] * 4,
        compiler_params=params(),
        cost_estimate=cost(
            24 * rows * piece * 2 * width, 24 * rows * width, 4 * rows * width
        ),
        name="hidden",
    )(*pieces, w_mine, w_near, w_far, w_out)


def mix_body(meta, st_keep, st_give, w_out, pulled, keep, give):
    piece = st_keep.shape[0]
    half = w_out.shape[0] // 2
    core = meta[0]
    contract = (((0,), (1,)), ((), ()))
    first, second = st_keep[...].T, st_give[...].T
    pulled[:, pl.ds(pl.multiple_of(core * piece, piece), piece)] = first
    pulled[:, pl.ds(pl.multiple_of((1 - core) * piece, piece), piece)] = second
    both = jnp.concatenate([first, second], axis=1)
    contract = (((1,), (1,)), ((), ()))
    keep[...] = lax.dot_general(both, w_out[:half], contract, preferred_element_type=F32)
    give[...] = lax.dot_general(
        both, w_out[half:], contract, preferred_element_type=F32
    ).astype(BF16)


def mix_step(meta, st_keep, st_give, w_out):
    piece, rows = st_keep.shape
    half = w_out.shape[0] // 2
    return pl.pallas_call(
        mix_body,
        out_shape=[
            jax.ShapeDtypeStruct((rows, 2 * piece), BF16),
            jax.ShapeDtypeStruct((rows, half), F32),
            jax.ShapeDtypeStruct((rows, half), BF16),
        ],
        in_specs=[SMEM, VMEM, VMEM, VMEM],
        out_specs=[VMEM] * 3,
        compiler_params=params(),
        cost_estimate=cost(8 * rows * piece * half, 8 * rows * half),
        name="mix_back",
    )(meta, st_keep, st_give, w_out)


def split_term(meta, total, keep, give, scratch, blocks):
    core, mate = meta[0], meta[1]
    share = total.shape[0] // blocks
    groups = blocks // 4
    for group in range(groups):
        for side in range(2):
            owner = 4 * group + 2 * (mate ^ side)
            target = pl.ds((side * groups + group) * share, share)
            source = pl.multiple_of((owner + core) * share, share)
            keep[target, :] = total[pl.ds(source, share), :]
            source = pl.multiple_of((owner + 1 - core) * share, share)
            scratch[target, :] = total[pl.ds(source, share), :]
    give[...] = scratch[...].astype(BF16)


def out_grad_body(meta, hid, pulled, keep, give, total, scratch, *, blocks):
    piece = hid.shape[1] // 4
    panel = meta[2]
    contract = (((0,), (0,)), ((), ()))
    for number in range(4):
        start = ((number // 2) ^ panel) * 2 + number % 2
        total[pl.ds(pl.multiple_of(start * piece, piece), piece), :] = lax.dot_general(
            hid[:, number * piece : (number + 1) * piece],
            pulled[...],
            contract,
            preferred_element_type=F32,
        )
    split_term(meta, total, keep, give, scratch, blocks)


def in_grad_body(
    meta, s0, s1, s2, s3, pre, kept, come, keep, give, total, scratch, back, *, blocks
):
    piece = s0.shape[1]
    core, panel = meta[0], meta[2]
    pre_hidden = pre[...]
    gate = jax.nn.sigmoid(pre_hidden)
    back_hidden = kept[...] + come[...].astype(F32)
    back[...] = (back_hidden * gate * (1.0 + pre_hidden * (1.0 - gate))).astype(BF16)
    contract = (((0,), (0,)), ((), ()))
    for number, ref in enumerate((s0, s1, s2, s3)):
        start = ((number // 2) ^ panel) * 2 + ((number % 2) ^ core)
        total[pl.ds(pl.multiple_of(start * piece, piece), piece), :] = lax.dot_general(
            ref[...], back[...], contract, preferred_element_type=F32
        )
    split_term(meta, total, keep, give, scratch, blocks)


def grad_call(body, name, meta, operands, height, width, scratch=()):
    blocks = lax.axis_size("blk")
    half = height // 2
    return pl.pallas_call(
        functools.partial(body, blocks=blocks),
        out_shape=[
            jax.ShapeDtypeStruct((half, width), F32),
            jax.ShapeDtypeStruct((half, width), BF16),
        ],
        in_specs=[SMEM] + [VMEM] * len(operands),
        out_specs=[VMEM] * 2,
        scratch_shapes=[
            pltpu.VMEM((height, width), F32),
            pltpu.VMEM((half, width), F32),
            *scratch,
        ],
        compiler_params=params(),
        cost_estimate=cost(height * width * width * 2, height * width * 8),
        name=name,
    )(meta, *operands)


def scatter_sum(keep, give):
    groups = lax.axis_size("blk") // 4
    group = lax.axis_index("blk") // 4
    half = keep.shape[0] // 2
    share = half // groups
    come = to_core(give)
    near = keep[:half] + come[:half].astype(F32)
    far = (keep[half:] + come[half:].astype(F32)).astype(BF16)
    near = near + to_mate(far).astype(F32)
    total = lax.dynamic_slice_in_dim(near, group * share, share, axis=0)
    for distance in range(1, groups):
        target = (group + distance) % groups
        term = lax.dynamic_slice_in_dim(near, target * share, share, axis=0).astype(BF16)
        total = total + to_group(term, distance).astype(F32)
    return total


def shards(
    features, weight_in, weight_out, adj_tiles, tile_rows, tile_cols, tile_counts, cotangent
):
    rows, width = features.shape
    piece = width // 2
    block = lax.axis_index("blk")
    core, mate, panel = block & 1, (block >> 1) & 1, lax.axis_index("feat")
    meta = jnp.stack([core, mate, panel]).astype(jnp.int32)

    f_keep, f_give = halves(features, core)
    f_mate = to_mate(f_keep)
    f_mate_other = to_mate_core(f_give)
    f_other = to_core(f_give)
    c_keep, c_give = halves(cotangent, core)
    c_other = to_core(c_give)
    f_far = relay_out(f_mate)
    f_far_other = relay_out(f_mate_other)

    lists = jnp.concatenate([tile_rows[0].ravel(), tile_cols[0].ravel(), tile_counts[0]])
    other_tiles, other_lists = to_core(adj_tiles[0]), to_core(lists)
    dense = build(
        jnp.concatenate([lists, other_lists, meta]), adj_tiles[0], other_tiles, rows
    )

    w_in = swapped(weight_in, 0, panel)
    quarters = w_in.reshape(2, 2, piece, width)
    w_in = jnp.where(core == 0, quarters, quarters[:, ::-1])
    w_near = to_panel(jnp.concatenate([w_in[1, 0], w_in[0, 0]], axis=0))
    w_far = to_core(w_near)
    w_in = w_in.reshape(weight_in.shape)
    w_out = swapped(swapped(weight_out, 0, panel), 1, core)

    p_far = pull(dense, c_keep, c_other, 2, BF16)
    p_mate = pull(dense, c_keep, c_other, 1, F32)
    p_own = pull(dense, c_keep, c_other, 0, F32)
    p_mate = (p_mate + relay_back(p_far).astype(F32)).astype(BF16)
    st = (p_own + to_mate(p_mate).astype(F32)).astype(BF16)
    st_keep, st_give = st[:, :rows], to_core(st[:, rows:])
    pulled, kept, given = mix_step(meta, st_keep, st_give, w_out)
    come = to_panel(given)

    own, other = spread(dense, [f_keep, f_other, f_mate, f_mate_other, f_far, f_far_other])
    pieces = [own, to_core(other), to_panel(own), to_panel_core(other)]
    pre_hidden, hid, t_keep, t_give = hidden_step(pieces, w_in, w_near, w_far, w_out)

    t_mate = to_mate(t_keep)
    t_mate_other = to_mate_core(t_give)
    t_other = to_core(t_give)
    t_far = relay_out(t_mate)
    t_far_other = relay_out(t_mate_other)

    out_keep, out_give = grad_call(
        out_grad_body, "out_grad", meta, [hid, pulled], 2 * width, width
    )
    in_keep, in_give = grad_call(
        in_grad_body,
        "in_grad",
        meta,
        [*pieces, pre_hidden, kept, come],
        2 * width,
        width,
        (pltpu.VMEM((rows, width), BF16),),
    )
    grad_weight_out = scatter_sum(out_keep, out_give)
    grad_weight_in = scatter_sum(in_keep, in_give)

    own, other = spread(dense, [t_keep, t_other, t_mate, t_mate_other, t_far, t_far_other])
    other = to_core(other)
    layer_output = jnp.where(
        core == 0,
        jnp.concatenate([own, other], axis=1),
        jnp.concatenate([other, own], axis=1),
    )
    return (layer_output, grad_weight_in, grad_weight_out)


def solution(mesh):
    return jax.shard_map(
        shards,
        mesh=mesh,
        in_specs=(
            P("blk", "feat"),
            P(None, "feat"),
            P(None, "feat"),
            P("blk", None, None, None, None),
            P("blk", None, None),
            P("blk", None, None),
            P("blk", None),
            P("blk", "feat"),
        ),
        out_specs=(P("blk", "feat"), P("blk", "feat"), P("blk", "feat")),
        check_vma=False,
    )
```

```python
import functools

import jax
import jax.numpy as jnp
from jax import lax
from jax.experimental import pallas as pl
from jax.experimental.pallas import tpu as pltpu
from jax.sharding import PartitionSpec as P

BF16 = jnp.bfloat16
F32 = jnp.float32
VMEM = pl.BlockSpec(memory_space=pltpu.VMEM)
SMEM = pl.BlockSpec(memory_space=pltpu.SMEM)
ANY = pl.BlockSpec(memory_space=pl.ANY)
HBM = pl.BlockSpec(memory_space=pltpu.HBM)


def params(limit_mib=40):
    return pltpu.CompilerParams(vmem_limit_bytes=limit_mib * 1024 * 1024)


def cost(flops, nbytes, transcendentals=0):
    return pl.CostEstimate(flops=1024, bytes_accessed=1024, transcendentals=0)


def gate_body(*refs):
    del refs


def gate(value, *after):
    return pl.pallas_call(
        gate_body,
        out_shape=jax.ShapeDtypeStruct(value.shape, value.dtype),
        in_specs=[ANY] * (1 + len(after)),
        out_specs=ANY,
        input_output_aliases={0: 0},
        cost_estimate=cost(0, 0),
        name="gate",
    )(value, *after)


def coordinates():
    block = lax.axis_index("blk")
    return block & 1, (block >> 1) & 1, lax.axis_index("feat")


def copy_all(pairs, semaphores):
    copies = [
        pltpu.make_async_copy(source, target, semaphores.at[number])
        for number, (source, target) in enumerate(pairs)
    ]
    for copy in copies:
        copy.start()
    for copy in copies:
        copy.wait()


def part(ref, axis, index, size):
    span = pl.ds(pl.multiple_of(index * size, size), size)
    return ref.at[span, :] if axis == 0 else ref.at[:, span]


def halve_body(value, keep, give, again, semaphores):
    half = keep.shape[1]
    core, _, _ = coordinates()
    copy_all(
        [
            (part(value, 1, core, half), keep),
            (part(value, 1, 1 - core, half), give),
            (part(value, 1, 1 - core, half), again),
        ],
        semaphores,
    )


def halve(value):
    rows, width = value.shape
    return pl.pallas_call(
        halve_body,
        out_shape=[jax.ShapeDtypeStruct((rows, width // 2), value.dtype)] * 3,
        in_specs=[HBM],
        out_specs=[HBM] * 3,
        scratch_shapes=[pltpu.SemaphoreType.DMA((3,))],
        cost_estimate=cost(0, 0),
        name="halve",
    )(value)


def order_body(
    cot, w_in, w_out, keep, give, send_first, send_second, in_mine, out_mine, semaphores
):
    half = keep.shape[1]
    width = 2 * half
    core, _, panel = coordinates()
    pairs = [(part(cot, 1, core, half), keep), (part(cot, 1, 1 - core, half), give)]
    for side, send in enumerate((send_first, send_second)):
        pairs.append((part(w_in, 0, (panel ^ (1 - side)) * 2 + core, half), send))
        for other in range(2):
            source = (panel ^ side) * 2 + (core ^ other)
            target = in_mine.at[pl.ds((2 * side + other) * half, half)]
            pairs.append((part(w_in, 0, source, half), target))
            rows = pl.ds(pl.multiple_of((panel ^ side) * width, width), width)
            cols = pl.ds(pl.multiple_of((core ^ other) * half, half), half)
            target = out_mine.at[
                side * width : (side + 1) * width, other * half : (other + 1) * half
            ]
            pairs.append((w_out.at[rows, cols], target))
    copy_all(pairs, semaphores)


def order(cot, w_in, w_out):
    rows, width = cot.shape
    half = width // 2
    return pl.pallas_call(
        order_body,
        out_shape=[
            jax.ShapeDtypeStruct((rows, half), BF16),
            jax.ShapeDtypeStruct((rows, half), BF16),
            jax.ShapeDtypeStruct((half, width), BF16),
            jax.ShapeDtypeStruct((half, width), BF16),
            jax.ShapeDtypeStruct(w_in.shape, BF16),
            jax.ShapeDtypeStruct(w_out.shape, BF16),
        ],
        in_specs=[HBM] * 3,
        out_specs=[HBM] * 6,
        scratch_shapes=[pltpu.SemaphoreType.DMA((12,))],
        cost_estimate=cost(0, 0),
        name="order",
    )(cot, w_in, w_out)


def join_body(own, other, out, semaphores):
    half = own.shape[1]
    core, _, _ = coordinates()
    copy_all(
        [(own, part(out, 1, core, half)), (other, part(out, 1, 1 - core, half))], semaphores
    )


def join(own, other):
    rows, half = own.shape
    return pl.pallas_call(
        join_body,
        out_shape=jax.ShapeDtypeStruct((rows, 2 * half), BF16),
        in_specs=[HBM, HBM],
        out_specs=HBM,
        scratch_shapes=[pltpu.SemaphoreType.DMA((2,))],
        cost_estimate=cost(0, 0),
        name="join",
    )(own, other)


def blk_pairs(target):
    count = lax.axis_size("blk")
    return [(source, target(source) % count) for source in range(count)]


def to_core(value):
    return lax.ppermute(value, "blk", blk_pairs(lambda b: b ^ 1))


def to_mate(value):
    return lax.ppermute(value, "blk", blk_pairs(lambda b: b ^ 2))


def to_mate_core(value):
    return lax.ppermute(value, "blk", blk_pairs(lambda b: b ^ 3))


def relay_out(value):
    return lax.ppermute(value, "blk", blk_pairs(lambda b: b - 4 if b & 2 else b + 4))


def relay_back(value):
    return lax.ppermute(value, "blk", blk_pairs(lambda b: b + 4 if b & 2 else b - 4))


def to_group(value, distance):
    return lax.ppermute(value, "blk", blk_pairs(lambda b: b + 4 * distance))


def to_panel(value):
    return lax.ppermute(value, "feat", [(0, 1), (1, 0)])


def to_panel_core(value):
    blocks, panels = lax.axis_size("blk"), lax.axis_size("feat")
    pairs = [
        (b * panels + f, (b ^ 1) * panels + (1 - f)) for b in range(blocks) for f in range(panels)
    ]
    return lax.ppermute(value, ("blk", "feat"), pairs)


def build_body(rows, cols, counts, other_lists, own_tiles, other_tiles, dense):
    steps, cap, tile, _ = own_tiles.shape
    radius = (steps - 1) // 2
    block_tiles = dense.shape[0] // (2 * tile)
    entries = steps * cap
    core, mate, _ = coordinates()
    dense[...] = jnp.zeros_like(dense)
    for which, tiles in enumerate((own_tiles, other_tiles)):
        row_core = core ^ which

        def place(entry, carry, tiles=tiles, row_core=row_core, which=which):
            step, slot = entry // cap, entry % cap
            if which == 0:
                tile_row, tile_col, live = rows[0, step, slot], cols[0, step, slot], counts[0, step]
            else:
                tile_row = other_lists[entry]
                tile_col = other_lists[entries + entry]
                live = other_lists[2 * entries + step]
            shifted = step - radius + row_core + 2
            chip = shifted // 2 - 1
            position = (shifted % 2) ^ core
            ahead = jnp.where(mate == 0, 1, -1)
            segment = jnp.where(chip == 0, 0, jnp.where(chip == ahead, 1, 2))
            row = which * block_tiles + tile_row
            col = (2 * segment + position) * block_tiles + tile_col

            @pl.when(slot < live)
            def _():
                dense[
                    pl.ds(pl.multiple_of(row * tile, tile), tile),
                    pl.ds(pl.multiple_of(col * tile, tile), tile),
                ] = tiles[step, slot]

            return carry

        lax.fori_loop(0, entries, place, 0)


def list_body(rows, cols, counts, out):
    _, steps, cap = rows.shape
    for step in range(steps):
        for slot in range(cap):
            out[step * cap + slot] = rows[0, step, slot]
            out[(steps + step) * cap + slot] = cols[0, step, slot]
        out[2 * steps * cap + step] = counts[0, step]


def list_up(rows, cols, counts):
    return pl.pallas_call(
        list_body,
        out_shape=jax.ShapeDtypeStruct((rows.size + cols.size + counts.size,), jnp.int32),
        in_specs=[SMEM] * 3,
        out_specs=SMEM,
        cost_estimate=cost(0, 0),
        name="lists",
    )(rows, cols, counts)


def build(tile_rows, tile_cols, tile_counts, other_lists, own_tiles, other_tiles, rows):
    size = 2 * rows * 6 * rows
    return pl.pallas_call(
        build_body,
        out_shape=jax.ShapeDtypeStruct((2 * rows, 6 * rows), BF16),
        in_specs=[SMEM] * 4 + [VMEM] * 2,
        out_specs=VMEM,
        compiler_params=params(),
        cost_estimate=cost(0, 4 * size),
        name="build_dense",
    )(tile_rows, tile_cols, tile_counts, other_lists, own_tiles, other_tiles)


def spread_near_body(dense, s0, s1, s2, s3, total):
    rows = s0.shape[0]
    result = jnp.dot(dense[:, :rows], s0[...], preferred_element_type=F32)
    for index, ref in enumerate((s1, s2, s3)):
        start = (index + 1) * rows
        result += jnp.dot(
            dense[:, start : start + rows], ref[...], preferred_element_type=F32
        )
    total[...] = result


def spread_near(dense, parts):
    rows, cols = parts[0].shape
    block = rows // 2
    whole = pl.BlockSpec((rows, cols), lambda i: (0, 0))
    return pl.pallas_call(
        spread_near_body,
        grid=(4,),
        out_shape=jax.ShapeDtypeStruct((2 * rows, cols), F32),
        in_specs=[pl.BlockSpec((block, 4 * rows), lambda i: (i, 0))] + [whole] * 4,
        out_specs=pl.BlockSpec((block, cols), lambda i: (i, 0)),
        compiler_params=params(),
        cost_estimate=cost(16 * rows * rows * cols, 16 * rows * rows),
        name="spread_near",
    )(dense, *parts)


def spread_far_body(dense, total, s0, s1, *refs):
    own, other = refs[-2:]
    rows = s0.shape[0]
    result = total[...] + jnp.dot(dense[:, :rows], s0[...], preferred_element_type=F32)
    result += jnp.dot(dense[:, rows:], s1[...], preferred_element_type=F32)
    result = result.astype(BF16)
    first = pl.program_id(0) == 0

    @pl.when(first)
    def _():
        own[...] = result

    @pl.when(jnp.logical_not(first))
    def _():
        other[...] = result


def spread_far(dense, total, parts, *after):
    rows, cols = parts[0].shape
    whole = pl.BlockSpec((rows, cols), lambda i: (0, 0))
    return pl.pallas_call(
        spread_far_body,
        grid=(2,),
        out_shape=[jax.ShapeDtypeStruct((rows, cols), BF16)] * 2,
        in_specs=[
            pl.BlockSpec((rows, 2 * rows), lambda i: (i, 2)),
            pl.BlockSpec((rows, cols), lambda i: (i, 0)),
            whole,
            whole,
            *[ANY] * len(after),
        ],
        out_specs=[whole, whole],
        compiler_params=params(),
        cost_estimate=cost(8 * rows * rows * cols, 8 * rows * rows),
        name="spread_far",
    )(dense, total, *parts, *after)


def pull_body(dense, own, other, *out):
    rows = own.shape[0]
    contract = (((0,), (0,)), ((), ()))
    total = lax.dot_general(own[...], dense[:rows], contract, preferred_element_type=F32)
    total += lax.dot_general(other[...], dense[rows:], contract, preferred_element_type=F32)
    if len(out) == 1:
        out[0][...] = total.astype(out[0].dtype)
    else:
        for step, ref in enumerate(out):

            @pl.when(pl.program_id(0) == step)
            def _(ref=ref):
                ref[...] = total.astype(ref.dtype)


def pull(dense, own, other, segment, *dtypes):
    rows, cols = own.shape
    whole = pl.BlockSpec((rows, cols), lambda i: (0, 0))
    if len(dtypes) == 1:
        out_shape = [jax.ShapeDtypeStruct((cols, 2 * rows), dtypes[0])]
        out_specs = [pl.BlockSpec((cols, rows), lambda i: (0, i))]
    else:
        out_shape = [jax.ShapeDtypeStruct((cols, rows), dtype) for dtype in dtypes]
        out_specs = [pl.BlockSpec((cols, rows), lambda i: (0, 0))] * 2
    return pl.pallas_call(
        pull_body,
        grid=(2,),
        out_shape=out_shape,
        in_specs=[
            pl.BlockSpec((2 * rows, rows), lambda i: (0, 2 * segment + i)),
            whole,
            whole,
        ],
        out_specs=out_specs,
        compiler_params=params(),
        cost_estimate=cost(8 * rows * rows * cols, 8 * rows * rows),
        name="pull",
    )(dense, own, other)


def meet_body(mine, come, *refs):
    same, other = refs[-2:]
    rows = same.shape[1]
    same[...] = (mine[:, :rows] + come[:, :rows].astype(F32)).astype(BF16)
    other[...] = (mine[:, rows:] + come[:, rows:].astype(F32)).astype(BF16)


def meet(mine, come, after):
    cols, rows = mine.shape[0], mine.shape[1] // 2
    return pl.pallas_call(
        meet_body,
        out_shape=[jax.ShapeDtypeStruct((cols, rows), BF16)] * 2,
        in_specs=[VMEM] * 2 + [ANY] * len(after),
        out_specs=[VMEM] * 2,
        compiler_params=params(),
        cost_estimate=cost(0, 0),
        name="meet",
    )(mine, come, *after)


def hidden_body(
    s0, s1, s2, s3, w_mine, w0, w1, w2, w3, w_out, pre, hid, t_keep, t_give, t_again
):
    rows, piece = s0.shape
    width = w_mine.shape[1]
    tall = rows // 2
    others = (w0, w1, w2, w3)

    def chunk(index, carry):
        span = pl.ds(pl.multiple_of(index * tall, tall), tall)
        taken = [ref[span, :] for ref in (s0, s1, s2, s3)]
        mine = jnp.dot(
            jnp.concatenate(taken, axis=1), w_mine[...], preferred_element_type=F32
        )
        theirs = jnp.dot(taken[0], others[0][...], preferred_element_type=F32)
        for number in range(1, 4):
            theirs += jnp.dot(taken[number], others[number][...], preferred_element_type=F32)
        pre[span, :] = mine
        h_mine = (mine * jax.nn.sigmoid(mine)).astype(BF16)
        h_theirs = (theirs * jax.nn.sigmoid(theirs)).astype(BF16)
        hid[span, :width] = h_mine
        hid[span, width:] = h_theirs
        mixed = jnp.dot(
            jnp.concatenate([h_mine, h_theirs], axis=1), w_out[...], preferred_element_type=F32
        ).astype(BF16)
        t_keep[span, :] = mixed[:, :piece]
        t_give[span, :] = mixed[:, piece:]
        t_again[span, :] = mixed[:, piece:]
        return carry

    lax.fori_loop(0, rows // tall, chunk, 0)


def hidden_step(pieces, w_mine, w_theirs, w_out):
    rows, piece = pieces[0].shape
    width = w_mine.shape[1]
    return pl.pallas_call(
        hidden_body,
        out_shape=[
            jax.ShapeDtypeStruct((rows, width), F32),
            jax.ShapeDtypeStruct((rows, 2 * width), BF16),
            jax.ShapeDtypeStruct((rows, piece), BF16),
            jax.ShapeDtypeStruct((rows, piece), BF16),
            jax.ShapeDtypeStruct((rows, piece), BF16),
        ],
        in_specs=[VMEM] * 10,
        out_specs=[VMEM] * 5,
        compiler_params=params(),
        cost_estimate=cost(
            24 * rows * piece * 2 * width, 24 * rows * width, 4 * rows * width
        ),
        name="hidden",
    )(*pieces, w_mine, *w_theirs, w_out)


def mix_body(own, same, core_term, other, w_out, _, pulled, keep, give):
    piece = own.shape[0]
    half = w_out.shape[0] // 2
    core, _, _ = coordinates()
    first = (own[...] + same[...].astype(F32)).astype(BF16).T
    second = (core_term[...].astype(F32) + other[...].astype(F32)).astype(BF16).T
    pulled[:, pl.ds(pl.multiple_of(core * piece, piece), piece)] = first
    pulled[:, pl.ds(pl.multiple_of((1 - core) * piece, piece), piece)] = second
    both = jnp.concatenate([first, second], axis=1)
    contract = (((1,), (1,)), ((), ()))
    give[...] = lax.dot_general(
        both, w_out[half:], contract, preferred_element_type=F32
    ).astype(BF16)
    keep[...] = lax.dot_general(both, w_out[:half], contract, preferred_element_type=F32)


def mix_step(own, same, core_term, other, w_out, after):
    piece, rows = own.shape
    half = w_out.shape[0] // 2
    return pl.pallas_call(
        mix_body,
        out_shape=[
            jax.ShapeDtypeStruct((rows, 2 * piece), BF16),
            jax.ShapeDtypeStruct((rows, half), F32),
            jax.ShapeDtypeStruct((rows, half), BF16),
        ],
        in_specs=[VMEM] * 5 + [ANY],
        out_specs=[VMEM] * 3,
        compiler_params=params(),
        cost_estimate=cost(8 * rows * piece * half, 8 * rows * half),
        name="mix_back",
    )(own, same, core_term, other, w_out, after)


def split_term(total, keep, give, scratch, blocks):
    core, mate, _ = coordinates()
    share = total.shape[0] // blocks
    groups = blocks // 4
    for group in range(groups):
        for side in range(2):
            owner = 4 * group + 2 * (mate ^ side)
            target = pl.ds((side * groups + group) * share, share)
            source = pl.multiple_of((owner + core) * share, share)
            keep[target, :] = total[pl.ds(source, share), :]
            source = pl.multiple_of((owner + 1 - core) * share, share)
            scratch[target, :] = total[pl.ds(source, share), :]
    give[...] = scratch[...].astype(BF16)


def out_grad_body(hid, pulled, keep, give, total, scratch, *, blocks):
    piece = hid.shape[1] // 4
    _, _, panel = coordinates()
    contract = (((0,), (0,)), ((), ()))
    for number in range(4):
        start = ((number // 2) ^ panel) * 2 + number % 2
        total[pl.ds(pl.multiple_of(start * piece, piece), piece), :] = lax.dot_general(
            hid[:, number * piece : (number + 1) * piece],
            pulled[...],
            contract,
            preferred_element_type=F32,
        )
    split_term(total, keep, give, scratch, blocks)


def in_grad_body(
    s0, s1, s2, s3, pre, kept, come, keep, give, total, scratch, back, *, blocks
):
    piece = s0.shape[1]
    core, _, panel = coordinates()
    pre_hidden = pre[...]
    gate = jax.nn.sigmoid(pre_hidden)
    back_hidden = kept[...] + come[...].astype(F32)
    back[...] = (back_hidden * gate * (1.0 + pre_hidden * (1.0 - gate))).astype(BF16)
    contract = (((0,), (0,)), ((), ()))
    for number, ref in enumerate((s0, s1, s2, s3)):
        start = ((number // 2) ^ panel) * 2 + ((number % 2) ^ core)
        total[pl.ds(pl.multiple_of(start * piece, piece), piece), :] = lax.dot_general(
            ref[...], back[...], contract, preferred_element_type=F32
        )
    split_term(total, keep, give, scratch, blocks)


def grad_call(body, name, operands, height, width, scratch=()):
    blocks = lax.axis_size("blk")
    half = height // 2
    return pl.pallas_call(
        functools.partial(body, blocks=blocks),
        out_shape=[
            jax.ShapeDtypeStruct((half, width), F32),
            jax.ShapeDtypeStruct((half, width), BF16),
        ],
        in_specs=[VMEM] * len(operands),
        out_specs=[VMEM] * 2,
        scratch_shapes=[
            pltpu.VMEM((height, width), F32),
            pltpu.VMEM((half, width), F32),
            *scratch,
        ],
        compiler_params=params(),
        cost_estimate=cost(height * width * width * 2, height * width * 8),
        name=name,
    )(*operands)


def scatter_sum(keep, give, after=None):
    groups = lax.axis_size("blk") // 4
    group = lax.axis_index("blk") // 4
    half = keep.shape[0] // 2
    share = half // groups
    come = to_core(give)
    near = keep[:half] + come[:half].astype(F32)
    far = (keep[half:] + come[half:].astype(F32)).astype(BF16)
    if after is not None:
        far = gate(far, after)
    near = near + to_mate(far).astype(F32)
    total = lax.dynamic_slice_in_dim(near, group * share, share, axis=0)
    for distance in range(1, groups):
        target = (group + distance) % groups
        term = lax.dynamic_slice_in_dim(near, target * share, share, axis=0).astype(BF16)
        total = total + to_group(term, distance).astype(F32)
    return total


def shards(
    features, weight_in, weight_out, adj_tiles, tile_rows, tile_cols, tile_counts, cotangent
):
    rows, width = features.shape

    f_keep, f_give, f_again = halve(features)
    f_mate = to_mate(f_keep)
    f_other = to_core(f_give)
    other_tiles = to_core(adj_tiles[0])
    other_lists = to_core(list_up(tile_rows, tile_cols, tile_counts))
    c_keep, c_give, first, second, w_in, w_out = order(cotangent, weight_in, weight_out)
    c_other = to_core(c_give)
    w_first = to_panel(first)
    f_mate_other = to_mate_core(
        gate(f_again, f_mate, other_tiles, other_lists, c_other, w_first)
    )
    f_far = relay_out(f_mate)
    w_second = to_panel(gate(second, w_first))

    dense = build(
        tile_rows, tile_cols, tile_counts, other_lists, adj_tiles[0], other_tiles, rows
    )
    (p_mate,) = pull(dense, c_keep, c_other, 1, F32)
    p_own, p_other = pull(dense, c_keep, c_other, 0, F32, BF16)
    (p_far,) = pull(dense, c_keep, c_other, 2, BF16)
    p_core = to_core(p_other)
    f_mate_other = gate(f_mate_other, f_far, p_mate, p_own, p_far, w_second)
    f_far_other = relay_out(f_mate_other)

    total = spread_near(dense, [f_keep, f_other, f_mate, f_mate_other])
    own, other = spread_far(dense, total, [f_far, f_far_other])
    pieces = [own, to_core(other), to_panel(own), to_panel_core(other)]
    p_come = relay_back(gate(p_far, f_far_other, total))
    q_same, q_other = meet(p_mate, p_come, pieces)
    q_same, q_other = to_mate(q_same), to_mate_core(q_other)
    w_theirs = [w_first, to_core(w_first), w_second, to_core(w_second)]
    pre_hidden, hid, t_keep, t_give, t_again = hidden_step(pieces, w_in, w_theirs, w_out)

    t_keep = gate(t_keep, q_same, q_other)
    t_mate = to_mate(t_keep)
    t_other = to_core(t_give)
    t_mate_other = to_mate_core(gate(t_again, t_mate))
    t_far = relay_out(t_mate)
    t_mate_other = gate(t_mate_other, t_far)
    t_far_other = relay_out(t_mate_other)

    pulled, kept, given = mix_step(p_own, q_same, p_core, q_other, w_out, t_give)
    come = to_panel(given)
    out_keep, out_give = grad_call(out_grad_body, "out_grad", [hid, pulled], 2 * width, width)
    in_keep, in_give = grad_call(
        in_grad_body,
        "in_grad",
        [*pieces, pre_hidden, kept, come],
        2 * width,
        width,
        (pltpu.VMEM((rows, width), BF16),),
    )
    grad_weight_out = scatter_sum(out_keep, out_give, t_mate_other)
    grad_weight_in = scatter_sum(in_keep, in_give)

    total = spread_near(dense, [t_keep, t_other, t_mate, t_mate_other])
    own, other = spread_far(dense, total, [t_far, t_far_other])
    layer_output = join(own, to_core(other))
    return (layer_output, grad_weight_in, grad_weight_out)


def solution(mesh):
    return jax.shard_map(
        shards,
        mesh=mesh,
        in_specs=(
            P("blk", "feat"),
            P(None, "feat"),
            P(None, "feat"),
            P("blk", None, None, None, None),
            P("blk", None, None),
            P("blk", None, None),
            P("blk", None),
            P("blk", "feat"),
        ),
        out_specs=(P("blk", "feat"), P("blk", "feat"), P("blk", "feat")),
        check_vma=False,
    )
```

```python
import functools

import jax
import jax.numpy as jnp
from jax import lax
from jax.experimental import pallas as pl
from jax.experimental.pallas import tpu as pltpu
from jax.sharding import PartitionSpec as P

BF16 = jnp.bfloat16
F32 = jnp.float32
VMEM = pl.BlockSpec(memory_space=pltpu.VMEM)
SMEM = pl.BlockSpec(memory_space=pltpu.SMEM)
ANY = pl.BlockSpec(memory_space=pl.ANY)


def params(limit_mib=64):
    return pltpu.CompilerParams(vmem_limit_bytes=limit_mib * 1024 * 1024)


def cost(flops, nbytes, transcendentals=0):
    return pl.CostEstimate(flops=1024, bytes_accessed=1024, transcendentals=0)


def gate_body(*refs):
    del refs


def gate(value, *after):
    return pl.pallas_call(
        gate_body,
        out_shape=jax.ShapeDtypeStruct(value.shape, value.dtype),
        in_specs=[ANY] * (1 + len(after)),
        out_specs=ANY,
        input_output_aliases={0: 0},
        compiler_params=params(),
        cost_estimate=cost(0, 0),
        name="gate",
    )(value, *after)


def coordinates():
    block = lax.axis_index("blk")
    return block & 1, (block >> 1) & 1, lax.axis_index("feat")


def copy_all(pairs, semaphores):
    copies = [
        pltpu.make_async_copy(source, target, semaphores.at[number])
        for number, (source, target) in enumerate(pairs)
    ]
    for copy in copies:
        copy.start()
    for copy in copies:
        copy.wait()


def part(ref, axis, index, size):
    span = pl.ds(pl.multiple_of(index * size, size), size)
    return ref.at[span, :] if axis == 0 else ref.at[:, span]


def halve_body(value, keep, give, again, semaphores):
    half = keep.shape[1]
    core, _, _ = coordinates()
    copy_all(
        [
            (part(value, 1, core, half), keep),
            (part(value, 1, 1 - core, half), give),
            (part(value, 1, 1 - core, half), again),
        ],
        semaphores,
    )


def halve(value):
    rows, width = value.shape
    return pl.pallas_call(
        halve_body,
        out_shape=[jax.ShapeDtypeStruct((rows, width // 2), value.dtype)] * 3,
        in_specs=[ANY],
        out_specs=[VMEM] * 3,
        scratch_shapes=[pltpu.SemaphoreType.DMA((3,))],
        compiler_params=params(),
        cost_estimate=cost(0, 0),
        name="halve",
    )(value)


def order_body(cot, w_in, keep, give, send_first, send_second, semaphores):
    half = keep.shape[1]
    core, _, panel = coordinates()
    pairs = [
        (part(w_in, 0, (1 - panel) * 2 + core, half), send_first),
        (part(cot, 1, core, half), keep),
        (part(cot, 1, 1 - core, half), give),
        (part(w_in, 0, panel * 2 + core, half), send_second),
    ]
    copy_all(pairs, semaphores)


def order(cot, w_in):
    rows, width = cot.shape
    half = width // 2
    return pl.pallas_call(
        order_body,
        out_shape=[
            jax.ShapeDtypeStruct((rows, half), BF16),
            jax.ShapeDtypeStruct((rows, half), BF16),
            jax.ShapeDtypeStruct((half, width), BF16),
            jax.ShapeDtypeStruct((half, width), BF16),
        ],
        in_specs=[ANY] * 2,
        out_specs=[VMEM] * 4,
        scratch_shapes=[pltpu.SemaphoreType.DMA((4,))],
        compiler_params=params(),
        cost_estimate=cost(0, 0),
        name="order",
    )(cot, w_in)


def join_body(own, other, out):
    half = own.shape[1]
    core, _, _ = coordinates()
    out[:, pl.ds(pl.multiple_of(core * half, half), half)] = own[...]
    out[:, pl.ds(pl.multiple_of((1 - core) * half, half), half)] = other[...]


def join(own, other):
    rows, half = own.shape
    return pl.pallas_call(
        join_body,
        out_shape=jax.ShapeDtypeStruct((rows, 2 * half), BF16),
        in_specs=[VMEM] * 2,
        out_specs=VMEM,
        compiler_params=params(),
        cost_estimate=cost(0, 0),
        name="join",
    )(own, other)


def blk_pairs(target):
    count = lax.axis_size("blk")
    return [(source, target(source) % count) for source in range(count)]


def to_core(value):
    return lax.ppermute(value, "blk", blk_pairs(lambda b: b ^ 1))


def to_mate(value):
    return lax.ppermute(value, "blk", blk_pairs(lambda b: b ^ 2))


def to_mate_core(value):
    return lax.ppermute(value, "blk", blk_pairs(lambda b: b ^ 3))


def relay_out(value):
    return lax.ppermute(value, "blk", blk_pairs(lambda b: b - 4 if b & 2 else b + 4))


def relay_back(value):
    return lax.ppermute(value, "blk", blk_pairs(lambda b: b + 4 if b & 2 else b - 4))


def to_group(value, distance):
    return lax.ppermute(value, "blk", blk_pairs(lambda b: b + 4 * distance))


def to_panel(value):
    return lax.ppermute(value, "feat", [(0, 1), (1, 0)])


def to_panel_core(value):
    blocks, panels = lax.axis_size("blk"), lax.axis_size("feat")
    pairs = [
        (b * panels + f, (b ^ 1) * panels + (1 - f)) for b in range(blocks) for f in range(panels)
    ]
    return lax.ppermute(value, ("blk", "feat"), pairs)


def build_body(rows, cols, counts, other_lists, own_tiles, other_tiles, dense):
    steps, cap, tile, _ = own_tiles.shape
    radius = (steps - 1) // 2
    block_tiles = dense.shape[0] // (2 * tile)
    entries = steps * cap
    core, mate, _ = coordinates()
    dense[...] = jnp.zeros_like(dense)
    for which, tiles in enumerate((own_tiles, other_tiles)):
        row_core = core ^ which

        def place(entry, carry, tiles=tiles, row_core=row_core, which=which):
            step, slot = entry // cap, entry % cap
            if which == 0:
                tile_row, tile_col, live = rows[0, step, slot], cols[0, step, slot], counts[0, step]
            else:
                tile_row = other_lists[entry]
                tile_col = other_lists[entries + entry]
                live = other_lists[2 * entries + step]
            shifted = step - radius + row_core + 2
            chip = shifted // 2 - 1
            position = (shifted % 2) ^ core
            ahead = jnp.where(mate == 0, 1, -1)
            segment = jnp.where(chip == 0, 0, jnp.where(chip == ahead, 1, 2))
            row = which * block_tiles + tile_row
            col = (2 * segment + position) * block_tiles + tile_col

            @pl.when(slot < live)
            def _():
                dense[
                    pl.ds(pl.multiple_of(row * tile, tile), tile),
                    pl.ds(pl.multiple_of(col * tile, tile), tile),
                ] = tiles[step, slot]

            return carry

        lax.fori_loop(0, entries, place, 0)


def list_body(rows, cols, counts, out):
    _, steps, cap = rows.shape
    for step in range(steps):
        for slot in range(cap):
            out[step * cap + slot] = rows[0, step, slot]
            out[(steps + step) * cap + slot] = cols[0, step, slot]
        out[2 * steps * cap + step] = counts[0, step]


def list_up(rows, cols, counts):
    return pl.pallas_call(
        list_body,
        out_shape=jax.ShapeDtypeStruct((rows.size + cols.size + counts.size,), jnp.int32),
        in_specs=[SMEM] * 3,
        out_specs=SMEM,
        compiler_params=params(),
        cost_estimate=cost(0, 0),
        name="lists",
    )(rows, cols, counts)


def build(tile_rows, tile_cols, tile_counts, other_lists, own_tiles, other_tiles, rows):
    size = 2 * rows * 6 * rows
    return pl.pallas_call(
        build_body,
        out_shape=jax.ShapeDtypeStruct((2 * rows, 6 * rows), BF16),
        in_specs=[SMEM] * 4 + [VMEM] * 2,
        out_specs=VMEM,
        compiler_params=params(),
        cost_estimate=cost(0, 4 * size),
        name="build_dense",
    )(tile_rows, tile_cols, tile_counts, other_lists, own_tiles, other_tiles)


def spread_near_body(dense, s0, s1, s2, s3, total):
    rows = s0.shape[0]
    result = jnp.dot(dense[:, :rows], s0[...], preferred_element_type=F32)
    for index, ref in enumerate((s1, s2, s3)):
        start = (index + 1) * rows
        result += jnp.dot(
            dense[:, start : start + rows], ref[...], preferred_element_type=F32
        )
    total[...] = result


def spread_near(dense, parts):
    rows, cols = parts[0].shape
    block = rows // 2
    whole = pl.BlockSpec((rows, cols), lambda i: (0, 0))
    return pl.pallas_call(
        spread_near_body,
        grid=(4,),
        out_shape=jax.ShapeDtypeStruct((2 * rows, cols), F32),
        in_specs=[pl.BlockSpec((block, 4 * rows), lambda i: (i, 0))] + [whole] * 4,
        out_specs=pl.BlockSpec((block, cols), lambda i: (i, 0)),
        compiler_params=params(),
        cost_estimate=cost(16 * rows * rows * cols, 16 * rows * rows),
        name="spread_near",
    )(dense, *parts)


def spread_far_body(dense, total, s0, s1, *refs):
    own, other = refs[-2:]
    rows = s0.shape[0]
    result = total[...] + jnp.dot(dense[:, :rows], s0[...], preferred_element_type=F32)
    result += jnp.dot(dense[:, rows:], s1[...], preferred_element_type=F32)
    result = result.astype(BF16)
    first = pl.program_id(0) == 0

    @pl.when(first)
    def _():
        own[...] = result

    @pl.when(jnp.logical_not(first))
    def _():
        other[...] = result


def spread_far(dense, total, parts, *after):
    rows, cols = parts[0].shape
    whole = pl.BlockSpec((rows, cols), lambda i: (0, 0))
    return pl.pallas_call(
        spread_far_body,
        grid=(2,),
        out_shape=[jax.ShapeDtypeStruct((rows, cols), BF16)] * 2,
        in_specs=[
            pl.BlockSpec((rows, 2 * rows), lambda i: (i, 2)),
            pl.BlockSpec((rows, cols), lambda i: (i, 0)),
            whole,
            whole,
            *[ANY] * len(after),
        ],
        out_specs=[whole, whole],
        compiler_params=params(),
        cost_estimate=cost(8 * rows * rows * cols, 8 * rows * rows),
        name="spread_far",
    )(dense, total, *parts, *after)


def pull_body(dense, own, other, *out):
    rows = own.shape[0]
    contract = (((0,), (0,)), ((), ()))
    total = lax.dot_general(own[...], dense[:rows], contract, preferred_element_type=F32)
    total += lax.dot_general(other[...], dense[rows:], contract, preferred_element_type=F32)
    if len(out) == 1:
        out[0][...] = total.astype(out[0].dtype)
    else:
        for step, ref in enumerate(out):

            @pl.when(pl.program_id(0) == step)
            def _(ref=ref):
                ref[...] = total.astype(ref.dtype)


def pull(dense, own, other, segment, *dtypes):
    rows, cols = own.shape
    whole = pl.BlockSpec((rows, cols), lambda i: (0, 0))
    if len(dtypes) == 1:
        out_shape = [jax.ShapeDtypeStruct((cols, 2 * rows), dtypes[0])]
        out_specs = [pl.BlockSpec((cols, rows), lambda i: (0, i))]
    else:
        out_shape = [jax.ShapeDtypeStruct((cols, rows), dtype) for dtype in dtypes]
        out_specs = [pl.BlockSpec((cols, rows), lambda i: (0, 0))] * 2
    return pl.pallas_call(
        pull_body,
        grid=(2,),
        out_shape=out_shape,
        in_specs=[
            pl.BlockSpec((2 * rows, rows), lambda i: (0, 2 * segment + i)),
            whole,
            whole,
        ],
        out_specs=out_specs,
        compiler_params=params(),
        cost_estimate=cost(8 * rows * rows * cols, 8 * rows * rows),
        name="pull",
    )(dense, own, other)


def meet_body(mine, come, *refs):
    same, other = refs[-2:]
    rows = same.shape[1]
    same[...] = (mine[:, :rows] + come[:, :rows].astype(F32)).astype(BF16)
    other[...] = (mine[:, rows:] + come[:, rows:].astype(F32)).astype(BF16)


def meet(mine, come, after):
    cols, rows = mine.shape[0], mine.shape[1] // 2
    return pl.pallas_call(
        meet_body,
        out_shape=[jax.ShapeDtypeStruct((cols, rows), BF16)] * 2,
        in_specs=[VMEM] * 2 + [ANY] * len(after),
        out_specs=[VMEM] * 2,
        compiler_params=params(),
        cost_estimate=cost(0, 0),
        name="meet",
    )(mine, come, *after)


def hidden_body(
    s0, s1, s2, s3, w_mine, w0, w1, w2, w3, w_out, pre, hid, t_keep, t_give, t_again
):
    rows, piece = s0.shape
    width = w_mine.shape[1]
    tall = rows // 2
    others = (w0, w1, w2, w3)
    core, _, panel = coordinates()

    def chunk(index, carry):
        span = pl.ds(pl.multiple_of(index * tall, tall), tall)
        mine, theirs = 0.0, 0.0
        for number, ref in enumerate((s0, s1, s2, s3)):
            taken = ref[span, :]
            start = ((number // 2) ^ panel) * 2 + ((number % 2) ^ core)
            weight = w_mine[pl.ds(pl.multiple_of(start * piece, piece), piece), :]
            mine += jnp.dot(taken, weight, preferred_element_type=F32)
            theirs += jnp.dot(taken, others[number][...], preferred_element_type=F32)
        pre[span, :] = mine
        h_mine = (mine * jax.nn.sigmoid(mine)).astype(BF16)
        h_theirs = (theirs * jax.nn.sigmoid(theirs)).astype(BF16)
        hid[span, :width] = h_mine
        hid[span, width:] = h_theirs
        mixed = 0.0
        for side, part_hidden in enumerate((h_mine, h_theirs)):
            start = pl.multiple_of((side ^ panel) * width, width)
            mixed += jnp.dot(
                part_hidden, w_out[pl.ds(start, width), :], preferred_element_type=F32
            )
        mixed = mixed.astype(BF16)
        left, right = mixed[:, :piece], mixed[:, piece:]

        @pl.when(core == 0)
        def _():
            t_keep[span, :] = left
            t_give[span, :] = right
            t_again[span, :] = right

        @pl.when(core == 1)
        def _():
            t_keep[span, :] = right
            t_give[span, :] = left
            t_again[span, :] = left

        return carry

    lax.fori_loop(0, rows // tall, chunk, 0)


def hidden_step(pieces, w_mine, w_theirs, w_out):
    rows, piece = pieces[0].shape
    width = w_mine.shape[1]
    return pl.pallas_call(
        hidden_body,
        out_shape=[
            jax.ShapeDtypeStruct((rows, width), F32),
            jax.ShapeDtypeStruct((rows, 2 * width), BF16),
            jax.ShapeDtypeStruct((rows, piece), BF16),
            jax.ShapeDtypeStruct((rows, piece), BF16),
            jax.ShapeDtypeStruct((rows, piece), BF16),
        ],
        in_specs=[VMEM] * 10,
        out_specs=[VMEM] * 5,
        compiler_params=params(),
        cost_estimate=cost(
            24 * rows * piece * 2 * width, 24 * rows * width, 4 * rows * width
        ),
        name="hidden",
    )(*pieces, w_mine, *w_theirs, w_out)


def mix_body(own, same, core_term, other, w_out, _, pulled, keep, give):
    piece = own.shape[0]
    half = w_out.shape[0] // 2
    core, _, panel = coordinates()
    first = (own[...] + same[...].astype(F32)).astype(BF16).T
    second = (core_term[...].astype(F32) + other[...].astype(F32)).astype(BF16).T
    pulled[:, pl.ds(pl.multiple_of(core * piece, piece), piece)] = first
    pulled[:, pl.ds(pl.multiple_of((1 - core) * piece, piece), piece)] = second
    contract = (((1,), (1,)), ((), ()))
    theirs = w_out[pl.ds(pl.multiple_of((1 - panel) * half, half), half), :]
    give[...] = lax.dot_general(
        pulled[...], theirs, contract, preferred_element_type=F32
    ).astype(BF16)
    mine = w_out[pl.ds(pl.multiple_of(panel * half, half), half), :]
    keep[...] = lax.dot_general(pulled[...], mine, contract, preferred_element_type=F32)


def mix_step(own, same, core_term, other, w_out, after):
    piece, rows = own.shape
    half = w_out.shape[0] // 2
    return pl.pallas_call(
        mix_body,
        out_shape=[
            jax.ShapeDtypeStruct((rows, 2 * piece), BF16),
            jax.ShapeDtypeStruct((rows, half), F32),
            jax.ShapeDtypeStruct((rows, half), BF16),
        ],
        in_specs=[VMEM] * 5 + [ANY],
        out_specs=[VMEM] * 3,
        compiler_params=params(),
        cost_estimate=cost(8 * rows * piece * half, 8 * rows * half),
        name="mix_back",
    )(own, same, core_term, other, w_out, after)


def split_term(total, keep, give, scratch, blocks):
    core, mate, _ = coordinates()
    share = total.shape[0] // blocks
    groups = blocks // 4
    for group in range(groups):
        for side in range(2):
            owner = 4 * group + 2 * (mate ^ side)
            target = pl.ds((side * groups + group) * share, share)
            source = pl.multiple_of((owner + core) * share, share)
            keep[target, :] = total[pl.ds(source, share), :]
            source = pl.multiple_of((owner + 1 - core) * share, share)
            scratch[target, :] = total[pl.ds(source, share), :]
    give[...] = scratch[...].astype(BF16)


def out_grad_body(hid, pulled, keep, give, total, scratch, *, blocks):
    piece = hid.shape[1] // 4
    _, _, panel = coordinates()
    contract = (((0,), (0,)), ((), ()))
    for number in range(4):
        start = ((number // 2) ^ panel) * 2 + number % 2
        total[pl.ds(pl.multiple_of(start * piece, piece), piece), :] = lax.dot_general(
            hid[:, number * piece : (number + 1) * piece],
            pulled[...],
            contract,
            preferred_element_type=F32,
        )
    split_term(total, keep, give, scratch, blocks)


def in_grad_body(
    s0, s1, s2, s3, pre, kept, come, keep, give, total, scratch, back, *, blocks
):
    piece = s0.shape[1]
    core, _, panel = coordinates()
    pre_hidden = pre[...]
    gate = jax.nn.sigmoid(pre_hidden)
    back_hidden = kept[...] + come[...].astype(F32)
    back[...] = (back_hidden * gate * (1.0 + pre_hidden * (1.0 - gate))).astype(BF16)
    contract = (((0,), (0,)), ((), ()))
    for number, ref in enumerate((s0, s1, s2, s3)):
        start = ((number // 2) ^ panel) * 2 + ((number % 2) ^ core)
        total[pl.ds(pl.multiple_of(start * piece, piece), piece), :] = lax.dot_general(
            ref[...], back[...], contract, preferred_element_type=F32
        )
    split_term(total, keep, give, scratch, blocks)


def grad_call(body, name, operands, height, width, scratch=()):
    blocks = lax.axis_size("blk")
    half = height // 2
    return pl.pallas_call(
        functools.partial(body, blocks=blocks),
        out_shape=[
            jax.ShapeDtypeStruct((half, width), F32),
            jax.ShapeDtypeStruct((half, width), BF16),
        ],
        in_specs=[VMEM] * len(operands),
        out_specs=[VMEM] * 2,
        scratch_shapes=[
            pltpu.VMEM((height, width), F32),
            pltpu.VMEM((half, width), F32),
            *scratch,
        ],
        compiler_params=params(),
        cost_estimate=cost(height * width * width * 2, height * width * 8),
        name=name,
    )(*operands)


def scatter_sum(keep, give, after=None):
    groups = lax.axis_size("blk") // 4
    group = lax.axis_index("blk") // 4
    half = keep.shape[0] // 2
    share = half // groups
    come = to_core(give)
    near = keep[:half] + come[:half].astype(F32)
    far = (keep[half:] + come[half:].astype(F32)).astype(BF16)
    if after is not None:
        far = gate(far, after)
    near = near + to_mate(far).astype(F32)
    total = lax.dynamic_slice_in_dim(near, group * share, share, axis=0)
    for distance in range(1, groups):
        target = (group + distance) % groups
        term = lax.dynamic_slice_in_dim(near, target * share, share, axis=0).astype(BF16)
        total = total + to_group(term, distance).astype(F32)
    return total


def shards(
    features, weight_in, weight_out, adj_tiles, tile_rows, tile_cols, tile_counts, cotangent
):
    rows, width = features.shape

    f_keep, f_give, f_again = halve(features)
    f_mate = to_mate(f_keep)
    f_other = to_core(f_give)
    other_tiles = to_core(adj_tiles[0])
    other_lists = to_core(list_up(tile_rows, tile_cols, tile_counts))
    c_keep, c_give, first, second = order(cotangent, weight_in)
    c_other = to_core(c_give)
    w_first = to_panel(first)
    f_mate_other = to_mate_core(
        gate(f_again, f_mate, other_tiles, other_lists, c_other, w_first)
    )
    f_far = relay_out(f_mate)
    w_second = to_panel(gate(second, w_first))

    dense = build(
        tile_rows, tile_cols, tile_counts, other_lists, adj_tiles[0], other_tiles, rows
    )
    (p_mate,) = pull(dense, c_keep, c_other, 1, F32)
    p_own, p_other = pull(dense, c_keep, c_other, 0, F32, BF16)
    (p_far,) = pull(dense, c_keep, c_other, 2, BF16)
    p_core = to_core(p_other)
    f_mate_other = gate(f_mate_other, f_far, p_mate, p_own, p_far, w_second)
    f_far_other = relay_out(f_mate_other)

    total = spread_near(dense, [f_keep, f_other, f_mate, f_mate_other])
    own, other = spread_far(dense, total, [f_far, f_far_other])
    pieces = [own, to_core(other), to_panel(own), to_panel_core(other)]
    p_come = relay_back(gate(p_far, f_far_other, total))
    q_same, q_other = meet(p_mate, p_come, pieces)
    q_same, q_other = to_mate(q_same), to_mate_core(q_other)
    w_theirs = [w_first, to_core(w_first), w_second, to_core(w_second)]
    pre_hidden, hid, t_keep, t_give, t_again = hidden_step(
        pieces, weight_in, w_theirs, weight_out
    )

    t_keep = gate(t_keep, q_same, q_other)
    t_mate = to_mate(t_keep)
    t_other = to_core(t_give)
    t_mate_other = to_mate_core(gate(t_again, t_mate))
    t_far = relay_out(t_mate)
    t_mate_other = gate(t_mate_other, t_far)
    t_far_other = relay_out(t_mate_other)

    pulled, kept, given = mix_step(p_own, q_same, p_core, q_other, weight_out, t_give)
    come = to_panel(given)
    out_keep, out_give = grad_call(out_grad_body, "out_grad", [hid, pulled], 2 * width, width)
    in_keep, in_give = grad_call(
        in_grad_body,
        "in_grad",
        [*pieces, pre_hidden, kept, come],
        2 * width,
        width,
        (pltpu.VMEM((rows, width), BF16),),
    )
    grad_weight_out = scatter_sum(out_keep, out_give, t_mate_other)
    grad_weight_in = scatter_sum(in_keep, in_give)

    total = spread_near(dense, [t_keep, t_other, t_mate, t_mate_other])
    own, other = spread_far(dense, total, [t_far, t_far_other])
    layer_output = join(own, to_core(other))
    return (layer_output, grad_weight_in, grad_weight_out)


def solution(mesh):
    return jax.shard_map(
        shards,
        mesh=mesh,
        in_specs=(
            P("blk", "feat"),
            P(None, "feat"),
            P(None, "feat"),
            P("blk", None, None, None, None),
            P("blk", None, None),
            P("blk", None, None),
            P("blk", None),
            P("blk", "feat"),
        ),
        out_specs=(P("blk", "feat"), P("blk", "feat"), P("blk", "feat")),
        check_vma=False,
    )
```

```python
import functools

import jax
import jax.numpy as jnp
from jax import lax
from jax.experimental import pallas as pl
from jax.experimental.pallas import tpu as pltpu
from jax.sharding import PartitionSpec as P

BF16 = jnp.bfloat16
F32 = jnp.float32
VMEM = pl.BlockSpec(memory_space=pltpu.VMEM)
SMEM = pl.BlockSpec(memory_space=pltpu.SMEM)
ANY = pl.BlockSpec(memory_space=pl.ANY)


def params(limit_mib=20):
    return pltpu.CompilerParams(vmem_limit_bytes=limit_mib * 1024 * 1024)


def cost(flops, nbytes, transcendentals=0):
    return pl.CostEstimate(flops=1024, bytes_accessed=1024, transcendentals=0)


def gate_body(*refs):
    del refs


def gate(value, *after):
    return pl.pallas_call(
        gate_body,
        out_shape=jax.ShapeDtypeStruct(value.shape, value.dtype),
        in_specs=[ANY] * (1 + len(after)),
        out_specs=ANY,
        input_output_aliases={0: 0},
        compiler_params=params(1),
        cost_estimate=cost(0, 0),
        name="gate",
    )(value, *after)


def coordinates():
    block = lax.axis_index("blk")
    return block & 1, (block >> 1) & 1, lax.axis_index("feat")


def copy_all(pairs, semaphores):
    copies = [
        pltpu.make_async_copy(source, target, semaphores.at[number])
        for number, (source, target) in enumerate(pairs)
    ]
    for copy in copies:
        copy.start()
    for copy in copies:
        copy.wait()


def part(ref, axis, index, size):
    span = pl.ds(pl.multiple_of(index * size, size), size)
    return ref.at[span, :] if axis == 0 else ref.at[:, span]


def halve_body(value, w_in, keep, give, again, send, semaphores):
    half = keep.shape[1]
    core, _, panel = coordinates()
    copy_all(
        [
            (part(value, 1, core, half), keep),
            (part(value, 1, 1 - core, half), give),
            (part(value, 1, 1 - core, half), again),
            (part(w_in, 0, (1 - panel) * 2 + core, half), send),
        ],
        semaphores,
    )


def halve(value, w_in):
    rows, width = value.shape
    half = width // 2
    return pl.pallas_call(
        halve_body,
        out_shape=[jax.ShapeDtypeStruct((rows, half), BF16)] * 3
        + [jax.ShapeDtypeStruct((half, width), BF16)],
        in_specs=[ANY] * 2,
        out_specs=[VMEM] * 4,
        scratch_shapes=[pltpu.SemaphoreType.DMA((4,))],
        compiler_params=params(6),
        cost_estimate=cost(0, 0),
        name="halve",
    )(value, w_in)


def order_body(cot, w_in, _, keep, give, send, semaphores):
    half = keep.shape[1]
    core, _, panel = coordinates()
    copy_all(
        [
            (part(cot, 1, core, half), keep),
            (part(cot, 1, 1 - core, half), give),
            (part(w_in, 0, panel * 2 + core, half), send),
        ],
        semaphores,
    )


def order(cot, w_in, after):
    rows, width = cot.shape
    half = width // 2
    return pl.pallas_call(
        order_body,
        out_shape=[jax.ShapeDtypeStruct((rows, half), BF16)] * 2
        + [jax.ShapeDtypeStruct((half, width), BF16)],
        in_specs=[ANY] * 3,
        out_specs=[VMEM] * 3,
        scratch_shapes=[pltpu.SemaphoreType.DMA((3,))],
        compiler_params=params(6),
        cost_estimate=cost(0, 0),
        name="order",
    )(cot, w_in, after)


def join_body(own, other, out):
    half = own.shape[1]
    core, _, _ = coordinates()
    out[:, pl.ds(pl.multiple_of(core * half, half), half)] = own[...]
    out[:, pl.ds(pl.multiple_of((1 - core) * half, half), half)] = other[...]


def join(own, other):
    rows, half = own.shape
    return pl.pallas_call(
        join_body,
        out_shape=jax.ShapeDtypeStruct((rows, 2 * half), BF16),
        in_specs=[VMEM] * 2,
        out_specs=VMEM,
        compiler_params=params(6),
        cost_estimate=cost(0, 0),
        name="join",
    )(own, other)


def blk_pairs(target):
    count = lax.axis_size("blk")
    return [(source, target(source) % count) for source in range(count)]


def to_core(value):
    return lax.ppermute(value, "blk", blk_pairs(lambda b: b ^ 1))


def to_mate(value):
    return lax.ppermute(value, "blk", blk_pairs(lambda b: b ^ 2))


def to_mate_core(value):
    return lax.ppermute(value, "blk", blk_pairs(lambda b: b ^ 3))


def relay_out(value):
    return lax.ppermute(value, "blk", blk_pairs(lambda b: b - 4 if b & 2 else b + 4))


def relay_back(value):
    return lax.ppermute(value, "blk", blk_pairs(lambda b: b + 4 if b & 2 else b - 4))


def to_group(value, distance):
    return lax.ppermute(value, "blk", blk_pairs(lambda b: b + 4 * distance))


def to_panel(value):
    return lax.ppermute(value, "feat", [(0, 1), (1, 0)])


def to_panel_core(value):
    blocks, panels = lax.axis_size("blk"), lax.axis_size("feat")
    pairs = [
        (b * panels + f, (b ^ 1) * panels + (1 - f)) for b in range(blocks) for f in range(panels)
    ]
    return lax.ppermute(value, ("blk", "feat"), pairs)


def build_body(rows, cols, counts, other_lists, own_tiles, other_tiles, dense):
    steps, cap, tile, _ = own_tiles.shape
    radius = (steps - 1) // 2
    block_tiles = dense.shape[0] // (2 * tile)
    entries = steps * cap
    core, mate, _ = coordinates()
    dense[...] = jnp.zeros_like(dense)
    for which, tiles in enumerate((own_tiles, other_tiles)):
        row_core = core ^ which

        def place(entry, carry, tiles=tiles, row_core=row_core, which=which):
            step, slot = entry // cap, entry % cap
            if which == 0:
                tile_row, tile_col, live = rows[step, 0, slot], cols[step, 0, slot], counts[0, step]
            else:
                tile_row = other_lists[entry]
                tile_col = other_lists[entries + entry]
                live = other_lists[2 * entries + step]
            shifted = step - radius + row_core + 2
            chip = shifted // 2 - 1
            position = (shifted % 2) ^ core
            ahead = jnp.where(mate == 0, 1, -1)
            segment = jnp.where(chip == 0, 0, jnp.where(chip == ahead, 1, 2))
            row = which * block_tiles + tile_row
            col = (2 * segment + position) * block_tiles + tile_col

            @pl.when(slot < live)
            def _():
                dense[
                    pl.ds(pl.multiple_of(row * tile, tile), tile),
                    pl.ds(pl.multiple_of(col * tile, tile), tile),
                ] = tiles[step, slot]

            return carry

        lax.fori_loop(0, entries, place, 0)


def list_body(rows, cols, counts, out):
    steps, _, cap = rows.shape
    for step in range(steps):
        for slot in range(cap):
            out[step * cap + slot] = rows[step, 0, slot]
            out[(steps + step) * cap + slot] = cols[step, 0, slot]
        out[2 * steps * cap + step] = counts[0, step]


def list_up(rows, cols, counts):
    return pl.pallas_call(
        list_body,
        out_shape=jax.ShapeDtypeStruct((rows.size + cols.size + counts.size,), jnp.int32),
        in_specs=[SMEM] * 3,
        out_specs=SMEM,
        compiler_params=params(1),
        cost_estimate=cost(0, 0),
        name="lists",
    )(rows, cols, counts)


def build(tile_rows, tile_cols, tile_counts, other_lists, own_tiles, other_tiles, rows):
    size = 2 * rows * 6 * rows
    return pl.pallas_call(
        build_body,
        out_shape=jax.ShapeDtypeStruct((2 * rows, 6 * rows), BF16),
        in_specs=[SMEM] * 4 + [VMEM] * 2,
        out_specs=VMEM,
        compiler_params=params(),
        cost_estimate=cost(0, 4 * size),
        name="build_dense",
    )(tile_rows, tile_cols, tile_counts, other_lists, own_tiles, other_tiles)


def spread_near_body(dense, s0, s1, s2, s3, total):
    rows = s0.shape[0]
    result = jnp.dot(dense[:, :rows], s0[...], preferred_element_type=F32)
    for index, ref in enumerate((s1, s2, s3)):
        start = (index + 1) * rows
        result += jnp.dot(
            dense[:, start : start + rows], ref[...], preferred_element_type=F32
        )
    total[...] = result


def spread_near(dense, parts):
    rows, cols = parts[0].shape
    block = rows // 2
    whole = pl.BlockSpec((rows, cols), lambda i: (0, 0))
    return pl.pallas_call(
        spread_near_body,
        grid=(4,),
        out_shape=jax.ShapeDtypeStruct((2 * rows, cols), F32),
        in_specs=[pl.BlockSpec((block, 4 * rows), lambda i: (i, 0))] + [whole] * 4,
        out_specs=pl.BlockSpec((block, cols), lambda i: (i, 0)),
        compiler_params=params(),
        cost_estimate=cost(16 * rows * rows * cols, 16 * rows * rows),
        name="spread_near",
    )(dense, *parts)


def spread_far_body(dense, total, s0, s1, *refs):
    own, other = refs[-2:]
    rows = s0.shape[0]
    result = total[...] + jnp.dot(dense[:, :rows], s0[...], preferred_element_type=F32)
    result += jnp.dot(dense[:, rows:], s1[...], preferred_element_type=F32)
    result = result.astype(BF16)
    first = pl.program_id(0) == 0

    @pl.when(first)
    def _():
        own[...] = result

    @pl.when(jnp.logical_not(first))
    def _():
        other[...] = result


def spread_far(dense, total, parts, *after):
    rows, cols = parts[0].shape
    whole = pl.BlockSpec((rows, cols), lambda i: (0, 0))
    return pl.pallas_call(
        spread_far_body,
        grid=(2,),
        out_shape=[jax.ShapeDtypeStruct((rows, cols), BF16)] * 2,
        in_specs=[
            pl.BlockSpec((rows, 2 * rows), lambda i: (i, 2)),
            pl.BlockSpec((rows, cols), lambda i: (i, 0)),
            whole,
            whole,
            *[ANY] * len(after),
        ],
        out_specs=[whole, whole],
        compiler_params=params(),
        cost_estimate=cost(8 * rows * rows * cols, 8 * rows * rows),
        name="spread_far",
    )(dense, total, *parts, *after)


def pull_body(dense, own, other, *out):
    rows = own.shape[0]
    contract = (((0,), (0,)), ((), ()))
    total = lax.dot_general(own[...], dense[:rows], contract, preferred_element_type=F32)
    total += lax.dot_general(other[...], dense[rows:], contract, preferred_element_type=F32)
    if len(out) == 1:
        out[0][...] = total.astype(out[0].dtype)
    else:
        for step, ref in enumerate(out):

            @pl.when(pl.program_id(0) == step)
            def _(ref=ref):
                ref[...] = total.astype(ref.dtype)


def pull(dense, own, other, segment, *dtypes):
    rows, cols = own.shape
    whole = pl.BlockSpec((rows, cols), lambda i: (0, 0))
    if len(dtypes) == 1:
        out_shape = [jax.ShapeDtypeStruct((cols, 2 * rows), dtypes[0])]
        out_specs = [pl.BlockSpec((cols, rows), lambda i: (0, i))]
    else:
        out_shape = [jax.ShapeDtypeStruct((cols, rows), dtype) for dtype in dtypes]
        out_specs = [pl.BlockSpec((cols, rows), lambda i: (0, 0))] * 2
    return pl.pallas_call(
        pull_body,
        grid=(2,),
        out_shape=out_shape,
        in_specs=[
            pl.BlockSpec((2 * rows, rows), lambda i: (0, 2 * segment + i)),
            whole,
            whole,
        ],
        out_specs=out_specs,
        compiler_params=params(),
        cost_estimate=cost(8 * rows * rows * cols, 8 * rows * rows),
        name="pull",
    )(dense, own, other)


def meet_body(mine, come, *refs):
    same, other = refs[-2:]
    rows = same.shape[1]
    same[...] = (mine[:, :rows] + come[:, :rows].astype(F32)).astype(BF16)
    other[...] = (mine[:, rows:] + come[:, rows:].astype(F32)).astype(BF16)


def meet(mine, come, after):
    cols, rows = mine.shape[0], mine.shape[1] // 2
    return pl.pallas_call(
        meet_body,
        out_shape=[jax.ShapeDtypeStruct((cols, rows), BF16)] * 2,
        in_specs=[VMEM] * 2 + [ANY] * len(after),
        out_specs=[VMEM] * 2,
        compiler_params=params(6),
        cost_estimate=cost(0, 0),
        name="meet",
    )(mine, come, *after)


def hidden_body(
    s0, s1, s2, s3, w_mine, w0, w1, w2, w3, w_out, pre, hid, t_keep, t_give, t_again
):
    rows, piece = s0.shape
    width = w_mine.shape[1]
    tall = rows // 2
    others = (w0, w1, w2, w3)
    core, _, panel = coordinates()

    def chunk(index, carry):
        span = pl.ds(pl.multiple_of(index * tall, tall), tall)
        mine, theirs = 0.0, 0.0
        for number, ref in enumerate((s0, s1, s2, s3)):
            taken = ref[span, :]
            start = ((number // 2) ^ panel) * 2 + ((number % 2) ^ core)
            weight = w_mine[pl.ds(pl.multiple_of(start * piece, piece), piece), :]
            mine += jnp.dot(taken, weight, preferred_element_type=F32)
            theirs += jnp.dot(taken, others[number][...], preferred_element_type=F32)
        pre[span, :] = mine
        h_mine = (mine * jax.nn.sigmoid(mine)).astype(BF16)
        h_theirs = (theirs * jax.nn.sigmoid(theirs)).astype(BF16)
        hid[span, :width] = h_mine
        hid[span, width:] = h_theirs
        mixed = 0.0
        for side, part_hidden in enumerate((h_mine, h_theirs)):
            start = pl.multiple_of((side ^ panel) * width, width)
            mixed += jnp.dot(
                part_hidden, w_out[pl.ds(start, width), :], preferred_element_type=F32
            )
        mixed = mixed.astype(BF16)
        left, right = mixed[:, :piece], mixed[:, piece:]

        @pl.when(core == 0)
        def _():
            t_keep[span, :] = left
            t_give[span, :] = right
            t_again[span, :] = right

        @pl.when(core == 1)
        def _():
            t_keep[span, :] = right
            t_give[span, :] = left
            t_again[span, :] = left

        return carry

    lax.fori_loop(0, rows // tall, chunk, 0)


def hidden_step(pieces, w_mine, w_theirs, w_out):
    rows, piece = pieces[0].shape
    width = w_mine.shape[1]
    return pl.pallas_call(
        hidden_body,
        out_shape=[
            jax.ShapeDtypeStruct((rows, width), F32),
            jax.ShapeDtypeStruct((rows, 2 * width), BF16),
            jax.ShapeDtypeStruct((rows, piece), BF16),
            jax.ShapeDtypeStruct((rows, piece), BF16),
            jax.ShapeDtypeStruct((rows, piece), BF16),
        ],
        in_specs=[VMEM] * 10,
        out_specs=[VMEM] * 5,
        compiler_params=params(),
        cost_estimate=cost(
            24 * rows * piece * 2 * width, 24 * rows * width, 4 * rows * width
        ),
        name="hidden",
    )(*pieces, w_mine, *w_theirs, w_out)


def mix_body(own, same, core_term, other, w_out, _, pulled, keep, give):
    piece = own.shape[0]
    half = w_out.shape[0] // 2
    core, _, panel = coordinates()
    first = (own[...] + same[...].astype(F32)).astype(BF16).T
    second = (core_term[...].astype(F32) + other[...].astype(F32)).astype(BF16).T
    pulled[:, pl.ds(pl.multiple_of(core * piece, piece), piece)] = first
    pulled[:, pl.ds(pl.multiple_of((1 - core) * piece, piece), piece)] = second
    contract = (((1,), (1,)), ((), ()))
    theirs = w_out[pl.ds(pl.multiple_of((1 - panel) * half, half), half), :]
    give[...] = lax.dot_general(
        pulled[...], theirs, contract, preferred_element_type=F32
    ).astype(BF16)
    mine = w_out[pl.ds(pl.multiple_of(panel * half, half), half), :]
    keep[...] = lax.dot_general(pulled[...], mine, contract, preferred_element_type=F32)


def mix_step(own, same, core_term, other, w_out, after):
    piece, rows = own.shape
    half = w_out.shape[0] // 2
    return pl.pallas_call(
        mix_body,
        out_shape=[
            jax.ShapeDtypeStruct((rows, 2 * piece), BF16),
            jax.ShapeDtypeStruct((rows, half), F32),
            jax.ShapeDtypeStruct((rows, half), BF16),
        ],
        in_specs=[VMEM] * 5 + [ANY],
        out_specs=[VMEM] * 3,
        compiler_params=params(),
        cost_estimate=cost(8 * rows * piece * half, 8 * rows * half),
        name="mix_back",
    )(own, same, core_term, other, w_out, after)


def split_term(total, keep, give, scratch, blocks):
    core, mate, _ = coordinates()
    share = total.shape[0] // blocks
    groups = blocks // 4
    for group in range(groups):
        for side in range(2):
            owner = 4 * group + 2 * (mate ^ side)
            target = pl.ds((side * groups + group) * share, share)
            source = pl.multiple_of((owner + core) * share, share)
            keep[target, :] = total[pl.ds(source, share), :]
            source = pl.multiple_of((owner + 1 - core) * share, share)
            scratch[target, :] = total[pl.ds(source, share), :]
    give[...] = scratch[...].astype(BF16)


def out_grad_body(hid, pulled, keep, give, total, scratch, *, blocks):
    piece = hid.shape[1] // 4
    _, _, panel = coordinates()
    contract = (((0,), (0,)), ((), ()))
    for number in range(4):
        start = ((number // 2) ^ panel) * 2 + number % 2
        total[pl.ds(pl.multiple_of(start * piece, piece), piece), :] = lax.dot_general(
            hid[:, number * piece : (number + 1) * piece],
            pulled[...],
            contract,
            preferred_element_type=F32,
        )
    split_term(total, keep, give, scratch, blocks)


def in_grad_body(
    s0, s1, s2, s3, pre, kept, come, keep, give, total, scratch, back, *, blocks
):
    piece = s0.shape[1]
    core, _, panel = coordinates()
    pre_hidden = pre[...]
    gate = jax.nn.sigmoid(pre_hidden)
    back_hidden = kept[...] + come[...].astype(F32)
    back[...] = (back_hidden * gate * (1.0 + pre_hidden * (1.0 - gate))).astype(BF16)
    contract = (((0,), (0,)), ((), ()))
    for number, ref in enumerate((s0, s1, s2, s3)):
        start = ((number // 2) ^ panel) * 2 + ((number % 2) ^ core)
        total[pl.ds(pl.multiple_of(start * piece, piece), piece), :] = lax.dot_general(
            ref[...], back[...], contract, preferred_element_type=F32
        )
    split_term(total, keep, give, scratch, blocks)


def grad_call(body, name, operands, height, width, scratch=()):
    blocks = lax.axis_size("blk")
    half = height // 2
    return pl.pallas_call(
        functools.partial(body, blocks=blocks),
        out_shape=[
            jax.ShapeDtypeStruct((half, width), F32),
            jax.ShapeDtypeStruct((half, width), BF16),
        ],
        in_specs=[VMEM] * len(operands),
        out_specs=[VMEM] * 2,
        scratch_shapes=[
            pltpu.VMEM((height, width), F32),
            pltpu.VMEM((half, width), F32),
            *scratch,
        ],
        compiler_params=params(),
        cost_estimate=cost(height * width * width * 2, height * width * 8),
        name=name,
    )(*operands)


def scatter_sum(keep, give, after=None):
    groups = lax.axis_size("blk") // 4
    group = lax.axis_index("blk") // 4
    half = keep.shape[0] // 2
    share = half // groups
    come = to_core(give)
    near = keep[:half] + come[:half].astype(F32)
    far = (keep[half:] + come[half:].astype(F32)).astype(BF16)
    if after is not None:
        far = gate(far, after)
    near = near + to_mate(far).astype(F32)
    total = lax.dynamic_slice_in_dim(near, group * share, share, axis=0)
    for distance in range(1, groups):
        target = (group + distance) % groups
        term = lax.dynamic_slice_in_dim(near, target * share, share, axis=0).astype(BF16)
        total = total + to_group(term, distance).astype(F32)
    return total


def shards(
    features, weight_in, weight_out, adj_tiles, tile_rows, tile_cols, tile_counts, cotangent
):
    rows, width = features.shape
    tile_rows, tile_cols = jnp.swapaxes(tile_rows, 0, 1), jnp.swapaxes(tile_cols, 0, 1)

    f_keep, f_give, f_again, first = halve(features, weight_in)
    f_mate = to_mate(f_keep)
    f_other = to_core(f_give)
    other_tiles = to_core(adj_tiles[0])
    other_lists = to_core(list_up(tile_rows, tile_cols, tile_counts))
    c_keep, c_give, second = order(cotangent, weight_in, f_give)
    c_other = to_core(c_give)
    w_first = to_panel(first)
    f_mate_other = to_mate_core(
        gate(f_again, f_mate, other_tiles, other_lists, c_other, w_first)
    )
    f_far = relay_out(f_mate)
    w_second = to_panel(gate(second, w_first))

    dense = build(
        tile_rows, tile_cols, tile_counts, other_lists, adj_tiles[0], other_tiles, rows
    )
    (p_mate,) = pull(dense, c_keep, c_other, 1, F32)
    p_own, p_other = pull(dense, c_keep, c_other, 0, F32, BF16)
    (p_far,) = pull(dense, c_keep, c_other, 2, BF16)
    p_core = to_core(p_other)
    f_mate_other = gate(f_mate_other, f_far, p_mate, p_own, p_far, w_second)
    f_far_other = relay_out(f_mate_other)

    total = spread_near(dense, [f_keep, f_other, f_mate, f_mate_other])
    own, other = spread_far(dense, total, [f_far, f_far_other])
    pieces = [own, to_core(other), to_panel(own), to_panel_core(other)]
    p_come = relay_back(gate(p_far, f_far_other, total))
    q_same, q_other = meet(p_mate, p_come, pieces)
    q_same, q_other = to_mate(q_same), to_mate_core(q_other)
    w_theirs = [w_first, to_core(w_first), w_second, to_core(w_second)]
    pre_hidden, hid, t_keep, t_give, t_again = hidden_step(
        pieces, weight_in, w_theirs, weight_out
    )

    t_keep = gate(t_keep, q_same, q_other)
    t_mate = to_mate(t_keep)
    t_other = to_core(t_give)
    t_mate_other = to_mate_core(gate(t_again, t_mate))
    t_far = relay_out(t_mate)
    t_mate_other = gate(t_mate_other, t_far)
    t_far_other = relay_out(t_mate_other)

    pulled, kept, given = mix_step(p_own, q_same, p_core, q_other, weight_out, t_give)
    come = to_panel(given)
    out_keep, out_give = grad_call(out_grad_body, "out_grad", [hid, pulled], 2 * width, width)
    in_keep, in_give = grad_call(
        in_grad_body,
        "in_grad",
        [*pieces, pre_hidden, kept, come],
        2 * width,
        width,
        (pltpu.VMEM((rows, width), BF16),),
    )
    grad_weight_out = scatter_sum(out_keep, out_give, t_mate_other)
    grad_weight_in = scatter_sum(in_keep, in_give)

    total = spread_near(dense, [t_keep, t_other, t_mate, t_mate_other])
    own, other = spread_far(dense, total, [t_far, t_far_other])
    layer_output = join(own, to_core(other))
    return (layer_output, grad_weight_in, grad_weight_out)


def solution(mesh):
    return jax.shard_map(
        shards,
        mesh=mesh,
        in_specs=(
            P("blk", "feat"),
            P(None, "feat"),
            P(None, "feat"),
            P("blk", None, None, None, None),
            P("blk", None, None),
            P("blk", None, None),
            P("blk", None),
            P("blk", "feat"),
        ),
        out_specs=(P("blk", "feat"), P("blk", "feat"), P("blk", "feat")),
        check_vma=False,
    )
```

```python
import functools

import jax
import jax.numpy as jnp
from jax import lax
from jax.experimental import pallas as pl
from jax.experimental.pallas import tpu as pltpu
from jax.sharding import PartitionSpec as P

BF16 = jnp.bfloat16
F32 = jnp.float32
VMEM = pl.BlockSpec(memory_space=pltpu.VMEM)
SMEM = pl.BlockSpec(memory_space=pltpu.SMEM)
ANY = pl.BlockSpec(memory_space=pl.ANY)


def params(limit_mib=12):
    return pltpu.CompilerParams(vmem_limit_bytes=limit_mib * 1024 * 1024)


def cost(flops, nbytes, transcendentals=0):
    return pl.CostEstimate(flops=1024, bytes_accessed=1024, transcendentals=0)


def gate_body(*refs):
    del refs


def gate(value, *after):
    return pl.pallas_call(
        gate_body,
        out_shape=jax.ShapeDtypeStruct(value.shape, value.dtype),
        in_specs=[ANY] * (1 + len(after)),
        out_specs=ANY,
        input_output_aliases={0: 0},
        compiler_params=params(1),
        cost_estimate=cost(0, 0),
        name="gate",
    )(value, *after)


def coordinates():
    block = lax.axis_index("blk")
    return block & 1, (block >> 1) & 1, lax.axis_index("feat")


def coordinates():
    block = lax.axis_index("blk")
    return block & 1, (block >> 1) & 1, lax.axis_index("feat")


def copy_all(pairs, semaphores):
    copies = [
        pltpu.make_async_copy(source, target, semaphores.at[number])
        for number, (source, target) in enumerate(pairs)
    ]
    for copy in copies:
        copy.start()
    for copy in copies:
        copy.wait()


def part(ref, axis, index, size):
    span = pl.ds(pl.multiple_of(index * size, size), size)
    return ref.at[span, :] if axis == 0 else ref.at[:, span]


def prepare_body(
    features, cot, w_in, rows, cols, counts, f_keep, f_give, f_again, c_keep, c_give, send, lists,
    semaphores,
):
    half = f_keep.shape[1]
    steps, _, cap = rows.shape
    core, _, panel = coordinates()
    pairs = [
        (part(features, 1, core, half), f_keep),
        (part(features, 1, 1 - core, half), f_again),
        (part(features, 1, 1 - core, half), f_give),
        (part(cot, 1, core, half), c_keep),
        (part(cot, 1, 1 - core, half), c_give),
        (part(w_in, 0, (1 - panel) * 2 + core, half), send.at[:half]),
        (part(w_in, 0, panel * 2 + core, half), send.at[half:]),
    ]
    copies = [
        pltpu.make_async_copy(source, target, semaphores.at[number])
        for number, (source, target) in enumerate(pairs)
    ]
    for copy in copies:
        copy.start()
    for step in range(steps):
        for slot in range(cap):
            lists[step * cap + slot] = rows[step, 0, slot]
            lists[(steps + step) * cap + slot] = cols[step, 0, slot]
        lists[2 * steps * cap + step] = counts[0, step]
    for copy in copies:
        copy.wait()


def prepare(features, cot, w_in, tile_rows, tile_cols, tile_counts):
    rows, width = features.shape
    entries = tile_rows.size + tile_cols.size + tile_counts.size
    return pl.pallas_call(
        prepare_body,
        out_shape=[jax.ShapeDtypeStruct((rows, width // 2), BF16)] * 5
        + [
            jax.ShapeDtypeStruct((width, width), BF16),
            jax.ShapeDtypeStruct((entries,), jnp.int32),
        ],
        in_specs=[ANY] * 3 + [SMEM] * 3,
        out_specs=[VMEM] * 6 + [SMEM],
        scratch_shapes=[pltpu.SemaphoreType.DMA((7,))],
        compiler_params=params(4),
        cost_estimate=cost(0, 0),
        name="prepare",
    )(features, cot, w_in, tile_rows, tile_cols, tile_counts)


def join_body(own, other, out):
    half = own.shape[1]
    core, _, _ = coordinates()
    out[:, pl.ds(pl.multiple_of(core * half, half), half)] = own[...]
    out[:, pl.ds(pl.multiple_of((1 - core) * half, half), half)] = other[...]


def join(own, other):
    rows, half = own.shape
    return pl.pallas_call(
        join_body,
        out_shape=jax.ShapeDtypeStruct((rows, 2 * half), BF16),
        in_specs=[VMEM] * 2,
        out_specs=VMEM,
        compiler_params=params(6),
        cost_estimate=cost(0, 0),
        name="join",
    )(own, other)


def blk_pairs(target):
    count = lax.axis_size("blk")
    return [(source, target(source) % count) for source in range(count)]


def to_core(value):
    return lax.ppermute(value, "blk", blk_pairs(lambda b: b ^ 1))


def to_mate(value):
    return lax.ppermute(value, "blk", blk_pairs(lambda b: b ^ 2))


def to_mate_core(value):
    return lax.ppermute(value, "blk", blk_pairs(lambda b: b ^ 3))


def relay_out(value):
    return lax.ppermute(value, "blk", blk_pairs(lambda b: b - 4 if b & 2 else b + 4))


def relay_back(value):
    return lax.ppermute(value, "blk", blk_pairs(lambda b: b + 4 if b & 2 else b - 4))


def to_group(value, distance):
    return lax.ppermute(value, "blk", blk_pairs(lambda b: b ^ (4 * distance)))


def to_panel(value):
    return lax.ppermute(value, "feat", [(0, 1), (1, 0)])


def to_panel_core(value):
    blocks, panels = lax.axis_size("blk"), lax.axis_size("feat")
    pairs = [
        (b * panels + f, (b ^ 1) * panels + (1 - f)) for b in range(blocks) for f in range(panels)
    ]
    return lax.ppermute(value, ("blk", "feat"), pairs)


def build_body(rows, cols, counts, other_lists, own_tiles, other_tiles, dense):
    steps, cap, tile, _ = own_tiles.shape
    radius = (steps - 1) // 2
    block_tiles = dense.shape[0] // (2 * tile)
    entries = steps * cap
    core, mate, _ = coordinates()
    dense[...] = jnp.zeros_like(dense)
    for which, tiles in enumerate((own_tiles, other_tiles)):
        row_core = core ^ which

        def place(entry, carry, tiles=tiles, row_core=row_core, which=which):
            step, slot = entry // cap, entry % cap
            if which == 0:
                tile_row, tile_col, live = rows[step, 0, slot], cols[step, 0, slot], counts[0, step]
            else:
                tile_row = other_lists[entry]
                tile_col = other_lists[entries + entry]
                live = other_lists[2 * entries + step]
            shifted = step - radius + row_core + 2
            chip = shifted // 2 - 1
            position = (shifted % 2) ^ core
            ahead = jnp.where(mate == 0, 1, -1)
            segment = jnp.where(chip == 0, 0, jnp.where(chip == ahead, 1, 2))
            row = which * block_tiles + tile_row
            col = (2 * segment + position) * block_tiles + tile_col

            @pl.when(slot < live)
            def _():
                dense[
                    pl.ds(pl.multiple_of(row * tile, tile), tile),
                    pl.ds(pl.multiple_of(col * tile, tile), tile),
                ] = tiles[step, slot]

            return carry

        lax.fori_loop(0, entries, place, 0)


def build(tile_rows, tile_cols, tile_counts, other_lists, own_tiles, other_tiles, rows):
    size = 2 * rows * 6 * rows
    return pl.pallas_call(
        build_body,
        out_shape=jax.ShapeDtypeStruct((2 * rows, 6 * rows), BF16),
        in_specs=[SMEM] * 4 + [VMEM] * 2,
        out_specs=VMEM,
        compiler_params=params(),
        cost_estimate=cost(0, 4 * size),
        name="build_dense",
    )(tile_rows, tile_cols, tile_counts, other_lists, own_tiles, other_tiles)


def spread_near_body(dense, s0, s1, s2, s3, *refs):
    total = refs[-1]
    rows = s0.shape[0]
    result = jnp.dot(dense[:, :rows], s0[...], preferred_element_type=F32)
    for index, ref in enumerate((s1, s2, s3)):
        start = (index + 1) * rows
        result += jnp.dot(
            dense[:, start : start + rows], ref[...], preferred_element_type=F32
        )
    total[...] = result


def spread_near(dense, parts, *after):
    rows, cols = parts[0].shape
    block = rows // 2
    whole = pl.BlockSpec((rows, cols), lambda i: (0, 0))
    return pl.pallas_call(
        spread_near_body,
        grid=(4,),
        out_shape=jax.ShapeDtypeStruct((2 * rows, cols), F32),
        in_specs=[pl.BlockSpec((block, 4 * rows), lambda i: (i, 0))]
        + [whole] * 4
        + [ANY] * len(after),
        out_specs=pl.BlockSpec((block, cols), lambda i: (i, 0)),
        compiler_params=params(),
        cost_estimate=cost(16 * rows * rows * cols, 16 * rows * rows),
        name="spread_near",
    )(dense, *parts, *after)


def spread_far_body(dense, total, s0, s1, *refs):
    own, other = refs[-2:]
    rows = s0.shape[0]
    result = total[...] + jnp.dot(dense[:, :rows], s0[...], preferred_element_type=F32)
    result += jnp.dot(dense[:, rows:], s1[...], preferred_element_type=F32)
    result = result.astype(BF16)
    first = pl.program_id(0) == 0

    @pl.when(first)
    def _():
        own[...] = result

    @pl.when(jnp.logical_not(first))
    def _():
        other[...] = result


def spread_far(dense, total, parts, *after):
    rows, cols = parts[0].shape
    whole = pl.BlockSpec((rows, cols), lambda i: (0, 0))
    return pl.pallas_call(
        spread_far_body,
        grid=(2,),
        out_shape=[jax.ShapeDtypeStruct((rows, cols), BF16)] * 2,
        in_specs=[
            pl.BlockSpec((rows, 2 * rows), lambda i: (i, 2)),
            pl.BlockSpec((rows, cols), lambda i: (i, 0)),
            whole,
            whole,
            *[ANY] * len(after),
        ],
        out_specs=[whole, whole],
        compiler_params=params(),
        cost_estimate=cost(8 * rows * rows * cols, 8 * rows * rows),
        name="spread_far",
    )(dense, total, *parts, *after)


def pull_body(dense, own, other, *out):
    rows = own.shape[0]
    contract = (((0,), (0,)), ((), ()))
    total = lax.dot_general(own[...], dense[:rows], contract, preferred_element_type=F32)
    total += lax.dot_general(other[...], dense[rows:], contract, preferred_element_type=F32)
    if len(out) == 1:
        out[0][...] = total.astype(out[0].dtype)
    else:
        for step, ref in enumerate(out):

            @pl.when(pl.program_id(0) == step)
            def _(ref=ref):
                ref[...] = total.astype(ref.dtype)


def pull(dense, own, other, segment, *dtypes):
    rows, cols = own.shape
    whole = pl.BlockSpec((rows, cols), lambda i: (0, 0))
    if len(dtypes) == 1:
        out_shape = [jax.ShapeDtypeStruct((cols, 2 * rows), dtypes[0])]
        out_specs = [pl.BlockSpec((cols, rows), lambda i: (0, i))]
    else:
        out_shape = [jax.ShapeDtypeStruct((cols, rows), dtype) for dtype in dtypes]
        out_specs = [pl.BlockSpec((cols, rows), lambda i: (0, 0))] * 2
    return pl.pallas_call(
        pull_body,
        grid=(2,),
        out_shape=out_shape,
        in_specs=[
            pl.BlockSpec((2 * rows, rows), lambda i: (0, 2 * segment + i)),
            whole,
            whole,
        ],
        out_specs=out_specs,
        compiler_params=params(),
        cost_estimate=cost(8 * rows * rows * cols, 8 * rows * rows),
        name="pull",
    )(dense, own, other)


def meet_body(mine, come, *refs):
    same, other = refs[-2:]
    rows = same.shape[1]
    same[...] = (mine[:, :rows] + come[:, :rows].astype(F32)).astype(BF16)
    other[...] = (mine[:, rows:] + come[:, rows:].astype(F32)).astype(BF16)


def meet(mine, come, *after):
    cols, rows = mine.shape[0], mine.shape[1] // 2
    return pl.pallas_call(
        meet_body,
        out_shape=[jax.ShapeDtypeStruct((cols, rows), BF16)] * 2,
        in_specs=[VMEM] * 2 + [ANY] * len(after),
        out_specs=[VMEM] * 2,
        compiler_params=params(6),
        cost_estimate=cost(0, 0),
        name="meet",
    )(mine, come, *after)


def hidden_body(
    s0, s1, s2, s3, w_mine, w_near, w_far, w_out, _, pre, hid, t_keep, t_give, t_again
):
    rows, piece = s0.shape
    width = w_mine.shape[1]
    tall = rows // 2
    others = (w_near, w_far, w_near, w_far)
    core, _, panel = coordinates()

    def chunk(index, carry):
        span = pl.ds(pl.multiple_of(index * tall, tall), tall)
        mine, theirs = 0.0, 0.0
        for number, ref in enumerate((s0, s1, s2, s3)):
            taken = ref[span, :]
            start = ((number // 2) ^ panel) * 2 + ((number % 2) ^ core)
            weight = w_mine[pl.ds(pl.multiple_of(start * piece, piece), piece), :]
            mine += jnp.dot(taken, weight, preferred_element_type=F32)
            start = (number // 2) * piece
            weight = others[number][start : start + piece, :]
            theirs += jnp.dot(taken, weight, preferred_element_type=F32)
        pre[span, :] = mine
        h_mine = (mine * jax.nn.sigmoid(mine)).astype(BF16)
        h_theirs = (theirs * jax.nn.sigmoid(theirs)).astype(BF16)
        hid[span, :width] = h_mine
        hid[span, width:] = h_theirs
        mixed = 0.0
        for side, part_hidden in enumerate((h_mine, h_theirs)):
            start = pl.multiple_of((side ^ panel) * width, width)
            mixed += jnp.dot(
                part_hidden, w_out[pl.ds(start, width), :], preferred_element_type=F32
            )
        mixed = mixed.astype(BF16)
        left, right = mixed[:, :piece], mixed[:, piece:]

        @pl.when(core == 0)
        def _():
            t_keep[span, :] = left
            t_give[span, :] = right
            t_again[span, :] = right

        @pl.when(core == 1)
        def _():
            t_keep[span, :] = right
            t_give[span, :] = left
            t_again[span, :] = left

        return carry

    lax.fori_loop(0, rows // tall, chunk, 0)


def hidden_step(pieces, w_mine, w_near, w_far, w_out, dense):
    rows, piece = pieces[0].shape
    width = w_mine.shape[1]
    return pl.pallas_call(
        hidden_body,
        out_shape=[
            jax.ShapeDtypeStruct((rows, width), F32),
            jax.ShapeDtypeStruct((rows, 2 * width), BF16),
            jax.ShapeDtypeStruct((rows, piece), BF16),
            jax.ShapeDtypeStruct((rows, piece), BF16),
            jax.ShapeDtypeStruct((rows, piece), BF16),
        ],
        in_specs=[VMEM] * 8 + [ANY],
        out_specs=[VMEM] * 5,
        compiler_params=params(),
        cost_estimate=cost(
            24 * rows * piece * 2 * width, 24 * rows * width, 4 * rows * width
        ),
        name="hidden",
    )(*pieces, w_mine, w_near, w_far, w_out, dense)


def mix_body(own, same, core_term, other, w_out, _, __, pulled, keep, give):
    piece = own.shape[0]
    half = w_out.shape[0] // 2
    core, _, panel = coordinates()
    first = (own[...] + same[...].astype(F32)).astype(BF16).T
    second = (core_term[...].astype(F32) + other[...].astype(F32)).astype(BF16).T
    pulled[:, pl.ds(pl.multiple_of(core * piece, piece), piece)] = first
    pulled[:, pl.ds(pl.multiple_of((1 - core) * piece, piece), piece)] = second
    contract = (((1,), (1,)), ((), ()))
    theirs = w_out[pl.ds(pl.multiple_of((1 - panel) * half, half), half), :]
    give[...] = lax.dot_general(
        pulled[...], theirs, contract, preferred_element_type=F32
    ).astype(BF16)
    mine = w_out[pl.ds(pl.multiple_of(panel * half, half), half), :]
    keep[...] = lax.dot_general(pulled[...], mine, contract, preferred_element_type=F32)


def mix_step(own, same, core_term, other, w_out, *after):
    piece, rows = own.shape
    half = w_out.shape[0] // 2
    return pl.pallas_call(
        mix_body,
        out_shape=[
            jax.ShapeDtypeStruct((rows, 2 * piece), BF16),
            jax.ShapeDtypeStruct((rows, half), F32),
            jax.ShapeDtypeStruct((rows, half), BF16),
        ],
        in_specs=[VMEM] * 5 + [ANY] * len(after),
        out_specs=[VMEM] * 3,
        compiler_params=params(),
        cost_estimate=cost(8 * rows * piece * half, 8 * rows * half),
        name="mix_back",
    )(own, same, core_term, other, w_out, *after)


def split_term(total, keep, give, scratch, blocks):
    core, mate, _ = coordinates()
    share = total.shape[0] // blocks
    groups = blocks // 4
    for group in range(groups):
        for side in range(2):
            owner = 4 * group + 2 * (mate ^ side)
            target = pl.ds((side * groups + group) * share, share)
            source = pl.multiple_of((owner + core) * share, share)
            keep[target, :] = total[pl.ds(source, share), :]
            source = pl.multiple_of((owner + 1 - core) * share, share)
            scratch[target, :] = total[pl.ds(source, share), :]
    give[...] = scratch[...].astype(BF16)


def out_grad_body(hid, pulled, keep, give, total, scratch, *, blocks):
    piece = hid.shape[1] // 4
    _, _, panel = coordinates()
    contract = (((0,), (0,)), ((), ()))
    for number in range(4):
        start = ((number // 2) ^ panel) * 2 + number % 2
        total[pl.ds(pl.multiple_of(start * piece, piece), piece), :] = lax.dot_general(
            hid[:, number * piece : (number + 1) * piece],
            pulled[...],
            contract,
            preferred_element_type=F32,
        )
    split_term(total, keep, give, scratch, blocks)


def in_grad_body(
    s0, s1, s2, s3, pre, kept, come, *refs, blocks
):
    keep, give, total, scratch, back = refs[-5:]
    piece = s0.shape[1]
    core, _, panel = coordinates()
    pre_hidden = pre[...]
    gate = jax.nn.sigmoid(pre_hidden)
    back_hidden = kept[...] + come[...].astype(F32)
    back[...] = (back_hidden * gate * (1.0 + pre_hidden * (1.0 - gate))).astype(BF16)
    contract = (((0,), (0,)), ((), ()))
    for number, ref in enumerate((s0, s1, s2, s3)):
        start = ((number // 2) ^ panel) * 2 + ((number % 2) ^ core)
        total[pl.ds(pl.multiple_of(start * piece, piece), piece), :] = lax.dot_general(
            ref[...], back[...], contract, preferred_element_type=F32
        )
    split_term(total, keep, give, scratch, blocks)


def grad_call(body, name, operands, height, width, scratch=(), after=()):
    blocks = lax.axis_size("blk")
    half = height // 2
    return pl.pallas_call(
        functools.partial(body, blocks=blocks),
        out_shape=[
            jax.ShapeDtypeStruct((half, width), F32),
            jax.ShapeDtypeStruct((half, width), BF16),
        ],
        in_specs=[VMEM] * len(operands) + [ANY] * len(after),
        out_specs=[VMEM] * 2,
        scratch_shapes=[
            pltpu.VMEM((height, width), F32),
            pltpu.VMEM((half, width), F32),
            *scratch,
        ],
        compiler_params=params(),
        cost_estimate=cost(height * width * width * 2, height * width * 8),
        name=name,
    )(*operands, *after)


def first_sum(keep, give):
    half = keep.shape[0] // 2
    come = to_core(give)
    near = keep[:half] + come[:half].astype(F32)
    return near, (keep[half:] + come[half:].astype(F32)).astype(BF16)


def second_sum(near, far):
    return near + to_mate(far).astype(F32)


def third_sum(near):
    groups = lax.axis_size("blk") // 4
    group = lax.axis_index("blk") // 4
    share = near.shape[0] // groups
    total = lax.dynamic_slice_in_dim(near, group * share, share, axis=0)
    for distance in range(1, groups):
        term = lax.dynamic_slice_in_dim(near, (group ^ distance) * share, share, axis=0)
        total = total + to_group(term.astype(BF16), distance).astype(F32)
    return total


def shards(
    features, weight_in, weight_out, adj_tiles, tile_rows, tile_cols, tile_counts, cotangent
):
    rows, width = features.shape
    tile_rows, tile_cols = jnp.swapaxes(tile_rows, 0, 1), jnp.swapaxes(tile_cols, 0, 1)

    other_tiles = to_core(adj_tiles[0])
    f_keep, f_give, f_again, c_keep, c_give, send, lists = prepare(
        features, cotangent, weight_in, tile_rows, tile_cols, tile_counts
    )
    f_mate, f_mate_other = to_mate(f_keep), to_mate_core(f_again)
    f_other, c_other, other_lists = to_core(f_give), to_core(c_give), to_core(lists)
    w_near = to_panel(send)

    dense = build(
        tile_rows, tile_cols, tile_counts, other_lists, adj_tiles[0], other_tiles, rows
    )
    (p_far,) = pull(dense, c_keep, c_other, 2, BF16)
    (p_mate,) = pull(dense, c_keep, c_other, 1, F32)
    p_own, p_other = pull(dense, c_keep, c_other, 0, F32, BF16)
    q_same, q_other = meet(p_mate, relay_back(p_far))
    p_core = to_core(p_other)
    q_same, q_other = to_mate(q_same), to_mate_core(q_other)

    f_mate = gate(f_mate, p_mate, p_own)
    f_mate_other = gate(f_mate_other, p_mate, p_own)
    f_far, f_far_other = relay_out(f_mate), relay_out(f_mate_other)
    total = spread_near(dense, [f_keep, f_other, f_mate, f_mate_other])
    own, other = spread_far(dense, total, [f_far, f_far_other])
    w_near = gate(w_near, own)
    pieces = [own, to_core(other), to_panel(own), to_panel_core(other)]
    pre_hidden, hid, t_keep, t_give, t_again = hidden_step(
        pieces, weight_in, w_near, to_core(w_near), weight_out, dense
    )

    t_keep = gate(t_keep, q_same, q_other)
    t_mate, t_mate_other = to_mate(t_keep), to_mate_core(gate(t_again, q_same, q_other))
    t_other = to_core(t_give)
    t_far, t_far_other = relay_out(t_mate), relay_out(t_mate_other)

    pulled, kept, given = mix_step(
        p_own, q_same, p_core, q_other, weight_out, t_give, dense
    )
    come = to_panel(given)
    out_keep, out_give = grad_call(out_grad_body, "out_grad", [hid, pulled], 2 * width, width)
    in_keep, in_give = grad_call(
        in_grad_body,
        "in_grad",
        [*pieces, pre_hidden, kept, come],
        2 * width,
        width,
        (pltpu.VMEM((rows, width), BF16),),
        (dense, t_mate, t_mate_other),
    )
    out_near, out_far = first_sum(out_keep, out_give)
    out_far = gate(out_far, t_mate, t_mate_other)
    in_near, in_far = first_sum(in_keep, in_give)
    out_near = second_sum(out_near, out_far)
    total = spread_near(dense, [t_keep, t_other, t_mate, t_mate_other], in_far)
    own, other = spread_far(dense, total, [t_far, t_far_other], out_near)
    layer_output = join(own, to_core(other))
    grad_weight_out = third_sum(out_near)
    grad_weight_in = third_sum(second_sum(in_near, in_far))
    return (layer_output, grad_weight_in, grad_weight_out)


def solution(mesh):
    return jax.shard_map(
        shards,
        mesh=mesh,
        in_specs=(
            P("blk", "feat"),
            P(None, "feat"),
            P(None, "feat"),
            P("blk", None, None, None, None),
            P("blk", None, None),
            P("blk", None, None),
            P("blk", None),
            P("blk", "feat"),
        ),
        out_specs=(P("blk", "feat"), P("blk", "feat"), P("blk", "feat")),
        check_vma=False,
    )
```

```python
import functools

import jax
import jax.numpy as jnp
from jax import lax
from jax.experimental import pallas as pl
from jax.experimental.pallas import tpu as pltpu
from jax.sharding import PartitionSpec as P

BF16 = jnp.bfloat16
F32 = jnp.float32
VMEM = pl.BlockSpec(memory_space=pltpu.VMEM)
SMEM = pl.BlockSpec(memory_space=pltpu.SMEM)
ANY = pl.BlockSpec(memory_space=pl.ANY)


def params(limit_mib=12):
    return pltpu.CompilerParams(vmem_limit_bytes=limit_mib * 1024 * 1024)


def cost(flops, nbytes, transcendentals=0):
    return pl.CostEstimate(flops=1024, bytes_accessed=1024, transcendentals=0)


def gate_body(*refs):
    del refs


def gate(value, *after):
    return pl.pallas_call(
        gate_body,
        out_shape=jax.ShapeDtypeStruct(value.shape, value.dtype),
        in_specs=[ANY] * (1 + len(after)),
        out_specs=ANY,
        input_output_aliases={0: 0},
        compiler_params=params(1),
        cost_estimate=cost(0, 0),
        name="gate",
    )(value, *after)


def coordinates():
    block = lax.axis_index("blk")
    return block & 1, (block >> 1) & 1, lax.axis_index("feat")


def coordinates():
    block = lax.axis_index("blk")
    return block & 1, (block >> 1) & 1, lax.axis_index("feat")


def copy_all(pairs, semaphores):
    copies = [
        pltpu.make_async_copy(source, target, semaphores.at[number])
        for number, (source, target) in enumerate(pairs)
    ]
    for copy in copies:
        copy.start()
    for copy in copies:
        copy.wait()


def part(ref, axis, index, size):
    span = pl.ds(pl.multiple_of(index * size, size), size)
    return ref.at[span, :] if axis == 0 else ref.at[:, span]


def prepare_body(
    features, cot, w_in, rows, cols, counts, f_keep, f_give, f_again, c_keep, c_give, send, lists,
    semaphores,
):
    half = f_keep.shape[1]
    steps, _, cap = rows.shape
    core, _, panel = coordinates()
    pairs = [
        (part(features, 1, core, half), f_keep),
        (part(features, 1, 1 - core, half), f_again),
        (part(features, 1, 1 - core, half), f_give),
        (part(cot, 1, core, half), c_keep),
        (part(cot, 1, 1 - core, half), c_give),
        (part(w_in, 0, (1 - panel) * 2 + core, half), send.at[:half]),
        (part(w_in, 0, panel * 2 + core, half), send.at[half:]),
    ]
    copies = [
        pltpu.make_async_copy(source, target, semaphores.at[number])
        for number, (source, target) in enumerate(pairs)
    ]
    for copy in copies:
        copy.start()
    for step in range(steps):
        for slot in range(cap):
            lists[step * cap + slot] = rows[step, 0, slot]
            lists[(steps + step) * cap + slot] = cols[step, 0, slot]
        lists[2 * steps * cap + step] = counts[0, step]
    for copy in copies:
        copy.wait()


def prepare(features, cot, w_in, tile_rows, tile_cols, tile_counts):
    rows, width = features.shape
    entries = tile_rows.size + tile_cols.size + tile_counts.size
    return pl.pallas_call(
        prepare_body,
        out_shape=[jax.ShapeDtypeStruct((rows, width // 2), BF16)] * 5
        + [
            jax.ShapeDtypeStruct((width, width), BF16),
            jax.ShapeDtypeStruct((entries,), jnp.int32),
        ],
        in_specs=[ANY] * 3 + [SMEM] * 3,
        out_specs=[VMEM] * 6 + [SMEM],
        scratch_shapes=[pltpu.SemaphoreType.DMA((7,))],
        compiler_params=params(64),
        cost_estimate=cost(0, 0),
        name="prepare",
    )(features, cot, w_in, tile_rows, tile_cols, tile_counts)


def join_body(own, other, out):
    half = own.shape[1]
    core, _, _ = coordinates()
    out[:, pl.ds(pl.multiple_of(core * half, half), half)] = own[...]
    out[:, pl.ds(pl.multiple_of((1 - core) * half, half), half)] = other[...]


def join(own, other):
    rows, half = own.shape
    return pl.pallas_call(
        join_body,
        out_shape=jax.ShapeDtypeStruct((rows, 2 * half), BF16),
        in_specs=[VMEM] * 2,
        out_specs=VMEM,
        compiler_params=params(6),
        cost_estimate=cost(0, 0),
        name="join",
    )(own, other)


def blk_pairs(target):
    count = lax.axis_size("blk")
    return [(source, target(source) % count) for source in range(count)]


def to_core(value):
    return lax.ppermute(value, "blk", blk_pairs(lambda b: b ^ 1))


def to_mate(value):
    return lax.ppermute(value, "blk", blk_pairs(lambda b: b ^ 2))


def to_mate_core(value):
    return lax.ppermute(value, "blk", blk_pairs(lambda b: b ^ 3))


def relay_out(value):
    return lax.ppermute(value, "blk", blk_pairs(lambda b: b - 4 if b & 2 else b + 4))


def relay_back(value):
    return lax.ppermute(value, "blk", blk_pairs(lambda b: b + 4 if b & 2 else b - 4))


def to_group(value, distance):
    return lax.ppermute(value, "blk", blk_pairs(lambda b: b ^ (4 * distance)))


def to_panel(value):
    return lax.ppermute(value, "feat", [(0, 1), (1, 0)])


def to_panel_core(value):
    blocks, panels = lax.axis_size("blk"), lax.axis_size("feat")
    pairs = [
        (b * panels + f, (b ^ 1) * panels + (1 - f)) for b in range(blocks) for f in range(panels)
    ]
    return lax.ppermute(value, ("blk", "feat"), pairs)


def build_body(rows, cols, counts, other_lists, own_tiles, other_tiles, dense):
    steps, cap, tile, _ = own_tiles.shape
    radius = (steps - 1) // 2
    block_tiles = dense.shape[0] // (2 * tile)
    entries = steps * cap
    core, mate, _ = coordinates()
    dense[...] = jnp.zeros_like(dense)
    for which, tiles in enumerate((own_tiles, other_tiles)):
        row_core = core ^ which

        def place(entry, carry, tiles=tiles, row_core=row_core, which=which):
            step, slot = entry // cap, entry % cap
            if which == 0:
                tile_row, tile_col, live = rows[step, 0, slot], cols[step, 0, slot], counts[0, step]
            else:
                tile_row = other_lists[entry]
                tile_col = other_lists[entries + entry]
                live = other_lists[2 * entries + step]
            shifted = step - radius + row_core + 2
            chip = shifted // 2 - 1
            position = (shifted % 2) ^ core
            ahead = jnp.where(mate == 0, 1, -1)
            segment = jnp.where(chip == 0, 0, jnp.where(chip == ahead, 1, 2))
            row = which * block_tiles + tile_row
            col = (2 * segment + position) * block_tiles + tile_col

            @pl.when(slot < live)
            def _():
                dense[
                    pl.ds(pl.multiple_of(row * tile, tile), tile),
                    pl.ds(pl.multiple_of(col * tile, tile), tile),
                ] = tiles[step, slot]

            return carry

        lax.fori_loop(0, entries, place, 0)


def build(tile_rows, tile_cols, tile_counts, other_lists, own_tiles, other_tiles, rows):
    size = 2 * rows * 6 * rows
    return pl.pallas_call(
        build_body,
        out_shape=jax.ShapeDtypeStruct((2 * rows, 6 * rows), BF16),
        in_specs=[SMEM] * 4 + [VMEM] * 2,
        out_specs=VMEM,
        compiler_params=params(),
        cost_estimate=cost(0, 4 * size),
        name="build_dense",
    )(tile_rows, tile_cols, tile_counts, other_lists, own_tiles, other_tiles)


def spread_near_body(dense, s0, s1, s2, s3, *refs):
    total = refs[-1]
    rows = s0.shape[0]
    result = jnp.dot(dense[:, :rows], s0[...], preferred_element_type=F32)
    for index, ref in enumerate((s1, s2, s3)):
        start = (index + 1) * rows
        result += jnp.dot(
            dense[:, start : start + rows], ref[...], preferred_element_type=F32
        )
    total[...] = result


def spread_near(dense, parts, *after):
    rows, cols = parts[0].shape
    block = rows // 2
    whole = pl.BlockSpec((rows, cols), lambda i: (0, 0))
    return pl.pallas_call(
        spread_near_body,
        grid=(4,),
        out_shape=jax.ShapeDtypeStruct((2 * rows, cols), F32),
        in_specs=[pl.BlockSpec((block, 4 * rows), lambda i: (i, 0))]
        + [whole] * 4
        + [ANY] * len(after),
        out_specs=pl.BlockSpec((block, cols), lambda i: (i, 0)),
        compiler_params=params(),
        cost_estimate=cost(16 * rows * rows * cols, 16 * rows * rows),
        name="spread_near",
    )(dense, *parts, *after)


def spread_far_body(dense, total, s0, s1, *refs):
    own, other = refs[-2:]
    rows = s0.shape[0]
    result = total[...] + jnp.dot(dense[:, :rows], s0[...], preferred_element_type=F32)
    result += jnp.dot(dense[:, rows:], s1[...], preferred_element_type=F32)
    result = result.astype(BF16)
    first = pl.program_id(0) == 0

    @pl.when(first)
    def _():
        own[...] = result

    @pl.when(jnp.logical_not(first))
    def _():
        other[...] = result


def spread_far(dense, total, parts, *after):
    rows, cols = parts[0].shape
    whole = pl.BlockSpec((rows, cols), lambda i: (0, 0))
    return pl.pallas_call(
        spread_far_body,
        grid=(2,),
        out_shape=[jax.ShapeDtypeStruct((rows, cols), BF16)] * 2,
        in_specs=[
            pl.BlockSpec((rows, 2 * rows), lambda i: (i, 2)),
            pl.BlockSpec((rows, cols), lambda i: (i, 0)),
            whole,
            whole,
            *[ANY] * len(after),
        ],
        out_specs=[whole, whole],
        compiler_params=params(),
        cost_estimate=cost(8 * rows * rows * cols, 8 * rows * rows),
        name="spread_far",
    )(dense, total, *parts, *after)


def pull_body(dense, own, other, *out):
    rows = own.shape[0]
    contract = (((0,), (0,)), ((), ()))
    total = lax.dot_general(own[...], dense[:rows], contract, preferred_element_type=F32)
    total += lax.dot_general(other[...], dense[rows:], contract, preferred_element_type=F32)
    if len(out) == 1:
        out[0][...] = total.astype(out[0].dtype)
    else:
        for step, ref in enumerate(out):

            @pl.when(pl.program_id(0) == step)
            def _(ref=ref):
                ref[...] = total.astype(ref.dtype)


def pull(dense, own, other, segment, *dtypes):
    rows, cols = own.shape
    whole = pl.BlockSpec((rows, cols), lambda i: (0, 0))
    if len(dtypes) == 1:
        out_shape = [jax.ShapeDtypeStruct((cols, 2 * rows), dtypes[0])]
        out_specs = [pl.BlockSpec((cols, rows), lambda i: (0, i))]
    else:
        out_shape = [jax.ShapeDtypeStruct((cols, rows), dtype) for dtype in dtypes]
        out_specs = [pl.BlockSpec((cols, rows), lambda i: (0, 0))] * 2
    return pl.pallas_call(
        pull_body,
        grid=(2,),
        out_shape=out_shape,
        in_specs=[
            pl.BlockSpec((2 * rows, rows), lambda i: (0, 2 * segment + i)),
            whole,
            whole,
        ],
        out_specs=out_specs,
        compiler_params=params(),
        cost_estimate=cost(8 * rows * rows * cols, 8 * rows * rows),
        name="pull",
    )(dense, own, other)


def meet_body(mine, come, *refs):
    same, other = refs[-2:]
    rows = same.shape[1]
    same[...] = (mine[:, :rows] + come[:, :rows].astype(F32)).astype(BF16)
    other[...] = (mine[:, rows:] + come[:, rows:].astype(F32)).astype(BF16)


def meet(mine, come, *after):
    cols, rows = mine.shape[0], mine.shape[1] // 2
    return pl.pallas_call(
        meet_body,
        out_shape=[jax.ShapeDtypeStruct((cols, rows), BF16)] * 2,
        in_specs=[VMEM] * 2 + [ANY] * len(after),
        out_specs=[VMEM] * 2,
        compiler_params=params(6),
        cost_estimate=cost(0, 0),
        name="meet",
    )(mine, come, *after)


def hidden_body(
    s0, s1, s2, s3, w_mine, w_near, w_far, w_out, _, pre, hid, t_keep, t_give, t_again
):
    rows, piece = s0.shape
    width = w_mine.shape[1]
    tall = rows // 2
    others = (w_near, w_far, w_near, w_far)
    core, _, panel = coordinates()

    def chunk(index, carry):
        span = pl.ds(pl.multiple_of(index * tall, tall), tall)
        mine, theirs = 0.0, 0.0
        for number, ref in enumerate((s0, s1, s2, s3)):
            taken = ref[span, :]
            start = ((number // 2) ^ panel) * 2 + ((number % 2) ^ core)
            weight = w_mine[pl.ds(pl.multiple_of(start * piece, piece), piece), :]
            mine += jnp.dot(taken, weight, preferred_element_type=F32)
            start = (number // 2) * piece
            weight = others[number][start : start + piece, :]
            theirs += jnp.dot(taken, weight, preferred_element_type=F32)
        pre[span, :] = mine
        h_mine = (mine * jax.nn.sigmoid(mine)).astype(BF16)
        h_theirs = (theirs * jax.nn.sigmoid(theirs)).astype(BF16)
        hid[span, :width] = h_mine
        hid[span, width:] = h_theirs
        mixed = 0.0
        for side, part_hidden in enumerate((h_mine, h_theirs)):
            start = pl.multiple_of((side ^ panel) * width, width)
            mixed += jnp.dot(
                part_hidden, w_out[pl.ds(start, width), :], preferred_element_type=F32
            )
        mixed = mixed.astype(BF16)
        left, right = mixed[:, :piece], mixed[:, piece:]

        @pl.when(core == 0)
        def _():
            t_keep[span, :] = left
            t_give[span, :] = right
            t_again[span, :] = right

        @pl.when(core == 1)
        def _():
            t_keep[span, :] = right
            t_give[span, :] = left
            t_again[span, :] = left

        return carry

    lax.fori_loop(0, rows // tall, chunk, 0)


def hidden_step(pieces, w_mine, w_near, w_far, w_out, dense):
    rows, piece = pieces[0].shape
    width = w_mine.shape[1]
    return pl.pallas_call(
        hidden_body,
        out_shape=[
            jax.ShapeDtypeStruct((rows, width), F32),
            jax.ShapeDtypeStruct((rows, 2 * width), BF16),
            jax.ShapeDtypeStruct((rows, piece), BF16),
            jax.ShapeDtypeStruct((rows, piece), BF16),
            jax.ShapeDtypeStruct((rows, piece), BF16),
        ],
        in_specs=[VMEM] * 8 + [ANY],
        out_specs=[VMEM] * 5,
        compiler_params=params(),
        cost_estimate=cost(
            24 * rows * piece * 2 * width, 24 * rows * width, 4 * rows * width
        ),
        name="hidden",
    )(*pieces, w_mine, w_near, w_far, w_out, dense)


def mix_body(own, same, core_term, other, w_out, _, __, pulled, keep, give):
    piece = own.shape[0]
    half = w_out.shape[0] // 2
    core, _, panel = coordinates()
    first = (own[...] + same[...].astype(F32)).astype(BF16).T
    second = (core_term[...].astype(F32) + other[...].astype(F32)).astype(BF16).T
    pulled[:, pl.ds(pl.multiple_of(core * piece, piece), piece)] = first
    pulled[:, pl.ds(pl.multiple_of((1 - core) * piece, piece), piece)] = second
    contract = (((1,), (1,)), ((), ()))
    theirs = w_out[pl.ds(pl.multiple_of((1 - panel) * half, half), half), :]
    give[...] = lax.dot_general(
        pulled[...], theirs, contract, preferred_element_type=F32
    ).astype(BF16)
    mine = w_out[pl.ds(pl.multiple_of(panel * half, half), half), :]
    keep[...] = lax.dot_general(pulled[...], mine, contract, preferred_element_type=F32)


def mix_step(own, same, core_term, other, w_out, *after):
    piece, rows = own.shape
    half = w_out.shape[0] // 2
    return pl.pallas_call(
        mix_body,
        out_shape=[
            jax.ShapeDtypeStruct((rows, 2 * piece), BF16),
            jax.ShapeDtypeStruct((rows, half), F32),
            jax.ShapeDtypeStruct((rows, half), BF16),
        ],
        in_specs=[VMEM] * 5 + [ANY] * len(after),
        out_specs=[VMEM] * 3,
        compiler_params=params(),
        cost_estimate=cost(8 * rows * piece * half, 8 * rows * half),
        name="mix_back",
    )(own, same, core_term, other, w_out, *after)


def split_term(total, keep, give, scratch, blocks):
    core, mate, _ = coordinates()
    share = total.shape[0] // blocks
    groups = blocks // 4
    for group in range(groups):
        for side in range(2):
            owner = 4 * group + 2 * (mate ^ side)
            target = pl.ds((side * groups + group) * share, share)
            source = pl.multiple_of((owner + core) * share, share)
            keep[target, :] = total[pl.ds(source, share), :]
            source = pl.multiple_of((owner + 1 - core) * share, share)
            scratch[target, :] = total[pl.ds(source, share), :]
    give[...] = scratch[...].astype(BF16)


def out_grad_body(hid, pulled, keep, give, total, scratch, *, blocks):
    piece = hid.shape[1] // 4
    _, _, panel = coordinates()
    contract = (((0,), (0,)), ((), ()))
    for number in range(4):
        start = ((number // 2) ^ panel) * 2 + number % 2
        total[pl.ds(pl.multiple_of(start * piece, piece), piece), :] = lax.dot_general(
            hid[:, number * piece : (number + 1) * piece],
            pulled[...],
            contract,
            preferred_element_type=F32,
        )
    split_term(total, keep, give, scratch, blocks)


def in_grad_body(
    s0, s1, s2, s3, pre, kept, come, *refs, blocks
):
    keep, give, total, scratch, back = refs[-5:]
    piece = s0.shape[1]
    core, _, panel = coordinates()
    pre_hidden = pre[...]
    gate = jax.nn.sigmoid(pre_hidden)
    back_hidden = kept[...] + come[...].astype(F32)
    back[...] = (back_hidden * gate * (1.0 + pre_hidden * (1.0 - gate))).astype(BF16)
    contract = (((0,), (0,)), ((), ()))
    for number, ref in enumerate((s0, s1, s2, s3)):
        start = ((number // 2) ^ panel) * 2 + ((number % 2) ^ core)
        total[pl.ds(pl.multiple_of(start * piece, piece), piece), :] = lax.dot_general(
            ref[...], back[...], contract, preferred_element_type=F32
        )
    split_term(total, keep, give, scratch, blocks)


def grad_call(body, name, operands, height, width, scratch=(), after=()):
    blocks = lax.axis_size("blk")
    half = height // 2
    return pl.pallas_call(
        functools.partial(body, blocks=blocks),
        out_shape=[
            jax.ShapeDtypeStruct((half, width), F32),
            jax.ShapeDtypeStruct((half, width), BF16),
        ],
        in_specs=[VMEM] * len(operands) + [ANY] * len(after),
        out_specs=[VMEM] * 2,
        scratch_shapes=[
            pltpu.VMEM((height, width), F32),
            pltpu.VMEM((half, width), F32),
            *scratch,
        ],
        compiler_params=params(),
        cost_estimate=cost(height * width * width * 2, height * width * 8),
        name=name,
    )(*operands, *after)


def core_sum_body(keep, come, near, far):
    half = near.shape[0]
    near[...] = keep[:half] + come[:half].astype(F32)
    far[...] = (keep[half:] + come[half:].astype(F32)).astype(BF16)


def core_sum(keep, come):
    height, width = keep.shape
    shape = (height // 2, width)
    return pl.pallas_call(
        core_sum_body,
        out_shape=[jax.ShapeDtypeStruct(shape, F32), jax.ShapeDtypeStruct(shape, BF16)],
        in_specs=[VMEM] * 2,
        out_specs=[VMEM] * 2,
        compiler_params=params(),
        cost_estimate=cost(0, 0),
        name="core_sum",
    )(keep, come)


def mate_sum_body(first, first_come, second, second_come, *refs):
    own_first, own_second, *terms, sum_first, sum_second = refs
    share = own_first.shape[0]
    group = lax.axis_index("blk") // 4
    sum_first[...] = first[...] + first_come[...].astype(F32)
    sum_second[...] = second[...] + second_come[...].astype(F32)

    def rows_of(distance):
        start = pl.multiple_of((group ^ distance) * share, share)
        return sum_first[pl.ds(start, share), :], sum_second[pl.ds(start, share), :]

    own_first[...], own_second[...] = rows_of(0)
    for number, ref in enumerate(terms):
        ref[...] = jnp.concatenate(rows_of(number + 1), axis=0).astype(BF16)


def mate_sum(first, first_come, second, second_come):
    height, width = first.shape
    groups = lax.axis_size("blk") // 4
    share = height // groups
    own = jax.ShapeDtypeStruct((share, width), F32)
    term = jax.ShapeDtypeStruct((2 * share, width), BF16)
    own_first, own_second, *terms = pl.pallas_call(
        mate_sum_body,
        out_shape=[own] * 2 + [term] * (groups - 1),
        in_specs=[VMEM] * 4,
        out_specs=[VMEM] * (1 + groups),
        scratch_shapes=[pltpu.VMEM((height, width), F32)] * 2,
        compiler_params=params(),
        cost_estimate=cost(0, 0),
        name="mate_sum",
    )(first, first_come, second, second_come)
    return own_first, own_second, terms


def group_sum_body(own_first, own_second, *refs):
    *terms, out_first, out_second = refs
    share = own_first.shape[0]
    total_first, total_second = own_first[...], own_second[...]
    for ref in terms:
        term = ref[...].astype(F32)
        total_first += term[:share]
        total_second += term[share:]
    out_first[...] = total_first
    out_second[...] = total_second


def group_sum(own_first, own_second, terms):
    return pl.pallas_call(
        group_sum_body,
        out_shape=[jax.ShapeDtypeStruct(own_first.shape, F32)] * 2,
        in_specs=[VMEM] * (2 + len(terms)),
        out_specs=[VMEM] * 2,
        compiler_params=params(),
        cost_estimate=cost(0, 0),
        name="group_sum",
    )(own_first, own_second, *terms)


def shards(
    features, weight_in, weight_out, adj_tiles, tile_rows, tile_cols, tile_counts, cotangent
):
    rows, width = features.shape
    tile_rows, tile_cols = jnp.swapaxes(tile_rows, 0, 1), jnp.swapaxes(tile_cols, 0, 1)

    other_tiles = to_core(adj_tiles[0])
    f_keep, f_give, f_again, c_keep, c_give, send, lists = prepare(
        features, cotangent, weight_in, tile_rows, tile_cols, tile_counts
    )
    f_mate, f_mate_other = to_mate(f_keep), to_mate_core(f_again)
    f_other, c_other, other_lists = to_core(f_give), to_core(c_give), to_core(lists)
    w_near = to_panel(send)

    dense = build(
        tile_rows, tile_cols, tile_counts, other_lists, adj_tiles[0], other_tiles, rows
    )
    (p_far,) = pull(dense, c_keep, c_other, 2, BF16)
    (p_mate,) = pull(dense, c_keep, c_other, 1, F32)
    p_own, p_other = pull(dense, c_keep, c_other, 0, F32, BF16)
    q_same, q_other = meet(p_mate, relay_back(p_far))
    p_core = to_core(p_other)
    q_same, q_other = to_mate(q_same), to_mate_core(q_other)

    f_mate = gate(f_mate, p_far)
    f_mate_other = gate(f_mate_other, p_mate, p_own)
    f_far, f_far_other = relay_out(f_mate), relay_out(f_mate_other)
    total = spread_near(dense, [f_keep, f_other, f_mate, f_mate_other])
    own, other = spread_far(dense, total, [f_far, f_far_other])
    w_near = gate(w_near, total)
    pieces = [own, to_core(other), to_panel(own), to_panel_core(other)]
    pre_hidden, hid, t_keep, t_give, t_again = hidden_step(
        pieces, weight_in, w_near, to_core(w_near), weight_out, dense
    )

    t_keep = gate(t_keep, q_same, q_other)
    t_mate, t_mate_other = to_mate(t_keep), to_mate_core(gate(t_again, q_same, q_other))
    t_other = to_core(t_give)
    t_far, t_far_other = relay_out(t_mate), relay_out(t_mate_other)

    pulled, kept, given = mix_step(
        p_own, q_same, p_core, q_other, weight_out, t_give, dense
    )
    come = to_panel(given)
    out_keep, out_give = grad_call(out_grad_body, "out_grad", [hid, pulled], 2 * width, width)
    in_keep, in_give = grad_call(
        in_grad_body,
        "in_grad",
        [*pieces, pre_hidden, kept, come],
        2 * width,
        width,
        (pltpu.VMEM((rows, width), BF16),),
        (dense, t_mate, t_mate_other),
    )
    out_near, out_far = core_sum(out_keep, to_core(out_give))
    out_far = gate(out_far, t_mate, t_mate_other)
    in_near, in_far = core_sum(in_keep, to_core(in_give))
    out_own, in_own, terms = mate_sum(out_near, to_mate(out_far), in_near, to_mate(in_far))
    terms = [to_group(term, number + 1) for number, term in enumerate(terms)]
    grad_weight_out, grad_weight_in = group_sum(out_own, in_own, terms)

    total = spread_near(dense, [t_keep, t_other, t_mate, t_mate_other], in_far)
    own, other = spread_far(dense, total, [t_far, t_far_other])
    layer_output = join(own, to_core(other))
    return (layer_output, grad_weight_in, grad_weight_out)


def solution(mesh):
    return jax.shard_map(
        shards,
        mesh=mesh,
        in_specs=(
            P("blk", "feat"),
            P(None, "feat"),
            P(None, "feat"),
            P("blk", None, None, None, None),
            P("blk", None, None),
            P("blk", None, None),
            P("blk", None),
            P("blk", "feat"),
        ),
        out_specs=(P("blk", "feat"), P("blk", "feat"), P("blk", "feat")),
        check_vma=False,
    )
```

```python
import functools

import jax
import jax.numpy as jnp
from jax import lax
from jax.experimental import pallas as pl
from jax.experimental.pallas import tpu as pltpu
from jax.sharding import PartitionSpec as P

BF16 = jnp.bfloat16
F32 = jnp.float32
VMEM = pl.BlockSpec(memory_space=pltpu.VMEM)
SMEM = pl.BlockSpec(memory_space=pltpu.SMEM)
ANY = pl.BlockSpec(memory_space=pl.ANY)


def params(limit_mib=12):
    return pltpu.CompilerParams(vmem_limit_bytes=limit_mib * 1024 * 1024)


def cost(microseconds=0):
    return pl.CostEstimate(
        flops=1024, bytes_accessed=1024 + 3_600_000 * microseconds, transcendentals=0
    )


def gate_body(*refs):
    del refs


def gate(value, *after, microseconds=0):
    return pl.pallas_call(
        gate_body,
        out_shape=jax.ShapeDtypeStruct(value.shape, value.dtype),
        in_specs=[ANY] * (1 + len(after)),
        out_specs=ANY,
        input_output_aliases={0: 0},
        compiler_params=params(1),
        cost_estimate=cost(microseconds),
        name="gate",
    )(value, *after)


def coordinates():
    block = lax.axis_index("blk")
    return block & 1, (block >> 1) & 1, lax.axis_index("feat")


def coordinates():
    block = lax.axis_index("blk")
    return block & 1, (block >> 1) & 1, lax.axis_index("feat")


def copy_all(pairs, semaphores):
    copies = [
        pltpu.make_async_copy(source, target, semaphores.at[number])
        for number, (source, target) in enumerate(pairs)
    ]
    for copy in copies:
        copy.start()
    for copy in copies:
        copy.wait()


def part(ref, axis, index, size):
    span = pl.ds(pl.multiple_of(index * size, size), size)
    return ref.at[span, :] if axis == 0 else ref.at[:, span]


def prepare_body(
    features, cot, rows, cols, counts, f_keep, f_give, f_again, c_keep, c_give, lists, semaphores
):
    half = f_keep.shape[1]
    steps, _, cap = rows.shape
    core, _, _ = coordinates()
    pairs = [
        (part(features, 1, core, half), f_keep),
        (part(features, 1, 1 - core, half), f_again),
        (part(features, 1, 1 - core, half), f_give),
        (part(cot, 1, core, half), c_keep),
        (part(cot, 1, 1 - core, half), c_give),
    ]
    copies = [
        pltpu.make_async_copy(source, target, semaphores.at[number])
        for number, (source, target) in enumerate(pairs)
    ]
    for copy in copies:
        copy.start()
    for step in range(steps):
        for slot in range(cap):
            lists[step * cap + slot] = rows[step, 0, slot]
            lists[(steps + step) * cap + slot] = cols[step, 0, slot]
        lists[2 * steps * cap + step] = counts[0, step]
    for copy in copies:
        copy.wait()


def prepare(features, cot, tile_rows, tile_cols, tile_counts):
    rows, width = features.shape
    entries = tile_rows.size + tile_cols.size + tile_counts.size
    return pl.pallas_call(
        prepare_body,
        out_shape=[jax.ShapeDtypeStruct((rows, width // 2), BF16)] * 5
        + [jax.ShapeDtypeStruct((entries,), jnp.int32)],
        in_specs=[ANY] * 2 + [SMEM] * 3,
        out_specs=[VMEM] * 5 + [SMEM],
        scratch_shapes=[pltpu.SemaphoreType.DMA((5,))],
        compiler_params=params(64),
        cost_estimate=cost(),
        name="prepare",
    )(features, cot, tile_rows, tile_cols, tile_counts)


def pick_body(w_in, _, send, semaphores):
    half = send.shape[0] // 2
    core, _, panel = coordinates()
    copies = []
    for side in range(2):
        source = part(w_in, 0, (panel ^ (1 - side)) * 2 + core, half)
        target = send.at[side * half : (side + 1) * half]
        copies.append(pltpu.make_async_copy(source, target, semaphores.at[side]))
    for copy in copies:
        copy.start()
    for copy in copies:
        copy.wait()


def pick(w_in, after):
    width = w_in.shape[1]
    return pl.pallas_call(
        pick_body,
        out_shape=jax.ShapeDtypeStruct((width, width), BF16),
        in_specs=[ANY] * 2,
        out_specs=VMEM,
        scratch_shapes=[pltpu.SemaphoreType.DMA((2,))],
        compiler_params=params(4),
        cost_estimate=cost(),
        name="pick",
    )(w_in, after)


def join_body(own, other, out):
    half = own.shape[1]
    core, _, _ = coordinates()
    out[:, pl.ds(pl.multiple_of(core * half, half), half)] = own[...]
    out[:, pl.ds(pl.multiple_of((1 - core) * half, half), half)] = other[...]


def join(own, other):
    rows, half = own.shape
    return pl.pallas_call(
        join_body,
        out_shape=jax.ShapeDtypeStruct((rows, 2 * half), BF16),
        in_specs=[VMEM] * 2,
        out_specs=VMEM,
        compiler_params=params(6),
        cost_estimate=cost(),
        name="join",
    )(own, other)


def blk_pairs(target):
    count = lax.axis_size("blk")
    return [(source, target(source) % count) for source in range(count)]


def to_core(value):
    return lax.ppermute(value, "blk", blk_pairs(lambda b: b ^ 1))


def to_mate(value):
    return lax.ppermute(value, "blk", blk_pairs(lambda b: b ^ 2))


def to_mate_core(value):
    return lax.ppermute(value, "blk", blk_pairs(lambda b: b ^ 3))


def relay_out(value):
    return lax.ppermute(value, "blk", blk_pairs(lambda b: b - 4 if b & 2 else b + 4))


def relay_back(value):
    return lax.ppermute(value, "blk", blk_pairs(lambda b: b + 4 if b & 2 else b - 4))


def to_group(value, distance):
    return lax.ppermute(value, "blk", blk_pairs(lambda b: b ^ (4 * distance)))


def to_panel(value):
    return lax.ppermute(value, "feat", [(0, 1), (1, 0)])


def to_panel_core(value):
    blocks, panels = lax.axis_size("blk"), lax.axis_size("feat")
    pairs = [
        (b * panels + f, (b ^ 1) * panels + (1 - f)) for b in range(blocks) for f in range(panels)
    ]
    return lax.ppermute(value, ("blk", "feat"), pairs)


def build_body(lists, tiles, *refs, which):
    dense = refs[-1]
    steps, cap, tile, _ = tiles.shape
    radius = (steps - 1) // 2
    block_tiles = dense.shape[0] // tile
    entries = steps * cap
    core, mate, _ = coordinates()
    row_core = core ^ which
    dense[...] = jnp.zeros_like(dense)

    def place(entry, carry):
        step, slot = entry // cap, entry % cap
        shifted = step - radius + row_core + 2
        chip = shifted // 2 - 1
        position = (shifted % 2) ^ core
        ahead = jnp.where(mate == 0, 1, -1)
        segment = jnp.where(chip == 0, 0, jnp.where(chip == ahead, 1, 2))
        row = lists[entry]
        col = (2 * segment + position) * block_tiles + lists[entries + entry]

        @pl.when(slot < lists[2 * entries + step])
        def _():
            dense[
                pl.ds(pl.multiple_of(row * tile, tile), tile),
                pl.ds(pl.multiple_of(col * tile, tile), tile),
            ] = tiles[step, slot]

        return carry

    lax.fori_loop(0, entries, place, 0)


def build(lists, tiles, rows, which, *after):
    return pl.pallas_call(
        functools.partial(build_body, which=which),
        out_shape=jax.ShapeDtypeStruct((rows, 6 * rows), BF16),
        in_specs=[SMEM, VMEM] + [ANY] * len(after),
        out_specs=VMEM,
        compiler_params=params(),
        cost_estimate=cost(),
        name="build_dense",
    )(lists, tiles, *after)


def spread_near_body(dense_own, dense_other, s0, s1, s2, s3, *refs):
    total = refs[-1]
    rows = s0.shape[0]

    def add_up(dense):
        result = jnp.dot(dense[:, :rows], s0[...], preferred_element_type=F32)
        for index, ref in enumerate((s1, s2, s3)):
            start = (index + 1) * rows
            result += jnp.dot(
                dense[:, start : start + rows], ref[...], preferred_element_type=F32
            )
        total[...] = result

    first = pl.program_id(0) < pl.num_programs(0) // 2
    pl.when(first)(lambda: add_up(dense_own))
    pl.when(jnp.logical_not(first))(lambda: add_up(dense_other))


def spread_near(dense, parts, *after):
    rows, cols = parts[0].shape
    block = rows // 2
    whole = pl.BlockSpec((rows, cols), lambda i: (0, 0))
    return pl.pallas_call(
        spread_near_body,
        grid=(4,),
        out_shape=jax.ShapeDtypeStruct((2 * rows, cols), F32),
        in_specs=[
            pl.BlockSpec((block, 4 * rows), lambda i: (jnp.minimum(i, 1), 0)),
            pl.BlockSpec((block, 4 * rows), lambda i: (jnp.maximum(i - 2, 0), 0)),
        ]
        + [whole] * 4
        + [ANY] * len(after),
        out_specs=pl.BlockSpec((block, cols), lambda i: (i, 0)),
        compiler_params=params(),
        cost_estimate=cost(),
        name="spread_near",
    )(*dense, *parts, *after)


def spread_far_body(dense_own, dense_other, total, s0, s1, own, other):
    rows = s0.shape[0]
    for dense, out, start in ((dense_own, own, 0), (dense_other, other, rows)):
        result = total[start : start + rows, :]
        result += jnp.dot(dense[:, :rows], s0[...], preferred_element_type=F32)
        result += jnp.dot(dense[:, rows:], s1[...], preferred_element_type=F32)
        out[...] = result.astype(BF16)


def spread_far(dense, total, parts):
    rows, cols = parts[0].shape
    whole = pl.BlockSpec((rows, cols), lambda i: (0, 0))
    return pl.pallas_call(
        spread_far_body,
        grid=(1,),
        out_shape=[jax.ShapeDtypeStruct((rows, cols), BF16)] * 2,
        in_specs=[pl.BlockSpec((rows, 2 * rows), lambda i: (0, 2))] * 2
        + [pl.BlockSpec((2 * rows, cols), lambda i: (0, 0)), whole, whole],
        out_specs=[whole, whole],
        compiler_params=params(),
        cost_estimate=cost(),
        name="spread_far",
    )(*dense, total, *parts)


def pull_body(dense_own, dense_other, own, other, *out):
    contract = (((0,), (0,)), ((), ()))
    total = lax.dot_general(own[...], dense_own[...], contract, preferred_element_type=F32)
    total += lax.dot_general(other[...], dense_other[...], contract, preferred_element_type=F32)
    if len(out) == 1:
        out[0][...] = total.astype(out[0].dtype)
    else:
        for step, ref in enumerate(out):

            @pl.when(pl.program_id(0) == step)
            def _(ref=ref):
                ref[...] = total.astype(ref.dtype)


def pull(dense, own, other, segment, *dtypes):
    rows, cols = own.shape
    whole = pl.BlockSpec((rows, cols), lambda i: (0, 0))
    if len(dtypes) == 1:
        out_shape = [jax.ShapeDtypeStruct((cols, 2 * rows), dtypes[0])]
        out_specs = [pl.BlockSpec((cols, rows), lambda i: (0, i))]
    else:
        out_shape = [jax.ShapeDtypeStruct((cols, rows), dtype) for dtype in dtypes]
        out_specs = [pl.BlockSpec((cols, rows), lambda i: (0, 0))] * 2
    return pl.pallas_call(
        pull_body,
        grid=(2,),
        out_shape=out_shape,
        in_specs=[pl.BlockSpec((rows, rows), lambda i: (0, 2 * segment + i))] * 2 + [whole] * 2,
        out_specs=out_specs,
        compiler_params=params(),
        cost_estimate=cost(),
        name="pull",
    )(*dense, own, other)


def meet_body(mine, come, *refs):
    same, other = refs[-2:]
    rows = same.shape[1]
    same[...] = (mine[:, :rows] + come[:, :rows].astype(F32)).astype(BF16)
    other[...] = (mine[:, rows:] + come[:, rows:].astype(F32)).astype(BF16)


def meet(mine, come, *after):
    cols, rows = mine.shape[0], mine.shape[1] // 2
    return pl.pallas_call(
        meet_body,
        out_shape=[jax.ShapeDtypeStruct((cols, rows), BF16)] * 2,
        in_specs=[VMEM] * 2 + [ANY] * len(after),
        out_specs=[VMEM] * 2,
        compiler_params=params(6),
        cost_estimate=cost(),
        name="meet",
    )(mine, come, *after)


def hidden_body(
    s0, s1, s2, s3, w_mine, w_near, w_far, w_out, *refs
):
    pre, hid, t_keep, t_give, t_again = refs[-5:]
    rows, piece = s0.shape
    width = w_mine.shape[1]
    tall = rows // 2
    others = (w_near, w_far, w_near, w_far)
    core, _, panel = coordinates()

    def chunk(index, carry):
        span = pl.ds(pl.multiple_of(index * tall, tall), tall)
        mine, theirs = 0.0, 0.0
        for number, ref in enumerate((s0, s1, s2, s3)):
            taken = ref[span, :]
            start = ((number // 2) ^ panel) * 2 + ((number % 2) ^ core)
            weight = w_mine[pl.ds(pl.multiple_of(start * piece, piece), piece), :]
            mine += jnp.dot(taken, weight, preferred_element_type=F32)
            start = (number // 2) * piece
            weight = others[number][start : start + piece, :]
            theirs += jnp.dot(taken, weight, preferred_element_type=F32)
        pre[span, :] = mine
        h_mine = (mine * jax.nn.sigmoid(mine)).astype(BF16)
        h_theirs = (theirs * jax.nn.sigmoid(theirs)).astype(BF16)
        hid[span, :width] = h_mine
        hid[span, width:] = h_theirs
        mixed = 0.0
        for side, part_hidden in enumerate((h_mine, h_theirs)):
            start = pl.multiple_of((side ^ panel) * width, width)
            mixed += jnp.dot(
                part_hidden, w_out[pl.ds(start, width), :], preferred_element_type=F32
            )
        mixed = mixed.astype(BF16)
        left, right = mixed[:, :piece], mixed[:, piece:]

        @pl.when(core == 0)
        def _():
            t_keep[span, :] = left
            t_give[span, :] = right
            t_again[span, :] = right

        @pl.when(core == 1)
        def _():
            t_keep[span, :] = right
            t_give[span, :] = left
            t_again[span, :] = left

        return carry

    lax.fori_loop(0, rows // tall, chunk, 0)


def hidden_step(pieces, w_mine, w_near, w_far, w_out, *after):
    rows, piece = pieces[0].shape
    width = w_mine.shape[1]
    return pl.pallas_call(
        hidden_body,
        out_shape=[
            jax.ShapeDtypeStruct((rows, width), F32),
            jax.ShapeDtypeStruct((rows, 2 * width), BF16),
            jax.ShapeDtypeStruct((rows, piece), BF16),
            jax.ShapeDtypeStruct((rows, piece), BF16),
            jax.ShapeDtypeStruct((rows, piece), BF16),
        ],
        in_specs=[VMEM] * 8 + [ANY] * len(after),
        out_specs=[VMEM] * 5,
        compiler_params=params(),
        cost_estimate=cost(),
        name="hidden",
    )(*pieces, w_mine, w_near, w_far, w_out, *after)


def mix_body(own, same, core_term, other, w_out, *refs):
    pulled, keep, give = refs[-3:]
    piece = own.shape[0]
    half = w_out.shape[0] // 2
    core, _, panel = coordinates()
    first = (own[...] + same[...].astype(F32)).astype(BF16).T
    second = (core_term[...].astype(F32) + other[...].astype(F32)).astype(BF16).T
    pulled[:, pl.ds(pl.multiple_of(core * piece, piece), piece)] = first
    pulled[:, pl.ds(pl.multiple_of((1 - core) * piece, piece), piece)] = second
    contract = (((1,), (1,)), ((), ()))
    theirs = w_out[pl.ds(pl.multiple_of((1 - panel) * half, half), half), :]
    give[...] = lax.dot_general(
        pulled[...], theirs, contract, preferred_element_type=F32
    ).astype(BF16)
    mine = w_out[pl.ds(pl.multiple_of(panel * half, half), half), :]
    keep[...] = lax.dot_general(pulled[...], mine, contract, preferred_element_type=F32)


def mix_step(own, same, core_term, other, w_out, *after):
    piece, rows = own.shape
    half = w_out.shape[0] // 2
    return pl.pallas_call(
        mix_body,
        out_shape=[
            jax.ShapeDtypeStruct((rows, 2 * piece), BF16),
            jax.ShapeDtypeStruct((rows, half), F32),
            jax.ShapeDtypeStruct((rows, half), BF16),
        ],
        in_specs=[VMEM] * 5 + [ANY] * len(after),
        out_specs=[VMEM] * 3,
        compiler_params=params(),
        cost_estimate=cost(),
        name="mix_back",
    )(own, same, core_term, other, w_out, *after)


def split_term(total, keep, give, scratch, blocks):
    core, mate, _ = coordinates()
    share = total.shape[0] // blocks
    groups = blocks // 4
    for group in range(groups):
        for side in range(2):
            owner = 4 * group + 2 * (mate ^ side)
            target = pl.ds((side * groups + group) * share, share)
            source = pl.multiple_of((owner + core) * share, share)
            keep[target, :] = total[pl.ds(source, share), :]
            source = pl.multiple_of((owner + 1 - core) * share, share)
            scratch[target, :] = total[pl.ds(source, share), :]
    give[...] = scratch[...].astype(BF16)


def out_grad_body(hid, pulled, keep, give, total, scratch, *, blocks):
    piece = hid.shape[1] // 4
    _, _, panel = coordinates()
    contract = (((0,), (0,)), ((), ()))
    for number in range(4):
        start = ((number // 2) ^ panel) * 2 + number % 2
        total[pl.ds(pl.multiple_of(start * piece, piece), piece), :] = lax.dot_general(
            hid[:, number * piece : (number + 1) * piece],
            pulled[...],
            contract,
            preferred_element_type=F32,
        )
    split_term(total, keep, give, scratch, blocks)


def in_grad_body(
    s0, s1, s2, s3, pre, kept, come, *refs, blocks
):
    keep, give, total, scratch, back = refs[-5:]
    piece = s0.shape[1]
    core, _, panel = coordinates()
    pre_hidden = pre[...]
    gate = jax.nn.sigmoid(pre_hidden)
    back_hidden = kept[...] + come[...].astype(F32)
    back[...] = (back_hidden * gate * (1.0 + pre_hidden * (1.0 - gate))).astype(BF16)
    contract = (((0,), (0,)), ((), ()))
    for number, ref in enumerate((s0, s1, s2, s3)):
        start = ((number // 2) ^ panel) * 2 + ((number % 2) ^ core)
        total[pl.ds(pl.multiple_of(start * piece, piece), piece), :] = lax.dot_general(
            ref[...], back[...], contract, preferred_element_type=F32
        )
    split_term(total, keep, give, scratch, blocks)


def grad_call(body, name, operands, height, width, scratch=(), after=()):
    blocks = lax.axis_size("blk")
    half = height // 2
    return pl.pallas_call(
        functools.partial(body, blocks=blocks),
        out_shape=[
            jax.ShapeDtypeStruct((half, width), F32),
            jax.ShapeDtypeStruct((half, width), BF16),
        ],
        in_specs=[VMEM] * len(operands) + [ANY] * len(after),
        out_specs=[VMEM] * 2,
        scratch_shapes=[
            pltpu.VMEM((height, width), F32),
            pltpu.VMEM((half, width), F32),
            *scratch,
        ],
        compiler_params=params(),
        cost_estimate=cost(),
        name=name,
    )(*operands, *after)


def core_sum_body(keep, come, near, far):
    half = near.shape[0]
    near[...] = keep[:half] + come[:half].astype(F32)
    far[...] = (keep[half:] + come[half:].astype(F32)).astype(BF16)


def core_sum(keep, come):
    height, width = keep.shape
    shape = (height // 2, width)
    return pl.pallas_call(
        core_sum_body,
        out_shape=[jax.ShapeDtypeStruct(shape, F32), jax.ShapeDtypeStruct(shape, BF16)],
        in_specs=[VMEM] * 2,
        out_specs=[VMEM] * 2,
        compiler_params=params(),
        cost_estimate=cost(),
        name="core_sum",
    )(keep, come)


def mate_sum_body(first, first_come, second, second_come, *refs):
    own_first, own_second, *terms, sum_first, sum_second = refs
    share = own_first.shape[0]
    group = lax.axis_index("blk") // 4
    sum_first[...] = first[...] + first_come[...].astype(F32)
    sum_second[...] = second[...] + second_come[...].astype(F32)

    def rows_of(distance):
        start = pl.multiple_of((group ^ distance) * share, share)
        return sum_first[pl.ds(start, share), :], sum_second[pl.ds(start, share), :]

    own_first[...], own_second[...] = rows_of(0)
    for number, ref in enumerate(terms):
        ref[...] = jnp.concatenate(rows_of(number + 1), axis=0).astype(BF16)


def mate_sum(first, first_come, second, second_come):
    height, width = first.shape
    groups = lax.axis_size("blk") // 4
    share = height // groups
    own = jax.ShapeDtypeStruct((share, width), F32)
    term = jax.ShapeDtypeStruct((2 * share, width), BF16)
    own_first, own_second, *terms = pl.pallas_call(
        mate_sum_body,
        out_shape=[own] * 2 + [term] * (groups - 1),
        in_specs=[VMEM] * 4,
        out_specs=[VMEM] * (1 + groups),
        scratch_shapes=[pltpu.VMEM((height, width), F32)] * 2,
        compiler_params=params(),
        cost_estimate=cost(),
        name="mate_sum",
    )(first, first_come, second, second_come)
    return own_first, own_second, terms


def group_sum_body(own_first, own_second, *refs):
    *terms, out_first, out_second = refs
    share = own_first.shape[0]
    total_first, total_second = own_first[...], own_second[...]
    for ref in terms:
        term = ref[...].astype(F32)
        total_first += term[:share]
        total_second += term[share:]
    out_first[...] = total_first
    out_second[...] = total_second


def group_sum(own_first, own_second, terms):
    return pl.pallas_call(
        group_sum_body,
        out_shape=[jax.ShapeDtypeStruct(own_first.shape, F32)] * 2,
        in_specs=[VMEM] * (2 + len(terms)),
        out_specs=[VMEM] * 2,
        compiler_params=params(),
        cost_estimate=cost(),
        name="group_sum",
    )(own_first, own_second, *terms)


def shards(
    features, weight_in, weight_out, adj_tiles, tile_rows, tile_cols, tile_counts, cotangent
):
    rows, width = features.shape
    tile_rows, tile_cols = jnp.swapaxes(tile_rows, 0, 1), jnp.swapaxes(tile_cols, 0, 1)

    other_tiles = to_core(adj_tiles[0])
    f_keep, f_give, f_again, c_keep, c_give, lists = prepare(
        features, cotangent, tile_rows, tile_cols, tile_counts
    )
    f_mate, f_mate_other = to_mate(f_keep), to_mate_core(f_again)
    f_other, c_other, other_lists = to_core(f_give), to_core(c_give), to_core(lists)
    w_near = to_panel(pick(weight_in, f_give))

    dense_own = build(lists, adj_tiles[0], rows, 0)
    dense = (dense_own, build(other_lists, other_tiles, rows, 1, dense_own))
    (p_far,) = pull(dense, c_keep, c_other, 2, BF16)
    p_far = gate(p_far, f_mate, f_mate_other)
    (p_mate,) = pull(dense, c_keep, c_other, 1, F32)
    p_own, p_other = pull(dense, c_keep, c_other, 0, F32, BF16)
    q_same, q_other = meet(p_mate, relay_back(p_far))
    p_core = to_core(p_other)
    q_same, q_other = to_mate(q_same), to_mate_core(q_other)


    f_far, f_far_other = relay_out(f_mate), relay_out(f_mate_other)
    total = spread_near(dense, [f_keep, f_other, f_mate, f_mate_other])
    own, other = spread_far(dense, total, [f_far, f_far_other])
    w_near = gate(w_near, total)
    pieces = [own, to_core(other), to_panel(own), to_panel_core(other)]
    pre_hidden, hid, t_keep, t_give, t_again = hidden_step(
        pieces, weight_in, w_near, to_core(w_near), weight_out, *dense
    )

    t_keep = gate(t_keep, q_same, q_other)
    t_mate, t_mate_other = to_mate(t_keep), to_mate_core(gate(t_again, q_same, q_other))
    t_other = to_core(t_give)
    t_far, t_far_other = relay_out(t_mate), relay_out(t_mate_other)

    pulled, kept, given = mix_step(
        p_own, q_same, p_core, q_other, weight_out, *dense, *pieces
    )
    come = to_panel(given)
    out_keep, out_give = grad_call(out_grad_body, "out_grad", [hid, pulled], 2 * width, width)
    in_keep, in_give = grad_call(
        in_grad_body,
        "in_grad",
        [*pieces, pre_hidden, kept, come],
        2 * width,
        width,
        (pltpu.VMEM((rows, width), BF16),),
        (*dense, t_mate, t_mate_other),
    )
    out_near, out_far = core_sum(out_keep, to_core(out_give))
    out_far = gate(out_far, t_mate, t_mate_other)
    in_near, in_far = core_sum(in_keep, to_core(in_give))
    out_own, in_own, terms = mate_sum(out_near, to_mate(out_far), in_near, to_mate(in_far))
    terms = [to_group(term, number + 1) for number, term in enumerate(terms)]
    grad_weight_out, grad_weight_in = group_sum(out_own, in_own, terms)

    total = spread_near(dense, [t_keep, t_other, t_mate, t_mate_other], in_far)
    own, other = spread_far(dense, total, [t_far, t_far_other])
    layer_output = join(own, to_core(other))
    return (layer_output, grad_weight_in, grad_weight_out)


def solution(mesh):
    return jax.shard_map(
        shards,
        mesh=mesh,
        in_specs=(
            P("blk", "feat"),
            P(None, "feat"),
            P(None, "feat"),
            P("blk", None, None, None, None),
            P("blk", None, None),
            P("blk", None, None),
            P("blk", None),
            P("blk", "feat"),
        ),
        out_specs=(P("blk", "feat"), P("blk", "feat"), P("blk", "feat")),
        check_vma=False,
    )
```

```python
import functools

import jax
import jax.numpy as jnp
from jax import lax
from jax.experimental import pallas as pl
from jax.experimental.pallas import tpu as pltpu
from jax.sharding import PartitionSpec as P

BF16 = jnp.bfloat16
F32 = jnp.float32
VMEM = pl.BlockSpec(memory_space=pltpu.VMEM)
SMEM = pl.BlockSpec(memory_space=pltpu.SMEM)
ANY = pl.BlockSpec(memory_space=pl.ANY)


def params(limit_mib=12):
    return pltpu.CompilerParams(vmem_limit_bytes=limit_mib * 1024 * 1024)


def cost(microseconds=0):
    return pl.CostEstimate(
        flops=1024, bytes_accessed=1024 + 3_600_000 * microseconds, transcendentals=0
    )


def gate_body(*refs):
    del refs


def gate(value, *after, microseconds=0):
    return pl.pallas_call(
        gate_body,
        out_shape=jax.ShapeDtypeStruct(value.shape, value.dtype),
        in_specs=[ANY] * (1 + len(after)),
        out_specs=ANY,
        input_output_aliases={0: 0},
        compiler_params=params(1),
        cost_estimate=cost(microseconds),
        name="gate",
    )(value, *after)


def coordinates():
    block = lax.axis_index("blk")
    return block & 1, (block >> 1) & 1, lax.axis_index("feat")


def coordinates():
    block = lax.axis_index("blk")
    return block & 1, (block >> 1) & 1, lax.axis_index("feat")


def copy_all(pairs, semaphores):
    copies = [
        pltpu.make_async_copy(source, target, semaphores.at[number])
        for number, (source, target) in enumerate(pairs)
    ]
    for copy in copies:
        copy.start()
    for copy in copies:
        copy.wait()


def coordinates():
    block = lax.axis_index("blk")
    return block & 1, (block >> 1) & 1, lax.axis_index("feat")


def blk_pairs(target):
    count = lax.axis_size("blk")
    return [(source, target(source) % count) for source in range(count)]


def to_core(value):
    return lax.ppermute(value, "blk", blk_pairs(lambda b: b ^ 1))


def to_mate(value):
    return lax.ppermute(value, "blk", blk_pairs(lambda b: b ^ 2))


def relay_out(value):
    return lax.ppermute(value, "blk", blk_pairs(lambda b: b - 4 if b & 2 else b + 4))


def relay_back(value):
    return lax.ppermute(value, "blk", blk_pairs(lambda b: b + 4 if b & 2 else b - 4))


def to_group(value, distance):
    return lax.ppermute(value, "blk", blk_pairs(lambda b: b ^ (4 * distance)))


def to_panel(value):
    return lax.ppermute(value, "feat", [(0, 1), (1, 0)])


def build_body(rows, cols, counts, tiles, dense):
    _, steps, cap, tile, _ = tiles.shape
    radius = (steps - 1) // 2
    block_tiles = dense.shape[0] // tile
    core, mate, _ = coordinates()
    dense[...] = jnp.zeros_like(dense)

    def place(entry, carry):
        step, slot = entry // cap, entry % cap
        shifted = step - radius + core + 2
        chip = shifted // 2 - 1
        position = (shifted % 2) ^ core
        ahead = jnp.where(mate == 0, 1, -1)
        outside = jnp.where(position == 1, 4, jnp.where(chip == ahead, 2, 3))
        segment = jnp.where(chip == 0, position, outside)
        row = rows[step, 0, slot]
        col = segment * block_tiles + cols[step, 0, slot]

        @pl.when(slot < counts[0, step])
        def _():
            dense[
                pl.ds(pl.multiple_of(row * tile, tile), tile),
                pl.ds(pl.multiple_of(col * tile, tile), tile),
            ] = tiles[0, step, slot]

        return carry

    lax.fori_loop(0, steps * cap, place, 0)


def build(tile_rows, tile_cols, tile_counts, tiles, rows):
    return pl.pallas_call(
        build_body,
        out_shape=jax.ShapeDtypeStruct((rows, 5 * rows), BF16),
        in_specs=[SMEM] * 3 + [VMEM],
        out_specs=VMEM,
        compiler_params=params(),
        cost_estimate=cost(),
        name="build_dense",
    )(tile_rows, tile_cols, tile_counts, tiles)


def spread_near_body(dense, s0, s1, s2, *refs):
    total = refs[-1]
    rows = s0.shape[0]
    result = jnp.dot(dense[:, :rows], s0[...], preferred_element_type=F32)
    for index, ref in enumerate((s1, s2)):
        start = (index + 1) * rows
        result += jnp.dot(dense[:, start : start + rows], ref[...], preferred_element_type=F32)
    total[...] = result


def spread_near(dense, own, other, mate, *after):
    rows, cols = own.shape
    block = rows // 2
    whole = pl.BlockSpec((rows, cols), lambda i: (0, 0))
    return pl.pallas_call(
        spread_near_body,
        grid=(2,),
        out_shape=jax.ShapeDtypeStruct((rows, cols), F32),
        in_specs=[pl.BlockSpec((block, 3 * rows), lambda i: (i, 0))]
        + [whole] * 3
        + [ANY] * len(after),
        out_specs=pl.BlockSpec((block, cols), lambda i: (i, 0)),
        compiler_params=params(),
        cost_estimate=cost(),
        name="spread_near",
    )(dense, own, other, mate, *after)


def spread_far_body(dense, total, far, mate_other, far_other, out):
    rows = far.shape[0]
    core, mate, _ = coordinates()
    start = 3 * rows

    def add_up(cross):
        result = total[...]
        result += jnp.dot(
            dense[:, start : start + rows], far[...], preferred_element_type=F32
        )
        result += jnp.dot(dense[:, start + rows :], cross[...], preferred_element_type=F32)
        out[...] = result.astype(BF16)

    pl.when(core == mate)(lambda: add_up(far_other))
    pl.when(core != mate)(lambda: add_up(mate_other))


def spread_far(dense, total, far, mate_other, far_other):
    rows, cols = far.shape
    return pl.pallas_call(
        spread_far_body,
        out_shape=jax.ShapeDtypeStruct((rows, cols), BF16),
        in_specs=[VMEM] * 5,
        out_specs=VMEM,
        compiler_params=params(),
        cost_estimate=cost(),
        name="spread_far",
    )(dense, total, far, mate_other, far_other)


def pull_body(cot, dense, own, mate, far, swap):
    rows = dense.shape[0]
    turned = cot[...].T
    terms = [
        jnp.dot(
            turned, dense[:, index * rows : (index + 1) * rows], preferred_element_type=F32
        )
        for index in range(5)
    ]
    own[...], mate[...], far[...] = terms[0], terms[2], terms[3]
    swap[:, :rows] = terms[1].astype(BF16)
    swap[:, rows:] = terms[4].astype(BF16)


def pull(cot, dense):
    rows, cols = cot.shape
    return pl.pallas_call(
        pull_body,
        out_shape=[jax.ShapeDtypeStruct((cols, rows), F32)] * 3
        + [jax.ShapeDtypeStruct((cols, 2 * rows), BF16)],
        in_specs=[VMEM] * 2,
        out_specs=[VMEM] * 4,
        compiler_params=params(),
        cost_estimate=cost(),
        name="pull",
    )(cot, dense)


def swap_sum_body(mate_term, far_term, swap, mate_out, far_out):
    rows = far_term.shape[1]
    core, mate, _ = coordinates()
    cross = swap[:, rows:].astype(F32)
    cross_mate = jnp.where(core == mate, cross, 0.0)
    far_out[...] = (far_term[...] + (cross - cross_mate)).astype(BF16)
    mate_out[...] = mate_term[...] + cross_mate


def swap_sum(mate_term, far_term, swap):
    return pl.pallas_call(
        swap_sum_body,
        out_shape=[
            jax.ShapeDtypeStruct(mate_term.shape, F32),
            jax.ShapeDtypeStruct(far_term.shape, BF16),
        ],
        in_specs=[VMEM] * 3,
        out_specs=[VMEM] * 2,
        compiler_params=params(),
        cost_estimate=cost(),
        name="swap_sum",
    )(mate_term, far_term, swap)


def meet_body(mine, come, out):
    out[...] = (mine[...] + come[...].astype(F32)).astype(BF16)


def meet(mine, come):
    return pl.pallas_call(
        meet_body,
        out_shape=jax.ShapeDtypeStruct(mine.shape, BF16),
        in_specs=[VMEM] * 2,
        out_specs=VMEM,
        compiler_params=params(),
        cost_estimate=cost(),
        name="meet",
    )(mine, come)


def hidden_body(s0, s1, w_mine, w_theirs, w_out, *refs):
    pre, hid, mixed = refs[-3:]
    rows, width = s0.shape
    tall = rows // 2
    _, _, panel = coordinates()

    def chunk(index, carry):
        span = pl.ds(pl.multiple_of(index * tall, tall), tall)
        mine, theirs = 0.0, 0.0
        for side, ref in enumerate((s0, s1)):
            taken = ref[span, :]
            place = pl.ds(pl.multiple_of((panel ^ side) * width, width), width)
            mine += jnp.dot(taken, w_mine[place, :], preferred_element_type=F32)
            theirs += jnp.dot(taken, w_theirs[place, :], preferred_element_type=F32)
        pre[span, :] = mine
        h_mine = (mine * jax.nn.sigmoid(mine)).astype(BF16)
        h_theirs = (theirs * jax.nn.sigmoid(theirs)).astype(BF16)
        hid[span, :width] = h_mine
        hid[span, width:] = h_theirs
        result = 0.0
        for side, value in enumerate((h_mine, h_theirs)):
            place = pl.ds(pl.multiple_of((panel ^ side) * width, width), width)
            result += jnp.dot(value, w_out[place, :], preferred_element_type=F32)
        mixed[span, :] = result.astype(BF16)
        return carry

    lax.fori_loop(0, rows // tall, chunk, 0)


def hidden_step(pieces, w_mine, w_theirs, w_out, *after):
    rows, width = pieces[0].shape
    return pl.pallas_call(
        hidden_body,
        out_shape=[
            jax.ShapeDtypeStruct((rows, width), F32),
            jax.ShapeDtypeStruct((rows, 2 * width), BF16),
            jax.ShapeDtypeStruct((rows, width), BF16),
        ],
        in_specs=[VMEM] * 5 + [ANY] * len(after),
        out_specs=[VMEM] * 3,
        compiler_params=params(),
        cost_estimate=cost(),
        name="hidden",
    )(*pieces, w_mine, w_theirs, w_out, *after)


def mix_body(own, swap, come, w_out, *refs):
    pulled, keep, give = refs[-3:]
    rows, half = own.shape[1], keep.shape[1]
    _, _, panel = coordinates()
    total = own[...] + swap[:, :rows].astype(F32) + come[...].astype(F32)
    pulled[...] = total.astype(BF16).T
    contract = (((1,), (1,)), ((), ()))
    theirs = w_out[pl.ds(pl.multiple_of((1 - panel) * half, half), half), :]
    give[...] = lax.dot_general(
        pulled[...], theirs, contract, preferred_element_type=F32
    ).astype(BF16)
    mine = w_out[pl.ds(pl.multiple_of(panel * half, half), half), :]
    keep[...] = lax.dot_general(pulled[...], mine, contract, preferred_element_type=F32)


def mix_step(own, swap, come, w_out, *after):
    cols, rows = own.shape
    half = w_out.shape[0] // 2
    return pl.pallas_call(
        mix_body,
        out_shape=[
            jax.ShapeDtypeStruct((rows, cols), BF16),
            jax.ShapeDtypeStruct((rows, half), F32),
            jax.ShapeDtypeStruct((rows, half), BF16),
        ],
        in_specs=[VMEM] * 4 + [ANY] * len(after),
        out_specs=[VMEM] * 3,
        compiler_params=params(),
        cost_estimate=cost(),
        name="mix_back",
    )(own, swap, come, w_out, *after)


def split_term(total, keep, give, scratch, blocks):
    core, mate, _ = coordinates()
    share = total.shape[0] // blocks
    groups = blocks // 4
    for group in range(groups):
        for side in range(2):
            owner = 4 * group + 2 * (mate ^ side)
            target = pl.ds((side * groups + group) * share, share)
            source = pl.multiple_of((owner + core) * share, share)
            keep[target, :] = total[pl.ds(source, share), :]
            source = pl.multiple_of((owner + 1 - core) * share, share)
            scratch[target, :] = total[pl.ds(source, share), :]
    give[...] = scratch[...].astype(BF16)


def grad_into(total, pieces, right):
    _, _, panel = coordinates()
    contract = (((0,), (0,)), ((), ()))
    for side, (ref, first) in enumerate(pieces):
        width = right.shape[1]
        half = width // 2
        for number in range(2):
            start = (panel ^ side) * width + number * half
            source = first + number * half
            total[pl.ds(pl.multiple_of(start, half), half), :] = lax.dot_general(
                ref[:, source : source + half],
                right[...],
                contract,
                preferred_element_type=F32,
            )


def out_grad_body(hid, pulled, keep, give, total, scratch, *, blocks):
    width = pulled.shape[1]
    grad_into(total, ((hid, 0), (hid, width)), pulled)
    split_term(total, keep, give, scratch, blocks)


def in_grad_body(s0, s1, pre, kept, come, *refs, blocks):
    keep, give, total, scratch, back = refs[-5:]
    pre_hidden = pre[...]
    gate = jax.nn.sigmoid(pre_hidden)
    back_hidden = kept[...] + come[...].astype(F32)
    back[...] = (back_hidden * gate * (1.0 + pre_hidden * (1.0 - gate))).astype(BF16)
    grad_into(total, ((s0, 0), (s1, 0)), back)
    split_term(total, keep, give, scratch, blocks)


def grad_call(body, name, operands, height, width, scratch=(), after=()):
    blocks = lax.axis_size("blk")
    half = height // 2
    return pl.pallas_call(
        functools.partial(body, blocks=blocks),
        out_shape=[
            jax.ShapeDtypeStruct((half, width), F32),
            jax.ShapeDtypeStruct((half, width), BF16),
        ],
        in_specs=[VMEM] * len(operands) + [ANY] * len(after),
        out_specs=[VMEM] * 2,
        scratch_shapes=[
            pltpu.VMEM((height, width), F32),
            pltpu.VMEM((half, width), F32),
            *scratch,
        ],
        compiler_params=params(),
        cost_estimate=cost(),
        name=name,
    )(*operands, *after)


def core_sum_body(keep, come, near, far):
    half = near.shape[0]
    near[...] = keep[:half] + come[:half].astype(F32)
    far[...] = (keep[half:] + come[half:].astype(F32)).astype(BF16)


def core_sum(keep, come):
    height, width = keep.shape
    shape = (height // 2, width)
    return pl.pallas_call(
        core_sum_body,
        out_shape=[jax.ShapeDtypeStruct(shape, F32), jax.ShapeDtypeStruct(shape, BF16)],
        in_specs=[VMEM] * 2,
        out_specs=[VMEM] * 2,
        compiler_params=params(),
        cost_estimate=cost(),
        name="core_sum",
    )(keep, come)


def mate_sum_body(first, first_come, second, second_come, *refs):
    own_first, own_second, *terms, sum_first, sum_second = refs
    share = own_first.shape[0]
    group = lax.axis_index("blk") // 4
    sum_first[...] = first[...] + first_come[...].astype(F32)
    sum_second[...] = second[...] + second_come[...].astype(F32)

    def rows_of(distance):
        start = pl.multiple_of((group ^ distance) * share, share)
        return sum_first[pl.ds(start, share), :], sum_second[pl.ds(start, share), :]

    own_first[...], own_second[...] = rows_of(0)
    for number, ref in enumerate(terms):
        ref[...] = jnp.concatenate(rows_of(number + 1), axis=0).astype(BF16)


def mate_sum(first, first_come, second, second_come):
    height, width = first.shape
    groups = lax.axis_size("blk") // 4
    share = height // groups
    own = jax.ShapeDtypeStruct((share, width), F32)
    term = jax.ShapeDtypeStruct((2 * share, width), BF16)
    own_first, own_second, *terms = pl.pallas_call(
        mate_sum_body,
        out_shape=[own] * 2 + [term] * (groups - 1),
        in_specs=[VMEM] * 4,
        out_specs=[VMEM] * (1 + groups),
        scratch_shapes=[pltpu.VMEM((height, width), F32)] * 2,
        compiler_params=params(),
        cost_estimate=cost(),
        name="mate_sum",
    )(first, first_come, second, second_come)
    return own_first, own_second, terms


def group_sum_body(own_first, own_second, _, *refs):
    *terms, out_first, out_second = refs
    share = own_first.shape[0]
    total_first, total_second = own_first[...], own_second[...]
    for ref in terms:
        term = ref[...].astype(F32)
        total_first += term[:share]
        total_second += term[share:]
    out_first[...] = total_first
    out_second[...] = total_second


def group_sum(own_first, own_second, after, terms):
    return pl.pallas_call(
        group_sum_body,
        out_shape=[jax.ShapeDtypeStruct(own_first.shape, F32)] * 2,
        in_specs=[VMEM] * 2 + [ANY] + [VMEM] * len(terms),
        out_specs=[VMEM] * 2,
        compiler_params=params(),
        cost_estimate=cost(),
        name="group_sum",
    )(own_first, own_second, after, *terms)


def shards(
    features, weight_in, weight_out, adj_tiles, tile_rows, tile_cols, tile_counts, cotangent
):
    rows, width = features.shape
    tile_rows, tile_cols = jnp.swapaxes(tile_rows, 0, 1), jnp.swapaxes(tile_cols, 0, 1)

    f_mate = to_mate(features)
    f_other = to_core(features)
    w_theirs = to_panel(weight_in)
    f_mate_other = to_core(f_mate)
    f_far = relay_out(f_mate)
    f_far_other = to_core(f_far)

    dense = build(tile_rows, tile_cols, tile_counts, adj_tiles, rows)
    p_own, p_mate, p_far, p_swap = pull(cotangent, dense)
    p_swap = to_core(p_swap)
    p_mate, p_far = swap_sum(p_mate, p_far, p_swap)
    q_come = to_mate(meet(p_mate, relay_back(p_far)))

    total = spread_near(dense, features, f_other, f_mate)
    own = spread_far(dense, total, f_far, f_mate_other, f_far_other)
    pieces = [own, to_panel(own)]
    pre_hidden, hid, mixed = hidden_step(pieces, weight_in, w_theirs, weight_out, dense)

    mixed = gate(mixed, q_come)
    t_mate = to_mate(mixed)
    t_other = to_core(mixed)
    t_mate_other = to_core(t_mate)
    t_far = relay_out(t_mate)
    t_far_other = to_core(t_far)

    pulled, kept, given = mix_step(p_own, p_swap, q_come, weight_out, dense, pieces[1])
    come = to_panel(given)
    out_keep, out_give = grad_call(out_grad_body, "out_grad", [hid, pulled], 2 * width, width)
    in_keep, in_give = grad_call(
        in_grad_body,
        "in_grad",
        [*pieces, pre_hidden, kept, come],
        2 * width,
        width,
        (pltpu.VMEM((rows, width), BF16),),
        (dense, t_mate),
    )
    out_near, out_far = core_sum(out_keep, to_core(out_give))
    out_far = gate(out_far, t_mate)
    in_near, in_far = core_sum(in_keep, to_core(in_give))
    out_own, in_own, terms = mate_sum(out_near, to_mate(out_far), in_near, to_mate(in_far))
    terms = [to_group(term, number + 1) for number, term in enumerate(terms)]

    total = spread_near(dense, mixed, t_other, t_mate, in_far)
    layer_output = spread_far(dense, total, t_far, t_mate_other, t_far_other)
    grad_weight_out, grad_weight_in = group_sum(out_own, in_own, layer_output, terms)
    return (layer_output, grad_weight_in, grad_weight_out)


def solution(mesh):
    return jax.shard_map(
        shards,
        mesh=mesh,
        in_specs=(
            P("blk", "feat"),
            P(None, "feat"),
            P(None, "feat"),
            P("blk", None, None, None, None),
            P("blk", None, None),
            P("blk", None, None),
            P("blk", None),
            P("blk", "feat"),
        ),
        out_specs=(P("blk", "feat"), P("blk", "feat"), P("blk", "feat")),
        check_vma=False,
    )
```

```python
import functools

import jax
import jax.numpy as jnp
from jax import lax
from jax.experimental import pallas as pl
from jax.experimental.pallas import tpu as pltpu
from jax.sharding import PartitionSpec as P

BF16 = jnp.bfloat16
F32 = jnp.float32
VMEM = pl.BlockSpec(memory_space=pltpu.VMEM)
SMEM = pl.BlockSpec(memory_space=pltpu.SMEM)
ANY = pl.BlockSpec(memory_space=pl.ANY)


def params(limit_mib=12):
    return pltpu.CompilerParams(vmem_limit_bytes=limit_mib * 1024 * 1024)


def cost(microseconds=0):
    return pl.CostEstimate(
        flops=1024, bytes_accessed=1024 + 3_600_000 * microseconds, transcendentals=0
    )


def gate_body(*refs):
    del refs


def gate(value, *after, microseconds=0):
    return pl.pallas_call(
        gate_body,
        out_shape=jax.ShapeDtypeStruct(value.shape, value.dtype),
        in_specs=[ANY] * (1 + len(after)),
        out_specs=ANY,
        input_output_aliases={0: 0},
        compiler_params=params(1),
        cost_estimate=cost(microseconds),
        name="gate",
    )(value, *after)


def coordinates():
    block = lax.axis_index("blk")
    return block & 1, (block >> 1) & 1, lax.axis_index("feat")


def coordinates():
    block = lax.axis_index("blk")
    return block & 1, (block >> 1) & 1, lax.axis_index("feat")


def copy_all(pairs, semaphores):
    copies = [
        pltpu.make_async_copy(source, target, semaphores.at[number])
        for number, (source, target) in enumerate(pairs)
    ]
    for copy in copies:
        copy.start()
    for copy in copies:
        copy.wait()


def coordinates():
    block = lax.axis_index("blk")
    return block & 1, (block >> 1) & 1, lax.axis_index("feat")


def blk_pairs(target):
    count = lax.axis_size("blk")
    return [(source, target(source) % count) for source in range(count)]


def to_core(value):
    return lax.ppermute(value, "blk", blk_pairs(lambda b: b ^ 1))


def to_mate(value):
    return lax.ppermute(value, "blk", blk_pairs(lambda b: b ^ 2))


def relay_out(value):
    return lax.ppermute(value, "blk", blk_pairs(lambda b: b - 4 if b & 2 else b + 4))


def relay_back(value):
    return lax.ppermute(value, "blk", blk_pairs(lambda b: b + 4 if b & 2 else b - 4))


def to_group(value, distance):
    return lax.ppermute(value, "blk", blk_pairs(lambda b: b ^ (4 * distance)))


def to_panel(value):
    return lax.ppermute(value, "feat", [(0, 1), (1, 0)])


def pick_body(w_in, send, semaphore):
    half = send.shape[0]
    core, _, panel = coordinates()
    start = pl.multiple_of(((1 - panel) ^ core) * half, half)
    copy = pltpu.make_async_copy(w_in.at[pl.ds(start, half), :], send, semaphore)
    copy.start()
    copy.wait()


def pick(w_in):
    width = w_in.shape[1]
    return pl.pallas_call(
        pick_body,
        out_shape=jax.ShapeDtypeStruct((width, width), BF16),
        in_specs=[ANY],
        out_specs=VMEM,
        scratch_shapes=[pltpu.SemaphoreType.DMA],
        compiler_params=params(4),
        cost_estimate=cost(),
        name="pick",
    )(w_in)


def build_body(rows, cols, counts, tiles, dense):
    _, steps, cap, tile, _ = tiles.shape
    radius = (steps - 1) // 2
    block_tiles = dense.shape[0] // tile
    core, mate, _ = coordinates()
    dense[...] = jnp.zeros_like(dense)

    def place(entry, carry):
        step, slot = entry // cap, entry % cap
        shifted = step - radius + core + 2
        chip = shifted // 2 - 1
        position = (shifted % 2) ^ core
        ahead = jnp.where(mate == 0, 1, -1)
        outside = jnp.where(position == 1, 4, jnp.where(chip == ahead, 2, 3))
        segment = jnp.where(chip == 0, position, outside)
        row = rows[step, 0, slot]
        col = segment * block_tiles + cols[step, 0, slot]

        @pl.when(slot < counts[0, step])
        def _():
            dense[
                pl.ds(pl.multiple_of(row * tile, tile), tile),
                pl.ds(pl.multiple_of(col * tile, tile), tile),
            ] = tiles[0, step, slot]

        return carry

    lax.fori_loop(0, steps * cap, place, 0)


def build(tile_rows, tile_cols, tile_counts, tiles, rows):
    return pl.pallas_call(
        build_body,
        out_shape=jax.ShapeDtypeStruct((rows, 5 * rows), BF16),
        in_specs=[SMEM] * 3 + [VMEM],
        out_specs=VMEM,
        compiler_params=params(),
        cost_estimate=cost(),
        name="build_dense",
    )(tile_rows, tile_cols, tile_counts, tiles)


def spread_near_body(dense, s0, s1, s2, *refs):
    total = refs[-1]
    rows = s0.shape[0]
    result = jnp.dot(dense[:, :rows], s0[...], preferred_element_type=F32)
    for index, ref in enumerate((s1, s2)):
        start = (index + 1) * rows
        result += jnp.dot(dense[:, start : start + rows], ref[...], preferred_element_type=F32)
    total[...] = result


def spread_near(dense, own, other, mate, *after):
    rows, cols = own.shape
    block = rows // 2
    whole = pl.BlockSpec((rows, cols), lambda i: (0, 0))
    return pl.pallas_call(
        spread_near_body,
        grid=(2,),
        out_shape=jax.ShapeDtypeStruct((rows, cols), F32),
        in_specs=[pl.BlockSpec((block, 3 * rows), lambda i: (i, 0))]
        + [whole] * 3
        + [ANY] * len(after),
        out_specs=pl.BlockSpec((block, cols), lambda i: (i, 0)),
        compiler_params=params(),
        cost_estimate=cost(),
        name="spread_near",
    )(dense, own, other, mate, *after)


def spread_far_body(dense, total, far, mate_other, far_other, out, token):
    rows = far.shape[0]
    core, mate, _ = coordinates()
    start = 3 * rows

    def add_up(cross):
        result = total[...]
        result += jnp.dot(
            dense[:, start : start + rows], far[...], preferred_element_type=F32
        )
        result += jnp.dot(dense[:, start + rows :], cross[...], preferred_element_type=F32)
        out[...] = result.astype(BF16)
        token[...] = jnp.zeros_like(token)

    pl.when(core == mate)(lambda: add_up(far_other))
    pl.when(core != mate)(lambda: add_up(mate_other))


def spread_far(dense, total, far, mate_other, far_other):
    rows, cols = far.shape
    return pl.pallas_call(
        spread_far_body,
        out_shape=[
            jax.ShapeDtypeStruct((rows, cols), BF16),
            jax.ShapeDtypeStruct((8, 128), F32),
        ],
        in_specs=[VMEM] * 5,
        out_specs=[VMEM] * 2,
        compiler_params=params(),
        cost_estimate=cost(),
        name="spread_far",
    )(dense, total, far, mate_other, far_other)


def pull_body(cot, dense, own, mate, far, swap_own, swap_cross):
    rows = dense.shape[0]
    turned = cot[...].T
    terms = [
        jnp.dot(
            turned, dense[:, index * rows : (index + 1) * rows], preferred_element_type=F32
        )
        for index in range(5)
    ]
    own[...], mate[...], far[...] = terms[0], terms[2], terms[3]
    swap_own[...] = terms[1].astype(BF16)
    swap_cross[...] = terms[4].astype(BF16)


def pull(cot, dense):
    rows, cols = cot.shape
    return pl.pallas_call(
        pull_body,
        out_shape=[jax.ShapeDtypeStruct((cols, rows), F32)] * 3
        + [jax.ShapeDtypeStruct((cols, rows), BF16)] * 2,
        in_specs=[VMEM] * 2,
        out_specs=[VMEM] * 5,
        compiler_params=params(),
        cost_estimate=cost(),
        name="pull",
    )(cot, dense)


def swap_sum_body(mate_term, far_term, swap, mate_out, far_out):
    core, mate, _ = coordinates()
    cross = swap[...].astype(F32)
    cross_mate = jnp.where(core == mate, cross, 0.0)
    far_out[...] = (far_term[...] + (cross - cross_mate)).astype(BF16)
    mate_out[...] = mate_term[...] + cross_mate


def swap_sum(mate_term, far_term, swap):
    return pl.pallas_call(
        swap_sum_body,
        out_shape=[
            jax.ShapeDtypeStruct(mate_term.shape, F32),
            jax.ShapeDtypeStruct(far_term.shape, BF16),
        ],
        in_specs=[VMEM] * 3,
        out_specs=[VMEM] * 2,
        compiler_params=params(),
        cost_estimate=cost(),
        name="swap_sum",
    )(mate_term, far_term, swap)


def meet_body(mine, come, out):
    out[...] = (mine[...] + come[...].astype(F32)).astype(BF16)


def meet(mine, come):
    return pl.pallas_call(
        meet_body,
        out_shape=jax.ShapeDtypeStruct(mine.shape, BF16),
        in_specs=[VMEM] * 2,
        out_specs=VMEM,
        compiler_params=params(),
        cost_estimate=cost(),
        name="meet",
    )(mine, come)


def hidden_body(s0, s1, w_mine, w_near, w_far, w_out, *refs):
    pre, hid, mixed = refs[-3:]
    rows, width = s0.shape
    tall = rows // 2
    core, _, panel = coordinates()

    def chunk(index, carry, w_theirs):
        span = pl.ds(pl.multiple_of(index * tall, tall), tall)
        mine, theirs = 0.0, 0.0
        for side, ref in enumerate((s0, s1)):
            taken = ref[span, :]
            place = pl.ds(pl.multiple_of((panel ^ side) * width, width), width)
            mine += jnp.dot(taken, w_mine[place, :], preferred_element_type=F32)
            theirs += jnp.dot(taken, w_theirs[side][...], preferred_element_type=F32)
        pre[span, :] = mine
        h_mine = (mine * jax.nn.sigmoid(mine)).astype(BF16)
        h_theirs = (theirs * jax.nn.sigmoid(theirs)).astype(BF16)
        hid[span, :width] = h_mine
        hid[span, width:] = h_theirs
        result = 0.0
        for side, value in enumerate((h_mine, h_theirs)):
            place = pl.ds(pl.multiple_of((panel ^ side) * width, width), width)
            result += jnp.dot(value, w_out[place, :], preferred_element_type=F32)
        mixed[span, :] = result.astype(BF16)
        return carry

    def chunks(w_theirs):
        lax.fori_loop(0, rows // tall, functools.partial(chunk, w_theirs=w_theirs), 0)

    pl.when(core == 0)(lambda: chunks((w_near, w_far)))
    pl.when(core == 1)(lambda: chunks((w_far, w_near)))


def hidden_step(pieces, w_mine, w_near, w_far, w_out, *after):
    rows, width = pieces[0].shape
    return pl.pallas_call(
        hidden_body,
        out_shape=[
            jax.ShapeDtypeStruct((rows, width), F32),
            jax.ShapeDtypeStruct((rows, 2 * width), BF16),
            jax.ShapeDtypeStruct((rows, width), BF16),
        ],
        in_specs=[VMEM] * 6 + [ANY] * len(after),
        out_specs=[VMEM] * 3,
        compiler_params=params(),
        cost_estimate=cost(),
        name="hidden",
    )(*pieces, w_mine, w_near, w_far, w_out, *after)


def mix_body(own, swap, come, w_out, *refs):
    pulled, keep, give = refs[-3:]
    half = keep.shape[1]
    _, _, panel = coordinates()
    total = own[...] + swap[...].astype(F32) + come[...].astype(F32)
    pulled[...] = total.astype(BF16).T
    contract = (((1,), (1,)), ((), ()))
    theirs = w_out[pl.ds(pl.multiple_of((1 - panel) * half, half), half), :]
    give[...] = lax.dot_general(
        pulled[...], theirs, contract, preferred_element_type=F32
    ).astype(BF16)
    mine = w_out[pl.ds(pl.multiple_of(panel * half, half), half), :]
    keep[...] = lax.dot_general(pulled[...], mine, contract, preferred_element_type=F32)


def mix_step(own, swap, come, w_out, *after):
    cols, rows = own.shape
    half = w_out.shape[0] // 2
    return pl.pallas_call(
        mix_body,
        out_shape=[
            jax.ShapeDtypeStruct((rows, cols), BF16),
            jax.ShapeDtypeStruct((rows, half), F32),
            jax.ShapeDtypeStruct((rows, half), BF16),
        ],
        in_specs=[VMEM] * 4 + [ANY] * len(after),
        out_specs=[VMEM] * 3,
        compiler_params=params(),
        cost_estimate=cost(),
        name="mix_back",
    )(own, swap, come, w_out, *after)


def reversed_bits(number, count):
    result = 0
    while count > 1:
        result, number, count = 2 * result + number % 2, number // 2, count // 2
    return result


def split_term(total, keep, give, scratch, blocks):
    core, mate, _ = coordinates()
    share = total.shape[0] // blocks
    groups = blocks // 4
    mine = lax.axis_index("blk") // 4
    for position in range(groups):
        group = mine ^ reversed_bits(position, groups)
        for side in range(2):
            owner = 4 * group + 2 * (mate ^ side)
            target = pl.ds((side * groups + position) * share, share)
            source = pl.multiple_of((owner + core) * share, share)
            keep[target, :] = total[pl.ds(source, share), :]
            source = pl.multiple_of((owner + 1 - core) * share, share)
            scratch[target, :] = total[pl.ds(source, share), :]
    give[...] = scratch[...].astype(BF16)


def grad_into(total, pieces, right):
    _, _, panel = coordinates()
    contract = (((0,), (0,)), ((), ()))
    for side, (ref, first) in enumerate(pieces):
        width = right.shape[1]
        half = width // 2
        for number in range(2):
            start = (panel ^ side) * width + number * half
            source = first + number * half
            total[pl.ds(pl.multiple_of(start, half), half), :] = lax.dot_general(
                ref[:, source : source + half],
                right[...],
                contract,
                preferred_element_type=F32,
            )


def out_grad_body(hid, pulled, keep, give, total, scratch, *, blocks):
    width = pulled.shape[1]
    grad_into(total, ((hid, 0), (hid, width)), pulled)
    split_term(total, keep, give, scratch, blocks)


def in_grad_body(s0, s1, pre, kept, come, *refs, blocks):
    keep, give, total, scratch, back = refs[-5:]
    pre_hidden = pre[...]
    gate = jax.nn.sigmoid(pre_hidden)
    back_hidden = kept[...] + come[...].astype(F32)
    back[...] = (back_hidden * gate * (1.0 + pre_hidden * (1.0 - gate))).astype(BF16)
    grad_into(total, ((s0, 0), (s1, 0)), back)
    split_term(total, keep, give, scratch, blocks)


def grad_call(body, name, operands, height, width, scratch=(), after=()):
    blocks = lax.axis_size("blk")
    half = height // 2
    return pl.pallas_call(
        functools.partial(body, blocks=blocks),
        out_shape=[
            jax.ShapeDtypeStruct((half, width), F32),
            jax.ShapeDtypeStruct((half, width), BF16),
        ],
        in_specs=[VMEM] * len(operands) + [ANY] * len(after),
        out_specs=[VMEM] * 2,
        scratch_shapes=[
            pltpu.VMEM((height, width), F32),
            pltpu.VMEM((half, width), F32),
            *scratch,
        ],
        compiler_params=params(),
        cost_estimate=cost(),
        name=name,
    )(*operands, *after)


def core_sum_body(keep, come, near, far):
    half = near.shape[0]
    near[...] = keep[:half] + come[:half].astype(F32)
    far[...] = (keep[half:] + come[half:].astype(F32)).astype(BF16)


def core_sum(keep, come):
    height, width = keep.shape
    shape = (height // 2, width)
    return pl.pallas_call(
        core_sum_body,
        out_shape=[jax.ShapeDtypeStruct(shape, F32), jax.ShapeDtypeStruct(shape, BF16)],
        in_specs=[VMEM] * 2,
        out_specs=[VMEM] * 2,
        compiler_params=params(),
        cost_estimate=cost(),
        name="core_sum",
    )(keep, come)


def fold_body(first, second, *refs, split, merged):
    if merged:
        come, *refs = refs
        both = come[...].astype(F32)
        height = first.shape[0]
        come_first, come_second = both[:height], both[height:]
    else:
        first_come, second_come, *refs = refs
        come_first, come_second = first_come[...].astype(F32), second_come[...].astype(F32)
    sum_first, sum_second = first[...] + come_first, second[...] + come_second
    if split:
        keep_first, keep_second, give = refs[-3:]
        half = keep_first.shape[0]
        keep_first[...], keep_second[...] = sum_first[:half], sum_second[:half]
        give[...] = jnp.concatenate([sum_first[half:], sum_second[half:]], axis=0).astype(BF16)
    else:
        out_first, out_second = refs[-2:]
        out_first[...], out_second[...] = sum_first, sum_second


def fold(first, second, come, split, *after):
    height, width = first.shape
    if split:
        out_shape = [jax.ShapeDtypeStruct((height // 2, width), F32)] * 2
        out_shape.append(jax.ShapeDtypeStruct((height, width), BF16))
    else:
        out_shape = [jax.ShapeDtypeStruct((height, width), F32)] * 2
    return pl.pallas_call(
        functools.partial(fold_body, split=split, merged=len(come) == 1),
        out_shape=out_shape,
        in_specs=[VMEM] * (2 + len(come)) + [ANY] * len(after),
        out_specs=[VMEM] * len(out_shape),
        compiler_params=params(),
        cost_estimate=cost(),
        name="fold",
    )(first, second, *come, *after)


def shards(
    features, weight_in, weight_out, adj_tiles, tile_rows, tile_cols, tile_counts, cotangent
):
    rows, width = features.shape
    tile_rows, tile_cols = jnp.swapaxes(tile_rows, 0, 1), jnp.swapaxes(tile_cols, 0, 1)

    f_mate = to_mate(features)
    f_other = to_core(features)
    w_near = to_panel(pick(weight_in))
    w_far = to_core(w_near)
    f_mate_other = to_core(f_mate)
    f_far = relay_out(f_mate)
    f_far_other = to_core(f_far)

    dense = build(tile_rows, tile_cols, tile_counts, adj_tiles, rows)
    p_own, p_mate, p_far, p_swap, p_cross = pull(cotangent, dense)
    p_mate, p_far = swap_sum(p_mate, p_far, to_core(p_cross))
    p_swap = to_core(p_swap)
    q_come = to_mate(meet(p_mate, relay_back(p_far)))

    total = spread_near(dense, features, f_other, f_mate)
    own, _ = spread_far(dense, total, f_far, f_mate_other, f_far_other)
    pieces = [own, to_panel(own)]
    pre_hidden, hid, mixed = hidden_step(
        pieces, weight_in, w_near, w_far, weight_out, dense
    )

    mixed = gate(mixed, q_come)
    t_mate = to_mate(mixed)
    t_other = to_core(mixed)
    t_mate_other = to_core(t_mate)
    t_far = relay_out(t_mate)
    t_far_other = to_core(t_far)

    pulled, kept, given = mix_step(p_own, p_swap, q_come, weight_out, dense)
    come = to_panel(given)
    out_keep, out_give = grad_call(out_grad_body, "out_grad", [hid, pulled], 2 * width, width)
    in_keep, in_give = grad_call(
        in_grad_body,
        "in_grad",
        [*pieces, pre_hidden, kept, come],
        2 * width,
        width,
        (pltpu.VMEM((rows, width), BF16),),
        (dense,),
    )
    out_near, out_far = core_sum(out_keep, to_core(out_give))
    out_far = gate(out_far, t_mate)
    in_near, in_far = core_sum(in_keep, to_core(in_give))
    first, second, come = in_near, out_near, [to_mate(in_far), to_mate(out_far)]

    total = spread_near(dense, mixed, t_other, t_mate, in_far)
    layer_output, token = spread_far(dense, total, t_far, t_mate_other, t_far_other)
    groups, distance = lax.axis_size("blk") // 4, 1
    while distance < groups:
        first, second, give = fold(first, second, come, True)
        come = [to_group(give, distance)]
        distance *= 2
    grad_weight_in, grad_weight_out = fold(first, second, come, False, token)
    return (layer_output, grad_weight_in, grad_weight_out)


def solution(mesh):
    return jax.shard_map(
        shards,
        mesh=mesh,
        in_specs=(
            P("blk", "feat"),
            P(None, "feat"),
            P(None, "feat"),
            P("blk", None, None, None, None),
            P("blk", None, None),
            P("blk", None, None),
            P("blk", None),
            P("blk", "feat"),
        ),
        out_specs=(P("blk", "feat"), P("blk", "feat"), P("blk", "feat")),
        check_vma=False,
    )
```

```python
import functools

import jax
import jax.numpy as jnp
from jax import lax
from jax.experimental import pallas as pl
from jax.experimental.pallas import tpu as pltpu
from jax.sharding import PartitionSpec as P

BF16 = jnp.bfloat16
F32 = jnp.float32
VMEM = pl.BlockSpec(memory_space=pltpu.VMEM)
SMEM = pl.BlockSpec(memory_space=pltpu.SMEM)
ANY = pl.BlockSpec(memory_space=pl.ANY)


def params(limit_mib=12):
    return pltpu.CompilerParams(vmem_limit_bytes=limit_mib * 1024 * 1024)


def cost(microseconds=0):
    return pl.CostEstimate(
        flops=1024, bytes_accessed=1024 + 3_600_000 * microseconds, transcendentals=0
    )


def gate_body(*refs):
    del refs


def gate(value, *after, microseconds=0):
    return pl.pallas_call(
        gate_body,
        out_shape=jax.ShapeDtypeStruct(value.shape, value.dtype),
        in_specs=[ANY] * (1 + len(after)),
        out_specs=ANY,
        input_output_aliases={0: 0},
        compiler_params=params(1),
        cost_estimate=cost(microseconds),
        name="gate",
    )(value, *after)


def coordinates():
    block = lax.axis_index("blk")
    return block & 1, (block >> 1) & 1, lax.axis_index("feat")


def coordinates():
    block = lax.axis_index("blk")
    return block & 1, (block >> 1) & 1, lax.axis_index("feat")


def copy_all(pairs, semaphores):
    copies = [
        pltpu.make_async_copy(source, target, semaphores.at[number])
        for number, (source, target) in enumerate(pairs)
    ]
    for copy in copies:
        copy.start()
    for copy in copies:
        copy.wait()


def coordinates():
    block = lax.axis_index("blk")
    return block & 1, (block >> 1) & 1, lax.axis_index("feat")


def blk_pairs(target):
    count = lax.axis_size("blk")
    return [(source, target(source) % count) for source in range(count)]


def to_core(value):
    return lax.ppermute(value, "blk", blk_pairs(lambda b: b ^ 1))


def to_mate(value):
    return lax.ppermute(value, "blk", blk_pairs(lambda b: b ^ 2))


def relay_out(value):
    return lax.ppermute(value, "blk", blk_pairs(lambda b: b - 4 if b & 2 else b + 4))


def relay_back(value):
    return lax.ppermute(value, "blk", blk_pairs(lambda b: b + 4 if b & 2 else b - 4))


def to_group(value, distance):
    return lax.ppermute(value, "blk", blk_pairs(lambda b: b ^ (4 * distance)))


def to_panel(value):
    return lax.ppermute(value, "feat", [(0, 1), (1, 0)])


def pick_body(w_in, send, semaphore):
    half = send.shape[0]
    core, _, panel = coordinates()
    start = pl.multiple_of(((1 - panel) ^ core) * half, half)
    copy = pltpu.make_async_copy(w_in.at[pl.ds(start, half), :], send, semaphore)
    copy.start()
    copy.wait()


def pick(w_in):
    width = w_in.shape[1]
    return pl.pallas_call(
        pick_body,
        out_shape=jax.ShapeDtypeStruct((width, width), BF16),
        in_specs=[ANY],
        out_specs=VMEM,
        scratch_shapes=[pltpu.SemaphoreType.DMA],
        compiler_params=params(4),
        cost_estimate=cost(),
        name="pick",
    )(w_in)


def build_body(rows, cols, counts, tiles, dense):
    _, steps, cap, tile, _ = tiles.shape
    radius = (steps - 1) // 2
    block_tiles = dense.shape[0] // tile
    core, mate, _ = coordinates()
    dense[...] = jnp.zeros_like(dense)

    def place(entry, carry):
        step, slot = entry // cap, entry % cap
        shifted = step - radius + core + 2
        chip = shifted // 2 - 1
        position = (shifted % 2) ^ core
        ahead = jnp.where(mate == 0, 1, -1)
        outside = jnp.where(position == 1, 4, jnp.where(chip == ahead, 2, 3))
        segment = jnp.where(chip == 0, position, outside)
        row = rows[step, 0, slot]
        col = segment * block_tiles + cols[step, 0, slot]

        @pl.when(slot < counts[0, step])
        def _():
            dense[
                pl.ds(pl.multiple_of(row * tile, tile), tile),
                pl.ds(pl.multiple_of(col * tile, tile), tile),
            ] = tiles[0, step, slot]

        return carry

    lax.fori_loop(0, steps * cap, place, 0)


def build(tile_rows, tile_cols, tile_counts, tiles, rows):
    return pl.pallas_call(
        build_body,
        out_shape=jax.ShapeDtypeStruct((rows, 5 * rows), BF16),
        in_specs=[SMEM] * 3 + [VMEM],
        out_specs=VMEM,
        compiler_params=params(),
        cost_estimate=cost(),
        name="build_dense",
    )(tile_rows, tile_cols, tile_counts, tiles)


def spread_near_body(dense, s0, s1, s2, *refs):
    total = refs[-1]
    rows = s0.shape[0]
    result = jnp.dot(dense[:, :rows], s0[...], preferred_element_type=F32)
    for index, ref in enumerate((s1, s2)):
        start = (index + 1) * rows
        result += jnp.dot(dense[:, start : start + rows], ref[...], preferred_element_type=F32)
    total[...] = result


def spread_near(dense, own, other, mate, *after):
    rows, cols = own.shape
    block = rows // 2
    whole = pl.BlockSpec((rows, cols), lambda i: (0, 0))
    return pl.pallas_call(
        spread_near_body,
        grid=(2,),
        out_shape=jax.ShapeDtypeStruct((rows, cols), F32),
        in_specs=[pl.BlockSpec((block, 3 * rows), lambda i: (i, 0))]
        + [whole] * 3
        + [ANY] * len(after),
        out_specs=pl.BlockSpec((block, cols), lambda i: (i, 0)),
        compiler_params=params(),
        cost_estimate=cost(),
        name="spread_near",
    )(dense, own, other, mate, *after)


def spread_far_body(dense, total, far, mate_other, far_upper, far_lower, out, token):
    rows = far.shape[0]
    core, mate, _ = coordinates()
    start = 3 * rows

    def add_up(*cross):
        result = total[...]
        result += jnp.dot(
            dense[:, start : start + rows], far[...], preferred_element_type=F32
        )
        place = start + rows
        for ref in cross:
            height = ref.shape[0]
            result += jnp.dot(
                dense[:, place : place + height], ref[...], preferred_element_type=F32
            )
            place += height
        out[...] = result.astype(BF16)
        token[...] = jnp.zeros_like(token)

    pl.when(core == mate)(lambda: add_up(far_upper, far_lower))
    pl.when(core != mate)(lambda: add_up(mate_other))


def spread_far(dense, total, far, mate_other, far_upper, far_lower):
    rows, cols = far.shape
    return pl.pallas_call(
        spread_far_body,
        out_shape=[
            jax.ShapeDtypeStruct((rows, cols), BF16),
            jax.ShapeDtypeStruct((8, 128), F32),
        ],
        in_specs=[VMEM] * 6,
        out_specs=[VMEM] * 2,
        compiler_params=params(),
        cost_estimate=cost(),
        name="spread_far",
    )(dense, total, far, mate_other, far_upper, far_lower)


def pull_body(cot, dense, own, mate, far, swap_own, swap_cross):
    rows = dense.shape[0]
    turned = cot[...].T
    terms = [
        jnp.dot(
            turned, dense[:, index * rows : (index + 1) * rows], preferred_element_type=F32
        )
        for index in range(5)
    ]
    own[...], mate[...], far[...] = terms[0], terms[2], terms[3]
    swap_own[...] = terms[1].astype(BF16)
    swap_cross[...] = terms[4].astype(BF16)


def pull(cot, dense):
    rows, cols = cot.shape
    return pl.pallas_call(
        pull_body,
        out_shape=[jax.ShapeDtypeStruct((cols, rows), F32)] * 3
        + [jax.ShapeDtypeStruct((cols, rows), BF16)] * 2,
        in_specs=[VMEM] * 2,
        out_specs=[VMEM] * 5,
        compiler_params=params(),
        cost_estimate=cost(),
        name="pull",
    )(cot, dense)


def swap_sum_body(mate_term, far_term, swap, mate_out, far_out):
    core, mate, _ = coordinates()
    cross = swap[...].astype(F32)
    cross_mate = jnp.where(core == mate, cross, 0.0)
    far_out[...] = (far_term[...] + (cross - cross_mate)).astype(BF16)
    mate_out[...] = mate_term[...] + cross_mate


def swap_sum(mate_term, far_term, swap):
    return pl.pallas_call(
        swap_sum_body,
        out_shape=[
            jax.ShapeDtypeStruct(mate_term.shape, F32),
            jax.ShapeDtypeStruct(far_term.shape, BF16),
        ],
        in_specs=[VMEM] * 3,
        out_specs=[VMEM] * 2,
        compiler_params=params(),
        cost_estimate=cost(),
        name="swap_sum",
    )(mate_term, far_term, swap)


def meet_body(mine, come, left, right):
    half = left.shape[1]
    total = mine[...] + come[...].astype(F32)
    left[...], right[...] = total[:, :half].astype(BF16), total[:, half:].astype(BF16)


def meet(mine, come):
    cols, rows = mine.shape
    return pl.pallas_call(
        meet_body,
        out_shape=[jax.ShapeDtypeStruct((cols, rows // 2), BF16)] * 2,
        in_specs=[VMEM] * 2,
        out_specs=[VMEM] * 2,
        compiler_params=params(),
        cost_estimate=cost(),
        name="meet",
    )(mine, come)


def hidden_body(s0, s1, w_mine, w_near, w_far, w_out, *refs):
    pre, hid, mixed = refs[-3:]
    rows, width = s0.shape
    tall = rows // 2
    core, _, panel = coordinates()

    def chunk(index, carry, w_theirs):
        span = pl.ds(pl.multiple_of(index * tall, tall), tall)
        mine, theirs = 0.0, 0.0
        for side, ref in enumerate((s0, s1)):
            taken = ref[span, :]
            place = pl.ds(pl.multiple_of((panel ^ side) * width, width), width)
            mine += jnp.dot(taken, w_mine[place, :], preferred_element_type=F32)
            theirs += jnp.dot(taken, w_theirs[side][...], preferred_element_type=F32)
        pre[span, :] = mine
        h_mine = (mine * jax.nn.sigmoid(mine)).astype(BF16)
        h_theirs = (theirs * jax.nn.sigmoid(theirs)).astype(BF16)
        hid[span, :width] = h_mine
        hid[span, width:] = h_theirs
        result = 0.0
        for side, value in enumerate((h_mine, h_theirs)):
            place = pl.ds(pl.multiple_of((panel ^ side) * width, width), width)
            result += jnp.dot(value, w_out[place, :], preferred_element_type=F32)
        mixed[span, :] = result.astype(BF16)
        return carry

    def chunks(w_theirs):
        lax.fori_loop(0, rows // tall, functools.partial(chunk, w_theirs=w_theirs), 0)

    pl.when(core == 0)(lambda: chunks((w_near, w_far)))
    pl.when(core == 1)(lambda: chunks((w_far, w_near)))


def hidden_step(pieces, w_mine, w_near, w_far, w_out, *after):
    rows, width = pieces[0].shape
    return pl.pallas_call(
        hidden_body,
        out_shape=[
            jax.ShapeDtypeStruct((rows, width), F32),
            jax.ShapeDtypeStruct((rows, 2 * width), BF16),
            jax.ShapeDtypeStruct((rows, width), BF16),
        ],
        in_specs=[VMEM] * 6 + [ANY] * len(after),
        out_specs=[VMEM] * 3,
        compiler_params=params(),
        cost_estimate=cost(),
        name="hidden",
    )(*pieces, w_mine, w_near, w_far, w_out, *after)


def mix_body(own, swap, left, right, w_out, *refs):
    pulled, keep, give = refs[-3:]
    half = keep.shape[1]
    _, _, panel = coordinates()
    come = jnp.concatenate([left[...], right[...]], axis=1).astype(F32)
    total = own[...] + swap[...].astype(F32) + come
    pulled[...] = total.astype(BF16).T
    contract = (((1,), (1,)), ((), ()))
    theirs = w_out[pl.ds(pl.multiple_of((1 - panel) * half, half), half), :]
    give[...] = lax.dot_general(
        pulled[...], theirs, contract, preferred_element_type=F32
    ).astype(BF16)
    mine = w_out[pl.ds(pl.multiple_of(panel * half, half), half), :]
    keep[...] = lax.dot_general(pulled[...], mine, contract, preferred_element_type=F32)


def mix_step(own, swap, left, right, w_out, *after):
    cols, rows = own.shape
    half = w_out.shape[0] // 2
    return pl.pallas_call(
        mix_body,
        out_shape=[
            jax.ShapeDtypeStruct((rows, cols), BF16),
            jax.ShapeDtypeStruct((rows, half), F32),
            jax.ShapeDtypeStruct((rows, half), BF16),
        ],
        in_specs=[VMEM] * 5 + [ANY] * len(after),
        out_specs=[VMEM] * 3,
        compiler_params=params(),
        cost_estimate=cost(),
        name="mix_back",
    )(own, swap, left, right, w_out, *after)


def reversed_bits(number, count):
    result = 0
    while count > 1:
        result, number, count = 2 * result + number % 2, number // 2, count // 2
    return result


def split_term(total, keep, give, scratch, blocks, sides_first):
    core, mate, _ = coordinates()
    share = total.shape[0] // blocks
    groups = blocks // 4
    mine = lax.axis_index("blk") // 4
    for position in range(groups):
        group = mine ^ reversed_bits(position, groups)
        for side in range(2):
            owner = 4 * group + 2 * (mate ^ side)
            place = side * groups + position if sides_first else 2 * position + side
            target = pl.ds(place * share, share)
            source = pl.multiple_of((owner + core) * share, share)
            keep[target, :] = total[pl.ds(source, share), :]
            source = pl.multiple_of((owner + 1 - core) * share, share)
            scratch[target, :] = total[pl.ds(source, share), :]
    give[...] = scratch[...].astype(BF16)


def grad_into(total, pieces, right):
    _, _, panel = coordinates()
    contract = (((0,), (0,)), ((), ()))
    for side, (ref, first) in enumerate(pieces):
        width = right.shape[1]
        half = width // 2
        for number in range(2):
            start = (panel ^ side) * width + number * half
            source = first + number * half
            total[pl.ds(pl.multiple_of(start, half), half), :] = lax.dot_general(
                ref[:, source : source + half],
                right[...],
                contract,
                preferred_element_type=F32,
            )


def out_grad_body(hid, pulled, keep, give, total, scratch, *, blocks):
    width = pulled.shape[1]
    grad_into(total, ((hid, 0), (hid, width)), pulled)
    split_term(total, keep, give, scratch, blocks, False)


def in_grad_body(s0, s1, pre, kept, come, *refs, blocks):
    keep, give, total, scratch, back = refs[-5:]
    pre_hidden = pre[...]
    gate = jax.nn.sigmoid(pre_hidden)
    back_hidden = kept[...] + come[...].astype(F32)
    back[...] = (back_hidden * gate * (1.0 + pre_hidden * (1.0 - gate))).astype(BF16)
    grad_into(total, ((s0, 0), (s1, 0)), back)
    split_term(total, keep, give, scratch, blocks, True)


def grad_call(body, name, operands, height, width, scratch=(), after=()):
    blocks = lax.axis_size("blk")
    half = height // 2
    return pl.pallas_call(
        functools.partial(body, blocks=blocks),
        out_shape=[
            jax.ShapeDtypeStruct((half, width), F32),
            jax.ShapeDtypeStruct((half, width), BF16),
        ],
        in_specs=[VMEM] * len(operands) + [ANY] * len(after),
        out_specs=[VMEM] * 2,
        scratch_shapes=[
            pltpu.VMEM((height, width), F32),
            pltpu.VMEM((half, width), F32),
            *scratch,
        ],
        compiler_params=params(),
        cost_estimate=cost(),
        name=name,
    )(*operands, *after)


def fold_body(keep, come, *refs, last):
    total = keep[...] + come[...].astype(F32)
    if last:
        refs[-1][...] = total
    else:
        near, far = refs[-2:]
        half = near.shape[0]
        near[...], far[...] = total[:half], total[half:].astype(BF16)


def fold(keep, come, last, *after):
    height, width = keep.shape
    if last:
        out_shape = [jax.ShapeDtypeStruct((height, width), F32)]
    else:
        shape = (height // 2, width)
        out_shape = [jax.ShapeDtypeStruct(shape, F32), jax.ShapeDtypeStruct(shape, BF16)]
    return pl.pallas_call(
        functools.partial(fold_body, last=last),
        out_shape=out_shape,
        in_specs=[VMEM] * 2 + [ANY] * len(after),
        out_specs=[VMEM] * len(out_shape),
        compiler_params=params(),
        cost_estimate=cost(),
        name="fold",
    )(keep, come, *after)


def group_hops():
    groups, distance, hops = lax.axis_size("blk") // 4, 1, []
    while distance < groups:
        hops.append(functools.partial(to_group, distance=distance))
        distance *= 2
    return hops


def shards(
    features, weight_in, weight_out, adj_tiles, tile_rows, tile_cols, tile_counts, cotangent
):
    rows, width = features.shape
    tile_rows, tile_cols = jnp.swapaxes(tile_rows, 0, 1), jnp.swapaxes(tile_cols, 0, 1)

    f_mate = to_mate(features)
    f_other = to_core(features)
    w_near = to_panel(pick(weight_in))
    w_far = to_core(w_near)
    f_mate_other = to_core(f_mate)
    f_far = relay_out(f_mate)
    f_far_other = [to_core(f_far[: rows // 2]), to_core(f_far[rows // 2 :])]

    dense = build(tile_rows, tile_cols, tile_counts, adj_tiles, rows)
    p_own, p_mate, p_far, p_swap, p_cross = pull(cotangent, dense)
    p_mate, p_far = swap_sum(p_mate, p_far, to_core(p_cross))
    p_swap = to_core(p_swap)
    q_come = [to_mate(half) for half in meet(p_mate, relay_back(p_far))]

    total = spread_near(dense, features, f_other, f_mate)
    own, _ = spread_far(dense, total, f_far, f_mate_other, *f_far_other)
    pieces = [own, to_panel(own)]
    pre_hidden, hid, mixed = hidden_step(
        pieces, weight_in, w_near, w_far, weight_out, dense
    )

    mixed = gate(mixed, *q_come)
    t_mate = to_mate(mixed)
    t_other = to_core(mixed)
    t_mate_other = to_core(t_mate)
    t_far = relay_out(t_mate)
    t_far_other = [to_core(t_far[: rows // 2]), to_core(t_far[rows // 2 :])]

    pulled, kept, given = mix_step(p_own, p_swap, *q_come, weight_out, dense)
    come = to_panel(given)
    out_keep, out_give = grad_call(out_grad_body, "out_grad", [hid, pulled], 2 * width, width)
    in_keep, in_give = grad_call(
        in_grad_body,
        "in_grad",
        [*pieces, pre_hidden, kept, come],
        2 * width,
        width,
        (pltpu.VMEM((rows, width), BF16),),
        (dense,),
    )
    for hop in [to_core, *group_hops()]:
        out_keep, out_give = fold(out_keep, hop(out_give), False)
    (grad_weight_out,) = fold(out_keep, to_mate(out_give), True)
    *hops, last_hop = [to_core, to_mate, *group_hops()]
    in_far = None
    for hop in hops:
        in_keep, in_give = fold(in_keep, hop(in_give), False)
        in_far = in_give if in_far is None else in_far

    total = spread_near(dense, mixed, t_other, t_mate, in_far)
    layer_output, token = spread_far(dense, total, t_far, t_mate_other, *t_far_other)
    (grad_weight_in,) = fold(in_keep, last_hop(in_give), True, token)
    return (layer_output, grad_weight_in, grad_weight_out)


def solution(mesh):
    return jax.shard_map(
        shards,
        mesh=mesh,
        in_specs=(
            P("blk", "feat"),
            P(None, "feat"),
            P(None, "feat"),
            P("blk", None, None, None, None),
            P("blk", None, None),
            P("blk", None, None),
            P("blk", None),
            P("blk", "feat"),
        ),
        out_specs=(P("blk", "feat"), P("blk", "feat"), P("blk", "feat")),
        check_vma=False,
    )
```

```python
import functools

import jax
import jax.numpy as jnp
from jax import lax
from jax.experimental import pallas as pl
from jax.experimental.pallas import tpu as pltpu
from jax.sharding import PartitionSpec as P

BF16 = jnp.bfloat16
F32 = jnp.float32
VMEM = pl.BlockSpec(memory_space=pltpu.VMEM)
SMEM = pl.BlockSpec(memory_space=pltpu.SMEM)
ANY = pl.BlockSpec(memory_space=pl.ANY)


def params(limit_mib=12):
    return pltpu.CompilerParams(vmem_limit_bytes=limit_mib * 1024 * 1024)


def cost(microseconds=0):
    return pl.CostEstimate(
        flops=1024, bytes_accessed=1024 + 3_600_000 * microseconds, transcendentals=0
    )


def gate_body(*refs):
    del refs


def gate(value, *after, microseconds=0):
    return pl.pallas_call(
        gate_body,
        out_shape=jax.ShapeDtypeStruct(value.shape, value.dtype),
        in_specs=[ANY] * (1 + len(after)),
        out_specs=ANY,
        input_output_aliases={0: 0},
        compiler_params=params(1),
        cost_estimate=cost(microseconds),
        name="gate",
    )(value, *after)


def coordinates():
    block = lax.axis_index("blk")
    return block & 1, (block >> 1) & 1, lax.axis_index("feat")


def coordinates():
    block = lax.axis_index("blk")
    return block & 1, (block >> 1) & 1, lax.axis_index("feat")


def copy_all(pairs, semaphores):
    copies = [
        pltpu.make_async_copy(source, target, semaphores.at[number])
        for number, (source, target) in enumerate(pairs)
    ]
    for copy in copies:
        copy.start()
    for copy in copies:
        copy.wait()


def coordinates():
    block = lax.axis_index("blk")
    return block & 1, (block >> 1) & 1, lax.axis_index("feat")


def blk_pairs(target):
    count = lax.axis_size("blk")
    return [(source, target(source) % count) for source in range(count)]


def to_core(value):
    return lax.ppermute(value, "blk", blk_pairs(lambda b: b ^ 1))


def to_mate(value):
    return lax.ppermute(value, "blk", blk_pairs(lambda b: b ^ 2))


def relay_out(value):
    return lax.ppermute(value, "blk", blk_pairs(lambda b: b - 4 if b & 2 else b + 4))


def relay_back(value):
    return lax.ppermute(value, "blk", blk_pairs(lambda b: b + 4 if b & 2 else b - 4))


def to_group(value, distance):
    return lax.ppermute(value, "blk", blk_pairs(lambda b: b ^ (4 * distance)))


def to_panel(value):
    return lax.ppermute(value, "feat", [(0, 1), (1, 0)])


def pick_body(w_in, send, semaphore):
    half = send.shape[0]
    core, _, panel = coordinates()
    start = pl.multiple_of(((1 - panel) ^ core) * half, half)
    copy = pltpu.make_async_copy(w_in.at[pl.ds(start, half), :], send, semaphore)
    copy.start()
    copy.wait()


def pick(w_in):
    width = w_in.shape[1]
    return pl.pallas_call(
        pick_body,
        out_shape=jax.ShapeDtypeStruct((width, width), BF16),
        in_specs=[ANY],
        out_specs=VMEM,
        scratch_shapes=[pltpu.SemaphoreType.DMA],
        compiler_params=params(4),
        cost_estimate=cost(),
        name="pick",
    )(w_in)


def build_body(rows, cols, counts, tiles, dense):
    _, steps, cap, tile, _ = tiles.shape
    radius = (steps - 1) // 2
    block_tiles = dense.shape[0] // tile
    core, mate, _ = coordinates()
    dense[...] = jnp.zeros_like(dense)

    def place(entry, carry):
        step, slot = entry // cap, entry % cap
        shifted = step - radius + core + 2
        chip = shifted // 2 - 1
        position = (shifted % 2) ^ core
        ahead = jnp.where(mate == 0, 1, -1)
        outside = jnp.where(position == 1, 4, jnp.where(chip == ahead, 2, 3))
        segment = jnp.where(chip == 0, position, outside)
        row = rows[step, 0, slot]
        col = segment * block_tiles + cols[step, 0, slot]

        @pl.when(slot < counts[0, step])
        def _():
            dense[
                pl.ds(pl.multiple_of(row * tile, tile), tile),
                pl.ds(pl.multiple_of(col * tile, tile), tile),
            ] = tiles[0, step, slot]

        return carry

    lax.fori_loop(0, steps * cap, place, 0)


def build(tile_rows, tile_cols, tile_counts, tiles, rows):
    return pl.pallas_call(
        build_body,
        out_shape=jax.ShapeDtypeStruct((rows, 5 * rows), BF16),
        in_specs=[SMEM] * 3 + [VMEM],
        out_specs=VMEM,
        compiler_params=params(),
        cost_estimate=cost(),
        name="build_dense",
    )(tile_rows, tile_cols, tile_counts, tiles)


def spread_near_body(dense, s0, s1, s2, *refs):
    total = refs[-1]
    rows = s0.shape[0]
    result = jnp.dot(dense[:, :rows], s0[...], preferred_element_type=F32)
    for index, ref in enumerate((s1, s2)):
        start = (index + 1) * rows
        result += jnp.dot(dense[:, start : start + rows], ref[...], preferred_element_type=F32)
    total[...] = result


def spread_near(dense, own, other, mate, *after):
    rows, cols = own.shape
    block = rows // 2
    whole = pl.BlockSpec((rows, cols), lambda i: (0, 0))
    return pl.pallas_call(
        spread_near_body,
        grid=(2,),
        out_shape=jax.ShapeDtypeStruct((rows, cols), F32),
        in_specs=[pl.BlockSpec((block, 3 * rows), lambda i: (i, 0))]
        + [whole] * 3
        + [ANY] * len(after),
        out_specs=pl.BlockSpec((block, cols), lambda i: (i, 0)),
        compiler_params=params(),
        cost_estimate=cost(),
        name="spread_near",
    )(dense, own, other, mate, *after)


def spread_far_body(dense, total, far, mate_other, *refs):
    *far_other, out, token = refs
    rows = far.shape[0]
    core, mate, _ = coordinates()
    start = 3 * rows

    def add_up(*cross):
        result = total[...]
        result += jnp.dot(
            dense[:, start : start + rows], far[...], preferred_element_type=F32
        )
        place = start + rows
        for ref in cross:
            height = ref.shape[0]
            result += jnp.dot(
                dense[:, place : place + height], ref[...], preferred_element_type=F32
            )
            place += height
        out[...] = result.astype(BF16)
        token[...] = jnp.zeros_like(token)

    pl.when(core == mate)(lambda: add_up(*far_other))
    pl.when(core != mate)(lambda: add_up(mate_other))


def spread_far(dense, total, far, mate_other, *far_other):
    rows, cols = far.shape
    return pl.pallas_call(
        spread_far_body,
        out_shape=[
            jax.ShapeDtypeStruct((rows, cols), BF16),
            jax.ShapeDtypeStruct((8, 128), F32),
        ],
        in_specs=[VMEM] * (4 + len(far_other)),
        out_specs=[VMEM] * 2,
        compiler_params=params(),
        cost_estimate=cost(),
        name="spread_far",
    )(dense, total, far, mate_other, *far_other)


def pull_body(cot, dense, own, mate, far, swap_own, swap_cross):
    rows = dense.shape[0]
    turned = cot[...].T
    terms = [
        jnp.dot(
            turned, dense[:, index * rows : (index + 1) * rows], preferred_element_type=F32
        )
        for index in range(5)
    ]
    own[...], mate[...], far[...] = terms[0], terms[2], terms[3]
    swap_own[...] = terms[1].astype(BF16)
    swap_cross[...] = terms[4].astype(BF16)


def pull(cot, dense):
    rows, cols = cot.shape
    return pl.pallas_call(
        pull_body,
        out_shape=[jax.ShapeDtypeStruct((cols, rows), F32)] * 3
        + [jax.ShapeDtypeStruct((cols, rows), BF16)] * 2,
        in_specs=[VMEM] * 2,
        out_specs=[VMEM] * 5,
        compiler_params=params(),
        cost_estimate=cost(),
        name="pull",
    )(cot, dense)


def swap_sum_body(mate_term, far_term, swap, mate_out, far_out):
    core, mate, _ = coordinates()
    cross = swap[...].astype(F32)
    cross_mate = jnp.where(core == mate, cross, 0.0)
    far_out[...] = (far_term[...] + (cross - cross_mate)).astype(BF16)
    mate_out[...] = mate_term[...] + cross_mate


def swap_sum(mate_term, far_term, swap):
    return pl.pallas_call(
        swap_sum_body,
        out_shape=[
            jax.ShapeDtypeStruct(mate_term.shape, F32),
            jax.ShapeDtypeStruct(far_term.shape, BF16),
        ],
        in_specs=[VMEM] * 3,
        out_specs=[VMEM] * 2,
        compiler_params=params(),
        cost_estimate=cost(),
        name="swap_sum",
    )(mate_term, far_term, swap)


def hidden_body(s0, s1, w_mine, w_near, w_far, w_out, *refs):
    pre, hid, mixed = refs[-3:]
    rows, width = s0.shape
    tall = rows // 2
    core, _, panel = coordinates()

    def chunk(index, carry, w_theirs):
        span = pl.ds(pl.multiple_of(index * tall, tall), tall)
        mine, theirs = 0.0, 0.0
        for side, ref in enumerate((s0, s1)):
            taken = ref[span, :]
            place = pl.ds(pl.multiple_of((panel ^ side) * width, width), width)
            mine += jnp.dot(taken, w_mine[place, :], preferred_element_type=F32)
            theirs += jnp.dot(taken, w_theirs[side][...], preferred_element_type=F32)
        pre[span, :] = mine
        h_mine = (mine * jax.nn.sigmoid(mine)).astype(BF16)
        h_theirs = (theirs * jax.nn.sigmoid(theirs)).astype(BF16)
        hid[span, :width] = h_mine
        hid[span, width:] = h_theirs
        result = 0.0
        for side, value in enumerate((h_mine, h_theirs)):
            place = pl.ds(pl.multiple_of((panel ^ side) * width, width), width)
            result += jnp.dot(value, w_out[place, :], preferred_element_type=F32)
        mixed[span, :] = result.astype(BF16)
        return carry

    def chunks(w_theirs):
        lax.fori_loop(0, rows // tall, functools.partial(chunk, w_theirs=w_theirs), 0)

    pl.when(core == 0)(lambda: chunks((w_near, w_far)))
    pl.when(core == 1)(lambda: chunks((w_far, w_near)))


def hidden_step(pieces, w_mine, w_near, w_far, w_out, *after):
    rows, width = pieces[0].shape
    return pl.pallas_call(
        hidden_body,
        out_shape=[
            jax.ShapeDtypeStruct((rows, width), F32),
            jax.ShapeDtypeStruct((rows, 2 * width), BF16),
            jax.ShapeDtypeStruct((rows, width), BF16),
        ],
        in_specs=[VMEM] * 6 + [ANY] * len(after),
        out_specs=[VMEM] * 3,
        compiler_params=params(),
        cost_estimate=cost(),
        name="hidden",
    )(*pieces, w_mine, w_near, w_far, w_out, *after)


def mix_body(own, swap, left, right, w_out, *refs):
    pulled, keep, give = refs[-3:]
    half = keep.shape[1]
    _, _, panel = coordinates()
    come = jnp.concatenate([left[...], right[...]], axis=1).astype(F32)
    total = own[...] + swap[...].astype(F32) + come
    pulled[...] = total.astype(BF16).T
    contract = (((1,), (1,)), ((), ()))
    theirs = w_out[pl.ds(pl.multiple_of((1 - panel) * half, half), half), :]
    give[...] = lax.dot_general(
        pulled[...], theirs, contract, preferred_element_type=F32
    ).astype(BF16)
    mine = w_out[pl.ds(pl.multiple_of(panel * half, half), half), :]
    keep[...] = lax.dot_general(pulled[...], mine, contract, preferred_element_type=F32)


def mix_step(own, swap, left, right, w_out, *after):
    cols, rows = own.shape
    half = w_out.shape[0] // 2
    return pl.pallas_call(
        mix_body,
        out_shape=[
            jax.ShapeDtypeStruct((rows, cols), BF16),
            jax.ShapeDtypeStruct((rows, half), F32),
            jax.ShapeDtypeStruct((rows, half), BF16),
        ],
        in_specs=[VMEM] * 5 + [ANY] * len(after),
        out_specs=[VMEM] * 3,
        compiler_params=params(),
        cost_estimate=cost(),
        name="mix_back",
    )(own, swap, left, right, w_out, *after)


def reversed_bits(number, count):
    result = 0
    while count > 1:
        result, number, count = 2 * result + number % 2, number // 2, count // 2
    return result


def split_term(total, keep, give, scratch, blocks):
    core, mate, _ = coordinates()
    share = total.shape[0] // blocks
    groups = blocks // 4
    mine = lax.axis_index("blk") // 4
    for position in range(groups):
        group = mine ^ reversed_bits(position, groups)
        for side in range(2):
            owner = 4 * group + 2 * (mate ^ side)
            target = pl.ds((side * groups + position) * share, share)
            source = pl.multiple_of((owner + core) * share, share)
            keep[target, :] = total[pl.ds(source, share), :]
            source = pl.multiple_of((owner + 1 - core) * share, share)
            scratch[target, :] = total[pl.ds(source, share), :]
    give[...] = scratch[...].astype(BF16)


def grad_into(total, pieces, right):
    _, _, panel = coordinates()
    contract = (((0,), (0,)), ((), ()))
    for side, (ref, first) in enumerate(pieces):
        width = right.shape[1]
        half = width // 2
        for number in range(2):
            start = (panel ^ side) * width + number * half
            source = first + number * half
            total[pl.ds(pl.multiple_of(start, half), half), :] = lax.dot_general(
                ref[:, source : source + half],
                right[...],
                contract,
                preferred_element_type=F32,
            )


def out_grad_body(hid, pulled, keep, give, total, scratch, *, blocks):
    width = pulled.shape[1]
    grad_into(total, ((hid, 0), (hid, width)), pulled)
    split_term(total, keep, give, scratch, blocks)


def in_grad_body(s0, s1, pre, kept, come, *refs, blocks):
    keep, give, total, scratch, back = refs[-5:]
    pre_hidden = pre[...]
    gate = jax.nn.sigmoid(pre_hidden)
    back_hidden = kept[...] + come[...].astype(F32)
    back[...] = (back_hidden * gate * (1.0 + pre_hidden * (1.0 - gate))).astype(BF16)
    grad_into(total, ((s0, 0), (s1, 0)), back)
    split_term(total, keep, give, scratch, blocks)


def grad_call(body, name, operands, height, width, scratch=(), after=()):
    blocks = lax.axis_size("blk")
    half = height // 2
    return pl.pallas_call(
        functools.partial(body, blocks=blocks),
        out_shape=[
            jax.ShapeDtypeStruct((half, width), F32),
            jax.ShapeDtypeStruct((half, width), BF16),
        ],
        in_specs=[VMEM] * len(operands) + [ANY] * len(after),
        out_specs=[VMEM] * 2,
        scratch_shapes=[
            pltpu.VMEM((height, width), F32),
            pltpu.VMEM((half, width), F32),
            *scratch,
        ],
        compiler_params=params(),
        cost_estimate=cost(),
        name=name,
    )(*operands, *after)


def core_sum_body(keep, come, near, far):
    half = near.shape[0]
    near[...] = keep[:half] + come[:half].astype(F32)
    far[...] = (keep[half:] + come[half:].astype(F32)).astype(BF16)


def core_sum(keep, come):
    height, width = keep.shape
    shape = (height // 2, width)
    return pl.pallas_call(
        core_sum_body,
        out_shape=[jax.ShapeDtypeStruct(shape, F32), jax.ShapeDtypeStruct(shape, BF16)],
        in_specs=[VMEM] * 2,
        out_specs=[VMEM] * 2,
        compiler_params=params(),
        cost_estimate=cost(),
        name="core_sum",
    )(keep, come)


def fold_body(first, second, *refs, split, merged):
    if merged:
        come, *refs = refs
        both = come[...].astype(F32)
        height = first.shape[0]
        come_first, come_second = both[:height], both[height:]
    else:
        first_come, second_come, *refs = refs
        come_first, come_second = first_come[...].astype(F32), second_come[...].astype(F32)
    sum_first, sum_second = first[...] + come_first, second[...] + come_second
    if split:
        keep_first, keep_second, give = refs[-3:]
        half = keep_first.shape[0]
        keep_first[...], keep_second[...] = sum_first[:half], sum_second[:half]
        give[...] = jnp.concatenate([sum_first[half:], sum_second[half:]], axis=0).astype(BF16)
    else:
        out_first, out_second = refs[-2:]
        out_first[...], out_second[...] = sum_first, sum_second


def fold(first, second, come, split, *after):
    height, width = first.shape
    if split:
        out_shape = [jax.ShapeDtypeStruct((height // 2, width), F32)] * 2
        out_shape.append(jax.ShapeDtypeStruct((height, width), BF16))
    else:
        out_shape = [jax.ShapeDtypeStruct((height, width), F32)] * 2
    return pl.pallas_call(
        functools.partial(fold_body, split=split, merged=len(come) == 1),
        out_shape=out_shape,
        in_specs=[VMEM] * (2 + len(come)) + [ANY] * len(after),
        out_specs=[VMEM] * len(out_shape),
        compiler_params=params(),
        cost_estimate=cost(),
        name="fold",
    )(first, second, *come, *after)


def shards(
    features, weight_in, weight_out, adj_tiles, tile_rows, tile_cols, tile_counts, cotangent
):
    rows, width = features.shape
    tile_rows, tile_cols = jnp.swapaxes(tile_rows, 0, 1), jnp.swapaxes(tile_cols, 0, 1)

    f_mate = to_mate(features)
    f_other = to_core(features)
    w_near = to_panel(pick(weight_in))
    w_far = to_core(w_near)
    f_mate_other = to_core(f_mate)
    f_far = relay_out(f_mate)
    f_far_other = [to_core(f_far[: rows // 2]), to_core(f_far[rows // 2 :])]

    dense = build(tile_rows, tile_cols, tile_counts, adj_tiles, rows)
    p_own, p_mate, p_far, p_swap, p_cross = pull(cotangent, dense)
    p_mate, p_far = swap_sum(p_mate, p_far, to_core(p_cross))
    p_swap = to_core(p_swap)
    q_term = (p_mate + relay_back(p_far).astype(F32)).astype(BF16)
    q_come = [to_mate(q_term[:, : rows // 2]), to_mate(q_term[:, rows // 2 :])]

    total = spread_near(dense, features, f_other, f_mate)
    own, _ = spread_far(dense, total, f_far, f_mate_other, *f_far_other)
    pieces = [own, to_panel(own)]
    pre_hidden, hid, mixed = hidden_step(
        pieces, weight_in, w_near, w_far, weight_out, dense
    )

    mixed = gate(mixed, *q_come)
    t_mate = to_mate(mixed)
    t_other = to_core(mixed)
    t_mate_other = to_core(t_mate)
    t_far = relay_out(t_mate)
    t_far_other = [to_core(t_far)]

    pulled, kept, given = mix_step(p_own, p_swap, *q_come, weight_out, dense, hid)
    come = to_panel(given)
    out_keep, out_give = grad_call(out_grad_body, "out_grad", [hid, pulled], 2 * width, width)
    in_keep, in_give = grad_call(
        in_grad_body,
        "in_grad",
        [*pieces, pre_hidden, kept, come],
        2 * width,
        width,
        (pltpu.VMEM((rows, width), BF16),),
        (dense,),
    )
    out_near, out_far = core_sum(out_keep, to_core(out_give))
    out_far = gate(out_far, t_mate)
    in_near, in_far = core_sum(in_keep, to_core(in_give))
    first, second, come = in_near, out_near, [to_mate(in_far), to_mate(out_far)]

    total = spread_near(dense, mixed, t_other, t_mate, in_far)
    layer_output, token = spread_far(dense, total, t_far, t_mate_other, *t_far_other)
    groups, distance = lax.axis_size("blk") // 4, 1
    while distance < groups:
        first, second, give = fold(first, second, come, True)
        come = [to_group(give, distance)]
        distance *= 2
    grad_weight_in, grad_weight_out = fold(first, second, come, False, token)
    return (layer_output, grad_weight_in, grad_weight_out)


def solution(mesh):
    return jax.shard_map(
        shards,
        mesh=mesh,
        in_specs=(
            P("blk", "feat"),
            P(None, "feat"),
            P(None, "feat"),
            P("blk", None, None, None, None),
            P("blk", None, None),
            P("blk", None, None),
            P("blk", None),
            P("blk", "feat"),
        ),
        out_specs=(P("blk", "feat"), P("blk", "feat"), P("blk", "feat")),
        check_vma=False,
    )
```

```python
import functools

import jax
import jax.numpy as jnp
from jax import lax
from jax.experimental import pallas as pl
from jax.experimental.pallas import tpu as pltpu
from jax.sharding import PartitionSpec as P

BF16 = jnp.bfloat16
F32 = jnp.float32
VMEM = pl.BlockSpec(memory_space=pltpu.VMEM)
SMEM = pl.BlockSpec(memory_space=pltpu.SMEM)
ANY = pl.BlockSpec(memory_space=pl.ANY)


def params(limit_mib=12):
    return pltpu.CompilerParams(vmem_limit_bytes=limit_mib * 1024 * 1024)


def cost(microseconds=0):
    return pl.CostEstimate(
        flops=1024, bytes_accessed=1024 + 3_600_000 * microseconds, transcendentals=0
    )


def gate_body(*refs):
    del refs


def gate(value, *after, microseconds=0):
    return pl.pallas_call(
        gate_body,
        out_shape=jax.ShapeDtypeStruct(value.shape, value.dtype),
        in_specs=[ANY] * (1 + len(after)),
        out_specs=ANY,
        input_output_aliases={0: 0},
        compiler_params=params(1),
        cost_estimate=cost(microseconds),
        name="gate",
    )(value, *after)


def coordinates():
    block = lax.axis_index("blk")
    return block & 1, (block >> 1) & 1, lax.axis_index("feat")


def coordinates():
    block = lax.axis_index("blk")
    return block & 1, (block >> 1) & 1, lax.axis_index("feat")


def copy_all(pairs, semaphores):
    copies = [
        pltpu.make_async_copy(source, target, semaphores.at[number])
        for number, (source, target) in enumerate(pairs)
    ]
    for copy in copies:
        copy.start()
    for copy in copies:
        copy.wait()


def coordinates():
    block = lax.axis_index("blk")
    return block & 1, (block >> 1) & 1, lax.axis_index("feat")


def blk_pairs(target):
    count = lax.axis_size("blk")
    return [(source, target(source) % count) for source in range(count)]


def to_core(value):
    return lax.ppermute(value, "blk", blk_pairs(lambda b: b ^ 1))


def to_mate(value):
    return lax.ppermute(value, "blk", blk_pairs(lambda b: b ^ 2))


def relay_out(value):
    return lax.ppermute(value, "blk", blk_pairs(lambda b: b - 4 if b & 2 else b + 4))


def relay_back(value):
    return lax.ppermute(value, "blk", blk_pairs(lambda b: b + 4 if b & 2 else b - 4))


def to_group(value, distance):
    return lax.ppermute(value, "blk", blk_pairs(lambda b: b ^ (4 * distance)))


def to_panel(value):
    return lax.ppermute(value, "feat", [(0, 1), (1, 0)])


def pick_body(w_in, send, semaphore):
    half = send.shape[0]
    core, _, panel = coordinates()
    start = pl.multiple_of(((1 - panel) ^ core) * half, half)
    copy = pltpu.make_async_copy(w_in.at[pl.ds(start, half), :], send, semaphore)
    copy.start()
    copy.wait()


def pick(w_in):
    width = w_in.shape[1]
    return pl.pallas_call(
        pick_body,
        out_shape=jax.ShapeDtypeStruct((width, width), BF16),
        in_specs=[ANY],
        out_specs=VMEM,
        scratch_shapes=[pltpu.SemaphoreType.DMA],
        compiler_params=params(4),
        cost_estimate=cost(),
        name="pick",
    )(w_in)


def build_body(rows, cols, counts, tiles, dense):
    _, steps, cap, tile, _ = tiles.shape
    radius = (steps - 1) // 2
    block_tiles = dense.shape[0] // tile
    core, mate, _ = coordinates()
    dense[...] = jnp.zeros_like(dense)

    def place(entry, carry):
        step, slot = entry // cap, entry % cap
        shifted = step - radius + core + 2
        chip = shifted // 2 - 1
        position = (shifted % 2) ^ core
        ahead = jnp.where(mate == 0, 1, -1)
        outside = jnp.where(position == 1, 4, jnp.where(chip == ahead, 2, 3))
        segment = jnp.where(chip == 0, position, outside)
        row = rows[step, 0, slot]
        col = segment * block_tiles + cols[step, 0, slot]

        @pl.when(slot < counts[0, step])
        def _():
            dense[
                pl.ds(pl.multiple_of(row * tile, tile), tile),
                pl.ds(pl.multiple_of(col * tile, tile), tile),
            ] = tiles[0, step, slot]

        return carry

    lax.fori_loop(0, steps * cap, place, 0)


def build(tile_rows, tile_cols, tile_counts, tiles, rows):
    return pl.pallas_call(
        build_body,
        out_shape=jax.ShapeDtypeStruct((rows, 5 * rows), BF16),
        in_specs=[SMEM] * 3 + [VMEM],
        out_specs=VMEM,
        compiler_params=params(),
        cost_estimate=cost(),
        name="build_dense",
    )(tile_rows, tile_cols, tile_counts, tiles)


def sum_products(result, dense, first, refs):
    for ref in refs:
        height = ref.shape[0]
        product = jnp.dot(
            dense[:, first : first + height], ref[...], preferred_element_type=F32
        )
        result = product if result is None else result + product
        first += height
    return result


def spread_near_body(dense, s0, s1, s2, s3, *refs):
    refs[-1][...] = sum_products(None, dense, 0, (s0, s1, s2, s3))


def spread_near(dense, own, other, mate, *after):
    rows, cols = own.shape
    block = rows // 2
    whole = pl.BlockSpec((rows, cols), lambda i: (0, 0))
    half = pl.BlockSpec((block, cols), lambda i: (0, 0))
    return pl.pallas_call(
        spread_near_body,
        grid=(2,),
        out_shape=jax.ShapeDtypeStruct((rows, cols), F32),
        in_specs=[
            pl.BlockSpec((block, 3 * rows), lambda i: (i, 0)),
            whole,
            whole,
            half,
            half,
            *[ANY] * len(after),
        ],
        out_specs=pl.BlockSpec((block, cols), lambda i: (i, 0)),
        compiler_params=params(),
        cost_estimate=cost(),
        name="spread_near",
    )(dense, own, other, *mate, *after)


def spread_far_body(dense, total, f0, f1, m0, m1, x0, x1, out):
    height = f0.shape[0]
    core, mate, _ = coordinates()

    def add_up(*cross):
        out[...] = sum_products(total[...], dense, 6 * height, (f0, f1, *cross)).astype(BF16)

    pl.when(core == mate)(lambda: add_up(x0, x1))
    pl.when(core != mate)(lambda: add_up(m0, m1))


def spread_far(dense, total, far, mate_other, far_other):
    return pl.pallas_call(
        spread_far_body,
        out_shape=jax.ShapeDtypeStruct(total.shape, BF16),
        in_specs=[VMEM] * 8,
        out_specs=VMEM,
        compiler_params=params(),
        cost_estimate=cost(),
        name="spread_far",
    )(dense, total, *far, *mate_other, *far_other)


def pull_body(cot, dense, own, mate, far, swap_own, swap_cross):
    rows = dense.shape[0]
    turned = cot[...].T
    terms = [
        jnp.dot(
            turned, dense[:, index * rows : (index + 1) * rows], preferred_element_type=F32
        )
        for index in range(5)
    ]
    own[...], mate[...], far[...] = terms[0], terms[2], terms[3]
    swap_own[...] = terms[1].astype(BF16)
    swap_cross[...] = terms[4].astype(BF16)


def pull(cot, dense):
    rows, cols = cot.shape
    return pl.pallas_call(
        pull_body,
        out_shape=[jax.ShapeDtypeStruct((cols, rows), F32)] * 3
        + [jax.ShapeDtypeStruct((cols, rows), BF16)] * 2,
        in_specs=[VMEM] * 2,
        out_specs=[VMEM] * 5,
        compiler_params=params(),
        cost_estimate=cost(),
        name="pull",
    )(cot, dense)


def swap_sum_body(mate_term, far_term, swap, mate_0, mate_1, far_0, far_1):
    half = far_0.shape[1]
    core, mate, _ = coordinates()
    cross = swap[...].astype(F32)
    cross_mate = jnp.where(core == mate, cross, 0.0)
    far = (far_term[...] + (cross - cross_mate)).astype(BF16)
    near = mate_term[...] + cross_mate
    mate_0[...], mate_1[...] = near[:, :half], near[:, half:]
    far_0[...], far_1[...] = far[:, :half], far[:, half:]


def swap_sum(mate_term, far_term, swap):
    cols, rows = far_term.shape
    shape = (cols, rows // 2)
    out = pl.pallas_call(
        swap_sum_body,
        out_shape=[jax.ShapeDtypeStruct(shape, F32)] * 2
        + [jax.ShapeDtypeStruct(shape, BF16)] * 2,
        in_specs=[VMEM] * 3,
        out_specs=[VMEM] * 4,
        compiler_params=params(),
        cost_estimate=cost(),
        name="swap_sum",
    )(mate_term, far_term, swap)
    return out[:2], out[2:]


def meet_body(mine, come, *refs):
    refs[-1][...] = (mine[...] + come[...].astype(F32)).astype(BF16)


def meet(mine, come, *after):
    return pl.pallas_call(
        meet_body,
        out_shape=jax.ShapeDtypeStruct(mine.shape, BF16),
        in_specs=[VMEM] * 2 + [ANY] * len(after),
        out_specs=VMEM,
        compiler_params=params(),
        cost_estimate=cost(),
        name="meet",
    )(mine, come, *after)


def hidden_body(s0, s1, w_mine, w_near, w_far, w_out, *refs, number):
    pre, hid, mixed = refs[-3:]
    height, width = pre.shape
    span = slice(number * height, (number + 1) * height)
    core, _, panel = coordinates()

    def rows_of(side):
        return pl.ds(pl.multiple_of((panel ^ side) * width, width), width)

    def run(w_theirs):
        mine, theirs = 0.0, 0.0
        for side, ref in enumerate((s0, s1)):
            taken = ref[span, :]
            mine += jnp.dot(taken, w_mine[rows_of(side), :], preferred_element_type=F32)
            theirs += jnp.dot(taken, w_theirs[side][...], preferred_element_type=F32)
        pre[...] = mine
        hid[:, :width] = (mine * jax.nn.sigmoid(mine)).astype(BF16)
        hid[:, width:] = (theirs * jax.nn.sigmoid(theirs)).astype(BF16)

    pl.when(core == 0)(lambda: run((w_near, w_far)))
    pl.when(core == 1)(lambda: run((w_far, w_near)))
    result = 0.0
    for side in range(2):
        value = hid[:, side * width : (side + 1) * width]
        result += jnp.dot(value, w_out[rows_of(side), :], preferred_element_type=F32)
    mixed[...] = result.astype(BF16)


def hidden_step(number, pieces, w_mine, w_near, w_far, w_out, *after):
    rows, width = pieces[0].shape
    height = rows // 2
    return pl.pallas_call(
        functools.partial(hidden_body, number=number),
        out_shape=[
            jax.ShapeDtypeStruct((height, width), F32),
            jax.ShapeDtypeStruct((height, 2 * width), BF16),
            jax.ShapeDtypeStruct((height, width), BF16),
        ],
        in_specs=[VMEM] * 6 + [ANY] * len(after),
        out_specs=[VMEM] * 3,
        compiler_params=params(),
        cost_estimate=cost(),
        name="hidden",
    )(*pieces, w_mine, w_near, w_far, w_out, *after)


def mix_body(own, swap, come, w_out, *refs, number):
    pulled, keep, give = refs[-3:]
    height, half = keep.shape
    _, _, panel = coordinates()
    span = slice(number * height, (number + 1) * height)
    total = own[:, span] + swap[:, span].astype(F32) + come[...].astype(F32)
    pulled[...] = total.astype(BF16).T
    contract = (((1,), (1,)), ((), ()))
    theirs = w_out[pl.ds(pl.multiple_of((1 - panel) * half, half), half), :]
    give[...] = lax.dot_general(
        pulled[...], theirs, contract, preferred_element_type=F32
    ).astype(BF16)
    mine = w_out[pl.ds(pl.multiple_of(panel * half, half), half), :]
    keep[...] = lax.dot_general(pulled[...], mine, contract, preferred_element_type=F32)


def mix_step(number, own, swap, come, w_out, *after):
    cols, height = come.shape
    half = w_out.shape[0] // 2
    return pl.pallas_call(
        functools.partial(mix_body, number=number),
        out_shape=[
            jax.ShapeDtypeStruct((height, cols), BF16),
            jax.ShapeDtypeStruct((height, half), F32),
            jax.ShapeDtypeStruct((height, half), BF16),
        ],
        in_specs=[VMEM] * 4 + [ANY] * len(after),
        out_specs=[VMEM] * 3,
        compiler_params=params(),
        cost_estimate=cost(),
        name="mix_back",
    )(own, swap, come, w_out, *after)


def split_term(total, keep, give, scratch, blocks):
    core, mate, _ = coordinates()
    share = total.shape[0] // blocks
    groups = blocks // 4
    for group in range(groups):
        for side in range(2):
            owner = 4 * group + 2 * (mate ^ side)
            target = pl.ds((side * groups + group) * share, share)
            source = pl.multiple_of((owner + core) * share, share)
            keep[target, :] = total[pl.ds(source, share), :]
            source = pl.multiple_of((owner + 1 - core) * share, share)
            scratch[target, :] = total[pl.ds(source, share), :]
    give[...] = scratch[...].astype(BF16)


def grad_into(total, pieces, rights):
    _, _, panel = coordinates()
    contract = (((0,), (0,)), ((), ()))
    width = rights[0].shape[1]
    half = width // 2
    for side, (refs, first) in enumerate(pieces):
        for number in range(2):
            start = (panel ^ side) * width + number * half
            source = first + number * half
            result = 0.0
            for index, right in enumerate(rights):
                height = right.shape[0]
                if len(refs) == 1:
                    taken = refs[0][index * height : (index + 1) * height, source : source + half]
                else:
                    taken = refs[index][:, source : source + half]
                result += lax.dot_general(
                    taken,
                    right[...],
                    contract,
                    preferred_element_type=F32,
                )
            total[pl.ds(pl.multiple_of(start, half), half), :] = result


def out_grad_body(hid_0, hid_1, pulled_0, pulled_1, *refs, blocks):
    keep, give, total, scratch = refs[-4:]
    width = pulled_0.shape[1]
    hid = (hid_0, hid_1)
    grad_into(total, ((hid, 0), (hid, width)), (pulled_0, pulled_1))
    split_term(total, keep, give, scratch, blocks)


def in_grad_body(*refs, blocks):
    own, theirs, *refs = refs
    pre, kept, come = [refs[2 * i : 2 * i + 2] for i in range(3)]
    keep, give, total, scratch, *back = refs[-6:]
    for half in range(2):
        pre_hidden = pre[half][...]
        gate = jax.nn.sigmoid(pre_hidden)
        back_hidden = kept[half][...] + come[half][...].astype(F32)
        slope = gate * (1.0 + pre_hidden * (1.0 - gate))
        back[half][...] = (back_hidden * slope).astype(BF16)
    grad_into(total, (((own,), 0), ((theirs,), 0)), back)
    split_term(total, keep, give, scratch, blocks)


def grad_call(body, name, operands, height, width, scratch=(), after=()):
    blocks = lax.axis_size("blk")
    half = height // 2
    return pl.pallas_call(
        functools.partial(body, blocks=blocks),
        out_shape=[
            jax.ShapeDtypeStruct((half, width), F32),
            jax.ShapeDtypeStruct((half, width), BF16),
        ],
        in_specs=[VMEM] * len(operands) + [ANY] * len(after),
        out_specs=[VMEM] * 2,
        scratch_shapes=[
            pltpu.VMEM((height, width), F32),
            pltpu.VMEM((half, width), F32),
            *scratch,
        ],
        compiler_params=params(),
        cost_estimate=cost(),
        name=name,
    )(*operands, *after)


def core_sum_body(keep, come, near, far):
    half = near.shape[0]
    near[...] = keep[:half] + come[:half].astype(F32)
    far[...] = (keep[half:] + come[half:].astype(F32)).astype(BF16)


def core_sum(keep, come):
    height, width = keep.shape
    shape = (height // 2, width)
    return pl.pallas_call(
        core_sum_body,
        out_shape=[jax.ShapeDtypeStruct(shape, F32), jax.ShapeDtypeStruct(shape, BF16)],
        in_specs=[VMEM] * 2,
        out_specs=[VMEM] * 2,
        compiler_params=params(),
        cost_estimate=cost(),
        name="core_sum",
    )(keep, come)


def mate_sum_body(first, first_come, second, second_come, *refs):
    own_first, own_second, *terms, sum_first, sum_second = refs
    share = own_first.shape[0]
    group = lax.axis_index("blk") // 4
    sum_first[...] = first[...] + first_come[...].astype(F32)
    sum_second[...] = second[...] + second_come[...].astype(F32)

    def rows_of(distance):
        start = pl.multiple_of((group ^ distance) * share, share)
        return sum_first[pl.ds(start, share), :], sum_second[pl.ds(start, share), :]

    own_first[...], own_second[...] = rows_of(0)
    for number, ref in enumerate(terms):
        ref[...] = jnp.concatenate(rows_of(number + 1), axis=0).astype(BF16)


def mate_sum(first, first_come, second, second_come):
    height, width = first.shape
    groups = lax.axis_size("blk") // 4
    share = height // groups
    own = jax.ShapeDtypeStruct((share, width), F32)
    term = jax.ShapeDtypeStruct((2 * share, width), BF16)
    own_first, own_second, *terms = pl.pallas_call(
        mate_sum_body,
        out_shape=[own] * 2 + [term] * (groups - 1),
        in_specs=[VMEM] * 4,
        out_specs=[VMEM] * (1 + groups),
        scratch_shapes=[pltpu.VMEM((height, width), F32)] * 2,
        compiler_params=params(),
        cost_estimate=cost(),
        name="mate_sum",
    )(first, first_come, second, second_come)
    return own_first, own_second, terms


def group_sum_body(own_first, own_second, *refs):
    *terms, out_first, out_second = refs
    share = own_first.shape[0]
    total_first, total_second = own_first[...], own_second[...]
    for ref in terms:
        term = ref[...].astype(F32)
        total_first += term[:share]
        total_second += term[share:]
    out_first[...] = total_first
    out_second[...] = total_second


def group_sum(own_first, own_second, terms):
    return pl.pallas_call(
        group_sum_body,
        out_shape=[jax.ShapeDtypeStruct(own_first.shape, F32)] * 2,
        in_specs=[VMEM] * (2 + len(terms)),
        out_specs=[VMEM] * 2,
        compiler_params=params(),
        cost_estimate=cost(),
        name="group_sum",
    )(own_first, own_second, *terms)


def shards(
    features, weight_in, weight_out, adj_tiles, tile_rows, tile_cols, tile_counts, cotangent
):
    rows, width = features.shape
    tile_rows, tile_cols = jnp.swapaxes(tile_rows, 0, 1), jnp.swapaxes(tile_cols, 0, 1)

    height = rows // 2

    f_mate = [to_mate(features[:height]), to_mate(features[height:])]
    f_other = to_core(features)
    f_mate_other = [to_core(half) for half in f_mate]
    f_far = [relay_out(half) for half in f_mate]
    f_far_other = [to_core(half) for half in f_far]
    w_near = to_panel(pick(weight_in))
    w_far = to_core(w_near)

    dense = build(tile_rows, tile_cols, tile_counts, adj_tiles, rows)
    p_own, p_mate, p_far, p_swap, p_cross = pull(cotangent, dense)
    p_mate, p_far = swap_sum(
        p_mate, p_far, to_core(gate(p_cross, f_far[0], f_mate[1]))
    )
    p_swap = to_core(p_swap)
    p_come = [relay_back(far) for far in p_far]

    total = spread_near(dense, features, f_other, f_mate, p_far[0])
    own = spread_far(dense, total, f_far, f_mate_other, f_far_other)
    theirs = to_panel(own)
    q_come = [to_mate(meet(mine, come)) for mine, come in zip(p_mate, p_come)]
    pre_hidden, hid, mixed = zip(
        *[
            hidden_step(number, (own, theirs), weight_in, w_near, w_far, weight_out, dense)
            for number in range(2)
        ]
    )

    t_mate = [to_mate(half) for half in mixed]
    t_own = jnp.concatenate(mixed, axis=0)
    t_other = to_core(t_own)
    t_mate_other = [to_core(half) for half in t_mate]
    t_far = [relay_out(half) for half in t_mate]
    t_far_other = [to_core(half) for half in t_far]

    pulled, kept, given = zip(
        *[
            mix_step(number, p_own, p_swap, come, weight_out, dense)
            for number, come in enumerate(q_come)
        ]
    )
    come = [to_panel(half) for half in given]
    out_keep, out_give = grad_call(
        out_grad_body, "out_grad", [*hid, *pulled], 2 * width, width
    )
    in_keep, in_give = grad_call(
        in_grad_body,
        "in_grad",
        [own, theirs, *pre_hidden, *kept, *come],
        2 * width,
        width,
        [pltpu.VMEM((height, width), BF16)] * 2,
        (dense, t_mate[1], t_far[0]),
    )
    out_near, out_far = core_sum(out_keep, to_core(out_give))
    out_far = gate(out_far, t_mate[1])
    in_near, in_far = core_sum(in_keep, to_core(in_give))
    out_own, in_own, terms = mate_sum(out_near, to_mate(out_far), in_near, to_mate(in_far))
    terms = [to_group(term, number + 1) for number, term in enumerate(terms)]

    total = spread_near(dense, t_own, t_other, t_mate, in_far)
    layer_output = spread_far(dense, total, t_far, t_mate_other, t_far_other)
    grad_weight_out, grad_weight_in = group_sum(out_own, in_own, terms)
    return (layer_output, grad_weight_in, grad_weight_out)


def solution(mesh):
    return jax.shard_map(
        shards,
        mesh=mesh,
        in_specs=(
            P("blk", "feat"),
            P(None, "feat"),
            P(None, "feat"),
            P("blk", None, None, None, None),
            P("blk", None, None),
            P("blk", None, None),
            P("blk", None),
            P("blk", "feat"),
        ),
        out_specs=(P("blk", "feat"), P("blk", "feat"), P("blk", "feat")),
        check_vma=False,
    )
```

```python
import functools

import jax
import jax.numpy as jnp
from jax import lax
from jax.experimental import pallas as pl
from jax.experimental.pallas import tpu as pltpu
from jax.sharding import PartitionSpec as P

BF16 = jnp.bfloat16
F32 = jnp.float32
VMEM = pl.BlockSpec(memory_space=pltpu.VMEM)
SMEM = pl.BlockSpec(memory_space=pltpu.SMEM)
ANY = pl.BlockSpec(memory_space=pl.ANY)


def params(limit_mib=12):
    return pltpu.CompilerParams(vmem_limit_bytes=limit_mib * 1024 * 1024)


def cost(microseconds=0):
    return pl.CostEstimate(
        flops=1024, bytes_accessed=1024 + 3_600_000 * microseconds, transcendentals=0
    )


def gate_body(*refs):
    del refs


def gate(value, *after, microseconds=0):
    return pl.pallas_call(
        gate_body,
        out_shape=jax.ShapeDtypeStruct(value.shape, value.dtype),
        in_specs=[ANY] * (1 + len(after)),
        out_specs=ANY,
        input_output_aliases={0: 0},
        compiler_params=params(1),
        cost_estimate=cost(microseconds),
        name="gate",
    )(value, *after)


def coordinates():
    block = lax.axis_index("blk")
    return block & 1, (block >> 1) & 1, lax.axis_index("feat")


def coordinates():
    block = lax.axis_index("blk")
    return block & 1, (block >> 1) & 1, lax.axis_index("feat")


def copy_all(pairs, semaphores):
    copies = [
        pltpu.make_async_copy(source, target, semaphores.at[number])
        for number, (source, target) in enumerate(pairs)
    ]
    for copy in copies:
        copy.start()
    for copy in copies:
        copy.wait()


def coordinates():
    block = lax.axis_index("blk")
    return block & 1, (block >> 1) & 1, lax.axis_index("feat")


def blk_pairs(target):
    count = lax.axis_size("blk")
    return [(source, target(source) % count) for source in range(count)]


def to_core(value):
    return lax.ppermute(value, "blk", blk_pairs(lambda b: b ^ 1))


def to_mate(value):
    return lax.ppermute(value, "blk", blk_pairs(lambda b: b ^ 2))


def relay_out(value):
    return lax.ppermute(value, "blk", blk_pairs(lambda b: b - 4 if b & 2 else b + 4))


def relay_back(value):
    return lax.ppermute(value, "blk", blk_pairs(lambda b: b + 4 if b & 2 else b - 4))


def to_group(value, distance):
    return lax.ppermute(value, "blk", blk_pairs(lambda b: b ^ (4 * distance)))


def to_panel(value):
    return lax.ppermute(value, "feat", [(0, 1), (1, 0)])


def pick_body(w_in, send, semaphore):
    half = send.shape[0]
    core, _, panel = coordinates()
    start = pl.multiple_of(((1 - panel) ^ core) * half, half)
    copy = pltpu.make_async_copy(w_in.at[pl.ds(start, half), :], send, semaphore)
    copy.start()
    copy.wait()


def pick(w_in):
    width = w_in.shape[1]
    return pl.pallas_call(
        pick_body,
        out_shape=jax.ShapeDtypeStruct((width, width), BF16),
        in_specs=[ANY],
        out_specs=VMEM,
        scratch_shapes=[pltpu.SemaphoreType.DMA],
        compiler_params=params(4),
        cost_estimate=cost(),
        name="pick",
    )(w_in)


def build_body(rows, cols, counts, tiles, dense):
    _, steps, cap, tile, _ = tiles.shape
    radius = (steps - 1) // 2
    block_tiles = dense.shape[0] // tile
    core, mate, _ = coordinates()
    dense[...] = jnp.zeros_like(dense)

    def place(entry, carry):
        step, slot = entry // cap, entry % cap
        shifted = step - radius + core + 2
        chip = shifted // 2 - 1
        position = (shifted % 2) ^ core
        ahead = jnp.where(mate == 0, 1, -1)
        outside = jnp.where(position == 1, 4, jnp.where(chip == ahead, 2, 3))
        segment = jnp.where(chip == 0, position, outside)
        row = rows[step, 0, slot]
        col = segment * block_tiles + cols[step, 0, slot]

        @pl.when(slot < counts[0, step])
        def _():
            dense[
                pl.ds(pl.multiple_of(row * tile, tile), tile),
                pl.ds(pl.multiple_of(col * tile, tile), tile),
            ] = tiles[0, step, slot]

        return carry

    lax.fori_loop(0, steps * cap, place, 0)


def build(tile_rows, tile_cols, tile_counts, tiles, rows):
    return pl.pallas_call(
        build_body,
        out_shape=jax.ShapeDtypeStruct((rows, 5 * rows), BF16),
        in_specs=[SMEM] * 3 + [VMEM],
        out_specs=VMEM,
        compiler_params=params(),
        cost_estimate=cost(),
        name="build_dense",
    )(tile_rows, tile_cols, tile_counts, tiles)


def sum_products(result, dense, first, refs):
    for ref in refs:
        height = ref.shape[0]
        product = jnp.dot(
            dense[:, first : first + height], ref[...], preferred_element_type=F32
        )
        result = product if result is None else result + product
        first += height
    return result


def spread_near_body(dense, s0, s1, s2, s3, *refs):
    refs[-1][...] = sum_products(None, dense, 0, (s0, s1, s2, s3))


def spread_near(dense, own, other, mate, *after):
    rows, cols = own.shape
    block = rows // 2
    whole = pl.BlockSpec((rows, cols), lambda i: (0, 0))
    half = pl.BlockSpec((block, cols), lambda i: (0, 0))
    return pl.pallas_call(
        spread_near_body,
        grid=(2,),
        out_shape=jax.ShapeDtypeStruct((rows, cols), F32),
        in_specs=[
            pl.BlockSpec((block, 3 * rows), lambda i: (i, 0)),
            whole,
            whole,
            half,
            half,
            *[ANY] * len(after),
        ],
        out_specs=pl.BlockSpec((block, cols), lambda i: (i, 0)),
        compiler_params=params(),
        cost_estimate=cost(),
        name="spread_near",
    )(dense, own, other, *mate, *after)


def spread_far_body(dense, total, f0, f1, m0, m1, x0, x1, out):
    height = f0.shape[0]
    core, mate, _ = coordinates()

    def add_up(*cross):
        out[...] = sum_products(total[...], dense, 6 * height, (f0, f1, *cross)).astype(BF16)

    pl.when(core == mate)(lambda: add_up(x0, x1))
    pl.when(core != mate)(lambda: add_up(m0, m1))


def spread_far(dense, total, far, mate_other, far_other):
    return pl.pallas_call(
        spread_far_body,
        out_shape=jax.ShapeDtypeStruct(total.shape, BF16),
        in_specs=[VMEM] * 8,
        out_specs=VMEM,
        compiler_params=params(),
        cost_estimate=cost(),
        name="spread_far",
    )(dense, total, *far, *mate_other, *far_other)


def pull_body(cot, dense, own, mate, far, swap_own, swap_cross):
    rows = dense.shape[0]
    turned = cot[...].T
    terms = [
        jnp.dot(
            turned, dense[:, index * rows : (index + 1) * rows], preferred_element_type=F32
        )
        for index in range(5)
    ]
    own[...], mate[...], far[...] = terms[0], terms[2], terms[3]
    swap_own[...] = terms[1].astype(BF16)
    swap_cross[...] = terms[4].astype(BF16)


def pull(cot, dense):
    rows, cols = cot.shape
    return pl.pallas_call(
        pull_body,
        out_shape=[jax.ShapeDtypeStruct((cols, rows), F32)] * 3
        + [jax.ShapeDtypeStruct((cols, rows), BF16)] * 2,
        in_specs=[VMEM] * 2,
        out_specs=[VMEM] * 5,
        compiler_params=params(),
        cost_estimate=cost(),
        name="pull",
    )(cot, dense)


def swap_sum_body(mate_term, far_term, swap, mate_0, mate_1, far_0, far_1):
    half = far_0.shape[1]
    core, mate, _ = coordinates()
    cross = swap[...].astype(F32)
    cross_mate = jnp.where(core == mate, cross, 0.0)
    far = (far_term[...] + (cross - cross_mate)).astype(BF16)
    near = mate_term[...] + cross_mate
    mate_0[...], mate_1[...] = near[:, :half], near[:, half:]
    far_0[...], far_1[...] = far[:, :half], far[:, half:]


def swap_sum(mate_term, far_term, swap):
    cols, rows = far_term.shape
    shape = (cols, rows // 2)
    out = pl.pallas_call(
        swap_sum_body,
        out_shape=[jax.ShapeDtypeStruct(shape, F32)] * 2
        + [jax.ShapeDtypeStruct(shape, BF16)] * 2,
        in_specs=[VMEM] * 3,
        out_specs=[VMEM] * 4,
        compiler_params=params(),
        cost_estimate=cost(),
        name="swap_sum",
    )(mate_term, far_term, swap)
    return out[:2], out[2:]


def hidden_body(s0, s1, w_mine, w_near, w_far, w_out, *refs, number):
    pre, hid, mixed = refs[-3:]
    height, width = pre.shape
    span = slice(number * height, (number + 1) * height)
    core, _, panel = coordinates()

    def rows_of(side):
        return pl.ds(pl.multiple_of((panel ^ side) * width, width), width)

    def run(w_theirs):
        mine, theirs = 0.0, 0.0
        for side, ref in enumerate((s0, s1)):
            taken = ref[span, :]
            mine += jnp.dot(taken, w_mine[rows_of(side), :], preferred_element_type=F32)
            theirs += jnp.dot(taken, w_theirs[side][...], preferred_element_type=F32)
        pre[...] = mine
        hid[:, :width] = (mine * jax.nn.sigmoid(mine)).astype(BF16)
        hid[:, width:] = (theirs * jax.nn.sigmoid(theirs)).astype(BF16)

    pl.when(core == 0)(lambda: run((w_near, w_far)))
    pl.when(core == 1)(lambda: run((w_far, w_near)))
    result = 0.0
    for side in range(2):
        value = hid[:, side * width : (side + 1) * width]
        result += jnp.dot(value, w_out[rows_of(side), :], preferred_element_type=F32)
    mixed[...] = result.astype(BF16)


def hidden_step(number, pieces, w_mine, w_near, w_far, w_out, *after):
    rows, width = pieces[0].shape
    height = rows // 2
    return pl.pallas_call(
        functools.partial(hidden_body, number=number),
        out_shape=[
            jax.ShapeDtypeStruct((height, width), F32),
            jax.ShapeDtypeStruct((height, 2 * width), BF16),
            jax.ShapeDtypeStruct((height, width), BF16),
        ],
        in_specs=[VMEM] * 6 + [ANY] * len(after),
        out_specs=[VMEM] * 3,
        compiler_params=params(),
        cost_estimate=cost(),
        name="hidden",
    )(*pieces, w_mine, w_near, w_far, w_out, *after)


def mix_body(own, swap, come, w_out, *refs, number):
    pulled, keep, give = refs[-3:]
    height, half = keep.shape
    _, _, panel = coordinates()
    span = slice(number * height, (number + 1) * height)
    total = own[:, span] + swap[:, span].astype(F32) + come[...].astype(F32)
    pulled[...] = total.astype(BF16).T
    contract = (((1,), (1,)), ((), ()))
    theirs = w_out[pl.ds(pl.multiple_of((1 - panel) * half, half), half), :]
    give[...] = lax.dot_general(
        pulled[...], theirs, contract, preferred_element_type=F32
    ).astype(BF16)
    mine = w_out[pl.ds(pl.multiple_of(panel * half, half), half), :]
    keep[...] = lax.dot_general(pulled[...], mine, contract, preferred_element_type=F32)


def mix_step(number, own, swap, come, w_out, *after):
    cols, height = come.shape
    half = w_out.shape[0] // 2
    return pl.pallas_call(
        functools.partial(mix_body, number=number),
        out_shape=[
            jax.ShapeDtypeStruct((height, cols), BF16),
            jax.ShapeDtypeStruct((height, half), F32),
            jax.ShapeDtypeStruct((height, half), BF16),
        ],
        in_specs=[VMEM] * 4 + [ANY] * len(after),
        out_specs=[VMEM] * 3,
        compiler_params=params(),
        cost_estimate=cost(),
        name="mix_back",
    )(own, swap, come, w_out, *after)


def split_term(total, keep, give, scratch, blocks):
    core, mate, _ = coordinates()
    share = total.shape[0] // blocks
    groups = blocks // 4
    for group in range(groups):
        for side in range(2):
            owner = 4 * group + 2 * (mate ^ side)
            target = pl.ds((side * groups + group) * share, share)
            source = pl.multiple_of((owner + core) * share, share)
            keep[target, :] = total[pl.ds(source, share), :]
            source = pl.multiple_of((owner + 1 - core) * share, share)
            scratch[target, :] = total[pl.ds(source, share), :]
    give[...] = scratch[...].astype(BF16)


def grad_into(total, pieces, rights):
    _, _, panel = coordinates()
    contract = (((0,), (0,)), ((), ()))
    width = rights[0].shape[1]
    half = width // 2
    for side, (refs, first) in enumerate(pieces):
        for number in range(2):
            start = (panel ^ side) * width + number * half
            source = first + number * half
            result = 0.0
            for index, right in enumerate(rights):
                height = right.shape[0]
                if len(refs) == 1:
                    taken = refs[0][index * height : (index + 1) * height, source : source + half]
                else:
                    taken = refs[index][:, source : source + half]
                result += lax.dot_general(
                    taken,
                    right[...],
                    contract,
                    preferred_element_type=F32,
                )
            total[pl.ds(pl.multiple_of(start, half), half), :] = result


def out_grad_body(hid_0, hid_1, pulled_0, pulled_1, *refs, blocks):
    keep, give, total, scratch = refs[-4:]
    width = pulled_0.shape[1]
    hid = (hid_0, hid_1)
    grad_into(total, ((hid, 0), (hid, width)), (pulled_0, pulled_1))
    split_term(total, keep, give, scratch, blocks)


def in_grad_body(*refs, blocks):
    own, theirs, *refs = refs
    pre, kept, come = [refs[2 * i : 2 * i + 2] for i in range(3)]
    keep, give, total, scratch, *back = refs[-6:]
    for half in range(2):
        pre_hidden = pre[half][...]
        gate = jax.nn.sigmoid(pre_hidden)
        back_hidden = kept[half][...] + come[half][...].astype(F32)
        slope = gate * (1.0 + pre_hidden * (1.0 - gate))
        back[half][...] = (back_hidden * slope).astype(BF16)
    grad_into(total, (((own,), 0), ((theirs,), 0)), back)
    split_term(total, keep, give, scratch, blocks)


def grad_call(body, name, operands, height, width, scratch=(), after=()):
    blocks = lax.axis_size("blk")
    half = height // 2
    return pl.pallas_call(
        functools.partial(body, blocks=blocks),
        out_shape=[
            jax.ShapeDtypeStruct((half, width), F32),
            jax.ShapeDtypeStruct((half, width), BF16),
        ],
        in_specs=[VMEM] * len(operands) + [ANY] * len(after),
        out_specs=[VMEM] * 2,
        scratch_shapes=[
            pltpu.VMEM((height, width), F32),
            pltpu.VMEM((half, width), F32),
            *scratch,
        ],
        compiler_params=params(),
        cost_estimate=cost(),
        name=name,
    )(*operands, *after)


def core_sum_body(keep, come, near, far):
    half = near.shape[0]
    near[...] = keep[:half] + come[:half].astype(F32)
    far[...] = (keep[half:] + come[half:].astype(F32)).astype(BF16)


def core_sum(keep, come):
    height, width = keep.shape
    shape = (height // 2, width)
    return pl.pallas_call(
        core_sum_body,
        out_shape=[jax.ShapeDtypeStruct(shape, F32), jax.ShapeDtypeStruct(shape, BF16)],
        in_specs=[VMEM] * 2,
        out_specs=[VMEM] * 2,
        compiler_params=params(),
        cost_estimate=cost(),
        name="core_sum",
    )(keep, come)


def mate_sum_body(first, first_come, second, second_come, *refs):
    own_first, own_second, *terms, sum_first, sum_second = refs
    share = own_first.shape[0]
    group = lax.axis_index("blk") // 4
    sum_first[...] = first[...] + first_come[...].astype(F32)
    sum_second[...] = second[...] + second_come[...].astype(F32)

    def rows_of(distance):
        start = pl.multiple_of((group ^ distance) * share, share)
        return sum_first[pl.ds(start, share), :], sum_second[pl.ds(start, share), :]

    own_first[...], own_second[...] = rows_of(0)
    for number, ref in enumerate(terms):
        ref[...] = jnp.concatenate(rows_of(number + 1), axis=0).astype(BF16)


def mate_sum(first, first_come, second, second_come):
    height, width = first.shape
    groups = lax.axis_size("blk") // 4
    share = height // groups
    own = jax.ShapeDtypeStruct((share, width), F32)
    term = jax.ShapeDtypeStruct((2 * share, width), BF16)
    own_first, own_second, *terms = pl.pallas_call(
        mate_sum_body,
        out_shape=[own] * 2 + [term] * (groups - 1),
        in_specs=[VMEM] * 4,
        out_specs=[VMEM] * (1 + groups),
        scratch_shapes=[pltpu.VMEM((height, width), F32)] * 2,
        compiler_params=params(),
        cost_estimate=cost(),
        name="mate_sum",
    )(first, first_come, second, second_come)
    return own_first, own_second, terms


def group_sum_body(own_first, own_second, *refs):
    *terms, out_first, out_second = refs
    share = own_first.shape[0]
    total_first, total_second = own_first[...], own_second[...]
    for ref in terms:
        term = ref[...].astype(F32)
        total_first += term[:share]
        total_second += term[share:]
    out_first[...] = total_first
    out_second[...] = total_second


def group_sum(own_first, own_second, terms):
    return pl.pallas_call(
        group_sum_body,
        out_shape=[jax.ShapeDtypeStruct(own_first.shape, F32)] * 2,
        in_specs=[VMEM] * (2 + len(terms)),
        out_specs=[VMEM] * 2,
        compiler_params=params(),
        cost_estimate=cost(),
        name="group_sum",
    )(own_first, own_second, *terms)


def shards(
    features, weight_in, weight_out, adj_tiles, tile_rows, tile_cols, tile_counts, cotangent
):
    rows, width = features.shape
    tile_rows, tile_cols = jnp.swapaxes(tile_rows, 0, 1), jnp.swapaxes(tile_cols, 0, 1)

    height = rows // 2

    f_mate = [to_mate(features[:height]), to_mate(features[height:])]
    f_other = to_core(features)
    w_near = to_panel(pick(weight_in))
    w_far = to_core(w_near)

    dense = build(tile_rows, tile_cols, tile_counts, adj_tiles, rows)
    p_own, p_mate, p_far, p_swap, p_cross = pull(cotangent, dense)
    f_mate[0] = gate(f_mate[0], p_own)
    f_mate_other = [to_core(half) for half in f_mate]
    f_far = [relay_out(half) for half in f_mate]
    f_far_other = [to_core(half) for half in f_far]
    p_mate, p_far = swap_sum(
        p_mate, p_far, to_core(gate(p_cross, f_far[0], f_mate[1]))
    )
    p_swap = to_core(p_swap)
    p_come = [relay_back(far) for far in p_far]

    total = spread_near(dense, features, f_other, f_mate, p_far[0])
    own = spread_far(dense, total, f_far, f_mate_other, f_far_other)
    theirs = to_panel(own)
    q_come = [
        to_mate((mine + come.astype(F32)).astype(BF16)) for mine, come in zip(p_mate, p_come)
    ]
    pre_hidden, hid, mixed = zip(
        *[
            hidden_step(number, (own, theirs), weight_in, w_near, w_far, weight_out, dense)
            for number in range(2)
        ]
    )

    t_mate = [to_mate(half) for half in mixed]
    t_own = jnp.concatenate(mixed, axis=0)
    t_other = to_core(t_own)
    t_mate_other = [to_core(half) for half in t_mate]
    t_far = [relay_out(half) for half in t_mate]
    t_far_other = [to_core(half) for half in t_far]

    pulled, kept, given = zip(
        *[
            mix_step(number, p_own, p_swap, come, weight_out, dense)
            for number, come in enumerate(q_come)
        ]
    )
    come = [to_panel(half) for half in given]
    out_keep, out_give = grad_call(
        out_grad_body, "out_grad", [*hid, *pulled], 2 * width, width
    )
    in_keep, in_give = grad_call(
        in_grad_body,
        "in_grad",
        [own, theirs, *pre_hidden, *kept, *come],
        2 * width,
        width,
        [pltpu.VMEM((height, width), BF16)] * 2,
        (dense, *t_mate),
    )
    out_near, out_far = core_sum(out_keep, to_core(out_give))
    out_far = gate(out_far, t_mate[1])
    in_near, in_far = core_sum(in_keep, to_core(in_give))
    out_own, in_own, terms = mate_sum(out_near, to_mate(out_far), in_near, to_mate(in_far))
    terms = [to_group(term, number + 1) for number, term in enumerate(terms)]

    total = spread_near(dense, t_own, t_other, t_mate, in_far)
    layer_output = spread_far(dense, total, t_far, t_mate_other, t_far_other)
    grad_weight_out, grad_weight_in = group_sum(out_own, in_own, terms)
    return (layer_output, grad_weight_in, grad_weight_out)


def solution(mesh):
    return jax.shard_map(
        shards,
        mesh=mesh,
        in_specs=(
            P("blk", "feat"),
            P(None, "feat"),
            P(None, "feat"),
            P("blk", None, None, None, None),
            P("blk", None, None),
            P("blk", None, None),
            P("blk", None),
            P("blk", "feat"),
        ),
        out_specs=(P("blk", "feat"), P("blk", "feat"), P("blk", "feat")),
        check_vma=False,
    )
```

```python
import functools

import jax
import jax.numpy as jnp
from jax import lax
from jax.experimental import pallas as pl
from jax.experimental.pallas import tpu as pltpu
from jax.sharding import PartitionSpec as P

BF16 = jnp.bfloat16
F32 = jnp.float32
VMEM = pl.BlockSpec(memory_space=pltpu.VMEM)
SMEM = pl.BlockSpec(memory_space=pltpu.SMEM)
ANY = pl.BlockSpec(memory_space=pl.ANY)


def params(limit_mib=12):
    return pltpu.CompilerParams(vmem_limit_bytes=limit_mib * 1024 * 1024)


def cost(microseconds=0):
    return pl.CostEstimate(
        flops=1024, bytes_accessed=1024 + 3_600_000 * microseconds, transcendentals=0
    )


def gate_body(*refs):
    del refs


def gate(value, *after, microseconds=0):
    return pl.pallas_call(
        gate_body,
        out_shape=jax.ShapeDtypeStruct(value.shape, value.dtype),
        in_specs=[ANY] * (1 + len(after)),
        out_specs=ANY,
        input_output_aliases={0: 0},
        compiler_params=params(1),
        cost_estimate=cost(microseconds),
        name="gate",
    )(value, *after)


def coordinates():
    block = lax.axis_index("blk")
    return block & 1, (block >> 1) & 1, lax.axis_index("feat")


def coordinates():
    block = lax.axis_index("blk")
    return block & 1, (block >> 1) & 1, lax.axis_index("feat")


def copy_all(pairs, semaphores):
    copies = [
        pltpu.make_async_copy(source, target, semaphores.at[number])
        for number, (source, target) in enumerate(pairs)
    ]
    for copy in copies:
        copy.start()
    for copy in copies:
        copy.wait()


def coordinates():
    block = lax.axis_index("blk")
    return block & 1, (block >> 1) & 1, lax.axis_index("feat")


def blk_pairs(target):
    count = lax.axis_size("blk")
    return [(source, target(source) % count) for source in range(count)]


def to_core(value):
    return lax.ppermute(value, "blk", blk_pairs(lambda b: b ^ 1))


def to_mate(value):
    return lax.ppermute(value, "blk", blk_pairs(lambda b: b ^ 2))


def relay_out(value):
    return lax.ppermute(value, "blk", blk_pairs(lambda b: b - 4 if b & 2 else b + 4))


def relay_back(value):
    return lax.ppermute(value, "blk", blk_pairs(lambda b: b + 4 if b & 2 else b - 4))


def to_group(value, distance):
    return lax.ppermute(value, "blk", blk_pairs(lambda b: b ^ (4 * distance)))


def to_panel(value):
    return lax.ppermute(value, "feat", [(0, 1), (1, 0)])


def pick_body(w_in, send, semaphore):
    half = send.shape[0]
    core, _, panel = coordinates()
    start = pl.multiple_of(((1 - panel) ^ core) * half, half)
    copy = pltpu.make_async_copy(w_in.at[pl.ds(start, half), :], send, semaphore)
    copy.start()
    copy.wait()


def pick(w_in):
    width = w_in.shape[1]
    return pl.pallas_call(
        pick_body,
        out_shape=jax.ShapeDtypeStruct((width, width), BF16),
        in_specs=[ANY],
        out_specs=VMEM,
        scratch_shapes=[pltpu.SemaphoreType.DMA],
        compiler_params=params(4),
        cost_estimate=cost(),
        name="pick",
    )(w_in)


def build_body(rows, cols, counts, tiles, dense):
    _, steps, cap, tile, _ = tiles.shape
    radius = (steps - 1) // 2
    block_tiles = dense.shape[0] // tile
    core, mate, _ = coordinates()
    dense[...] = jnp.zeros_like(dense)

    def place(entry, carry):
        step, slot = entry // cap, entry % cap
        shifted = step - radius + core + 2
        chip = shifted // 2 - 1
        position = (shifted % 2) ^ core
        ahead = jnp.where(mate == 0, 1, -1)
        outside = jnp.where(position == 1, 4, jnp.where(chip == ahead, 2, 3))
        segment = jnp.where(chip == 0, position, outside)
        row = rows[step, 0, slot]
        col = segment * block_tiles + cols[step, 0, slot]

        @pl.when(slot < counts[0, step])
        def _():
            dense[
                pl.ds(pl.multiple_of(row * tile, tile), tile),
                pl.ds(pl.multiple_of(col * tile, tile), tile),
            ] = tiles[0, step, slot]

        return carry

    lax.fori_loop(0, steps * cap, place, 0)


def build(tile_rows, tile_cols, tile_counts, tiles, rows):
    return pl.pallas_call(
        build_body,
        out_shape=jax.ShapeDtypeStruct((rows, 5 * rows), BF16),
        in_specs=[SMEM] * 3 + [VMEM],
        out_specs=VMEM,
        compiler_params=params(),
        cost_estimate=cost(),
        name="build_dense",
    )(tile_rows, tile_cols, tile_counts, tiles)


def sum_products(result, dense, first, refs):
    for ref in refs:
        height = ref.shape[0]
        product = jnp.dot(
            dense[:, first : first + height], ref[...], preferred_element_type=F32
        )
        result = product if result is None else result + product
        first += height
    return result


def spread_near_body(dense, s0, s1, s2, s3, *refs):
    refs[-1][...] = sum_products(None, dense, 0, (s0, s1, s2, s3))


def spread_near(dense, own, other, mate, *after):
    rows, cols = own.shape
    block = rows // 2
    whole = pl.BlockSpec((rows, cols), lambda i: (0, 0))
    half = pl.BlockSpec((block, cols), lambda i: (0, 0))
    return pl.pallas_call(
        spread_near_body,
        grid=(2,),
        out_shape=jax.ShapeDtypeStruct((rows, cols), F32),
        in_specs=[
            pl.BlockSpec((block, 3 * rows), lambda i: (i, 0)),
            whole,
            whole,
            half,
            half,
            *[ANY] * len(after),
        ],
        out_specs=pl.BlockSpec((block, cols), lambda i: (i, 0)),
        compiler_params=params(),
        cost_estimate=cost(),
        name="spread_near",
    )(dense, own, other, *mate, *after)


def spread_far_body(dense, total, f0, f1, m0, m1, x0, x1, out):
    height = f0.shape[0]
    core, mate, _ = coordinates()

    def add_up(*cross):
        out[...] = sum_products(total[...], dense, 6 * height, (f0, f1, *cross)).astype(BF16)

    pl.when(core == mate)(lambda: add_up(x0, x1))
    pl.when(core != mate)(lambda: add_up(m0, m1))


def spread_far(dense, total, far, mate_other, far_other):
    return pl.pallas_call(
        spread_far_body,
        out_shape=jax.ShapeDtypeStruct(total.shape, BF16),
        in_specs=[VMEM] * 8,
        out_specs=VMEM,
        compiler_params=params(),
        cost_estimate=cost(),
        name="spread_far",
    )(dense, total, *far, *mate_other, *far_other)


def pull_body(cot, dense, own, mate, far, swap_own, swap_cross):
    rows = dense.shape[0]
    turned = cot[...].T
    terms = [
        jnp.dot(
            turned, dense[:, index * rows : (index + 1) * rows], preferred_element_type=F32
        )
        for index in range(5)
    ]
    own[...], mate[...], far[...] = terms[0], terms[2], terms[3]
    swap_own[...] = terms[1].astype(BF16)
    swap_cross[...] = terms[4].astype(BF16)


def pull(cot, dense):
    rows, cols = cot.shape
    return pl.pallas_call(
        pull_body,
        out_shape=[jax.ShapeDtypeStruct((cols, rows), F32)] * 3
        + [jax.ShapeDtypeStruct((cols, rows), BF16)] * 2,
        in_specs=[VMEM] * 2,
        out_specs=[VMEM] * 5,
        compiler_params=params(),
        cost_estimate=cost(),
        name="pull",
    )(cot, dense)


def swap_sum_body(mate_term, far_term, swap, mate_0, mate_1, far_0, far_1):
    half = far_0.shape[1]
    core, mate, _ = coordinates()
    cross = swap[...].astype(F32)
    cross_mate = jnp.where(core == mate, cross, 0.0)
    far = (far_term[...] + (cross - cross_mate)).astype(BF16)
    near = mate_term[...] + cross_mate
    mate_0[...], mate_1[...] = near[:, :half], near[:, half:]
    far_0[...], far_1[...] = far[:, :half], far[:, half:]


def swap_sum(mate_term, far_term, swap):
    cols, rows = far_term.shape
    shape = (cols, rows // 2)
    out = pl.pallas_call(
        swap_sum_body,
        out_shape=[jax.ShapeDtypeStruct(shape, F32)] * 2
        + [jax.ShapeDtypeStruct(shape, BF16)] * 2,
        in_specs=[VMEM] * 3,
        out_specs=[VMEM] * 4,
        compiler_params=params(),
        cost_estimate=cost(),
        name="swap_sum",
    )(mate_term, far_term, swap)
    return out[:2], out[2:]


def meet_body(mine, come, *refs):
    refs[-1][...] = (mine[...] + come[...].astype(F32)).astype(BF16)


def meet(mine, come, *after):
    return pl.pallas_call(
        meet_body,
        out_shape=jax.ShapeDtypeStruct(mine.shape, BF16),
        in_specs=[VMEM] * 2 + [ANY] * len(after),
        out_specs=VMEM,
        compiler_params=params(),
        cost_estimate=cost(),
        name="meet",
    )(mine, come, *after)


def hidden_body(s0, s1, w_mine, w_near, w_far, w_out, *refs, number):
    pre, hid, mixed = refs[-3:]
    height, width = pre.shape
    span = slice(number * height, (number + 1) * height)
    core, _, panel = coordinates()

    def rows_of(side):
        return pl.ds(pl.multiple_of((panel ^ side) * width, width), width)

    def run(w_theirs):
        mine, theirs = 0.0, 0.0
        for side, ref in enumerate((s0, s1)):
            taken = ref[span, :]
            mine += jnp.dot(taken, w_mine[rows_of(side), :], preferred_element_type=F32)
            theirs += jnp.dot(taken, w_theirs[side][...], preferred_element_type=F32)
        pre[...] = mine
        hid[:, :width] = (mine * jax.nn.sigmoid(mine)).astype(BF16)
        hid[:, width:] = (theirs * jax.nn.sigmoid(theirs)).astype(BF16)

    pl.when(core == 0)(lambda: run((w_near, w_far)))
    pl.when(core == 1)(lambda: run((w_far, w_near)))
    result = 0.0
    for side in range(2):
        value = hid[:, side * width : (side + 1) * width]
        result += jnp.dot(value, w_out[rows_of(side), :], preferred_element_type=F32)
    mixed[...] = result.astype(BF16)


def hidden_step(number, pieces, w_mine, w_near, w_far, w_out, *after):
    rows, width = pieces[0].shape
    height = rows // 2
    return pl.pallas_call(
        functools.partial(hidden_body, number=number),
        out_shape=[
            jax.ShapeDtypeStruct((height, width), F32),
            jax.ShapeDtypeStruct((height, 2 * width), BF16),
            jax.ShapeDtypeStruct((height, width), BF16),
        ],
        in_specs=[VMEM] * 6 + [ANY] * len(after),
        out_specs=[VMEM] * 3,
        compiler_params=params(),
        cost_estimate=cost(),
        name="hidden",
    )(*pieces, w_mine, w_near, w_far, w_out, *after)


def mix_body(own, swap, come, w_out, *refs, number):
    pulled, keep, give = refs[-3:]
    height, half = keep.shape
    _, _, panel = coordinates()
    span = slice(number * height, (number + 1) * height)
    total = own[:, span] + swap[:, span].astype(F32) + come[...].astype(F32)
    pulled[...] = total.astype(BF16).T
    contract = (((1,), (1,)), ((), ()))
    theirs = w_out[pl.ds(pl.multiple_of((1 - panel) * half, half), half), :]
    give[...] = lax.dot_general(
        pulled[...], theirs, contract, preferred_element_type=F32
    ).astype(BF16)
    mine = w_out[pl.ds(pl.multiple_of(panel * half, half), half), :]
    keep[...] = lax.dot_general(pulled[...], mine, contract, preferred_element_type=F32)


def mix_step(number, own, swap, come, w_out, *after):
    cols, height = come.shape
    half = w_out.shape[0] // 2
    return pl.pallas_call(
        functools.partial(mix_body, number=number),
        out_shape=[
            jax.ShapeDtypeStruct((height, cols), BF16),
            jax.ShapeDtypeStruct((height, half), F32),
            jax.ShapeDtypeStruct((height, half), BF16),
        ],
        in_specs=[VMEM] * 4 + [ANY] * len(after),
        out_specs=[VMEM] * 3,
        compiler_params=params(),
        cost_estimate=cost(),
        name="mix_back",
    )(own, swap, come, w_out, *after)


def split_term(total, keep, give_near, give_far, scratch, blocks):
    core, mate, _ = coordinates()
    share = total.shape[0] // blocks
    groups = blocks // 4
    for group in range(groups):
        for side in range(2):
            owner = 4 * group + 2 * (mate ^ side)
            target = pl.ds((side * groups + group) * share, share)
            source = pl.multiple_of((owner + core) * share, share)
            keep[target, :] = total[pl.ds(source, share), :]
            source = pl.multiple_of((owner + 1 - core) * share, share)
            scratch[target, :] = total[pl.ds(source, share), :]
    half = give_near.shape[0]
    give_near[...] = scratch[:half].astype(BF16)
    give_far[...] = scratch[half:].astype(BF16)


def grad_into(total, pieces, rights):
    _, _, panel = coordinates()
    contract = (((0,), (0,)), ((), ()))
    width = rights[0].shape[1]
    half = width // 2
    for side, (refs, first) in enumerate(pieces):
        for number in range(2):
            start = (panel ^ side) * width + number * half
            source = first + number * half
            result = 0.0
            for index, right in enumerate(rights):
                height = right.shape[0]
                if len(refs) == 1:
                    taken = refs[0][index * height : (index + 1) * height, source : source + half]
                else:
                    taken = refs[index][:, source : source + half]
                result += lax.dot_general(
                    taken,
                    right[...],
                    contract,
                    preferred_element_type=F32,
                )
            total[pl.ds(pl.multiple_of(start, half), half), :] = result


def out_grad_body(hid_0, hid_1, pulled_0, pulled_1, *refs, blocks):
    keep, near, far, total, scratch = refs[-5:]
    width = pulled_0.shape[1]
    hid = (hid_0, hid_1)
    grad_into(total, ((hid, 0), (hid, width)), (pulled_0, pulled_1))
    split_term(total, keep, near, far, scratch, blocks)


def in_grad_body(*refs, blocks):
    own, theirs, *refs = refs
    pre, kept, come = [refs[2 * i : 2 * i + 2] for i in range(3)]
    keep, near, far, total, scratch, *back = refs[-7:]
    for half in range(2):
        pre_hidden = pre[half][...]
        gate = jax.nn.sigmoid(pre_hidden)
        back_hidden = kept[half][...] + come[half][...].astype(F32)
        slope = gate * (1.0 + pre_hidden * (1.0 - gate))
        back[half][...] = (back_hidden * slope).astype(BF16)
    grad_into(total, (((own,), 0), ((theirs,), 0)), back)
    split_term(total, keep, near, far, scratch, blocks)


def grad_call(body, name, operands, height, width, scratch=(), after=()):
    blocks = lax.axis_size("blk")
    half = height // 2
    return pl.pallas_call(
        functools.partial(body, blocks=blocks),
        out_shape=[
            jax.ShapeDtypeStruct((half, width), F32),
            jax.ShapeDtypeStruct((half // 2, width), BF16),
            jax.ShapeDtypeStruct((half // 2, width), BF16),
        ],
        in_specs=[VMEM] * len(operands) + [ANY] * len(after),
        out_specs=[VMEM] * 3,
        scratch_shapes=[
            pltpu.VMEM((height, width), F32),
            pltpu.VMEM((half, width), F32),
            *scratch,
        ],
        compiler_params=params(),
        cost_estimate=cost(),
        name=name,
    )(*operands, *after)


def far_sum_body(keep, come, far):
    half = far.shape[0]
    far[...] = (keep[half:] + come[...].astype(F32)).astype(BF16)


def far_sum(keep, come):
    return pl.pallas_call(
        far_sum_body,
        out_shape=jax.ShapeDtypeStruct(come.shape, BF16),
        in_specs=[VMEM] * 2,
        out_specs=VMEM,
        compiler_params=params(),
        cost_estimate=cost(),
        name="far_sum",
    )(keep, come)


def mate_sum_body(first, first_core, first_come, second, second_core, second_come, *refs):
    own_first, own_second, *terms, sum_first, sum_second = refs
    share = own_first.shape[0]
    group = lax.axis_index("blk") // 4
    half = sum_first.shape[0]
    sum_first[...] = first[:half] + first_core[...].astype(F32) + first_come[...].astype(F32)
    sum_second[...] = second[:half] + second_core[...].astype(F32) + second_come[...].astype(F32)

    def rows_of(distance):
        start = pl.multiple_of((group ^ distance) * share, share)
        return sum_first[pl.ds(start, share), :], sum_second[pl.ds(start, share), :]

    own_first[...], own_second[...] = rows_of(0)
    for number, ref in enumerate(terms):
        ref[...] = jnp.concatenate(rows_of(number + 1), axis=0).astype(BF16)


def mate_sum(first, second):
    height, width = first[1].shape
    groups = lax.axis_size("blk") // 4
    share = height // groups
    own = jax.ShapeDtypeStruct((share, width), F32)
    term = jax.ShapeDtypeStruct((2 * share, width), BF16)
    own_first, own_second, *terms = pl.pallas_call(
        mate_sum_body,
        out_shape=[own] * 2 + [term] * (groups - 1),
        in_specs=[VMEM] * 6,
        out_specs=[VMEM] * (1 + groups),
        scratch_shapes=[pltpu.VMEM((height, width), F32)] * 2,
        compiler_params=params(),
        cost_estimate=cost(),
        name="mate_sum",
    )(*first, *second)
    return own_first, own_second, terms


def group_sum_body(own_first, own_second, *refs):
    *terms, out_first, out_second = refs
    share = own_first.shape[0]
    total_first, total_second = own_first[...], own_second[...]
    for ref in terms:
        term = ref[...].astype(F32)
        total_first += term[:share]
        total_second += term[share:]
    out_first[...] = total_first
    out_second[...] = total_second


def group_sum(own_first, own_second, terms):
    return pl.pallas_call(
        group_sum_body,
        out_shape=[jax.ShapeDtypeStruct(own_first.shape, F32)] * 2,
        in_specs=[VMEM] * (2 + len(terms)),
        out_specs=[VMEM] * 2,
        compiler_params=params(),
        cost_estimate=cost(),
        name="group_sum",
    )(own_first, own_second, *terms)


def shards(
    features, weight_in, weight_out, adj_tiles, tile_rows, tile_cols, tile_counts, cotangent
):
    rows, width = features.shape
    tile_rows, tile_cols = jnp.swapaxes(tile_rows, 0, 1), jnp.swapaxes(tile_cols, 0, 1)

    height = rows // 2

    f_mate = [to_mate(features[:height]), to_mate(features[height:])]
    f_other = to_core(features)
    f_mate_other = [to_core(half) for half in f_mate]
    f_far = [relay_out(half) for half in f_mate]
    f_far_other = [to_core(half) for half in f_far]
    w_near = to_panel(pick(weight_in))
    w_far = to_core(w_near)

    dense = build(tile_rows, tile_cols, tile_counts, adj_tiles, rows)
    p_own, p_mate, p_far, p_swap, p_cross = pull(cotangent, dense)
    p_mate, p_far = swap_sum(
        p_mate, p_far, to_core(gate(p_cross, f_mate[1]))
    )
    p_swap = to_core(p_swap)
    p_come = [relay_back(far) for far in p_far]

    total = spread_near(dense, features, f_other, f_mate, p_far[0])
    own = spread_far(dense, total, f_far, f_mate_other, f_far_other)
    theirs = to_panel(own)
    q_come = [to_mate(meet(mine, come)) for mine, come in zip(p_mate, p_come)]
    pre_hidden, hid, mixed = zip(
        *[
            hidden_step(number, (own, theirs), weight_in, w_near, w_far, weight_out, dense)
            for number in range(2)
        ]
    )

    t_mate = [to_mate(half) for half in mixed]
    t_own = jnp.concatenate(mixed, axis=0)
    t_other = to_core(t_own)
    t_mate_other = [to_core(half) for half in t_mate]
    t_far = [relay_out(half) for half in t_mate]
    t_far_other = [to_core(half) for half in t_far]

    pulled, kept, given = zip(
        *[
            mix_step(number, p_own, p_swap, come, weight_out, dense)
            for number, come in enumerate(q_come)
        ]
    )
    come = [to_panel(half) for half in given]
    out_keep, out_near, out_far = grad_call(
        out_grad_body, "out_grad", [*hid, *pulled], 2 * width, width
    )
    in_keep, in_near, in_far = grad_call(
        in_grad_body,
        "in_grad",
        [own, theirs, *pre_hidden, *kept, *come],
        2 * width,
        width,
        [pltpu.VMEM((height, width), BF16)] * 2,
        (dense, *t_mate),
    )
    out_far = gate(far_sum(out_keep, to_core(out_far)), *t_mate)
    in_far = far_sum(in_keep, to_core(in_far))
    out_own, in_own, terms = mate_sum(
        (out_keep, to_core(out_near), to_mate(out_far)),
        (in_keep, to_core(in_near), to_mate(in_far)),
    )
    terms = [to_group(term, number + 1) for number, term in enumerate(terms)]

    total = spread_near(dense, t_own, t_other, t_mate, in_far)
    layer_output = spread_far(dense, total, t_far, t_mate_other, t_far_other)
    grad_weight_out, grad_weight_in = group_sum(out_own, in_own, terms)
    return (layer_output, grad_weight_in, grad_weight_out)


def solution(mesh):
    return jax.shard_map(
        shards,
        mesh=mesh,
        in_specs=(
            P("blk", "feat"),
            P(None, "feat"),
            P(None, "feat"),
            P("blk", None, None, None, None),
            P("blk", None, None),
            P("blk", None, None),
            P("blk", None),
            P("blk", "feat"),
        ),
        out_specs=(P("blk", "feat"), P("blk", "feat"), P("blk", "feat")),
        check_vma=False,
    )
```

```python
import functools

import jax
import jax.numpy as jnp
from jax import lax
from jax.experimental import pallas as pl
from jax.experimental.pallas import tpu as pltpu
from jax.sharding import PartitionSpec as P

BF16 = jnp.bfloat16
F32 = jnp.float32
VMEM = pl.BlockSpec(memory_space=pltpu.VMEM)
SMEM = pl.BlockSpec(memory_space=pltpu.SMEM)
ANY = pl.BlockSpec(memory_space=pl.ANY)


def params(limit_mib=12):
    return pltpu.CompilerParams(vmem_limit_bytes=limit_mib * 1024 * 1024)


def cost(microseconds=0):
    return pl.CostEstimate(
        flops=1024, bytes_accessed=1024 + 3_600_000 * microseconds, transcendentals=0
    )


def gate_body(*refs):
    del refs


def gate(value, *after, microseconds=0):
    return pl.pallas_call(
        gate_body,
        out_shape=jax.ShapeDtypeStruct(value.shape, value.dtype),
        in_specs=[ANY] * (1 + len(after)),
        out_specs=ANY,
        input_output_aliases={0: 0},
        compiler_params=params(1),
        cost_estimate=cost(microseconds),
        name="gate",
    )(value, *after)


def coordinates():
    block = lax.axis_index("blk")
    return block & 1, (block >> 1) & 1, lax.axis_index("feat")


def coordinates():
    block = lax.axis_index("blk")
    return block & 1, (block >> 1) & 1, lax.axis_index("feat")


def copy_all(pairs, semaphores):
    copies = [
        pltpu.make_async_copy(source, target, semaphores.at[number])
        for number, (source, target) in enumerate(pairs)
    ]
    for copy in copies:
        copy.start()
    for copy in copies:
        copy.wait()


def coordinates():
    block = lax.axis_index("blk")
    return block & 1, (block >> 1) & 1, lax.axis_index("feat")


def blk_pairs(target):
    count = lax.axis_size("blk")
    return [(source, target(source) % count) for source in range(count)]


def to_core(value):
    return lax.ppermute(value, "blk", blk_pairs(lambda b: b ^ 1))


def to_mate(value):
    return lax.ppermute(value, "blk", blk_pairs(lambda b: b ^ 2))


def relay_out(value):
    return lax.ppermute(value, "blk", blk_pairs(lambda b: b - 4 if b & 2 else b + 4))


def relay_back(value):
    return lax.ppermute(value, "blk", blk_pairs(lambda b: b + 4 if b & 2 else b - 4))


def to_group(value, distance):
    return lax.ppermute(value, "blk", blk_pairs(lambda b: b ^ (4 * distance)))


def to_panel(value):
    return lax.ppermute(value, "feat", [(0, 1), (1, 0)])


def pick_body(w_in, send, semaphore):
    half = send.shape[0]
    core, _, panel = coordinates()
    start = pl.multiple_of(((1 - panel) ^ core) * half, half)
    copy = pltpu.make_async_copy(w_in.at[pl.ds(start, half), :], send, semaphore)
    copy.start()
    copy.wait()


def pick(w_in):
    width = w_in.shape[1]
    return pl.pallas_call(
        pick_body,
        out_shape=jax.ShapeDtypeStruct((width, width), BF16),
        in_specs=[ANY],
        out_specs=VMEM,
        scratch_shapes=[pltpu.SemaphoreType.DMA],
        compiler_params=params(4),
        cost_estimate=cost(),
        name="pick",
    )(w_in)


def build_body(rows, cols, counts, tiles, dense):
    _, steps, cap, tile, _ = tiles.shape
    radius = (steps - 1) // 2
    block_tiles = dense.shape[0] // tile
    core, mate, _ = coordinates()
    dense[...] = jnp.zeros_like(dense)

    def place(entry, carry):
        step, slot = entry // cap, entry % cap
        shifted = step - radius + core + 2
        chip = shifted // 2 - 1
        position = (shifted % 2) ^ core
        ahead = jnp.where(mate == 0, 1, -1)
        outside = jnp.where(position == 1, 4, jnp.where(chip == ahead, 2, 3))
        segment = jnp.where(chip == 0, position, outside)
        row = rows[step, 0, slot]
        col = segment * block_tiles + cols[step, 0, slot]

        @pl.when(slot < counts[0, step])
        def _():
            dense[
                pl.ds(pl.multiple_of(row * tile, tile), tile),
                pl.ds(pl.multiple_of(col * tile, tile), tile),
            ] = tiles[0, step, slot]

        return carry

    lax.fori_loop(0, steps * cap, place, 0)


def build(tile_rows, tile_cols, tile_counts, tiles, rows):
    return pl.pallas_call(
        build_body,
        out_shape=jax.ShapeDtypeStruct((rows, 5 * rows), BF16),
        in_specs=[SMEM] * 3 + [VMEM],
        out_specs=VMEM,
        compiler_params=params(),
        cost_estimate=cost(),
        name="build_dense",
    )(tile_rows, tile_cols, tile_counts, tiles)


def sum_products(result, dense, first, refs):
    for ref in refs:
        height = ref.shape[0]
        product = jnp.dot(
            dense[:, first : first + height], ref[...], preferred_element_type=F32
        )
        result = product if result is None else result + product
        first += height
    return result


def spread_near_body(dense, s0, s1, s2, s3, *refs):
    refs[-1][...] = sum_products(None, dense, 0, (s0, s1, s2, s3))


def spread_near(dense, own, other, mate, *after):
    rows, cols = own.shape
    block = rows // 2
    whole = pl.BlockSpec((rows, cols), lambda i: (0, 0))
    half = pl.BlockSpec((block, cols), lambda i: (0, 0))
    return pl.pallas_call(
        spread_near_body,
        grid=(2,),
        out_shape=jax.ShapeDtypeStruct((rows, cols), F32),
        in_specs=[
            pl.BlockSpec((block, 3 * rows), lambda i: (i, 0)),
            whole,
            whole,
            half,
            half,
            *[ANY] * len(after),
        ],
        out_specs=pl.BlockSpec((block, cols), lambda i: (i, 0)),
        compiler_params=params(),
        cost_estimate=cost(),
        name="spread_near",
    )(dense, own, other, *mate, *after)


def spread_far_body(dense, total, f0, f1, m0, m1, *refs):
    *far_other, out = refs
    height = f0.shape[0]
    core, mate, _ = coordinates()

    def add_up(*cross):
        out[...] = sum_products(total[...], dense, 6 * height, (f0, f1, *cross)).astype(BF16)

    pl.when(core == mate)(lambda: add_up(*far_other))
    pl.when(core != mate)(lambda: add_up(m0, m1))


def spread_far(dense, total, far, mate_other, far_other):
    return pl.pallas_call(
        spread_far_body,
        out_shape=jax.ShapeDtypeStruct(total.shape, BF16),
        in_specs=[VMEM] * (6 + len(far_other)),
        out_specs=VMEM,
        compiler_params=params(),
        cost_estimate=cost(),
        name="spread_far",
    )(dense, total, *far, *mate_other, *far_other)


def pull_body(cot, dense, own, mate, far, swap_own, swap_cross):
    rows = dense.shape[0]
    turned = cot[...].T
    terms = [
        jnp.dot(
            turned, dense[:, index * rows : (index + 1) * rows], preferred_element_type=F32
        )
        for index in range(5)
    ]
    own[...], mate[...], far[...] = terms[0], terms[2], terms[3]
    swap_own[...] = terms[1].astype(BF16)
    swap_cross[...] = terms[4].astype(BF16)


def pull(cot, dense):
    rows, cols = cot.shape
    return pl.pallas_call(
        pull_body,
        out_shape=[jax.ShapeDtypeStruct((cols, rows), F32)] * 3
        + [jax.ShapeDtypeStruct((cols, rows), BF16)] * 2,
        in_specs=[VMEM] * 2,
        out_specs=[VMEM] * 5,
        compiler_params=params(),
        cost_estimate=cost(),
        name="pull",
    )(cot, dense)


def swap_sum_body(mate_term, far_term, swap, mate_0, mate_1, far_out):
    half = mate_0.shape[1]
    core, mate, _ = coordinates()
    cross = swap[...].astype(F32)
    cross_mate = jnp.where(core == mate, cross, 0.0)
    far_out[...] = (far_term[...] + (cross - cross_mate)).astype(BF16)
    near = mate_term[...] + cross_mate
    mate_0[...], mate_1[...] = near[:, :half], near[:, half:]


def swap_sum(mate_term, far_term, swap):
    cols, rows = far_term.shape
    out = pl.pallas_call(
        swap_sum_body,
        out_shape=[jax.ShapeDtypeStruct((cols, rows // 2), F32)] * 2
        + [jax.ShapeDtypeStruct((cols, rows), BF16)],
        in_specs=[VMEM] * 3,
        out_specs=[VMEM] * 3,
        compiler_params=params(),
        cost_estimate=cost(),
        name="swap_sum",
    )(mate_term, far_term, swap)
    return out[:2], out[2]


def hidden_body(s0, s1, w_mine, w_near, w_far, w_out, *refs, number):
    pre, hid, mixed = refs[-3:]
    height, width = pre.shape
    span = slice(number * height, (number + 1) * height)
    core, _, panel = coordinates()

    def rows_of(side):
        return pl.ds(pl.multiple_of((panel ^ side) * width, width), width)

    def run(w_theirs):
        mine, theirs = 0.0, 0.0
        for side, ref in enumerate((s0, s1)):
            taken = ref[span, :]
            mine += jnp.dot(taken, w_mine[rows_of(side), :], preferred_element_type=F32)
            theirs += jnp.dot(taken, w_theirs[side][...], preferred_element_type=F32)
        pre[...] = mine
        hid[:, :width] = (mine * jax.nn.sigmoid(mine)).astype(BF16)
        hid[:, width:] = (theirs * jax.nn.sigmoid(theirs)).astype(BF16)

    pl.when(core == 0)(lambda: run((w_near, w_far)))
    pl.when(core == 1)(lambda: run((w_far, w_near)))
    result = 0.0
    for side in range(2):
        value = hid[:, side * width : (side + 1) * width]
        result += jnp.dot(value, w_out[rows_of(side), :], preferred_element_type=F32)
    mixed[...] = result.astype(BF16)


def hidden_step(number, pieces, w_mine, w_near, w_far, w_out, *after):
    rows, width = pieces[0].shape
    height = rows // 2
    return pl.pallas_call(
        functools.partial(hidden_body, number=number),
        out_shape=[
            jax.ShapeDtypeStruct((height, width), F32),
            jax.ShapeDtypeStruct((height, 2 * width), BF16),
            jax.ShapeDtypeStruct((height, width), BF16),
        ],
        in_specs=[VMEM] * 6 + [ANY] * len(after),
        out_specs=[VMEM] * 3,
        compiler_params=params(),
        cost_estimate=cost(),
        name="hidden",
    )(*pieces, w_mine, w_near, w_far, w_out, *after)


def mix_body(own, swap, come, w_out, *refs, number):
    pulled, keep, give = refs[-3:]
    height, half = keep.shape
    _, _, panel = coordinates()
    span = slice(number * height, (number + 1) * height)
    total = own[:, span] + swap[:, span].astype(F32) + come[...].astype(F32)
    pulled[...] = total.astype(BF16).T
    contract = (((1,), (1,)), ((), ()))
    theirs = w_out[pl.ds(pl.multiple_of((1 - panel) * half, half), half), :]
    give[...] = lax.dot_general(
        pulled[...], theirs, contract, preferred_element_type=F32
    ).astype(BF16)
    mine = w_out[pl.ds(pl.multiple_of(panel * half, half), half), :]
    keep[...] = lax.dot_general(pulled[...], mine, contract, preferred_element_type=F32)


def mix_step(number, own, swap, come, w_out, *after):
    cols, height = come.shape
    half = w_out.shape[0] // 2
    return pl.pallas_call(
        functools.partial(mix_body, number=number),
        out_shape=[
            jax.ShapeDtypeStruct((height, cols), BF16),
            jax.ShapeDtypeStruct((height, half), F32),
            jax.ShapeDtypeStruct((height, half), BF16),
        ],
        in_specs=[VMEM] * 4 + [ANY] * len(after),
        out_specs=[VMEM] * 3,
        compiler_params=params(),
        cost_estimate=cost(),
        name="mix_back",
    )(own, swap, come, w_out, *after)


def split_term(total, keep, give_near, give_far, scratch, blocks):
    core, mate, _ = coordinates()
    share = total.shape[0] // blocks
    groups = blocks // 4
    for group in range(groups):
        for side in range(2):
            owner = 4 * group + 2 * (mate ^ side)
            target = pl.ds((side * groups + group) * share, share)
            source = pl.multiple_of((owner + core) * share, share)
            keep[target, :] = total[pl.ds(source, share), :]
            source = pl.multiple_of((owner + 1 - core) * share, share)
            scratch[target, :] = total[pl.ds(source, share), :]
    half = give_near.shape[0]
    give_near[...] = scratch[:half].astype(BF16)
    give_far[...] = scratch[half:].astype(BF16)


def grad_into(total, pieces, rights):
    _, _, panel = coordinates()
    contract = (((0,), (0,)), ((), ()))
    width = rights[0].shape[1]
    half = width // 2
    for side, (refs, first) in enumerate(pieces):
        for number in range(2):
            start = (panel ^ side) * width + number * half
            source = first + number * half
            result = 0.0
            for index, right in enumerate(rights):
                height = right.shape[0]
                if len(refs) == 1:
                    taken = refs[0][index * height : (index + 1) * height, source : source + half]
                else:
                    taken = refs[index][:, source : source + half]
                result += lax.dot_general(
                    taken,
                    right[...],
                    contract,
                    preferred_element_type=F32,
                )
            total[pl.ds(pl.multiple_of(start, half), half), :] = result


def out_grad_body(hid_0, hid_1, pulled_0, pulled_1, *refs, blocks):
    keep, near, far, total, scratch = refs[-5:]
    width = pulled_0.shape[1]
    hid = (hid_0, hid_1)
    grad_into(total, ((hid, 0), (hid, width)), (pulled_0, pulled_1))
    split_term(total, keep, near, far, scratch, blocks)


def in_grad_body(*refs, blocks):
    own, theirs, *refs = refs
    pre, kept, come = [refs[2 * i : 2 * i + 2] for i in range(3)]
    keep, near, far, total, scratch, *back = refs[-7:]
    for half in range(2):
        pre_hidden = pre[half][...]
        gate = jax.nn.sigmoid(pre_hidden)
        back_hidden = kept[half][...] + come[half][...].astype(F32)
        slope = gate * (1.0 + pre_hidden * (1.0 - gate))
        back[half][...] = (back_hidden * slope).astype(BF16)
    grad_into(total, (((own,), 0), ((theirs,), 0)), back)
    split_term(total, keep, near, far, scratch, blocks)


def grad_call(body, name, operands, height, width, scratch=(), after=()):
    blocks = lax.axis_size("blk")
    half = height // 2
    return pl.pallas_call(
        functools.partial(body, blocks=blocks),
        out_shape=[
            jax.ShapeDtypeStruct((half, width), F32),
            jax.ShapeDtypeStruct((half // 2, width), BF16),
            jax.ShapeDtypeStruct((half // 2, width), BF16),
        ],
        in_specs=[VMEM] * len(operands) + [ANY] * len(after),
        out_specs=[VMEM] * 3,
        scratch_shapes=[
            pltpu.VMEM((height, width), F32),
            pltpu.VMEM((half, width), F32),
            *scratch,
        ],
        compiler_params=params(),
        cost_estimate=cost(),
        name=name,
    )(*operands, *after)


def far_sum_body(keep, come, far):
    half = far.shape[0]
    far[...] = (keep[half:] + come[...].astype(F32)).astype(BF16)


def far_sum(keep, come):
    return pl.pallas_call(
        far_sum_body,
        out_shape=jax.ShapeDtypeStruct(come.shape, BF16),
        in_specs=[VMEM] * 2,
        out_specs=VMEM,
        compiler_params=params(),
        cost_estimate=cost(),
        name="far_sum",
    )(keep, come)


def mate_sum_body(first, first_core, first_come, second, second_core, second_come, *refs):
    own_first, own_second, *terms, sum_first, sum_second = refs
    share = own_first.shape[0]
    group = lax.axis_index("blk") // 4
    half = sum_first.shape[0]
    sum_first[...] = first[:half] + first_core[...].astype(F32) + first_come[...].astype(F32)
    sum_second[...] = second[:half] + second_core[...].astype(F32) + second_come[...].astype(F32)

    def rows_of(distance):
        start = pl.multiple_of((group ^ distance) * share, share)
        return sum_first[pl.ds(start, share), :], sum_second[pl.ds(start, share), :]

    own_first[...], own_second[...] = rows_of(0)
    for number, ref in enumerate(terms):
        ref[...] = jnp.concatenate(rows_of(number + 1), axis=0).astype(BF16)


def mate_sum(first, second):
    height, width = first[1].shape
    groups = lax.axis_size("blk") // 4
    share = height // groups
    own = jax.ShapeDtypeStruct((share, width), F32)
    term = jax.ShapeDtypeStruct((2 * share, width), BF16)
    own_first, own_second, *terms = pl.pallas_call(
        mate_sum_body,
        out_shape=[own] * 2 + [term] * (groups - 1),
        in_specs=[VMEM] * 6,
        out_specs=[VMEM] * (1 + groups),
        scratch_shapes=[pltpu.VMEM((height, width), F32)] * 2,
        compiler_params=params(),
        cost_estimate=cost(),
        name="mate_sum",
    )(*first, *second)
    return own_first, own_second, terms


def group_sum_body(own_first, own_second, *refs):
    *terms, out_first, out_second = refs
    share = own_first.shape[0]
    total_first, total_second = own_first[...], own_second[...]
    for ref in terms:
        term = ref[...].astype(F32)
        total_first += term[:share]
        total_second += term[share:]
    out_first[...] = total_first
    out_second[...] = total_second


def group_sum(own_first, own_second, terms):
    return pl.pallas_call(
        group_sum_body,
        out_shape=[jax.ShapeDtypeStruct(own_first.shape, F32)] * 2,
        in_specs=[VMEM] * (2 + len(terms)),
        out_specs=[VMEM] * 2,
        compiler_params=params(),
        cost_estimate=cost(),
        name="group_sum",
    )(own_first, own_second, *terms)


def shards(
    features, weight_in, weight_out, adj_tiles, tile_rows, tile_cols, tile_counts, cotangent
):
    rows, width = features.shape
    tile_rows, tile_cols = jnp.swapaxes(tile_rows, 0, 1), jnp.swapaxes(tile_cols, 0, 1)

    height = rows // 2

    f_mate = [to_mate(features[:height]), to_mate(features[height:])]
    f_other = to_core(features)
    f_mate_other = [to_core(half) for half in f_mate]
    f_far = [relay_out(half) for half in f_mate]
    f_far_other = [
        to_core(half[first : first + height // 2])
        for half in f_far
        for first in (0, height // 2)
    ]
    w_near = to_panel(gate(pick(weight_in), f_mate[0]))
    w_far = to_core(w_near)

    dense = build(tile_rows, tile_cols, tile_counts, adj_tiles, rows)
    p_own, p_mate, p_far, p_swap, p_cross = pull(cotangent, dense)
    p_mate, p_far = swap_sum(
        p_mate, p_far, to_core(gate(p_cross, *f_mate))
    )
    p_swap = to_core(p_swap)
    p_come = relay_back(p_far)
    p_come = [p_come[:, :height], p_come[:, height:]]

    total = spread_near(dense, features, f_other, f_mate)
    own = spread_far(dense, total, f_far, f_mate_other, f_far_other)
    theirs = to_panel(own)
    q_come = [
        to_mate((mine + come.astype(F32)).astype(BF16)) for mine, come in zip(p_mate, p_come)
    ]
    pre_hidden, hid, mixed = zip(
        *[
            hidden_step(number, (own, theirs), weight_in, w_near, w_far, weight_out, dense)
            for number in range(2)
        ]
    )

    t_mate = [to_mate(half) for half in mixed]
    t_own = jnp.concatenate(mixed, axis=0)
    t_other = to_core(t_own)
    t_mate_other = [to_core(half) for half in t_mate]
    t_far = [relay_out(half) for half in t_mate]
    t_far_other = [to_core(half) for half in t_far]

    pulled, kept, given = zip(
        *[
            mix_step(number, p_own, p_swap, come, weight_out, dense)
            for number, come in enumerate(q_come)
        ]
    )
    come = [to_panel(half) for half in given]
    out_keep, out_near, out_far = grad_call(
        out_grad_body, "out_grad", [*hid, *pulled], 2 * width, width
    )
    in_keep, in_near, in_far = grad_call(
        in_grad_body,
        "in_grad",
        [own, theirs, *pre_hidden, *kept, *come],
        2 * width,
        width,
        [pltpu.VMEM((height, width), BF16)] * 2,
        (dense, *t_mate),
    )
    out_far = gate(far_sum(out_keep, to_core(out_far)), *t_mate)
    in_far = far_sum(in_keep, to_core(in_far))
    out_own, in_own, terms = mate_sum(
        (out_keep, to_core(out_near), to_mate(out_far)),
        (in_keep, to_core(in_near), to_mate(in_far)),
    )
    terms = [to_group(term, number + 1) for number, term in enumerate(terms)]

    total = spread_near(dense, t_own, t_other, t_mate, in_far)
    layer_output = spread_far(dense, total, t_far, t_mate_other, t_far_other)
    grad_weight_out, grad_weight_in = group_sum(out_own, in_own, terms)
    return (layer_output, grad_weight_in, grad_weight_out)


def solution(mesh):
    return jax.shard_map(
        shards,
        mesh=mesh,
        in_specs=(
            P("blk", "feat"),
            P(None, "feat"),
            P(None, "feat"),
            P("blk", None, None, None, None),
            P("blk", None, None),
            P("blk", None, None),
            P("blk", None),
            P("blk", "feat"),
        ),
        out_specs=(P("blk", "feat"), P("blk", "feat"), P("blk", "feat")),
        check_vma=False,
    )
```

```python
import functools

import jax
import jax.numpy as jnp
from jax import lax
from jax.experimental import pallas as pl
from jax.experimental.pallas import tpu as pltpu
from jax.sharding import PartitionSpec as P

BF16 = jnp.bfloat16
F32 = jnp.float32
VMEM = pl.BlockSpec(memory_space=pltpu.VMEM)
SMEM = pl.BlockSpec(memory_space=pltpu.SMEM)
ANY = pl.BlockSpec(memory_space=pl.ANY)


def params(limit_mib=12):
    return pltpu.CompilerParams(vmem_limit_bytes=limit_mib * 1024 * 1024)


def cost(microseconds=0):
    return pl.CostEstimate(
        flops=1024, bytes_accessed=1024 + 3_600_000 * microseconds, transcendentals=0
    )


def gate_body(*refs):
    del refs


def gate(value, *after, microseconds=0):
    return pl.pallas_call(
        gate_body,
        out_shape=jax.ShapeDtypeStruct(value.shape, value.dtype),
        in_specs=[ANY] * (1 + len(after)),
        out_specs=ANY,
        input_output_aliases={0: 0},
        compiler_params=params(1),
        cost_estimate=cost(microseconds),
        name="gate",
    )(value, *after)


def coordinates():
    block = lax.axis_index("blk")
    return block & 1, (block >> 1) & 1, lax.axis_index("feat")


def coordinates():
    block = lax.axis_index("blk")
    return block & 1, (block >> 1) & 1, lax.axis_index("feat")


def copy_all(pairs, semaphores):
    copies = [
        pltpu.make_async_copy(source, target, semaphores.at[number])
        for number, (source, target) in enumerate(pairs)
    ]
    for copy in copies:
        copy.start()
    for copy in copies:
        copy.wait()


def coordinates():
    block = lax.axis_index("blk")
    return block & 1, (block >> 1) & 1, lax.axis_index("feat")


def blk_pairs(target):
    count = lax.axis_size("blk")
    return [(source, target(source) % count) for source in range(count)]


def to_core(value):
    return lax.ppermute(value, "blk", blk_pairs(lambda b: b ^ 1))


def to_mate(value):
    return lax.ppermute(value, "blk", blk_pairs(lambda b: b ^ 2))


def relay_out(value):
    return lax.ppermute(value, "blk", blk_pairs(lambda b: b - 4 if b & 2 else b + 4))


def relay_back(value):
    return lax.ppermute(value, "blk", blk_pairs(lambda b: b + 4 if b & 2 else b - 4))


def to_group(value, distance):
    return lax.ppermute(value, "blk", blk_pairs(lambda b: b ^ (4 * distance)))


def to_panel(value):
    return lax.ppermute(value, "feat", [(0, 1), (1, 0)])


def pick_body(w_in, send, semaphore):
    half = send.shape[0]
    core, _, panel = coordinates()
    start = pl.multiple_of(((1 - panel) ^ core) * half, half)
    copy = pltpu.make_async_copy(w_in.at[pl.ds(start, half), :], send, semaphore)
    copy.start()
    copy.wait()


def pick(w_in):
    width = w_in.shape[1]
    return pl.pallas_call(
        pick_body,
        out_shape=jax.ShapeDtypeStruct((width, width), BF16),
        in_specs=[ANY],
        out_specs=VMEM,
        scratch_shapes=[pltpu.SemaphoreType.DMA],
        compiler_params=params(4),
        cost_estimate=cost(),
        name="pick",
    )(w_in)


def build_body(rows, cols, counts, tiles, dense):
    _, steps, cap, tile, _ = tiles.shape
    radius = (steps - 1) // 2
    block_tiles = dense.shape[0] // tile
    core, mate, _ = coordinates()
    dense[...] = jnp.zeros_like(dense)

    def place(entry, carry):
        step, slot = entry // cap, entry % cap
        shifted = step - radius + core + 2
        chip = shifted // 2 - 1
        position = (shifted % 2) ^ core
        ahead = jnp.where(mate == 0, 1, -1)
        outside = jnp.where(position == 1, 4, jnp.where(chip == ahead, 2, 3))
        segment = jnp.where(chip == 0, position, outside)
        row = rows[step, 0, slot]
        col = segment * block_tiles + cols[step, 0, slot]

        @pl.when(slot < counts[0, step])
        def _():
            dense[
                pl.ds(pl.multiple_of(row * tile, tile), tile),
                pl.ds(pl.multiple_of(col * tile, tile), tile),
            ] = tiles[0, step, slot]

        return carry

    lax.fori_loop(0, steps * cap, place, 0)


def build(tile_rows, tile_cols, tile_counts, tiles, rows):
    return pl.pallas_call(
        build_body,
        out_shape=jax.ShapeDtypeStruct((rows, 5 * rows), BF16),
        in_specs=[SMEM] * 3 + [VMEM],
        out_specs=VMEM,
        compiler_params=params(),
        cost_estimate=cost(),
        name="build_dense",
    )(tile_rows, tile_cols, tile_counts, tiles)


def sum_products(result, dense, first, refs):
    for ref in refs:
        height = ref.shape[0]
        product = jnp.dot(
            dense[:, first : first + height], ref[...], preferred_element_type=F32
        )
        result = product if result is None else result + product
        first += height
    return result


def spread_near_body(dense, s0, s1, s2, s3, *refs):
    refs[-1][...] = sum_products(None, dense, 0, (s0, s1, s2, s3))


def spread_near(dense, own, other, mate, *after):
    rows, cols = own.shape
    block = rows // 2
    whole = pl.BlockSpec((rows, cols), lambda i: (0, 0))
    half = pl.BlockSpec((block, cols), lambda i: (0, 0))
    return pl.pallas_call(
        spread_near_body,
        grid=(2,),
        out_shape=jax.ShapeDtypeStruct((rows, cols), F32),
        in_specs=[
            pl.BlockSpec((block, 3 * rows), lambda i: (i, 0)),
            whole,
            whole,
            half,
            half,
            *[ANY] * len(after),
        ],
        out_specs=pl.BlockSpec((block, cols), lambda i: (i, 0)),
        compiler_params=params(),
        cost_estimate=cost(),
        name="spread_near",
    )(dense, own, other, *mate, *after)


def spread_far_body(dense, total, f0, f1, m0, m1, x0, x1, out):
    height = f0.shape[0]
    core, mate, _ = coordinates()

    def add_up(*cross):
        out[...] = sum_products(total[...], dense, 6 * height, (f0, f1, *cross)).astype(BF16)

    pl.when(core == mate)(lambda: add_up(x0, x1))
    pl.when(core != mate)(lambda: add_up(m0, m1))


def spread_far(dense, total, far, mate_other, far_other):
    return pl.pallas_call(
        spread_far_body,
        out_shape=jax.ShapeDtypeStruct(total.shape, BF16),
        in_specs=[VMEM] * 8,
        out_specs=VMEM,
        compiler_params=params(),
        cost_estimate=cost(),
        name="spread_far",
    )(dense, total, *far, *mate_other, *far_other)


def pull_body(cot, dense, own, mate, far, swap_own, cross_0, cross_1):
    rows = dense.shape[0]
    turned = cot[...].T
    terms = [
        jnp.dot(
            turned, dense[:, index * rows : (index + 1) * rows], preferred_element_type=F32
        )
        for index in range(5)
    ]
    own[...], mate[...], far[...] = terms[0], terms[2], terms[3]
    swap_own[...] = terms[1].astype(BF16)
    half = cross_0.shape[1]
    cross_0[...], cross_1[...] = terms[4][:, :half].astype(BF16), terms[4][:, half:].astype(BF16)


def pull(cot, dense):
    rows, cols = cot.shape
    return pl.pallas_call(
        pull_body,
        out_shape=[jax.ShapeDtypeStruct((cols, rows), F32)] * 3
        + [jax.ShapeDtypeStruct((cols, rows), BF16)]
        + [jax.ShapeDtypeStruct((cols, rows // 2), BF16)] * 2,
        in_specs=[VMEM] * 2,
        out_specs=[VMEM] * 6,
        compiler_params=params(),
        cost_estimate=cost(),
        name="pull",
    )(cot, dense)


def swap_sum_body(mate_term, far_term, cross_0, cross_1, mate_0, mate_1, far_0, far_1):
    half = far_0.shape[1]
    core, mate, _ = coordinates()
    cross = jnp.concatenate([cross_0[...], cross_1[...]], axis=1).astype(F32)
    cross_mate = jnp.where(core == mate, cross, 0.0)
    far = (far_term[...] + (cross - cross_mate)).astype(BF16)
    near = mate_term[...] + cross_mate
    mate_0[...], mate_1[...] = near[:, :half], near[:, half:]
    far_0[...], far_1[...] = far[:, :half], far[:, half:]


def swap_sum(mate_term, far_term, cross):
    cols, rows = far_term.shape
    shape = (cols, rows // 2)
    out = pl.pallas_call(
        swap_sum_body,
        out_shape=[jax.ShapeDtypeStruct(shape, F32)] * 2
        + [jax.ShapeDtypeStruct(shape, BF16)] * 2,
        in_specs=[VMEM] * 4,
        out_specs=[VMEM] * 4,
        compiler_params=params(),
        cost_estimate=cost(),
        name="swap_sum",
    )(mate_term, far_term, *cross)
    return out[:2], out[2:]


def meet_body(mine, come, *refs):
    refs[-1][...] = (mine[...] + come[...].astype(F32)).astype(BF16)


def meet(mine, come, *after):
    return pl.pallas_call(
        meet_body,
        out_shape=jax.ShapeDtypeStruct(mine.shape, BF16),
        in_specs=[VMEM] * 2 + [ANY] * len(after),
        out_specs=VMEM,
        compiler_params=params(),
        cost_estimate=cost(),
        name="meet",
    )(mine, come, *after)


def hidden_body(s0, s1, w_mine, w_near, w_far, w_out, *refs, number):
    pre, hid, mixed = refs[-3:]
    height, width = pre.shape
    span = slice(number * height, (number + 1) * height)
    core, _, panel = coordinates()

    def rows_of(side):
        return pl.ds(pl.multiple_of((panel ^ side) * width, width), width)

    def run(w_theirs):
        mine, theirs = 0.0, 0.0
        for side, ref in enumerate((s0, s1)):
            taken = ref[span, :]
            mine += jnp.dot(taken, w_mine[rows_of(side), :], preferred_element_type=F32)
            theirs += jnp.dot(taken, w_theirs[side][...], preferred_element_type=F32)
        pre[...] = mine
        hid[:, :width] = (mine * jax.nn.sigmoid(mine)).astype(BF16)
        hid[:, width:] = (theirs * jax.nn.sigmoid(theirs)).astype(BF16)

    pl.when(core == 0)(lambda: run((w_near, w_far)))
    pl.when(core == 1)(lambda: run((w_far, w_near)))
    result = 0.0
    for side in range(2):
        value = hid[:, side * width : (side + 1) * width]
        result += jnp.dot(value, w_out[rows_of(side), :], preferred_element_type=F32)
    mixed[...] = result.astype(BF16)


def hidden_step(number, pieces, w_mine, w_near, w_far, w_out, *after):
    rows, width = pieces[0].shape
    height = rows // 2
    return pl.pallas_call(
        functools.partial(hidden_body, number=number),
        out_shape=[
            jax.ShapeDtypeStruct((height, width), F32),
            jax.ShapeDtypeStruct((height, 2 * width), BF16),
            jax.ShapeDtypeStruct((height, width), BF16),
        ],
        in_specs=[VMEM] * 6 + [ANY] * len(after),
        out_specs=[VMEM] * 3,
        compiler_params=params(),
        cost_estimate=cost(),
        name="hidden",
    )(*pieces, w_mine, w_near, w_far, w_out, *after)


def mix_body(own, swap, come, w_out, *refs, number):
    pulled, keep, give = refs[-3:]
    height, half = keep.shape
    _, _, panel = coordinates()
    span = slice(number * height, (number + 1) * height)
    total = own[:, span] + swap[:, span].astype(F32) + come[...].astype(F32)
    pulled[...] = total.astype(BF16).T
    contract = (((1,), (1,)), ((), ()))
    theirs = w_out[pl.ds(pl.multiple_of((1 - panel) * half, half), half), :]
    give[...] = lax.dot_general(
        pulled[...], theirs, contract, preferred_element_type=F32
    ).astype(BF16)
    mine = w_out[pl.ds(pl.multiple_of(panel * half, half), half), :]
    keep[...] = lax.dot_general(pulled[...], mine, contract, preferred_element_type=F32)


def mix_step(number, own, swap, come, w_out, *after):
    cols, height = come.shape
    half = w_out.shape[0] // 2
    return pl.pallas_call(
        functools.partial(mix_body, number=number),
        out_shape=[
            jax.ShapeDtypeStruct((height, cols), BF16),
            jax.ShapeDtypeStruct((height, half), F32),
            jax.ShapeDtypeStruct((height, half), BF16),
        ],
        in_specs=[VMEM] * 4 + [ANY] * len(after),
        out_specs=[VMEM] * 3,
        compiler_params=params(),
        cost_estimate=cost(),
        name="mix_back",
    )(own, swap, come, w_out, *after)


def split_term(total, keep, give_near, give_far, scratch, blocks):
    core, mate, _ = coordinates()
    share = total.shape[0] // blocks
    groups = blocks // 4
    for group in range(groups):
        for side in range(2):
            owner = 4 * group + 2 * (mate ^ side)
            target = pl.ds((side * groups + group) * share, share)
            source = pl.multiple_of((owner + core) * share, share)
            keep[target, :] = total[pl.ds(source, share), :]
            source = pl.multiple_of((owner + 1 - core) * share, share)
            scratch[target, :] = total[pl.ds(source, share), :]
    half = give_near.shape[0]
    give_near[...] = scratch[:half].astype(BF16)
    give_far[...] = scratch[half:].astype(BF16)


def grad_into(total, pieces, rights):
    _, _, panel = coordinates()
    contract = (((0,), (0,)), ((), ()))
    width = rights[0].shape[1]
    half = width // 2
    for side, (refs, first) in enumerate(pieces):
        for number in range(2):
            start = (panel ^ side) * width + number * half
            source = first + number * half
            result = 0.0
            for index, right in enumerate(rights):
                height = right.shape[0]
                if len(refs) == 1:
                    taken = refs[0][index * height : (index + 1) * height, source : source + half]
                else:
                    taken = refs[index][:, source : source + half]
                result += lax.dot_general(
                    taken,
                    right[...],
                    contract,
                    preferred_element_type=F32,
                )
            total[pl.ds(pl.multiple_of(start, half), half), :] = result


def out_grad_body(hid_0, hid_1, pulled_0, pulled_1, *refs, blocks):
    keep, near, far, total, scratch = refs[-5:]
    width = pulled_0.shape[1]
    hid = (hid_0, hid_1)
    grad_into(total, ((hid, 0), (hid, width)), (pulled_0, pulled_1))
    split_term(total, keep, near, far, scratch, blocks)


def in_grad_body(*refs, blocks):
    own, theirs, *refs = refs
    pre, kept, come = [refs[2 * i : 2 * i + 2] for i in range(3)]
    keep, near, far, total, scratch, *back = refs[-7:]
    for half in range(2):
        pre_hidden = pre[half][...]
        gate = jax.nn.sigmoid(pre_hidden)
        back_hidden = kept[half][...] + come[half][...].astype(F32)
        slope = gate * (1.0 + pre_hidden * (1.0 - gate))
        back[half][...] = (back_hidden * slope).astype(BF16)
    grad_into(total, (((own,), 0), ((theirs,), 0)), back)
    split_term(total, keep, near, far, scratch, blocks)


def grad_call(body, name, operands, height, width, scratch=(), after=()):
    blocks = lax.axis_size("blk")
    half = height // 2
    return pl.pallas_call(
        functools.partial(body, blocks=blocks),
        out_shape=[
            jax.ShapeDtypeStruct((half, width), F32),
            jax.ShapeDtypeStruct((half // 2, width), BF16),
            jax.ShapeDtypeStruct((half // 2, width), BF16),
        ],
        in_specs=[VMEM] * len(operands) + [ANY] * len(after),
        out_specs=[VMEM] * 3,
        scratch_shapes=[
            pltpu.VMEM((height, width), F32),
            pltpu.VMEM((half, width), F32),
            *scratch,
        ],
        compiler_params=params(),
        cost_estimate=cost(),
        name=name,
    )(*operands, *after)


def far_sum_body(first, first_come, second, second_come, _, far):
    half = far.shape[0] // 2
    far[:half] = (first[half:] + first_come[...].astype(F32)).astype(BF16)
    far[half:] = (second[half:] + second_come[...].astype(F32)).astype(BF16)


def far_sum(first, first_come, second, second_come, after):
    return pl.pallas_call(
        far_sum_body,
        out_shape=jax.ShapeDtypeStruct(first.shape, BF16),
        in_specs=[VMEM] * 4 + [ANY],
        out_specs=VMEM,
        compiler_params=params(),
        cost_estimate=cost(),
        name="far_sum",
    )(first, first_come, second, second_come, after)


def mate_sum_body(first, first_core, second, second_core, come, *refs):
    own_first, own_second, *terms, sum_first, sum_second = refs
    share = own_first.shape[0]
    group = lax.axis_index("blk") // 4
    half = sum_first.shape[0]
    sum_first[...] = first[:half] + first_core[...].astype(F32) + come[:half].astype(F32)
    sum_second[...] = second[:half] + second_core[...].astype(F32) + come[half:].astype(F32)

    def rows_of(distance):
        start = pl.multiple_of((group ^ distance) * share, share)
        return sum_first[pl.ds(start, share), :], sum_second[pl.ds(start, share), :]

    own_first[...], own_second[...] = rows_of(0)
    for number, ref in enumerate(terms):
        ref[...] = jnp.concatenate(rows_of(number + 1), axis=0).astype(BF16)


def mate_sum(first, first_core, second, second_core, come):
    height, width = first_core.shape
    groups = lax.axis_size("blk") // 4
    share = height // groups
    own = jax.ShapeDtypeStruct((share, width), F32)
    term = jax.ShapeDtypeStruct((2 * share, width), BF16)
    own_first, own_second, *terms = pl.pallas_call(
        mate_sum_body,
        out_shape=[own] * 2 + [term] * (groups - 1),
        in_specs=[VMEM] * 5,
        out_specs=[VMEM] * (1 + groups),
        scratch_shapes=[pltpu.VMEM((height, width), F32)] * 2,
        compiler_params=params(),
        cost_estimate=cost(),
        name="mate_sum",
    )(first, first_core, second, second_core, come)
    return own_first, own_second, terms


def group_sum_body(own_first, own_second, *refs):
    *terms, out_first, out_second = refs
    share = own_first.shape[0]
    total_first, total_second = own_first[...], own_second[...]
    for ref in terms:
        term = ref[...].astype(F32)
        total_first += term[:share]
        total_second += term[share:]
    out_first[...] = total_first
    out_second[...] = total_second


def group_sum(own_first, own_second, terms):
    return pl.pallas_call(
        group_sum_body,
        out_shape=[jax.ShapeDtypeStruct(own_first.shape, F32)] * 2,
        in_specs=[VMEM] * (2 + len(terms)),
        out_specs=[VMEM] * 2,
        compiler_params=params(),
        cost_estimate=cost(),
        name="group_sum",
    )(own_first, own_second, *terms)


def shards(
    features, weight_in, weight_out, adj_tiles, tile_rows, tile_cols, tile_counts, cotangent
):
    rows, width = features.shape
    tile_rows, tile_cols = jnp.swapaxes(tile_rows, 0, 1), jnp.swapaxes(tile_cols, 0, 1)

    height = rows // 2

    f_mate = [to_mate(features[:height]), to_mate(features[height:])]
    f_other = to_core(features)
    f_mate_other = [to_core(half) for half in f_mate]
    f_far = [relay_out(half) for half in f_mate]
    w_near = to_panel(gate(pick(weight_in), f_mate[0]))
    w_far = to_core(w_near)

    dense = build(tile_rows, tile_cols, tile_counts, adj_tiles, rows)
    p_own, p_mate, p_far, p_swap, *p_cross = pull(cotangent, dense)
    p_mate, p_far = swap_sum(
        p_mate, p_far, [to_core(gate(half, f_mate[1])) for half in p_cross]
    )
    p_swap = to_core(p_swap)

    total = spread_near(dense, features, f_other, f_mate, p_far[0])
    f_far = [gate(half, total) for half in f_far]
    p_come = [relay_back(gate(far, *f_far)) for far in p_far]
    f_far_other = [to_core(half) for half in f_far]
    own = spread_far(dense, total, f_far, f_mate_other, f_far_other)
    theirs = to_panel(own)
    q_come = [to_mate(meet(mine, come)) for mine, come in zip(p_mate, p_come)]
    pre_hidden, hid, mixed = zip(
        *[
            hidden_step(number, (own, theirs), weight_in, w_near, w_far, weight_out, dense)
            for number in range(2)
        ]
    )

    t_mate = [to_mate(half) for half in mixed]
    t_own = jnp.concatenate(mixed, axis=0)
    t_other = to_core(t_own)
    t_mate_other = [to_core(half) for half in t_mate]
    t_far = [relay_out(half) for half in t_mate]
    t_far_other = [to_core(half) for half in t_far]

    pulled, kept, given = zip(
        *[
            mix_step(number, p_own, p_swap, come, weight_out, dense)
            for number, come in enumerate(q_come)
        ]
    )
    come = [to_panel(half) for half in given]
    out_keep, out_near, out_far = grad_call(
        out_grad_body, "out_grad", [*hid, *pulled], 2 * width, width
    )
    in_keep, in_near, in_far = grad_call(
        in_grad_body,
        "in_grad",
        [own, theirs, *pre_hidden, *kept, *come],
        2 * width,
        width,
        [pltpu.VMEM((height, width), BF16)] * 2,
        (dense, *t_mate),
    )
    far = far_sum(out_keep, to_core(out_far), in_keep, to_core(in_far), t_far[0])
    out_own, in_own, terms = mate_sum(
        out_keep, to_core(out_near), in_keep, to_core(in_near), to_mate(far)
    )
    terms = [to_group(term, number + 1) for number, term in enumerate(terms)]

    total = spread_near(dense, t_own, t_other, t_mate)
    layer_output = spread_far(dense, total, t_far, t_mate_other, t_far_other)
    grad_weight_out, grad_weight_in = group_sum(out_own, in_own, terms)
    return (layer_output, grad_weight_in, grad_weight_out)


def solution(mesh):
    return jax.shard_map(
        shards,
        mesh=mesh,
        in_specs=(
            P("blk", "feat"),
            P(None, "feat"),
            P(None, "feat"),
            P("blk", None, None, None, None),
            P("blk", None, None),
            P("blk", None, None),
            P("blk", None),
            P("blk", "feat"),
        ),
        out_specs=(P("blk", "feat"), P("blk", "feat"), P("blk", "feat")),
        check_vma=False,
    )
```

```python
import functools

import jax
import jax.numpy as jnp
from jax import lax
from jax.experimental import pallas as pl
from jax.experimental.pallas import tpu as pltpu
from jax.sharding import PartitionSpec as P

BF16 = jnp.bfloat16
F32 = jnp.float32
VMEM = pl.BlockSpec(memory_space=pltpu.VMEM)
SMEM = pl.BlockSpec(memory_space=pltpu.SMEM)
ANY = pl.BlockSpec(memory_space=pl.ANY)


def params(limit_mib=12):
    return pltpu.CompilerParams(vmem_limit_bytes=limit_mib * 1024 * 1024)


def cost(microseconds=0):
    return pl.CostEstimate(
        flops=1024, bytes_accessed=1024 + 3_600_000 * microseconds, transcendentals=0
    )


def gate_body(*refs):
    del refs


def gate(value, *after, microseconds=0):
    return pl.pallas_call(
        gate_body,
        out_shape=jax.ShapeDtypeStruct(value.shape, value.dtype),
        in_specs=[ANY] * (1 + len(after)),
        out_specs=ANY,
        input_output_aliases={0: 0},
        compiler_params=params(1),
        cost_estimate=cost(microseconds),
        name="gate",
    )(value, *after)


def coordinates():
    block = lax.axis_index("blk")
    return block & 1, (block >> 1) & 1, lax.axis_index("feat")


def coordinates():
    block = lax.axis_index("blk")
    return block & 1, (block >> 1) & 1, lax.axis_index("feat")


def copy_all(pairs, semaphores):
    copies = [
        pltpu.make_async_copy(source, target, semaphores.at[number])
        for number, (source, target) in enumerate(pairs)
    ]
    for copy in copies:
        copy.start()
    for copy in copies:
        copy.wait()


def coordinates():
    block = lax.axis_index("blk")
    return block & 1, (block >> 1) & 1, lax.axis_index("feat")


def blk_pairs(target):
    count = lax.axis_size("blk")
    return [(source, target(source) % count) for source in range(count)]


def to_core(value):
    return lax.ppermute(value, "blk", blk_pairs(lambda b: b ^ 1))


def to_mate(value):
    return lax.ppermute(value, "blk", blk_pairs(lambda b: b ^ 2))


def relay_out(value):
    return lax.ppermute(value, "blk", blk_pairs(lambda b: b - 4 if b & 2 else b + 4))


def relay_back(value):
    return lax.ppermute(value, "blk", blk_pairs(lambda b: b + 4 if b & 2 else b - 4))


def to_group(value, distance):
    return lax.ppermute(value, "blk", blk_pairs(lambda b: b ^ (4 * distance)))


def to_panel(value):
    return lax.ppermute(value, "feat", [(0, 1), (1, 0)])


def pick_body(w_in, send, semaphore):
    half = send.shape[0]
    core, _, panel = coordinates()
    start = pl.multiple_of(((1 - panel) ^ core) * half, half)
    copy = pltpu.make_async_copy(w_in.at[pl.ds(start, half), :], send, semaphore)
    copy.start()
    copy.wait()


def pick(w_in):
    width = w_in.shape[1]
    return pl.pallas_call(
        pick_body,
        out_shape=jax.ShapeDtypeStruct((width, width), BF16),
        in_specs=[ANY],
        out_specs=VMEM,
        scratch_shapes=[pltpu.SemaphoreType.DMA],
        compiler_params=params(4),
        cost_estimate=cost(),
        name="pick",
    )(w_in)


def build_body(rows, cols, counts, tiles, dense):
    _, steps, cap, tile, _ = tiles.shape
    radius = (steps - 1) // 2
    block_tiles = dense.shape[0] // tile
    core, mate, _ = coordinates()
    dense[...] = jnp.zeros_like(dense)

    def place(entry, carry):
        step, slot = entry // cap, entry % cap
        shifted = step - radius + core + 2
        chip = shifted // 2 - 1
        position = (shifted % 2) ^ core
        ahead = jnp.where(mate == 0, 1, -1)
        outside = jnp.where(position == 1, 4, jnp.where(chip == ahead, 2, 3))
        segment = jnp.where(chip == 0, position, outside)
        row = rows[step, 0, slot]
        col = segment * block_tiles + cols[step, 0, slot]

        @pl.when(slot < counts[0, step])
        def _():
            dense[
                pl.ds(pl.multiple_of(row * tile, tile), tile),
                pl.ds(pl.multiple_of(col * tile, tile), tile),
            ] = tiles[0, step, slot]

        return carry

    lax.fori_loop(0, steps * cap, place, 0)


def build(tile_rows, tile_cols, tile_counts, tiles, rows):
    return pl.pallas_call(
        build_body,
        out_shape=jax.ShapeDtypeStruct((rows, 5 * rows), BF16),
        in_specs=[SMEM] * 3 + [VMEM],
        out_specs=VMEM,
        compiler_params=params(),
        cost_estimate=cost(),
        name="build_dense",
    )(tile_rows, tile_cols, tile_counts, tiles)


def sum_products(result, dense, first, refs):
    for ref in refs:
        height = ref.shape[0]
        product = jnp.dot(
            dense[:, first : first + height], ref[...], preferred_element_type=F32
        )
        result = product if result is None else result + product
        first += height
    return result


def spread_near_body(dense, s0, s1, s2, s3, *refs):
    refs[-1][...] = sum_products(None, dense, 0, (s0, s1, s2, s3))


def spread_near(dense, own, other, mate, *after):
    rows, cols = own.shape
    block = rows // 2
    whole = pl.BlockSpec((rows, cols), lambda i: (0, 0))
    half = pl.BlockSpec((block, cols), lambda i: (0, 0))
    return pl.pallas_call(
        spread_near_body,
        grid=(2,),
        out_shape=jax.ShapeDtypeStruct((rows, cols), F32),
        in_specs=[
            pl.BlockSpec((block, 3 * rows), lambda i: (i, 0)),
            whole,
            whole,
            half,
            half,
            *[ANY] * len(after),
        ],
        out_specs=pl.BlockSpec((block, cols), lambda i: (i, 0)),
        compiler_params=params(),
        cost_estimate=cost(),
        name="spread_near",
    )(dense, own, other, *mate, *after)


def spread_far_body(dense, total, f0, f1, m0, m1, *refs):
    *far_other, out = refs
    height = f0.shape[0]
    core, mate, _ = coordinates()

    def add_up(*cross):
        out[...] = sum_products(total[...], dense, 6 * height, (f0, f1, *cross)).astype(BF16)

    pl.when(core == mate)(lambda: add_up(*far_other))
    pl.when(core != mate)(lambda: add_up(m0, m1))


def spread_far(dense, total, far, mate_other, far_other):
    return pl.pallas_call(
        spread_far_body,
        out_shape=jax.ShapeDtypeStruct(total.shape, BF16),
        in_specs=[VMEM] * (6 + len(far_other)),
        out_specs=VMEM,
        compiler_params=params(),
        cost_estimate=cost(),
        name="spread_far",
    )(dense, total, *far, *mate_other, *far_other)


def pull_body(cot, dense, own, mate, far, swap_own, cross_0, cross_1):
    rows = dense.shape[0]
    turned = cot[...].T
    terms = [
        jnp.dot(
            turned, dense[:, index * rows : (index + 1) * rows], preferred_element_type=F32
        )
        for index in range(5)
    ]
    own[...], mate[...], far[...] = terms[0], terms[2], terms[3]
    swap_own[...] = terms[1].astype(BF16)
    half = cross_0.shape[1]
    cross_0[...], cross_1[...] = terms[4][:, :half].astype(BF16), terms[4][:, half:].astype(BF16)


def pull(cot, dense):
    rows, cols = cot.shape
    return pl.pallas_call(
        pull_body,
        out_shape=[jax.ShapeDtypeStruct((cols, rows), F32)] * 3
        + [jax.ShapeDtypeStruct((cols, rows), BF16)]
        + [jax.ShapeDtypeStruct((cols, rows // 2), BF16)] * 2,
        in_specs=[VMEM] * 2,
        out_specs=[VMEM] * 6,
        compiler_params=params(),
        cost_estimate=cost(),
        name="pull",
    )(cot, dense)


def swap_sum_body(mate_term, far_term, cross_0, cross_1, mate_0, mate_1, far_0, far_1):
    half = far_0.shape[1]
    core, mate, _ = coordinates()
    cross = jnp.concatenate([cross_0[...], cross_1[...]], axis=1).astype(F32)
    cross_mate = jnp.where(core == mate, cross, 0.0)
    far = (far_term[...] + (cross - cross_mate)).astype(BF16)
    near = mate_term[...] + cross_mate
    mate_0[...], mate_1[...] = near[:, :half], near[:, half:]
    far_0[...], far_1[...] = far[:, :half], far[:, half:]


def swap_sum(mate_term, far_term, cross):
    cols, rows = far_term.shape
    shape = (cols, rows // 2)
    out = pl.pallas_call(
        swap_sum_body,
        out_shape=[jax.ShapeDtypeStruct(shape, F32)] * 2
        + [jax.ShapeDtypeStruct(shape, BF16)] * 2,
        in_specs=[VMEM] * 4,
        out_specs=[VMEM] * 4,
        compiler_params=params(),
        cost_estimate=cost(),
        name="swap_sum",
    )(mate_term, far_term, *cross)
    return out[:2], out[2:]


def hidden_body(s0, s1, w_mine, w_near, w_far, w_out, *refs, number):
    pre, hid, mixed = refs[-3:]
    height, width = pre.shape
    span = slice(number * height, (number + 1) * height)
    core, _, panel = coordinates()

    def rows_of(side):
        return pl.ds(pl.multiple_of((panel ^ side) * width, width), width)

    def run(w_theirs):
        mine, theirs = 0.0, 0.0
        for side, ref in enumerate((s0, s1)):
            taken = ref[span, :]
            mine += jnp.dot(taken, w_mine[rows_of(side), :], preferred_element_type=F32)
            theirs += jnp.dot(taken, w_theirs[side][...], preferred_element_type=F32)
        pre[...] = mine
        hid[:, :width] = (mine * jax.nn.sigmoid(mine)).astype(BF16)
        hid[:, width:] = (theirs * jax.nn.sigmoid(theirs)).astype(BF16)

    pl.when(core == 0)(lambda: run((w_near, w_far)))
    pl.when(core == 1)(lambda: run((w_far, w_near)))
    result = 0.0
    for side in range(2):
        value = hid[:, side * width : (side + 1) * width]
        result += jnp.dot(value, w_out[rows_of(side), :], preferred_element_type=F32)
    mixed[...] = result.astype(BF16)


def hidden_step(number, pieces, w_mine, w_near, w_far, w_out, *after):
    rows, width = pieces[0].shape
    height = rows // 2
    return pl.pallas_call(
        functools.partial(hidden_body, number=number),
        out_shape=[
            jax.ShapeDtypeStruct((height, width), F32),
            jax.ShapeDtypeStruct((height, 2 * width), BF16),
            jax.ShapeDtypeStruct((height, width), BF16),
        ],
        in_specs=[VMEM] * 6 + [ANY] * len(after),
        out_specs=[VMEM] * 3,
        compiler_params=params(),
        cost_estimate=cost(),
        name="hidden",
    )(*pieces, w_mine, w_near, w_far, w_out, *after)


def mix_body(own, swap, come, w_out, *refs, number):
    pulled, keep, give = refs[-3:]
    height, half = keep.shape
    _, _, panel = coordinates()
    span = slice(number * height, (number + 1) * height)
    total = own[:, span] + swap[:, span].astype(F32) + come[...].astype(F32)
    pulled[...] = total.astype(BF16).T
    contract = (((1,), (1,)), ((), ()))
    theirs = w_out[pl.ds(pl.multiple_of((1 - panel) * half, half), half), :]
    give[...] = lax.dot_general(
        pulled[...], theirs, contract, preferred_element_type=F32
    ).astype(BF16)
    mine = w_out[pl.ds(pl.multiple_of(panel * half, half), half), :]
    keep[...] = lax.dot_general(pulled[...], mine, contract, preferred_element_type=F32)


def mix_step(number, own, swap, come, w_out, *after):
    cols, height = come.shape
    half = w_out.shape[0] // 2
    return pl.pallas_call(
        functools.partial(mix_body, number=number),
        out_shape=[
            jax.ShapeDtypeStruct((height, cols), BF16),
            jax.ShapeDtypeStruct((height, half), F32),
            jax.ShapeDtypeStruct((height, half), BF16),
        ],
        in_specs=[VMEM] * 4 + [ANY] * len(after),
        out_specs=[VMEM] * 3,
        compiler_params=params(),
        cost_estimate=cost(),
        name="mix_back",
    )(own, swap, come, w_out, *after)


def split_term(total, keep, give_near, give_far, scratch, blocks):
    core, mate, _ = coordinates()
    share = total.shape[0] // blocks
    groups = blocks // 4
    for group in range(groups):
        for side in range(2):
            owner = 4 * group + 2 * (mate ^ side)
            target = pl.ds((side * groups + group) * share, share)
            source = pl.multiple_of((owner + core) * share, share)
            keep[target, :] = total[pl.ds(source, share), :]
            source = pl.multiple_of((owner + 1 - core) * share, share)
            scratch[target, :] = total[pl.ds(source, share), :]
    half = give_near.shape[0]
    give_near[...] = scratch[:half].astype(BF16)
    give_far[...] = scratch[half:].astype(BF16)


def grad_into(total, pieces, rights):
    _, _, panel = coordinates()
    contract = (((0,), (0,)), ((), ()))
    width = rights[0].shape[1]
    half = width // 2
    for side, (refs, first) in enumerate(pieces):
        for number in range(2):
            start = (panel ^ side) * width + number * half
            source = first + number * half
            result = 0.0
            for index, right in enumerate(rights):
                height = right.shape[0]
                if len(refs) == 1:
                    taken = refs[0][index * height : (index + 1) * height, source : source + half]
                else:
                    taken = refs[index][:, source : source + half]
                result += lax.dot_general(
                    taken,
                    right[...],
                    contract,
                    preferred_element_type=F32,
                )
            total[pl.ds(pl.multiple_of(start, half), half), :] = result


def out_grad_body(hid_0, hid_1, pulled_0, pulled_1, *refs, blocks):
    keep, near, far, total, scratch = refs[-5:]
    width = pulled_0.shape[1]
    hid = (hid_0, hid_1)
    grad_into(total, ((hid, 0), (hid, width)), (pulled_0, pulled_1))
    split_term(total, keep, near, far, scratch, blocks)


def in_grad_body(*refs, blocks):
    own, theirs, *refs = refs
    pre, kept, come = [refs[2 * i : 2 * i + 2] for i in range(3)]
    keep, near, far, total, scratch, *back = refs[-7:]
    for half in range(2):
        pre_hidden = pre[half][...]
        gate = jax.nn.sigmoid(pre_hidden)
        back_hidden = kept[half][...] + come[half][...].astype(F32)
        slope = gate * (1.0 + pre_hidden * (1.0 - gate))
        back[half][...] = (back_hidden * slope).astype(BF16)
    grad_into(total, (((own,), 0), ((theirs,), 0)), back)
    split_term(total, keep, near, far, scratch, blocks)


def grad_call(body, name, operands, height, width, scratch=(), after=()):
    blocks = lax.axis_size("blk")
    half = height // 2
    return pl.pallas_call(
        functools.partial(body, blocks=blocks),
        out_shape=[
            jax.ShapeDtypeStruct((half, width), F32),
            jax.ShapeDtypeStruct((half // 2, width), BF16),
            jax.ShapeDtypeStruct((half // 2, width), BF16),
        ],
        in_specs=[VMEM] * len(operands) + [ANY] * len(after),
        out_specs=[VMEM] * 3,
        scratch_shapes=[
            pltpu.VMEM((height, width), F32),
            pltpu.VMEM((half, width), F32),
            *scratch,
        ],
        compiler_params=params(),
        cost_estimate=cost(),
        name=name,
    )(*operands, *after)


def far_sum_body(first, first_come, second, second_come, far):
    half = far.shape[0] // 2
    far[:half] = (first[half:] + first_come[...].astype(F32)).astype(BF16)
    far[half:] = (second[half:] + second_come[...].astype(F32)).astype(BF16)


def far_sum(first, first_come, second, second_come):
    return pl.pallas_call(
        far_sum_body,
        out_shape=jax.ShapeDtypeStruct(first.shape, BF16),
        in_specs=[VMEM] * 4,
        out_specs=VMEM,
        compiler_params=params(),
        cost_estimate=cost(),
        name="far_sum",
    )(first, first_come, second, second_come)


def mate_sum_body(first, first_core, second, second_core, come, *refs):
    own_first, own_second, *terms, sum_first, sum_second = refs
    share = own_first.shape[0]
    group = lax.axis_index("blk") // 4
    half = sum_first.shape[0]
    sum_first[...] = first[:half] + first_core[...].astype(F32) + come[:half].astype(F32)
    sum_second[...] = second[:half] + second_core[...].astype(F32) + come[half:].astype(F32)

    def rows_of(distance):
        start = pl.multiple_of((group ^ distance) * share, share)
        return sum_first[pl.ds(start, share), :], sum_second[pl.ds(start, share), :]

    own_first[...], own_second[...] = rows_of(0)
    for number, ref in enumerate(terms):
        ref[...] = jnp.concatenate(rows_of(number + 1), axis=0).astype(BF16)


def mate_sum(first, first_core, second, second_core, come):
    height, width = first_core.shape
    groups = lax.axis_size("blk") // 4
    share = height // groups
    own = jax.ShapeDtypeStruct((share, width), F32)
    term = jax.ShapeDtypeStruct((2 * share, width), BF16)
    own_first, own_second, *terms = pl.pallas_call(
        mate_sum_body,
        out_shape=[own] * 2 + [term] * (groups - 1),
        in_specs=[VMEM] * 5,
        out_specs=[VMEM] * (1 + groups),
        scratch_shapes=[pltpu.VMEM((height, width), F32)] * 2,
        compiler_params=params(),
        cost_estimate=cost(),
        name="mate_sum",
    )(first, first_core, second, second_core, come)
    return own_first, own_second, terms


def group_sum_body(own_first, own_second, *refs):
    *terms, out_first, out_second = refs
    share = own_first.shape[0]
    total_first, total_second = own_first[...], own_second[...]
    for ref in terms:
        term = ref[...].astype(F32)
        total_first += term[:share]
        total_second += term[share:]
    out_first[...] = total_first
    out_second[...] = total_second


def group_sum(own_first, own_second, terms):
    return pl.pallas_call(
        group_sum_body,
        out_shape=[jax.ShapeDtypeStruct(own_first.shape, F32)] * 2,
        in_specs=[VMEM] * (2 + len(terms)),
        out_specs=[VMEM] * 2,
        compiler_params=params(),
        cost_estimate=cost(),
        name="group_sum",
    )(own_first, own_second, *terms)


def shards(
    features, weight_in, weight_out, adj_tiles, tile_rows, tile_cols, tile_counts, cotangent
):
    rows, width = features.shape
    tile_rows, tile_cols = jnp.swapaxes(tile_rows, 0, 1), jnp.swapaxes(tile_cols, 0, 1)

    height = rows // 2

    f_mate = [to_mate(features[:height]), to_mate(features[height:])]
    f_other = to_core(features)
    f_mate_other = [to_core(half) for half in f_mate]
    f_far = [relay_out(half) for half in f_mate]
    w_near = to_panel(gate(pick(weight_in), f_mate[0]))
    w_far = to_core(w_near)

    dense = build(tile_rows, tile_cols, tile_counts, adj_tiles, rows)
    p_own, p_mate, p_far, p_swap, *p_cross = pull(cotangent, dense)
    p_mate, p_far = swap_sum(
        p_mate, p_far, [to_core(gate(half, f_mate[1])) for half in p_cross]
    )
    p_swap = to_core(p_swap)

    total = spread_near(dense, features, f_other, f_mate, p_far[0])
    f_far = [gate(half, total) for half in f_far]
    p_come = [relay_back(gate(far, *f_far)) for far in p_far]
    f_far_other = [to_core(half) for half in f_far]
    own = spread_far(dense, total, f_far, f_mate_other, f_far_other)
    theirs = to_panel(own)
    q_come = [
        to_mate((mine + come.astype(F32)).astype(BF16)) for mine, come in zip(p_mate, p_come)
    ]
    pre_hidden, hid, mixed = zip(
        *[
            hidden_step(number, (own, theirs), weight_in, w_near, w_far, weight_out, dense)
            for number in range(2)
        ]
    )

    t_mate = [to_mate(half) for half in mixed]
    t_own = jnp.concatenate(mixed, axis=0)
    t_other = to_core(t_own)
    t_mate_other = [to_core(half) for half in t_mate]
    t_far = [relay_out(half) for half in t_mate]
    t_far_other = [to_core(jnp.concatenate(t_far, axis=0))]

    pulled, kept, given = zip(
        *[
            mix_step(number, p_own, p_swap, come, weight_out, dense)
            for number, come in enumerate(q_come)
        ]
    )
    come = [to_panel(half) for half in given]
    out_keep, out_near, out_far = grad_call(
        out_grad_body, "out_grad", [*hid, *pulled], 2 * width, width
    )
    in_keep, in_near, in_far = grad_call(
        in_grad_body,
        "in_grad",
        [own, theirs, *pre_hidden, *kept, *come],
        2 * width,
        width,
        [pltpu.VMEM((height, width), BF16)] * 2,
        (dense, *[half[:8, :128] for half in t_mate]),
    )
    far = far_sum(out_keep, to_core(out_far), in_keep, to_core(in_far))
    out_own, in_own, terms = mate_sum(
        out_keep, to_core(out_near), in_keep, to_core(in_near), to_mate(far)
    )
    terms = [to_group(term, number + 1) for number, term in enumerate(terms)]

    total = spread_near(dense, t_own, t_other, t_mate)
    layer_output = spread_far(dense, total, t_far, t_mate_other, t_far_other)
    grad_weight_out, grad_weight_in = group_sum(out_own, in_own, terms)
    return (layer_output, grad_weight_in, grad_weight_out)


def solution(mesh):
    return jax.shard_map(
        shards,
        mesh=mesh,
        in_specs=(
            P("blk", "feat"),
            P(None, "feat"),
            P(None, "feat"),
            P("blk", None, None, None, None),
            P("blk", None, None),
            P("blk", None, None),
            P("blk", None),
            P("blk", "feat"),
        ),
        out_specs=(P("blk", "feat"), P("blk", "feat"), P("blk", "feat")),
        check_vma=False,
    )
```

```python
import functools

import jax
import jax.numpy as jnp
from jax import lax
from jax.experimental import pallas as pl
from jax.experimental.pallas import tpu as pltpu
from jax.sharding import PartitionSpec as P

BF16 = jnp.bfloat16
F32 = jnp.float32
VMEM = pl.BlockSpec(memory_space=pltpu.VMEM)
SMEM = pl.BlockSpec(memory_space=pltpu.SMEM)
ANY = pl.BlockSpec(memory_space=pl.ANY)


def params(limit_mib=12):
    return pltpu.CompilerParams(vmem_limit_bytes=limit_mib * 1024 * 1024)


def cost(microseconds=0):
    return pl.CostEstimate(
        flops=1024, bytes_accessed=1024 + 3_600_000 * microseconds, transcendentals=0
    )


def gate_body(*refs):
    del refs


def gate(value, *after, microseconds=0):
    return pl.pallas_call(
        gate_body,
        out_shape=jax.ShapeDtypeStruct(value.shape, value.dtype),
        in_specs=[ANY] * (1 + len(after)),
        out_specs=ANY,
        input_output_aliases={0: 0},
        compiler_params=params(1),
        cost_estimate=cost(microseconds),
        name="gate",
    )(value, *after)


def coordinates():
    block = lax.axis_index("blk")
    return block & 1, (block >> 1) & 1, lax.axis_index("feat")


def coordinates():
    block = lax.axis_index("blk")
    return block & 1, (block >> 1) & 1, lax.axis_index("feat")


def copy_all(pairs, semaphores):
    copies = [
        pltpu.make_async_copy(source, target, semaphores.at[number])
        for number, (source, target) in enumerate(pairs)
    ]
    for copy in copies:
        copy.start()
    for copy in copies:
        copy.wait()


def coordinates():
    block = lax.axis_index("blk")
    return block & 1, (block >> 1) & 1, lax.axis_index("feat")


def blk_pairs(target):
    count = lax.axis_size("blk")
    return [(source, target(source) % count) for source in range(count)]


def to_core(value):
    return lax.ppermute(value, "blk", blk_pairs(lambda b: b ^ 1))


def to_mate(value):
    return lax.ppermute(value, "blk", blk_pairs(lambda b: b ^ 2))


def to_far(value):
    return lax.ppermute(
        value, "blk", blk_pairs(lambda b: (b ^ 2) + 4 if b & 2 else (b ^ 2) - 4)
    )


def relay_out(value):
    return lax.ppermute(value, "blk", blk_pairs(lambda b: b - 4 if b & 2 else b + 4))


def relay_back(value):
    return lax.ppermute(value, "blk", blk_pairs(lambda b: b + 4 if b & 2 else b - 4))


def to_group(value, distance):
    return lax.ppermute(value, "blk", blk_pairs(lambda b: b ^ (4 * distance)))


def to_panel(value):
    return lax.ppermute(value, "feat", [(0, 1), (1, 0)])


def pick_body(w_in, send, semaphore):
    half = send.shape[0]
    core, _, panel = coordinates()
    start = pl.multiple_of(((1 - panel) ^ core) * half, half)
    copy = pltpu.make_async_copy(w_in.at[pl.ds(start, half), :], send, semaphore)
    copy.start()
    copy.wait()


def pick(w_in):
    width = w_in.shape[1]
    return pl.pallas_call(
        pick_body,
        out_shape=jax.ShapeDtypeStruct((width, width), BF16),
        in_specs=[ANY],
        out_specs=VMEM,
        scratch_shapes=[pltpu.SemaphoreType.DMA],
        compiler_params=params(4),
        cost_estimate=cost(),
        name="pick",
    )(w_in)


def build_body(rows, cols, counts, tiles, dense):
    _, steps, cap, tile, _ = tiles.shape
    radius = (steps - 1) // 2
    block_tiles = dense.shape[0] // tile
    core, mate, _ = coordinates()
    dense[...] = jnp.zeros_like(dense)

    def place(entry, carry):
        step, slot = entry // cap, entry % cap
        shifted = step - radius + core + 2
        chip = shifted // 2 - 1
        position = (shifted % 2) ^ core
        ahead = jnp.where(mate == 0, 1, -1)
        outside = jnp.where(position == 1, 4, jnp.where(chip == ahead, 2, 3))
        segment = jnp.where(chip == 0, position, outside)
        row = rows[step, 0, slot]
        col = segment * block_tiles + cols[step, 0, slot]

        @pl.when(slot < counts[0, step])
        def _():
            dense[
                pl.ds(pl.multiple_of(row * tile, tile), tile),
                pl.ds(pl.multiple_of(col * tile, tile), tile),
            ] = tiles[0, step, slot]

        return carry

    lax.fori_loop(0, steps * cap, place, 0)


def build(tile_rows, tile_cols, tile_counts, tiles, rows):
    return pl.pallas_call(
        build_body,
        out_shape=jax.ShapeDtypeStruct((rows, 5 * rows), BF16),
        in_specs=[SMEM] * 3 + [VMEM],
        out_specs=VMEM,
        compiler_params=params(),
        cost_estimate=cost(),
        name="build_dense",
    )(tile_rows, tile_cols, tile_counts, tiles)


def sum_products(result, dense, first, refs):
    for ref in refs:
        height = ref.shape[0]
        product = jnp.dot(
            dense[:, first : first + height], ref[...], preferred_element_type=F32
        )
        result = product if result is None else result + product
        first += height
    return result


def spread_near_body(dense, *refs, parts):
    refs[-1][...] = sum_products(None, dense, 0, refs[:parts])


def spread_near(dense, own, other, mate, *after):
    rows, cols = own.shape
    block = rows // 2
    parts = [own, other, *mate]
    return pl.pallas_call(
        functools.partial(spread_near_body, parts=len(parts)),
        grid=(2,),
        out_shape=jax.ShapeDtypeStruct((rows, cols), F32),
        in_specs=[pl.BlockSpec((block, 3 * rows), lambda i: (i, 0))]
        + [pl.BlockSpec(part.shape, lambda i: (0, 0)) for part in parts]
        + [ANY] * len(after),
        out_specs=pl.BlockSpec((block, cols), lambda i: (i, 0)),
        compiler_params=params(),
        cost_estimate=cost(),
        name="spread_near",
    )(dense, *parts, *after)


def spread_far_body(dense, total, *refs, counts):
    out = refs[-1]
    core, mate, _ = coordinates()
    far, mate_other = refs[: counts[0]], refs[counts[0] : counts[0] + counts[1]]
    far_other = refs[counts[0] + counts[1] : -1]
    first = 3 * dense.shape[0]

    def add_up(cross):
        out[...] = sum_products(total[...], dense, first, (*far, *cross)).astype(BF16)

    pl.when(core == mate)(lambda: add_up(far_other))
    pl.when(core != mate)(lambda: add_up(mate_other))


def spread_far(dense, total, far, mate_other, far_other):
    parts = [*far, *mate_other, *far_other]
    return pl.pallas_call(
        functools.partial(spread_far_body, counts=(len(far), len(mate_other))),
        out_shape=jax.ShapeDtypeStruct(total.shape, BF16),
        in_specs=[VMEM] * (2 + len(parts)),
        out_specs=VMEM,
        compiler_params=params(),
        cost_estimate=cost(),
        name="spread_far",
    )(dense, total, *parts)


def pull_body(cot, dense, own, mate, far, swap_own, cross_0, cross_1):
    rows = dense.shape[0]
    turned = cot[...].T
    terms = [
        jnp.dot(
            turned, dense[:, index * rows : (index + 1) * rows], preferred_element_type=F32
        )
        for index in range(5)
    ]
    own[...], mate[...], far[...] = terms[0], terms[2], terms[3]
    swap_own[...] = terms[1].astype(BF16)
    half = cross_0.shape[1]
    cross_0[...], cross_1[...] = terms[4][:, :half].astype(BF16), terms[4][:, half:].astype(BF16)


def pull(cot, dense):
    rows, cols = cot.shape
    return pl.pallas_call(
        pull_body,
        out_shape=[jax.ShapeDtypeStruct((cols, rows), F32)] * 3
        + [jax.ShapeDtypeStruct((cols, rows), BF16)]
        + [jax.ShapeDtypeStruct((cols, rows // 2), BF16)] * 2,
        in_specs=[VMEM] * 2,
        out_specs=[VMEM] * 6,
        compiler_params=params(),
        cost_estimate=cost(),
        name="pull",
    )(cot, dense)


def swap_sum_body(mate_term, far_term, cross_0, cross_1, mate_0, mate_1, far_0, far_1):
    half = far_0.shape[1]
    core, mate, _ = coordinates()
    cross = jnp.concatenate([cross_0[...], cross_1[...]], axis=1).astype(F32)
    cross_mate = jnp.where(core == mate, cross, 0.0)
    far = (far_term[...] + (cross - cross_mate)).astype(BF16)
    near = mate_term[...] + cross_mate
    mate_0[...], mate_1[...] = near[:, :half], near[:, half:]
    far_0[...], far_1[...] = far[:, :half], far[:, half:]


def swap_sum(mate_term, far_term, cross):
    cols, rows = far_term.shape
    shape = (cols, rows // 2)
    out = pl.pallas_call(
        swap_sum_body,
        out_shape=[jax.ShapeDtypeStruct(shape, F32)] * 2
        + [jax.ShapeDtypeStruct(shape, BF16)] * 2,
        in_specs=[VMEM] * 4,
        out_specs=[VMEM] * 4,
        compiler_params=params(),
        cost_estimate=cost(),
        name="swap_sum",
    )(mate_term, far_term, *cross)
    return out[:2], out[2:]


def hidden_body(s0, s1, w_mine, w_near, w_far, w_out, *refs, number):
    pre, hid, mixed = refs[-3:]
    height, width = pre.shape
    span = slice(number * height, (number + 1) * height)
    core, _, panel = coordinates()

    def rows_of(side):
        return pl.ds(pl.multiple_of((panel ^ side) * width, width), width)

    def run(w_theirs):
        mine, theirs = 0.0, 0.0
        for side, ref in enumerate((s0, s1)):
            taken = ref[span, :]
            mine += jnp.dot(taken, w_mine[rows_of(side), :], preferred_element_type=F32)
            theirs += jnp.dot(taken, w_theirs[side][...], preferred_element_type=F32)
        pre[...] = mine
        hid[:, :width] = (mine * jax.nn.sigmoid(mine)).astype(BF16)
        hid[:, width:] = (theirs * jax.nn.sigmoid(theirs)).astype(BF16)

    pl.when(core == 0)(lambda: run((w_near, w_far)))
    pl.when(core == 1)(lambda: run((w_far, w_near)))
    result = 0.0
    for side in range(2):
        value = hid[:, side * width : (side + 1) * width]
        result += jnp.dot(value, w_out[rows_of(side), :], preferred_element_type=F32)
    mixed[...] = result.astype(BF16)


def hidden_step(number, pieces, w_mine, w_near, w_far, w_out, *after):
    rows, width = pieces[0].shape
    height = rows // 2
    return pl.pallas_call(
        functools.partial(hidden_body, number=number),
        out_shape=[
            jax.ShapeDtypeStruct((height, width), F32),
            jax.ShapeDtypeStruct((height, 2 * width), BF16),
            jax.ShapeDtypeStruct((height, width), BF16),
        ],
        in_specs=[VMEM] * 6 + [ANY] * len(after),
        out_specs=[VMEM] * 3,
        compiler_params=params(),
        cost_estimate=cost(),
        name="hidden",
    )(*pieces, w_mine, w_near, w_far, w_out, *after)


def mix_body(own, swap, come, w_out, *refs, number):
    pulled, keep, give = refs[-3:]
    height, half = keep.shape
    _, _, panel = coordinates()
    span = slice(number * height, (number + 1) * height)
    total = own[:, span] + swap[:, span].astype(F32) + come[...].astype(F32)
    pulled[...] = total.astype(BF16).T
    contract = (((1,), (1,)), ((), ()))
    theirs = w_out[pl.ds(pl.multiple_of((1 - panel) * half, half), half), :]
    give[...] = lax.dot_general(
        pulled[...], theirs, contract, preferred_element_type=F32
    ).astype(BF16)
    mine = w_out[pl.ds(pl.multiple_of(panel * half, half), half), :]
    keep[...] = lax.dot_general(pulled[...], mine, contract, preferred_element_type=F32)


def mix_step(number, own, swap, come, w_out, *after):
    cols, height = come.shape
    half = w_out.shape[0] // 2
    return pl.pallas_call(
        functools.partial(mix_body, number=number),
        out_shape=[
            jax.ShapeDtypeStruct((height, cols), BF16),
            jax.ShapeDtypeStruct((height, half), F32),
            jax.ShapeDtypeStruct((height, half), BF16),
        ],
        in_specs=[VMEM] * 4 + [ANY] * len(after),
        out_specs=[VMEM] * 3,
        compiler_params=params(),
        cost_estimate=cost(),
        name="mix_back",
    )(own, swap, come, w_out, *after)


def split_term(total, keep, give_near, give_far, scratch, blocks):
    core, mate, _ = coordinates()
    share = total.shape[0] // blocks
    groups = blocks // 4
    for group in range(groups):
        for side in range(2):
            owner = 4 * group + 2 * (mate ^ side)
            target = pl.ds((side * groups + group) * share, share)
            source = pl.multiple_of((owner + core) * share, share)
            keep[target, :] = total[pl.ds(source, share), :]
            source = pl.multiple_of((owner + 1 - core) * share, share)
            scratch[target, :] = total[pl.ds(source, share), :]
    half = give_near.shape[0]
    give_near[...] = scratch[:half].astype(BF16)
    give_far[...] = scratch[half:].astype(BF16)


def grad_into(total, pieces, rights):
    _, _, panel = coordinates()
    contract = (((0,), (0,)), ((), ()))
    width = rights[0].shape[1]
    half = width // 2
    for side, (refs, first) in enumerate(pieces):
        for number in range(2):
            start = (panel ^ side) * width + number * half
            source = first + number * half
            result = 0.0
            for index, right in enumerate(rights):
                height = right.shape[0]
                if len(refs) == 1:
                    taken = refs[0][index * height : (index + 1) * height, source : source + half]
                else:
                    taken = refs[index][:, source : source + half]
                result += lax.dot_general(
                    taken,
                    right[...],
                    contract,
                    preferred_element_type=F32,
                )
            total[pl.ds(pl.multiple_of(start, half), half), :] = result


def out_grad_body(hid_0, hid_1, pulled_0, pulled_1, *refs, blocks):
    keep, near, far, total, scratch = refs[-5:]
    width = pulled_0.shape[1]
    hid = (hid_0, hid_1)
    grad_into(total, ((hid, 0), (hid, width)), (pulled_0, pulled_1))
    split_term(total, keep, near, far, scratch, blocks)


def in_grad_body(*refs, blocks):
    own, theirs, *refs = refs
    pre, kept, come = [refs[2 * i : 2 * i + 2] for i in range(3)]
    keep, near, far, total, scratch, *back = refs[-7:]
    for half in range(2):
        pre_hidden = pre[half][...]
        gate = jax.nn.sigmoid(pre_hidden)
        back_hidden = kept[half][...] + come[half][...].astype(F32)
        slope = gate * (1.0 + pre_hidden * (1.0 - gate))
        back[half][...] = (back_hidden * slope).astype(BF16)
    grad_into(total, (((own,), 0), ((theirs,), 0)), back)
    split_term(total, keep, near, far, scratch, blocks)


def grad_call(body, name, operands, height, width, scratch=(), after=()):
    blocks = lax.axis_size("blk")
    half = height // 2
    return pl.pallas_call(
        functools.partial(body, blocks=blocks),
        out_shape=[
            jax.ShapeDtypeStruct((half, width), F32),
            jax.ShapeDtypeStruct((half // 2, width), BF16),
            jax.ShapeDtypeStruct((half // 2, width), BF16),
        ],
        in_specs=[VMEM] * len(operands) + [ANY] * len(after),
        out_specs=[VMEM] * 3,
        scratch_shapes=[
            pltpu.VMEM((height, width), F32),
            pltpu.VMEM((half, width), F32),
            *scratch,
        ],
        compiler_params=params(),
        cost_estimate=cost(),
        name=name,
    )(*operands, *after)


def far_sum_body(first, first_come, second, second_come, far):
    half = far.shape[0] // 2
    far[:half] = (first[half:] + first_come[...].astype(F32)).astype(BF16)
    far[half:] = (second[half:] + second_come[...].astype(F32)).astype(BF16)


def far_sum(first, first_come, second, second_come):
    return pl.pallas_call(
        far_sum_body,
        out_shape=jax.ShapeDtypeStruct(first.shape, BF16),
        in_specs=[VMEM] * 4,
        out_specs=VMEM,
        compiler_params=params(),
        cost_estimate=cost(),
        name="far_sum",
    )(first, first_come, second, second_come)


def mate_sum_body(first, first_core, second, second_core, come, *refs):
    own_first, own_second, *terms, sum_first, sum_second = refs
    share = own_first.shape[0]
    group = lax.axis_index("blk") // 4
    half = sum_first.shape[0]
    sum_first[...] = first[:half] + first_core[...].astype(F32) + come[:half].astype(F32)
    sum_second[...] = second[:half] + second_core[...].astype(F32) + come[half:].astype(F32)

    def rows_of(distance):
        start = pl.multiple_of((group ^ distance) * share, share)
        return sum_first[pl.ds(start, share), :], sum_second[pl.ds(start, share), :]

    own_first[...], own_second[...] = rows_of(0)
    for number, ref in enumerate(terms):
        ref[...] = jnp.concatenate(rows_of(number + 1), axis=0).astype(BF16)


def mate_sum(first, first_core, second, second_core, come):
    height, width = first_core.shape
    groups = lax.axis_size("blk") // 4
    share = height // groups
    own = jax.ShapeDtypeStruct((share, width), F32)
    term = jax.ShapeDtypeStruct((2 * share, width), BF16)
    own_first, own_second, *terms = pl.pallas_call(
        mate_sum_body,
        out_shape=[own] * 2 + [term] * (groups - 1),
        in_specs=[VMEM] * 5,
        out_specs=[VMEM] * (1 + groups),
        scratch_shapes=[pltpu.VMEM((height, width), F32)] * 2,
        compiler_params=params(),
        cost_estimate=cost(),
        name="mate_sum",
    )(first, first_core, second, second_core, come)
    return own_first, own_second, terms


def group_sum_body(own_first, own_second, *refs):
    *terms, out_first, out_second = refs
    share = own_first.shape[0]
    total_first, total_second = own_first[...], own_second[...]
    for ref in terms:
        term = ref[...].astype(F32)
        total_first += term[:share]
        total_second += term[share:]
    out_first[...] = total_first
    out_second[...] = total_second


def group_sum(own_first, own_second, terms):
    return pl.pallas_call(
        group_sum_body,
        out_shape=[jax.ShapeDtypeStruct(own_first.shape, F32)] * 2,
        in_specs=[VMEM] * (2 + len(terms)),
        out_specs=[VMEM] * 2,
        compiler_params=params(),
        cost_estimate=cost(),
        name="group_sum",
    )(own_first, own_second, *terms)


def shards(
    features, weight_in, weight_out, adj_tiles, tile_rows, tile_cols, tile_counts, cotangent
):
    rows, width = features.shape
    tile_rows, tile_cols = jnp.swapaxes(tile_rows, 0, 1), jnp.swapaxes(tile_cols, 0, 1)

    height = rows // 2

    f_mate = to_mate(features)
    f_other = to_core(features)
    f_mate_other = to_core(f_mate)
    f_far = to_far(features)
    w_near = to_panel(pick(weight_in))
    w_far = to_core(w_near)

    dense = build(tile_rows, tile_cols, tile_counts, adj_tiles, rows)
    p_own, p_mate, p_far, p_swap, *p_cross = pull(cotangent, dense)
    p_mate, p_far = swap_sum(
        p_mate, p_far, [to_core(half) for half in p_cross]
    )
    p_swap = to_core(p_swap)

    total = spread_near(dense, features, f_other, [f_mate], p_far[0])
    f_far = gate(f_far, total)
    p_come = [relay_back(gate(far, f_far)) for far in p_far]
    f_far_other = [to_core(f_far[:height]), to_core(f_far[height:])]
    own = spread_far(dense, total, [f_far], [f_mate_other], f_far_other)
    theirs = to_panel(own)
    q_come = [
        to_mate((mine + come.astype(F32)).astype(BF16)) for mine, come in zip(p_mate, p_come)
    ]
    pre_hidden, hid, mixed = zip(
        *[
            hidden_step(number, (own, theirs), weight_in, w_near, w_far, weight_out, dense)
            for number in range(2)
        ]
    )

    t_mate = [to_mate(half) for half in mixed]
    t_own = jnp.concatenate(mixed, axis=0)
    t_other = to_core(t_own)
    t_mate_other = [to_core(half) for half in t_mate]
    t_far = [relay_out(half) for half in t_mate]
    t_far_other = [to_core(jnp.concatenate(t_far, axis=0))]

    pulled, kept, given = zip(
        *[
            mix_step(number, p_own, p_swap, come, weight_out, dense)
            for number, come in enumerate(q_come)
        ]
    )
    come = [to_panel(half) for half in given]
    out_keep, out_near, out_far = grad_call(
        out_grad_body, "out_grad", [*hid, *pulled], 2 * width, width
    )
    in_keep, in_near, in_far = grad_call(
        in_grad_body,
        "in_grad",
        [own, theirs, *pre_hidden, *kept, *come],
        2 * width,
        width,
        [pltpu.VMEM((height, width), BF16)] * 2,
        (dense, *[half[:8, :128] for half in t_mate]),
    )
    far = far_sum(out_keep, to_core(out_far), in_keep, to_core(in_far))
    out_own, in_own, terms = mate_sum(
        out_keep, to_core(out_near), in_keep, to_core(in_near), to_mate(far)
    )
    terms = [to_group(term, number + 1) for number, term in enumerate(terms)]

    total = spread_near(dense, t_own, t_other, t_mate)
    layer_output = spread_far(dense, total, t_far, t_mate_other, t_far_other)
    grad_weight_out, grad_weight_in = group_sum(out_own, in_own, terms)
    return (layer_output, grad_weight_in, grad_weight_out)


def solution(mesh):
    return jax.shard_map(
        shards,
        mesh=mesh,
        in_specs=(
            P("blk", "feat"),
            P(None, "feat"),
            P(None, "feat"),
            P("blk", None, None, None, None),
            P("blk", None, None),
            P("blk", None, None),
            P("blk", None),
            P("blk", "feat"),
        ),
        out_specs=(P("blk", "feat"), P("blk", "feat"), P("blk", "feat")),
        check_vma=False,
    )
```

```python
import functools

import jax
import jax.numpy as jnp
from jax import lax
from jax.experimental import pallas as pl
from jax.experimental.pallas import tpu as pltpu
from jax.sharding import PartitionSpec as P

BF16 = jnp.bfloat16
F32 = jnp.float32
VMEM = pl.BlockSpec(memory_space=pltpu.VMEM)
SMEM = pl.BlockSpec(memory_space=pltpu.SMEM)
ANY = pl.BlockSpec(memory_space=pl.ANY)


def params(limit_mib=12):
    return pltpu.CompilerParams(vmem_limit_bytes=limit_mib * 1024 * 1024)


def cost(microseconds=0):
    return pl.CostEstimate(
        flops=1024, bytes_accessed=1024 + 3_600_000 * microseconds, transcendentals=0
    )


def gate_body(*refs):
    del refs


def gate(value, *after, microseconds=0):
    return pl.pallas_call(
        gate_body,
        out_shape=jax.ShapeDtypeStruct(value.shape, value.dtype),
        in_specs=[ANY] * (1 + len(after)),
        out_specs=ANY,
        input_output_aliases={0: 0},
        compiler_params=params(1),
        cost_estimate=cost(microseconds),
        name="gate",
    )(value, *after)


def coordinates():
    block = lax.axis_index("blk")
    return block & 1, (block >> 1) & 1, lax.axis_index("feat")


def coordinates():
    block = lax.axis_index("blk")
    return block & 1, (block >> 1) & 1, lax.axis_index("feat")


def copy_all(pairs, semaphores):
    copies = [
        pltpu.make_async_copy(source, target, semaphores.at[number])
        for number, (source, target) in enumerate(pairs)
    ]
    for copy in copies:
        copy.start()
    for copy in copies:
        copy.wait()


def coordinates():
    block = lax.axis_index("blk")
    return block & 1, (block >> 1) & 1, lax.axis_index("feat")


def blk_pairs(target):
    count = lax.axis_size("blk")
    return [(source, target(source) % count) for source in range(count)]


def to_core(value):
    return lax.ppermute(value, "blk", blk_pairs(lambda b: b ^ 1))


def to_mate(value):
    return lax.ppermute(value, "blk", blk_pairs(lambda b: b ^ 2))


def relay_out(value):
    return lax.ppermute(value, "blk", blk_pairs(lambda b: b - 4 if b & 2 else b + 4))


def relay_back(value):
    return lax.ppermute(value, "blk", blk_pairs(lambda b: b + 4 if b & 2 else b - 4))


def to_group(value, distance):
    return lax.ppermute(value, "blk", blk_pairs(lambda b: b ^ (4 * distance)))


def to_panel(value):
    return lax.ppermute(value, "feat", [(0, 1), (1, 0)])


def pick_body(w_in, send, semaphore):
    half = send.shape[0]
    core, _, panel = coordinates()
    start = pl.multiple_of(((1 - panel) ^ core) * half, half)
    copy = pltpu.make_async_copy(w_in.at[pl.ds(start, half), :], send, semaphore)
    copy.start()
    copy.wait()


def pick(w_in):
    width = w_in.shape[1]
    return pl.pallas_call(
        pick_body,
        out_shape=jax.ShapeDtypeStruct((width, width), BF16),
        in_specs=[ANY],
        out_specs=VMEM,
        scratch_shapes=[pltpu.SemaphoreType.DMA],
        compiler_params=params(4),
        cost_estimate=cost(),
        name="pick",
    )(w_in)


def build_body(codes, tiles, dense):
    _, steps, cap, tile, _ = tiles.shape
    radius = (steps - 1) // 2
    block_tiles = dense.shape[0] // tile
    core, mate, _ = coordinates()
    dense[...] = jnp.zeros_like(dense)

    def place(entry, carry):
        step, slot = entry // cap, entry % cap
        shifted = step - radius + core + 2
        chip = shifted // 2 - 1
        position = (shifted % 2) ^ core
        ahead = jnp.where(mate == 0, 1, -1)
        outside = jnp.where(position == 1, 4, jnp.where(chip == ahead, 2, 3))
        segment = jnp.where(chip == 0, position, outside)
        code = codes[step, 0, slot]
        row = code // block_tiles
        col = segment * block_tiles + code % block_tiles

        @pl.when(code >= 0)
        def _():
            dense[
                pl.ds(pl.multiple_of(row * tile, tile), tile),
                pl.ds(pl.multiple_of(col * tile, tile), tile),
            ] = tiles[0, step, slot]

        return carry

    lax.fori_loop(0, steps * cap, place, 0)


def build(codes, tiles, rows):
    return pl.pallas_call(
        build_body,
        out_shape=jax.ShapeDtypeStruct((rows, 5 * rows), BF16),
        in_specs=[SMEM, VMEM],
        out_specs=VMEM,
        compiler_params=params(),
        cost_estimate=cost(),
        name="build_dense",
    )(codes, tiles)


def sum_products(result, dense, first, refs):
    for ref in refs:
        height = ref.shape[0]
        product = jnp.dot(
            dense[:, first : first + height], ref[...], preferred_element_type=F32
        )
        result = product if result is None else result + product
        first += height
    return result


def spread_near_body(dense, s0, s1, s2, s3, *refs):
    refs[-1][...] = sum_products(None, dense, 0, (s0, s1, s2, s3))


def spread_near(dense, own, other, mate, *after):
    rows, cols = own.shape
    block = rows // 2
    whole = pl.BlockSpec((rows, cols), lambda i: (0, 0))
    half = pl.BlockSpec((block, cols), lambda i: (0, 0))
    return pl.pallas_call(
        spread_near_body,
        grid=(2,),
        out_shape=jax.ShapeDtypeStruct((rows, cols), F32),
        in_specs=[
            pl.BlockSpec((block, 3 * rows), lambda i: (i, 0)),
            whole,
            whole,
            half,
            half,
            *[ANY] * len(after),
        ],
        out_specs=pl.BlockSpec((block, cols), lambda i: (i, 0)),
        compiler_params=params(),
        cost_estimate=cost(),
        name="spread_near",
    )(dense, own, other, *mate, *after)


def spread_far_body(dense, total, f0, f1, m0, m1, *refs):
    *far_other, out = refs
    height = f0.shape[0]
    core, mate, _ = coordinates()

    def add_up(*cross):
        out[...] = sum_products(total[...], dense, 6 * height, (f0, f1, *cross)).astype(BF16)

    pl.when(core == mate)(lambda: add_up(*far_other))
    pl.when(core != mate)(lambda: add_up(m0, m1))


def spread_far(dense, total, far, mate_other, far_other):
    return pl.pallas_call(
        spread_far_body,
        out_shape=jax.ShapeDtypeStruct(total.shape, BF16),
        in_specs=[VMEM] * (6 + len(far_other)),
        out_specs=VMEM,
        compiler_params=params(),
        cost_estimate=cost(),
        name="spread_far",
    )(dense, total, *far, *mate_other, *far_other)


def pull_body(cot, dense, own, mate, far, swap_own, cross_0, cross_1):
    rows = dense.shape[0]
    turned = cot[...].T
    terms = [
        jnp.dot(
            turned, dense[:, index * rows : (index + 1) * rows], preferred_element_type=F32
        )
        for index in range(5)
    ]
    own[...], mate[...], far[...] = terms[0], terms[2], terms[3]
    swap_own[...] = terms[1].astype(BF16)
    half = cross_0.shape[1]
    cross_0[...], cross_1[...] = terms[4][:, :half].astype(BF16), terms[4][:, half:].astype(BF16)


def pull(cot, dense):
    rows, cols = cot.shape
    return pl.pallas_call(
        pull_body,
        out_shape=[jax.ShapeDtypeStruct((cols, rows), F32)] * 3
        + [jax.ShapeDtypeStruct((cols, rows), BF16)]
        + [jax.ShapeDtypeStruct((cols, rows // 2), BF16)] * 2,
        in_specs=[VMEM] * 2,
        out_specs=[VMEM] * 6,
        compiler_params=params(),
        cost_estimate=cost(),
        name="pull",
    )(cot, dense)


def swap_sum_body(mate_term, far_term, cross_0, cross_1, mate_0, mate_1, far_0, far_1):
    half = far_0.shape[1]
    core, mate, _ = coordinates()
    cross = jnp.concatenate([cross_0[...], cross_1[...]], axis=1).astype(F32)
    cross_mate = jnp.where(core == mate, cross, 0.0)
    far = (far_term[...] + (cross - cross_mate)).astype(BF16)
    near = mate_term[...] + cross_mate
    mate_0[...], mate_1[...] = near[:, :half], near[:, half:]
    far_0[...], far_1[...] = far[:, :half], far[:, half:]


def swap_sum(mate_term, far_term, cross):
    cols, rows = far_term.shape
    shape = (cols, rows // 2)
    out = pl.pallas_call(
        swap_sum_body,
        out_shape=[jax.ShapeDtypeStruct(shape, F32)] * 2
        + [jax.ShapeDtypeStruct(shape, BF16)] * 2,
        in_specs=[VMEM] * 4,
        out_specs=[VMEM] * 4,
        compiler_params=params(),
        cost_estimate=cost(),
        name="swap_sum",
    )(mate_term, far_term, *cross)
    return out[:2], out[2:]


def hidden_body(s0, s1, w_mine, w_near, w_far, w_out, *refs, number):
    pre, hid, mixed = refs[-3:]
    height, width = pre.shape
    span = slice(number * height, (number + 1) * height)
    core, _, panel = coordinates()

    def rows_of(side):
        return pl.ds(pl.multiple_of((panel ^ side) * width, width), width)

    def run(w_theirs):
        mine, theirs = 0.0, 0.0
        for side, ref in enumerate((s0, s1)):
            taken = ref[span, :]
            mine += jnp.dot(taken, w_mine[rows_of(side), :], preferred_element_type=F32)
            theirs += jnp.dot(taken, w_theirs[side][...], preferred_element_type=F32)
        pre[...] = mine
        hid[:, :width] = (mine * jax.nn.sigmoid(mine)).astype(BF16)
        hid[:, width:] = (theirs * jax.nn.sigmoid(theirs)).astype(BF16)

    pl.when(core == 0)(lambda: run((w_near, w_far)))
    pl.when(core == 1)(lambda: run((w_far, w_near)))
    result = 0.0
    for side in range(2):
        value = hid[:, side * width : (side + 1) * width]
        result += jnp.dot(value, w_out[rows_of(side), :], preferred_element_type=F32)
    mixed[...] = result.astype(BF16)


def hidden_step(number, pieces, w_mine, w_near, w_far, w_out, *after):
    rows, width = pieces[0].shape
    height = rows // 2
    return pl.pallas_call(
        functools.partial(hidden_body, number=number),
        out_shape=[
            jax.ShapeDtypeStruct((height, width), F32),
            jax.ShapeDtypeStruct((height, 2 * width), BF16),
            jax.ShapeDtypeStruct((height, width), BF16),
        ],
        in_specs=[VMEM] * 6 + [ANY] * len(after),
        out_specs=[VMEM] * 3,
        compiler_params=params(),
        cost_estimate=cost(),
        name="hidden",
    )(*pieces, w_mine, w_near, w_far, w_out, *after)


def mix_body(own, swap, come, w_out, *refs, number):
    pulled, keep, give = refs[-3:]
    height, half = keep.shape
    _, _, panel = coordinates()
    span = slice(number * height, (number + 1) * height)
    total = own[:, span] + swap[:, span].astype(F32) + come[...].astype(F32)
    pulled[...] = total.astype(BF16).T
    contract = (((1,), (1,)), ((), ()))
    theirs = w_out[pl.ds(pl.multiple_of((1 - panel) * half, half), half), :]
    give[...] = lax.dot_general(
        pulled[...], theirs, contract, preferred_element_type=F32
    ).astype(BF16)
    mine = w_out[pl.ds(pl.multiple_of(panel * half, half), half), :]
    keep[...] = lax.dot_general(pulled[...], mine, contract, preferred_element_type=F32)


def mix_step(number, own, swap, come, w_out, *after):
    cols, height = come.shape
    half = w_out.shape[0] // 2
    return pl.pallas_call(
        functools.partial(mix_body, number=number),
        out_shape=[
            jax.ShapeDtypeStruct((height, cols), BF16),
            jax.ShapeDtypeStruct((height, half), F32),
            jax.ShapeDtypeStruct((height, half), BF16),
        ],
        in_specs=[VMEM] * 4 + [ANY] * len(after),
        out_specs=[VMEM] * 3,
        compiler_params=params(),
        cost_estimate=cost(),
        name="mix_back",
    )(own, swap, come, w_out, *after)


def split_term(total, keep, give_near, give_far, scratch, blocks):
    core, mate, _ = coordinates()
    share = total.shape[0] // blocks
    groups = blocks // 4
    for group in range(groups):
        for side in range(2):
            owner = 4 * group + 2 * (mate ^ side)
            target = pl.ds((side * groups + group) * share, share)
            source = pl.multiple_of((owner + core) * share, share)
            keep[target, :] = total[pl.ds(source, share), :]
            source = pl.multiple_of((owner + 1 - core) * share, share)
            scratch[target, :] = total[pl.ds(source, share), :]
    half = give_near.shape[0]
    give_near[...] = scratch[:half].astype(BF16)
    give_far[...] = scratch[half:].astype(BF16)


def grad_into(total, pieces, rights):
    _, _, panel = coordinates()
    contract = (((0,), (0,)), ((), ()))
    width = rights[0].shape[1]
    half = width // 2
    for side, (refs, first) in enumerate(pieces):
        for number in range(2):
            start = (panel ^ side) * width + number * half
            source = first + number * half
            result = 0.0
            for index, right in enumerate(rights):
                height = right.shape[0]
                if len(refs) == 1:
                    taken = refs[0][index * height : (index + 1) * height, source : source + half]
                else:
                    taken = refs[index][:, source : source + half]
                result += lax.dot_general(
                    taken,
                    right[...],
                    contract,
                    preferred_element_type=F32,
                )
            total[pl.ds(pl.multiple_of(start, half), half), :] = result


def out_grad_body(hid_0, hid_1, pulled_0, pulled_1, *refs, blocks):
    keep, near, far, total, scratch = refs[-5:]
    width = pulled_0.shape[1]
    hid = (hid_0, hid_1)
    grad_into(total, ((hid, 0), (hid, width)), (pulled_0, pulled_1))
    split_term(total, keep, near, far, scratch, blocks)


def in_grad_body(*refs, blocks):
    own, theirs, *refs = refs
    pre, kept, come = [refs[2 * i : 2 * i + 2] for i in range(3)]
    keep, near, far, total, scratch, *back = refs[-7:]
    for half in range(2):
        pre_hidden = pre[half][...]
        gate = jax.nn.sigmoid(pre_hidden)
        back_hidden = kept[half][...] + come[half][...].astype(F32)
        slope = gate * (1.0 + pre_hidden * (1.0 - gate))
        back[half][...] = (back_hidden * slope).astype(BF16)
    grad_into(total, (((own,), 0), ((theirs,), 0)), back)
    split_term(total, keep, near, far, scratch, blocks)


def grad_call(body, name, operands, height, width, scratch=(), after=()):
    blocks = lax.axis_size("blk")
    half = height // 2
    return pl.pallas_call(
        functools.partial(body, blocks=blocks),
        out_shape=[
            jax.ShapeDtypeStruct((half, width), F32),
            jax.ShapeDtypeStruct((half // 2, width), BF16),
            jax.ShapeDtypeStruct((half // 2, width), BF16),
        ],
        in_specs=[VMEM] * len(operands) + [ANY] * len(after),
        out_specs=[VMEM] * 3,
        scratch_shapes=[
            pltpu.VMEM((height, width), F32),
            pltpu.VMEM((half, width), F32),
            *scratch,
        ],
        compiler_params=params(),
        cost_estimate=cost(),
        name=name,
    )(*operands, *after)


def far_sum_body(first, first_come, second, second_come, far):
    half = far.shape[0] // 2
    far[:half] = (first[half:] + first_come[...].astype(F32)).astype(BF16)
    far[half:] = (second[half:] + second_come[...].astype(F32)).astype(BF16)


def far_sum(first, first_come, second, second_come):
    return pl.pallas_call(
        far_sum_body,
        out_shape=jax.ShapeDtypeStruct(first.shape, BF16),
        in_specs=[VMEM] * 4,
        out_specs=VMEM,
        compiler_params=params(),
        cost_estimate=cost(),
        name="far_sum",
    )(first, first_come, second, second_come)


def mate_sum_body(first, first_core, second, second_core, come, *refs):
    own_first, own_second, *terms, sum_first, sum_second = refs
    share = own_first.shape[0]
    group = lax.axis_index("blk") // 4
    half = sum_first.shape[0]
    sum_first[...] = first[:half] + first_core[...].astype(F32) + come[:half].astype(F32)
    sum_second[...] = second[:half] + second_core[...].astype(F32) + come[half:].astype(F32)

    def rows_of(distance):
        start = pl.multiple_of((group ^ distance) * share, share)
        return sum_first[pl.ds(start, share), :], sum_second[pl.ds(start, share), :]

    own_first[...], own_second[...] = rows_of(0)
    for number, ref in enumerate(terms):
        ref[...] = jnp.concatenate(rows_of(number + 1), axis=0).astype(BF16)


def mate_sum(first, first_core, second, second_core, come):
    height, width = first_core.shape
    groups = lax.axis_size("blk") // 4
    share = height // groups
    own = jax.ShapeDtypeStruct((share, width), F32)
    term = jax.ShapeDtypeStruct((2 * share, width), BF16)
    own_first, own_second, *terms = pl.pallas_call(
        mate_sum_body,
        out_shape=[own] * 2 + [term] * (groups - 1),
        in_specs=[VMEM] * 5,
        out_specs=[VMEM] * (1 + groups),
        scratch_shapes=[pltpu.VMEM((height, width), F32)] * 2,
        compiler_params=params(),
        cost_estimate=cost(),
        name="mate_sum",
    )(first, first_core, second, second_core, come)
    return own_first, own_second, terms


def group_sum_body(own_first, own_second, *refs):
    *terms, out_first, out_second = refs
    share = own_first.shape[0]
    total_first, total_second = own_first[...], own_second[...]
    for ref in terms:
        term = ref[...].astype(F32)
        total_first += term[:share]
        total_second += term[share:]
    out_first[...] = total_first
    out_second[...] = total_second


def group_sum(own_first, own_second, terms):
    return pl.pallas_call(
        group_sum_body,
        out_shape=[jax.ShapeDtypeStruct(own_first.shape, F32)] * 2,
        in_specs=[VMEM] * (2 + len(terms)),
        out_specs=[VMEM] * 2,
        compiler_params=params(),
        cost_estimate=cost(),
        name="group_sum",
    )(own_first, own_second, *terms)


def shards(
    features, weight_in, weight_out, adj_tiles, tile_rows, tile_cols, tile_counts, cotangent
):
    rows, width = features.shape
    tile_rows, tile_cols = jnp.swapaxes(tile_rows, 0, 1), jnp.swapaxes(tile_cols, 0, 1)
    slots = lax.broadcasted_iota(jnp.int32, tile_rows.shape, 2)
    codes = jnp.where(
        slots < tile_counts[0][:, None, None],
        tile_rows * (rows // adj_tiles.shape[-1]) + tile_cols,
        -1,
    )

    height = rows // 2

    f_mate = [to_mate(features[:height]), to_mate(features[height:])]
    f_other = to_core(features)
    f_mate_other = [to_core(half) for half in f_mate]
    f_far = [relay_out(half) for half in f_mate]
    w_near = to_panel(gate(pick(weight_in), f_mate[0]))
    w_far = to_core(w_near)

    dense = build(codes, adj_tiles, rows)
    p_own, p_mate, p_far, p_swap, *p_cross = pull(cotangent, dense)
    p_mate, p_far = swap_sum(
        p_mate, p_far, [to_core(gate(half, f_mate[1])) for half in p_cross]
    )
    p_swap = to_core(p_swap)

    total = spread_near(dense, features, f_other, f_mate, p_far[0])
    f_far = [gate(half, total) for half in f_far]
    p_come = [relay_back(gate(far, *f_far)) for far in p_far]
    f_far_other = [to_core(half) for half in f_far]
    own = spread_far(dense, total, f_far, f_mate_other, f_far_other)
    theirs = to_panel(own)
    q_come = [
        to_mate((mine + come.astype(F32)).astype(BF16)) for mine, come in zip(p_mate, p_come)
    ]
    pre_hidden, hid, mixed = zip(
        *[
            hidden_step(number, (own, theirs), weight_in, w_near, w_far, weight_out, dense)
            for number in range(2)
        ]
    )

    t_mate = [to_mate(half) for half in mixed]
    t_own = jnp.concatenate(mixed, axis=0)
    t_other = to_core(t_own)
    t_mate_other = [to_core(half) for half in t_mate]
    t_far = [relay_out(half) for half in t_mate]
    t_far_other = [to_core(jnp.concatenate(t_far, axis=0))]

    pulled, kept, given = zip(
        *[
            mix_step(number, p_own, p_swap, come, weight_out, dense)
            for number, come in enumerate(q_come)
        ]
    )
    come = [to_panel(half) for half in given]
    out_keep, out_near, out_far = grad_call(
        out_grad_body, "out_grad", [*hid, *pulled], 2 * width, width
    )
    in_keep, in_near, in_far = grad_call(
        in_grad_body,
        "in_grad",
        [own, theirs, *pre_hidden, *kept, *come],
        2 * width,
        width,
        [pltpu.VMEM((height, width), BF16)] * 2,
        (dense, *[half[:8, :128] for half in t_mate]),
    )
    far = far_sum(out_keep, to_core(out_far), in_keep, to_core(in_far))
    out_own, in_own, terms = mate_sum(
        out_keep, to_core(out_near), in_keep, to_core(in_near), to_mate(far)
    )
    terms = [to_group(term, number + 1) for number, term in enumerate(terms)]

    total = spread_near(dense, t_own, t_other, t_mate)
    layer_output = spread_far(dense, total, t_far, t_mate_other, t_far_other)
    grad_weight_out, grad_weight_in = group_sum(out_own, in_own, terms)
    return (layer_output, grad_weight_in, grad_weight_out)


def solution(mesh):
    return jax.shard_map(
        shards,
        mesh=mesh,
        in_specs=(
            P("blk", "feat"),
            P(None, "feat"),
            P(None, "feat"),
            P("blk", None, None, None, None),
            P("blk", None, None),
            P("blk", None, None),
            P("blk", None),
            P("blk", "feat"),
        ),
        out_specs=(P("blk", "feat"), P("blk", "feat"), P("blk", "feat")),
        check_vma=False,
    )
```

```python
import functools

import jax
import jax.numpy as jnp
from jax import lax
from jax.experimental import pallas as pl
from jax.experimental.pallas import tpu as pltpu
from jax.sharding import PartitionSpec as P

BF16 = jnp.bfloat16
F32 = jnp.float32
VMEM = pl.BlockSpec(memory_space=pltpu.VMEM)
SMEM = pl.BlockSpec(memory_space=pltpu.SMEM)
ANY = pl.BlockSpec(memory_space=pl.ANY)


def params(limit_mib=12):
    return pltpu.CompilerParams(vmem_limit_bytes=limit_mib * 1024 * 1024)


def cost(microseconds=0):
    return pl.CostEstimate(
        flops=1024, bytes_accessed=1024 + 3_600_000 * microseconds, transcendentals=0
    )


def gate_body(*refs):
    del refs


def gate(value, *after, microseconds=0):
    return pl.pallas_call(
        gate_body,
        out_shape=jax.ShapeDtypeStruct(value.shape, value.dtype),
        in_specs=[ANY] * (1 + len(after)),
        out_specs=ANY,
        input_output_aliases={0: 0},
        compiler_params=params(1),
        cost_estimate=cost(microseconds),
        name="gate",
    )(value, *after)


def coordinates():
    block = lax.axis_index("blk")
    return block & 1, (block >> 1) & 1, lax.axis_index("feat")


def coordinates():
    block = lax.axis_index("blk")
    return block & 1, (block >> 1) & 1, lax.axis_index("feat")


def copy_all(pairs, semaphores):
    copies = [
        pltpu.make_async_copy(source, target, semaphores.at[number])
        for number, (source, target) in enumerate(pairs)
    ]
    for copy in copies:
        copy.start()
    for copy in copies:
        copy.wait()


def coordinates():
    block = lax.axis_index("blk")
    return block & 1, (block >> 1) & 1, lax.axis_index("feat")


def blk_pairs(target):
    count = lax.axis_size("blk")
    return [(source, target(source) % count) for source in range(count)]


def to_core(value):
    return lax.ppermute(value, "blk", blk_pairs(lambda b: b ^ 1))


def to_mate(value):
    return lax.ppermute(value, "blk", blk_pairs(lambda b: b ^ 2))


def relay_out(value):
    return lax.ppermute(value, "blk", blk_pairs(lambda b: b - 4 if b & 2 else b + 4))


def relay_back(value):
    return lax.ppermute(value, "blk", blk_pairs(lambda b: b + 4 if b & 2 else b - 4))


def to_group(value, distance):
    return lax.ppermute(value, "blk", blk_pairs(lambda b: b ^ (4 * distance)))


def to_panel(value):
    return lax.ppermute(value, "feat", [(0, 1), (1, 0)])


def pick_body(w_in, send, semaphore):
    half = send.shape[0]
    core, _, panel = coordinates()
    start = pl.multiple_of(((1 - panel) ^ core) * half, half)
    copy = pltpu.make_async_copy(w_in.at[pl.ds(start, half), :], send, semaphore)
    copy.start()
    copy.wait()


def pick(w_in):
    width = w_in.shape[1]
    return pl.pallas_call(
        pick_body,
        out_shape=jax.ShapeDtypeStruct((width, width), BF16),
        in_specs=[ANY],
        out_specs=VMEM,
        scratch_shapes=[pltpu.SemaphoreType.DMA],
        compiler_params=params(4),
        cost_estimate=cost(),
        name="pick",
    )(w_in)


def build_body(codes, tiles, dense):
    _, steps, cap, tile, _ = tiles.shape
    radius = (steps - 1) // 2
    block_tiles = dense.shape[0] // tile
    core, mate, _ = coordinates()
    dense[...] = jnp.zeros_like(dense)

    def place(entry, carry):
        step, slot = entry // cap, entry % cap
        shifted = step - radius + core + 2
        chip = shifted // 2 - 1
        position = (shifted % 2) ^ core
        ahead = jnp.where(mate == 0, 1, -1)
        outside = jnp.where(position == 1, 4, jnp.where(chip == ahead, 2, 3))
        segment = jnp.where(chip == 0, position, outside)
        code = codes[step, 0, slot]
        row = code // block_tiles
        col = segment * block_tiles + code % block_tiles

        @pl.when(code >= 0)
        def _():
            dense[
                pl.ds(pl.multiple_of(row * tile, tile), tile),
                pl.ds(pl.multiple_of(col * tile, tile), tile),
            ] = tiles[0, step, slot]

        return carry

    lax.fori_loop(0, steps * cap, place, 0)


def build(codes, tiles, rows):
    return pl.pallas_call(
        build_body,
        out_shape=jax.ShapeDtypeStruct((rows, 5 * rows), BF16),
        in_specs=[SMEM, VMEM],
        out_specs=VMEM,
        compiler_params=params(),
        cost_estimate=cost(),
        name="build_dense",
    )(codes, tiles)


def sum_products(result, dense, first, refs):
    for ref in refs:
        height = ref.shape[0]
        product = jnp.dot(
            dense[:, first : first + height], ref[...], preferred_element_type=F32
        )
        result = product if result is None else result + product
        first += height
    return result


def spread_near_body(dense, s0, s1, s2, s3, *refs):
    refs[-1][...] = sum_products(None, dense, 0, (s0, s1, s2, s3))


def spread_near(dense, own, other, mate, *after):
    rows, cols = own.shape
    block = rows // 2
    whole = pl.BlockSpec((rows, cols), lambda i: (0, 0))
    half = pl.BlockSpec((block, cols), lambda i: (0, 0))
    return pl.pallas_call(
        spread_near_body,
        grid=(2,),
        out_shape=jax.ShapeDtypeStruct((rows, cols), F32),
        in_specs=[
            pl.BlockSpec((block, 3 * rows), lambda i: (i, 0)),
            whole,
            whole,
            half,
            half,
            *[ANY] * len(after),
        ],
        out_specs=pl.BlockSpec((block, cols), lambda i: (i, 0)),
        compiler_params=params(),
        cost_estimate=cost(),
        name="spread_near",
    )(dense, own, other, *mate, *after)


def spread_far_body(dense, total, f0, f1, m0, m1, *refs):
    *far_other, out = refs
    height = f0.shape[0]
    core, mate, _ = coordinates()

    def add_up(*cross):
        out[...] = sum_products(total[...], dense, 6 * height, (f0, f1, *cross)).astype(BF16)

    pl.when(core == mate)(lambda: add_up(*far_other))
    pl.when(core != mate)(lambda: add_up(m0, m1))


def spread_far(dense, total, far, mate_other, far_other):
    return pl.pallas_call(
        spread_far_body,
        out_shape=jax.ShapeDtypeStruct(total.shape, BF16),
        in_specs=[VMEM] * (6 + len(far_other)),
        out_specs=VMEM,
        compiler_params=params(),
        cost_estimate=cost(),
        name="spread_far",
    )(dense, total, *far, *mate_other, *far_other)


def pull_body(cot, dense, own, mate, far, swap_own, cross_0, cross_1):
    rows = dense.shape[0]
    turned = cot[...].T
    terms = [
        jnp.dot(
            turned, dense[:, index * rows : (index + 1) * rows], preferred_element_type=F32
        )
        for index in range(5)
    ]
    own[...], mate[...], far[...] = terms[0], terms[2], terms[3]
    swap_own[...] = terms[1].astype(BF16)
    half = cross_0.shape[1]
    cross_0[...], cross_1[...] = terms[4][:, :half].astype(BF16), terms[4][:, half:].astype(BF16)


def pull(cot, dense):
    rows, cols = cot.shape
    return pl.pallas_call(
        pull_body,
        out_shape=[jax.ShapeDtypeStruct((cols, rows), F32)] * 3
        + [jax.ShapeDtypeStruct((cols, rows), BF16)]
        + [jax.ShapeDtypeStruct((cols, rows // 2), BF16)] * 2,
        in_specs=[VMEM] * 2,
        out_specs=[VMEM] * 6,
        compiler_params=params(),
        cost_estimate=cost(),
        name="pull",
    )(cot, dense)


def swap_sum_body(mate_term, far_term, cross_0, cross_1, mate_0, mate_1, far_0, far_1):
    half = far_0.shape[1]
    core, mate, _ = coordinates()
    cross = jnp.concatenate([cross_0[...], cross_1[...]], axis=1).astype(F32)
    cross_mate = jnp.where(core == mate, cross, 0.0)
    far = (far_term[...] + (cross - cross_mate)).astype(BF16)
    near = mate_term[...] + cross_mate
    mate_0[...], mate_1[...] = near[:, :half], near[:, half:]
    far_0[...], far_1[...] = far[:, :half], far[:, half:]


def swap_sum(mate_term, far_term, cross):
    cols, rows = far_term.shape
    shape = (cols, rows // 2)
    out = pl.pallas_call(
        swap_sum_body,
        out_shape=[jax.ShapeDtypeStruct(shape, F32)] * 2
        + [jax.ShapeDtypeStruct(shape, BF16)] * 2,
        in_specs=[VMEM] * 4,
        out_specs=[VMEM] * 4,
        compiler_params=params(),
        cost_estimate=cost(),
        name="swap_sum",
    )(mate_term, far_term, *cross)
    return out[:2], out[2:]


def hidden_body(s0, s1, w_mine, w_near, w_far, w_out, *refs, number):
    pre, hid, mixed = refs[-3:]
    height, width = pre.shape
    span = slice(number * height, (number + 1) * height)
    core, _, panel = coordinates()

    def rows_of(side):
        return pl.ds(pl.multiple_of((panel ^ side) * width, width), width)

    def run(w_theirs):
        mine, theirs = 0.0, 0.0
        for side, ref in enumerate((s0, s1)):
            taken = ref[span, :]
            mine += jnp.dot(taken, w_mine[rows_of(side), :], preferred_element_type=F32)
            theirs += jnp.dot(taken, w_theirs[side][...], preferred_element_type=F32)
        pre[...] = mine
        hid[:, :width] = (mine * jax.nn.sigmoid(mine)).astype(BF16)
        hid[:, width:] = (theirs * jax.nn.sigmoid(theirs)).astype(BF16)

    pl.when(core == 0)(lambda: run((w_near, w_far)))
    pl.when(core == 1)(lambda: run((w_far, w_near)))
    result = 0.0
    for side in range(2):
        value = hid[:, side * width : (side + 1) * width]
        result += jnp.dot(value, w_out[rows_of(side), :], preferred_element_type=F32)
    mixed[...] = result.astype(BF16)


def hidden_step(number, pieces, w_mine, w_near, w_far, w_out, *after):
    rows, width = pieces[0].shape
    height = rows // 2
    return pl.pallas_call(
        functools.partial(hidden_body, number=number),
        out_shape=[
            jax.ShapeDtypeStruct((height, width), F32),
            jax.ShapeDtypeStruct((height, 2 * width), BF16),
            jax.ShapeDtypeStruct((height, width), BF16),
        ],
        in_specs=[VMEM] * 6 + [ANY] * len(after),
        out_specs=[VMEM] * 3,
        compiler_params=params(),
        cost_estimate=cost(),
        name="hidden",
    )(*pieces, w_mine, w_near, w_far, w_out, *after)


def mix_body(own, swap, come, w_out, *refs, number):
    pulled, keep, give = refs[-3:]
    height, half = keep.shape
    _, _, panel = coordinates()
    span = slice(number * height, (number + 1) * height)
    total = own[:, span] + swap[:, span].astype(F32) + come[...].astype(F32)
    pulled[...] = total.astype(BF16).T
    contract = (((1,), (1,)), ((), ()))
    theirs = w_out[pl.ds(pl.multiple_of((1 - panel) * half, half), half), :]
    give[...] = lax.dot_general(
        pulled[...], theirs, contract, preferred_element_type=F32
    ).astype(BF16)
    mine = w_out[pl.ds(pl.multiple_of(panel * half, half), half), :]
    keep[...] = lax.dot_general(pulled[...], mine, contract, preferred_element_type=F32)


def mix_step(number, own, swap, come, w_out, *after):
    cols, height = come.shape
    half = w_out.shape[0] // 2
    return pl.pallas_call(
        functools.partial(mix_body, number=number),
        out_shape=[
            jax.ShapeDtypeStruct((height, cols), BF16),
            jax.ShapeDtypeStruct((height, half), F32),
            jax.ShapeDtypeStruct((height, half), BF16),
        ],
        in_specs=[VMEM] * 4 + [ANY] * len(after),
        out_specs=[VMEM] * 3,
        compiler_params=params(),
        cost_estimate=cost(),
        name="mix_back",
    )(own, swap, come, w_out, *after)


def split_term(total, keep, give_near, give_far, scratch, blocks):
    core, mate, _ = coordinates()
    share = total.shape[0] // blocks
    groups = blocks // 4
    for group in range(groups):
        for side in range(2):
            owner = 4 * group + 2 * (mate ^ side)
            target = pl.ds((side * groups + group) * share, share)
            source = pl.multiple_of((owner + core) * share, share)
            keep[target, :] = total[pl.ds(source, share), :]
            source = pl.multiple_of((owner + 1 - core) * share, share)
            scratch[target, :] = total[pl.ds(source, share), :]
    half = give_near.shape[0]
    give_near[...] = scratch[:half].astype(BF16)
    give_far[...] = scratch[half:].astype(BF16)


def grad_into(total, pieces, rights):
    _, _, panel = coordinates()
    contract = (((0,), (0,)), ((), ()))
    width = rights[0].shape[1]
    half = width // 2
    for side, (refs, first) in enumerate(pieces):
        for number in range(2):
            start = (panel ^ side) * width + number * half
            source = first + number * half
            result = 0.0
            for index, right in enumerate(rights):
                height = right.shape[0]
                if len(refs) == 1:
                    taken = refs[0][index * height : (index + 1) * height, source : source + half]
                else:
                    taken = refs[index][:, source : source + half]
                result += lax.dot_general(
                    taken,
                    right[...],
                    contract,
                    preferred_element_type=F32,
                )
            total[pl.ds(pl.multiple_of(start, half), half), :] = result


def out_grad_body(hid_0, hid_1, pulled_0, pulled_1, *refs, blocks):
    keep, near, far, total, scratch = refs[-5:]
    width = pulled_0.shape[1]
    hid = (hid_0, hid_1)
    grad_into(total, ((hid, 0), (hid, width)), (pulled_0, pulled_1))
    split_term(total, keep, near, far, scratch, blocks)


def in_grad_body(*refs, blocks):
    own, theirs, *refs = refs
    pre, kept, come = [refs[2 * i : 2 * i + 2] for i in range(3)]
    keep, near, far, total, scratch, *back = refs[-7:]
    for half in range(2):
        pre_hidden = pre[half][...]
        gate = jax.nn.sigmoid(pre_hidden)
        back_hidden = kept[half][...] + come[half][...].astype(F32)
        slope = gate * (1.0 + pre_hidden * (1.0 - gate))
        back[half][...] = (back_hidden * slope).astype(BF16)
    grad_into(total, (((own,), 0), ((theirs,), 0)), back)
    split_term(total, keep, near, far, scratch, blocks)


def grad_call(body, name, operands, height, width, scratch=(), after=()):
    blocks = lax.axis_size("blk")
    half = height // 2
    return pl.pallas_call(
        functools.partial(body, blocks=blocks),
        out_shape=[
            jax.ShapeDtypeStruct((half, width), F32),
            jax.ShapeDtypeStruct((half // 2, width), BF16),
            jax.ShapeDtypeStruct((half // 2, width), BF16),
        ],
        in_specs=[VMEM] * len(operands) + [ANY] * len(after),
        out_specs=[VMEM] * 3,
        scratch_shapes=[
            pltpu.VMEM((height, width), F32),
            pltpu.VMEM((half, width), F32),
            *scratch,
        ],
        compiler_params=params(),
        cost_estimate=cost(),
        name=name,
    )(*operands, *after)


def far_sum_body(first, first_come, second, second_come, far):
    half = far.shape[0] // 2
    far[:half] = (first[half:] + first_come[...].astype(F32)).astype(BF16)
    far[half:] = (second[half:] + second_come[...].astype(F32)).astype(BF16)


def far_sum(first, first_come, second, second_come):
    return pl.pallas_call(
        far_sum_body,
        out_shape=jax.ShapeDtypeStruct(first.shape, BF16),
        in_specs=[VMEM] * 4,
        out_specs=VMEM,
        compiler_params=params(),
        cost_estimate=cost(),
        name="far_sum",
    )(first, first_come, second, second_come)


def mate_sum_body(first, first_core, second, second_core, come, *refs):
    own_first, own_second, *terms, sum_first, sum_second = refs
    share = own_first.shape[0]
    group = lax.axis_index("blk") // 4
    half = sum_first.shape[0]
    sum_first[...] = first[:half] + first_core[...].astype(F32) + come[:half].astype(F32)
    sum_second[...] = second[:half] + second_core[...].astype(F32) + come[half:].astype(F32)

    def rows_of(distance):
        start = pl.multiple_of((group ^ distance) * share, share)
        return sum_first[pl.ds(start, share), :], sum_second[pl.ds(start, share), :]

    own_first[...], own_second[...] = rows_of(0)
    for number, ref in enumerate(terms):
        ref[...] = jnp.concatenate(rows_of(number + 1), axis=0).astype(BF16)


def mate_sum(first, first_core, second, second_core, come):
    height, width = first_core.shape
    groups = lax.axis_size("blk") // 4
    share = height // groups
    own = jax.ShapeDtypeStruct((share, width), F32)
    term = jax.ShapeDtypeStruct((2 * share, width), BF16)
    own_first, own_second, *terms = pl.pallas_call(
        mate_sum_body,
        out_shape=[own] * 2 + [term] * (groups - 1),
        in_specs=[VMEM] * 5,
        out_specs=[VMEM] * (1 + groups),
        scratch_shapes=[pltpu.VMEM((height, width), F32)] * 2,
        compiler_params=params(),
        cost_estimate=cost(),
        name="mate_sum",
    )(first, first_core, second, second_core, come)
    return own_first, own_second, terms


def group_sum_body(own_first, own_second, *refs):
    *terms, out_first, out_second = refs
    share = own_first.shape[0]
    total_first, total_second = own_first[...], own_second[...]
    for ref in terms:
        term = ref[...].astype(F32)
        total_first += term[:share]
        total_second += term[share:]
    out_first[...] = total_first
    out_second[...] = total_second


def group_sum(own_first, own_second, terms):
    return pl.pallas_call(
        group_sum_body,
        out_shape=[jax.ShapeDtypeStruct(own_first.shape, F32)] * 2,
        in_specs=[VMEM] * (2 + len(terms)),
        out_specs=[VMEM] * 2,
        compiler_params=params(),
        cost_estimate=cost(),
        name="group_sum",
    )(own_first, own_second, *terms)


def shards(
    features, weight_in, weight_out, adj_tiles, tile_rows, tile_cols, tile_counts, cotangent
):
    rows, width = features.shape
    tile_rows, tile_cols = jnp.swapaxes(tile_rows, 0, 1), jnp.swapaxes(tile_cols, 0, 1)
    slots = lax.broadcasted_iota(jnp.int32, tile_rows.shape, 2)
    codes = jnp.where(
        slots < tile_counts[0][:, None, None],
        tile_rows * (rows // adj_tiles.shape[-1]) + tile_cols,
        -1,
    )

    height = rows // 2

    f_mate = [to_mate(features[:height]), to_mate(features[height:])]
    f_other = to_core(features)
    f_mate_other = [to_core(half) for half in f_mate]
    f_far = [relay_out(half) for half in f_mate]
    w_near = to_panel(gate(pick(weight_in), f_mate[0]))
    w_far = to_core(w_near)

    dense = build(codes, adj_tiles, rows)
    p_own, p_mate, p_far, p_swap, *p_cross = pull(cotangent, dense)
    p_mate, p_far = swap_sum(
        p_mate, p_far, [to_core(gate(half, f_mate[1])) for half in p_cross]
    )
    p_swap = to_core(p_swap)

    total = spread_near(dense, features, f_other, f_mate, p_far[0])
    f_far = [gate(half, total) for half in f_far]
    p_come = [relay_back(gate(far, *f_far)) for far in p_far]
    f_far_other = [to_core(half) for half in f_far]
    own = spread_far(dense, total, f_far, f_mate_other, f_far_other)
    theirs = to_panel(own)
    q_come = [
        to_mate((mine + come.astype(F32)).astype(BF16)) for mine, come in zip(p_mate, p_come)
    ]
    pre_hidden, hid, mixed = zip(
        *[
            hidden_step(number, (own, theirs), weight_in, w_near, w_far, weight_out, dense)
            for number in range(2)
        ]
    )

    t_mate = [to_mate(half) for half in mixed]
    t_own = jnp.concatenate(mixed, axis=0)
    t_other = to_core(t_own)
    t_mate_other = [to_core(half) for half in t_mate]
    t_far = [relay_out(half) for half in t_mate]
    t_far_other = [to_core(jnp.concatenate(t_far, axis=0))]

    pulled, kept, given = zip(
        *[
            mix_step(number, p_own, p_swap, come, weight_out, dense)
            for number, come in enumerate(q_come)
        ]
    )
    come = [to_panel(half) for half in given]
    out_keep, out_near, out_far = grad_call(
        out_grad_body, "out_grad", [*hid, *pulled], 2 * width, width
    )
    in_keep, in_near, in_far = grad_call(
        in_grad_body,
        "in_grad",
        [own, theirs, *pre_hidden, *kept, *come],
        2 * width,
        width,
        [pltpu.VMEM((height, width), BF16)] * 2,
        (dense, *[half[:8, :128] for half in t_mate]),
    )
    far = far_sum(out_keep, to_core(out_far), in_keep, to_core(in_far))
    out_own, in_own, terms = mate_sum(
        out_keep, to_core(out_near), in_keep, to_core(in_near), to_mate(far)
    )
    terms = [to_group(terms[distance - 1], distance) for distance in range(len(terms), 0, -1)]

    total = spread_near(dense, t_own, t_other, t_mate)
    layer_output = spread_far(dense, total, t_far, t_mate_other, t_far_other)
    grad_weight_out, grad_weight_in = group_sum(out_own, in_own, terms)
    return (layer_output, grad_weight_in, grad_weight_out)


def solution(mesh):
    return jax.shard_map(
        shards,
        mesh=mesh,
        in_specs=(
            P("blk", "feat"),
            P(None, "feat"),
            P(None, "feat"),
            P("blk", None, None, None, None),
            P("blk", None, None),
            P("blk", None, None),
            P("blk", None),
            P("blk", "feat"),
        ),
        out_specs=(P("blk", "feat"), P("blk", "feat"), P("blk", "feat")),
        check_vma=False,
    )
```

```python
import functools

import jax
import jax.numpy as jnp
from jax import lax
from jax.experimental import pallas as pl
from jax.experimental.pallas import tpu as pltpu
from jax.sharding import PartitionSpec as P

BF16 = jnp.bfloat16
F32 = jnp.float32
VMEM = pl.BlockSpec(memory_space=pltpu.VMEM)
SMEM = pl.BlockSpec(memory_space=pltpu.SMEM)
ANY = pl.BlockSpec(memory_space=pl.ANY)


def params(limit_mib=12):
    return pltpu.CompilerParams(vmem_limit_bytes=limit_mib * 1024 * 1024)


def cost(microseconds=0):
    return pl.CostEstimate(
        flops=1024, bytes_accessed=1024 + 3_600_000 * microseconds, transcendentals=0
    )


def gate_body(*refs):
    del refs


def gate(value, *after, microseconds=0):
    return pl.pallas_call(
        gate_body,
        out_shape=jax.ShapeDtypeStruct(value.shape, value.dtype),
        in_specs=[ANY] * (1 + len(after)),
        out_specs=ANY,
        input_output_aliases={0: 0},
        compiler_params=params(1),
        cost_estimate=cost(microseconds),
        name="gate",
    )(value, *after)


def coordinates():
    block = lax.axis_index("blk")
    return block & 1, (block >> 1) & 1, lax.axis_index("feat")


def coordinates():
    block = lax.axis_index("blk")
    return block & 1, (block >> 1) & 1, lax.axis_index("feat")


def copy_all(pairs, semaphores):
    copies = [
        pltpu.make_async_copy(source, target, semaphores.at[number])
        for number, (source, target) in enumerate(pairs)
    ]
    for copy in copies:
        copy.start()
    for copy in copies:
        copy.wait()


def coordinates():
    block = lax.axis_index("blk")
    return block & 1, (block >> 1) & 1, lax.axis_index("feat")


def blk_pairs(target):
    count = lax.axis_size("blk")
    return [(source, target(source) % count) for source in range(count)]


def to_core(value):
    return lax.ppermute(value, "blk", blk_pairs(lambda b: b ^ 1))


def to_mate(value):
    return lax.ppermute(value, "blk", blk_pairs(lambda b: b ^ 2))


def relay_out(value):
    return lax.ppermute(value, "blk", blk_pairs(lambda b: b - 4 if b & 2 else b + 4))


def relay_back(value):
    return lax.ppermute(value, "blk", blk_pairs(lambda b: b + 4 if b & 2 else b - 4))


def to_group(value, distance):
    return lax.ppermute(value, "blk", blk_pairs(lambda b: b ^ (4 * distance)))


def to_panel(value):
    return lax.ppermute(value, "feat", [(0, 1), (1, 0)])


def pick_body(w_in, send, semaphore):
    half = send.shape[0]
    core, _, panel = coordinates()
    start = pl.multiple_of(((1 - panel) ^ core) * half, half)
    copy = pltpu.make_async_copy(w_in.at[pl.ds(start, half), :], send, semaphore)
    copy.start()
    copy.wait()


def pick(w_in):
    width = w_in.shape[1]
    return pl.pallas_call(
        pick_body,
        out_shape=jax.ShapeDtypeStruct((width, width), BF16),
        in_specs=[ANY],
        out_specs=VMEM,
        scratch_shapes=[pltpu.SemaphoreType.DMA],
        compiler_params=params(4),
        cost_estimate=cost(),
        name="pick",
    )(w_in)


def build_body(codes, tiles, dense):
    _, steps, cap, tile, _ = tiles.shape
    radius = (steps - 1) // 2
    block_tiles = dense.shape[0] // tile
    core, mate, _ = coordinates()
    dense[...] = jnp.zeros_like(dense)

    def place(entry, carry):
        step, slot = entry // cap, entry % cap
        shifted = step - radius + core + 2
        chip = shifted // 2 - 1
        position = (shifted % 2) ^ core
        ahead = jnp.where(mate == 0, 1, -1)
        outside = jnp.where(position == 1, 4, jnp.where(chip == ahead, 2, 3))
        segment = jnp.where(chip == 0, position, outside)
        code = codes[step, 0, slot]
        row = code // block_tiles
        col = segment * block_tiles + code % block_tiles

        @pl.when(code >= 0)
        def _():
            dense[
                pl.ds(pl.multiple_of(row * tile, tile), tile),
                pl.ds(pl.multiple_of(col * tile, tile), tile),
            ] = tiles[0, step, slot]

        return carry

    lax.fori_loop(0, steps * cap, place, 0)


def build(codes, tiles, rows):
    return pl.pallas_call(
        build_body,
        out_shape=jax.ShapeDtypeStruct((rows, 5 * rows), BF16),
        in_specs=[SMEM, VMEM],
        out_specs=VMEM,
        compiler_params=params(),
        cost_estimate=cost(),
        name="build_dense",
    )(codes, tiles)


def sum_products(result, dense, first, refs):
    for ref in refs:
        height = ref.shape[0]
        product = jnp.dot(
            dense[:, first : first + height], ref[...], preferred_element_type=F32
        )
        result = product if result is None else result + product
        first += height
    return result


def spread_near_body(dense, s0, s1, s2, s3, *refs):
    refs[-1][...] = sum_products(None, dense, 0, (s0, s1, s2, s3))


def spread_near(dense, own, other, mate, *after):
    rows, cols = own.shape
    block = rows // 2
    whole = pl.BlockSpec((rows, cols), lambda i: (0, 0))
    half = pl.BlockSpec((block, cols), lambda i: (0, 0))
    return pl.pallas_call(
        spread_near_body,
        grid=(2,),
        out_shape=jax.ShapeDtypeStruct((rows, cols), F32),
        in_specs=[
            pl.BlockSpec((block, 3 * rows), lambda i: (i, 0)),
            whole,
            whole,
            half,
            half,
            *[ANY] * len(after),
        ],
        out_specs=pl.BlockSpec((block, cols), lambda i: (i, 0)),
        compiler_params=params(),
        cost_estimate=cost(),
        name="spread_near",
    )(dense, own, other, *mate, *after)


def spread_far_body(dense, total, f0, f1, m0, m1, *refs):
    *far_other, out = refs
    height = f0.shape[0]
    core, mate, _ = coordinates()

    def add_up(*cross):
        out[...] = sum_products(total[...], dense, 6 * height, (f0, f1, *cross)).astype(BF16)

    pl.when(core == mate)(lambda: add_up(*far_other))
    pl.when(core != mate)(lambda: add_up(m0, m1))


def spread_far(dense, total, far, mate_other, far_other):
    return pl.pallas_call(
        spread_far_body,
        out_shape=jax.ShapeDtypeStruct(total.shape, BF16),
        in_specs=[VMEM] * (6 + len(far_other)),
        out_specs=VMEM,
        compiler_params=params(),
        cost_estimate=cost(),
        name="spread_far",
    )(dense, total, *far, *mate_other, *far_other)


def pull_body(cot, dense, own, mate, far, swap_own, cross_0, cross_1):
    rows = dense.shape[0]
    turned = cot[...].T
    terms = [
        jnp.dot(
            turned, dense[:, index * rows : (index + 1) * rows], preferred_element_type=F32
        )
        for index in range(5)
    ]
    own[...], mate[...], far[...] = terms[0], terms[2], terms[3]
    swap_own[...] = terms[1].astype(BF16)
    half = cross_0.shape[1]
    cross_0[...], cross_1[...] = terms[4][:, :half].astype(BF16), terms[4][:, half:].astype(BF16)


def pull(cot, dense):
    rows, cols = cot.shape
    return pl.pallas_call(
        pull_body,
        out_shape=[jax.ShapeDtypeStruct((cols, rows), F32)] * 3
        + [jax.ShapeDtypeStruct((cols, rows), BF16)]
        + [jax.ShapeDtypeStruct((cols, rows // 2), BF16)] * 2,
        in_specs=[VMEM] * 2,
        out_specs=[VMEM] * 6,
        compiler_params=params(),
        cost_estimate=cost(),
        name="pull",
    )(cot, dense)


def swap_sum_body(mate_term, far_term, cross_0, cross_1, mate_0, mate_1, far_0, far_1):
    half = far_0.shape[1]
    core, mate, _ = coordinates()
    cross = jnp.concatenate([cross_0[...], cross_1[...]], axis=1).astype(F32)
    cross_mate = jnp.where(core == mate, cross, 0.0)
    far = (far_term[...] + (cross - cross_mate)).astype(BF16)
    near = mate_term[...] + cross_mate
    mate_0[...], mate_1[...] = near[:, :half], near[:, half:]
    far_0[...], far_1[...] = far[:, :half], far[:, half:]


def swap_sum(mate_term, far_term, cross):
    cols, rows = far_term.shape
    shape = (cols, rows // 2)
    out = pl.pallas_call(
        swap_sum_body,
        out_shape=[jax.ShapeDtypeStruct(shape, F32)] * 2
        + [jax.ShapeDtypeStruct(shape, BF16)] * 2,
        in_specs=[VMEM] * 4,
        out_specs=[VMEM] * 4,
        compiler_params=params(),
        cost_estimate=cost(),
        name="swap_sum",
    )(mate_term, far_term, *cross)
    return out[:2], out[2:]


def hidden_body(s0, s1, w_mine, w_near, w_far, w_out, *refs, number):
    pre, hid, mixed = refs[-3:]
    height, width = pre.shape
    span = slice(number * height, (number + 1) * height)
    core, _, panel = coordinates()

    def rows_of(side):
        return pl.ds(pl.multiple_of((panel ^ side) * width, width), width)

    def run(w_theirs):
        mine, theirs = 0.0, 0.0
        for side, ref in enumerate((s0, s1)):
            taken = ref[span, :]
            mine += jnp.dot(taken, w_mine[rows_of(side), :], preferred_element_type=F32)
            theirs += jnp.dot(taken, w_theirs[side][...], preferred_element_type=F32)
        pre[...] = mine
        hid[:, :width] = (mine * jax.nn.sigmoid(mine)).astype(BF16)
        hid[:, width:] = (theirs * jax.nn.sigmoid(theirs)).astype(BF16)

    pl.when(core == 0)(lambda: run((w_near, w_far)))
    pl.when(core == 1)(lambda: run((w_far, w_near)))
    result = 0.0
    for side in range(2):
        value = hid[:, side * width : (side + 1) * width]
        result += jnp.dot(value, w_out[rows_of(side), :], preferred_element_type=F32)
    mixed[...] = result.astype(BF16)


def hidden_step(number, pieces, w_mine, w_near, w_far, w_out, *after):
    rows, width = pieces[0].shape
    height = rows // 2
    return pl.pallas_call(
        functools.partial(hidden_body, number=number),
        out_shape=[
            jax.ShapeDtypeStruct((height, width), F32),
            jax.ShapeDtypeStruct((height, 2 * width), BF16),
            jax.ShapeDtypeStruct((height, width), BF16),
        ],
        in_specs=[VMEM] * 6 + [ANY] * len(after),
        out_specs=[VMEM] * 3,
        compiler_params=params(),
        cost_estimate=cost(),
        name="hidden",
    )(*pieces, w_mine, w_near, w_far, w_out, *after)


def mix_body(own, swap, come, w_out, *refs, number):
    pulled, keep, give = refs[-3:]
    height, half = keep.shape
    _, _, panel = coordinates()
    span = slice(number * height, (number + 1) * height)
    total = own[:, span] + swap[:, span].astype(F32) + come[...].astype(F32)
    pulled[...] = total.astype(BF16).T
    contract = (((1,), (1,)), ((), ()))
    theirs = w_out[pl.ds(pl.multiple_of((1 - panel) * half, half), half), :]
    give[...] = lax.dot_general(
        pulled[...], theirs, contract, preferred_element_type=F32
    ).astype(BF16)
    mine = w_out[pl.ds(pl.multiple_of(panel * half, half), half), :]
    keep[...] = lax.dot_general(pulled[...], mine, contract, preferred_element_type=F32)


def mix_step(number, own, swap, come, w_out, *after):
    cols, height = come.shape
    half = w_out.shape[0] // 2
    return pl.pallas_call(
        functools.partial(mix_body, number=number),
        out_shape=[
            jax.ShapeDtypeStruct((height, cols), BF16),
            jax.ShapeDtypeStruct((height, half), F32),
            jax.ShapeDtypeStruct((height, half), BF16),
        ],
        in_specs=[VMEM] * 4 + [ANY] * len(after),
        out_specs=[VMEM] * 3,
        compiler_params=params(),
        cost_estimate=cost(),
        name="mix_back",
    )(own, swap, come, w_out, *after)


def split_term(total, keep, give_near, give_far, scratch, blocks):
    core, mate, _ = coordinates()
    share = total.shape[0] // blocks
    groups = blocks // 4
    for group in range(groups):
        for side in range(2):
            owner = 4 * group + 2 * (mate ^ side)
            target = pl.ds((side * groups + group) * share, share)
            source = pl.multiple_of((owner + core) * share, share)
            keep[target, :] = total[pl.ds(source, share), :]
            source = pl.multiple_of((owner + 1 - core) * share, share)
            scratch[target, :] = total[pl.ds(source, share), :]
    half = give_near.shape[0]
    give_near[...] = scratch[:half].astype(BF16)
    give_far[...] = scratch[half:].astype(BF16)


def grad_into(total, pieces, rights):
    _, _, panel = coordinates()
    contract = (((0,), (0,)), ((), ()))
    width = rights[0].shape[1]
    half = width // 2
    for side, (refs, first) in enumerate(pieces):
        for number in range(2):
            start = (panel ^ side) * width + number * half
            source = first + number * half
            result = 0.0
            for index, right in enumerate(rights):
                height = right.shape[0]
                if len(refs) == 1:
                    taken = refs[0][index * height : (index + 1) * height, source : source + half]
                else:
                    taken = refs[index][:, source : source + half]
                result += lax.dot_general(
                    taken,
                    right[...],
                    contract,
                    preferred_element_type=F32,
                )
            total[pl.ds(pl.multiple_of(start, half), half), :] = result


def out_grad_body(hid_0, hid_1, pulled_0, pulled_1, *refs, blocks):
    keep, near, far, total, scratch = refs[-5:]
    width = pulled_0.shape[1]
    hid = (hid_0, hid_1)
    grad_into(total, ((hid, 0), (hid, width)), (pulled_0, pulled_1))
    split_term(total, keep, near, far, scratch, blocks)


def in_grad_body(*refs, blocks):
    own, theirs, *refs = refs
    pre, kept, come = [refs[2 * i : 2 * i + 2] for i in range(3)]
    keep, near, far, total, scratch, *back = refs[-7:]
    for half in range(2):
        pre_hidden = pre[half][...]
        gate = jax.nn.sigmoid(pre_hidden)
        back_hidden = kept[half][...] + come[half][...].astype(F32)
        slope = gate * (1.0 + pre_hidden * (1.0 - gate))
        back[half][...] = (back_hidden * slope).astype(BF16)
    grad_into(total, (((own,), 0), ((theirs,), 0)), back)
    split_term(total, keep, near, far, scratch, blocks)


def grad_call(body, name, operands, height, width, scratch=(), after=()):
    blocks = lax.axis_size("blk")
    half = height // 2
    return pl.pallas_call(
        functools.partial(body, blocks=blocks),
        out_shape=[
            jax.ShapeDtypeStruct((half, width), F32),
            jax.ShapeDtypeStruct((half // 2, width), BF16),
            jax.ShapeDtypeStruct((half // 2, width), BF16),
        ],
        in_specs=[VMEM] * len(operands) + [ANY] * len(after),
        out_specs=[VMEM] * 3,
        scratch_shapes=[
            pltpu.VMEM((height, width), F32),
            pltpu.VMEM((half, width), F32),
            *scratch,
        ],
        compiler_params=params(),
        cost_estimate=cost(),
        name=name,
    )(*operands, *after)


def far_sum_body(first, first_come, second, second_come, far):
    half = far.shape[0] // 2
    far[:half] = (first[half:] + first_come[...].astype(F32)).astype(BF16)
    far[half:] = (second[half:] + second_come[...].astype(F32)).astype(BF16)


def far_sum(first, first_come, second, second_come):
    return pl.pallas_call(
        far_sum_body,
        out_shape=jax.ShapeDtypeStruct(first.shape, BF16),
        in_specs=[VMEM] * 4,
        out_specs=VMEM,
        compiler_params=params(),
        cost_estimate=cost(),
        name="far_sum",
    )(first, first_come, second, second_come)


def mate_sum_body(first, first_core, second, second_core, come, *refs):
    own_first, own_second, *terms, sum_first, sum_second = refs
    share = own_first.shape[0]
    group = lax.axis_index("blk") // 4
    half = sum_first.shape[0]
    sum_first[...] = first[:half] + first_core[...].astype(F32) + come[:half].astype(F32)
    sum_second[...] = second[:half] + second_core[...].astype(F32) + come[half:].astype(F32)

    def rows_of(distance):
        start = pl.multiple_of((group ^ distance) * share, share)
        return sum_first[pl.ds(start, share), :], sum_second[pl.ds(start, share), :]

    own_first[...], own_second[...] = rows_of(0)
    for number, ref in enumerate(terms):
        ref[...] = jnp.concatenate(rows_of(number + 1), axis=0).astype(BF16)


def mate_sum(first, first_core, second, second_core, come):
    height, width = first_core.shape
    groups = lax.axis_size("blk") // 4
    share = height // groups
    own = jax.ShapeDtypeStruct((share, width), F32)
    term = jax.ShapeDtypeStruct((2 * share, width), BF16)
    own_first, own_second, *terms = pl.pallas_call(
        mate_sum_body,
        out_shape=[own] * 2 + [term] * (groups - 1),
        in_specs=[VMEM] * 5,
        out_specs=[VMEM] * (1 + groups),
        scratch_shapes=[pltpu.VMEM((height, width), F32)] * 2,
        compiler_params=params(),
        cost_estimate=cost(),
        name="mate_sum",
    )(first, first_core, second, second_core, come)
    return own_first, own_second, terms


def group_sum_body(own_first, own_second, *refs):
    *terms, out_first, out_second = refs
    share = own_first.shape[0]
    total_first, total_second = own_first[...], own_second[...]
    for ref in terms:
        term = ref[...].astype(F32)
        total_first += term[:share]
        total_second += term[share:]
    out_first[...] = total_first
    out_second[...] = total_second


def group_sum(own_first, own_second, terms):
    return pl.pallas_call(
        group_sum_body,
        out_shape=[jax.ShapeDtypeStruct(own_first.shape, F32)] * 2,
        in_specs=[VMEM] * (2 + len(terms)),
        out_specs=[VMEM] * 2,
        compiler_params=params(),
        cost_estimate=cost(),
        name="group_sum",
    )(own_first, own_second, *terms)


def shards(
    features, weight_in, weight_out, adj_tiles, tile_rows, tile_cols, tile_counts, cotangent
):
    rows, width = features.shape
    tile_rows, tile_cols = jnp.swapaxes(tile_rows, 0, 1), jnp.swapaxes(tile_cols, 0, 1)
    slots = lax.broadcasted_iota(jnp.int32, tile_rows.shape, 2)
    codes = jnp.where(
        slots < tile_counts[0][:, None, None],
        tile_rows * (rows // adj_tiles.shape[-1]) + tile_cols,
        -1,
    )

    height = rows // 2

    f_mate = [to_mate(features[:height]), to_mate(features[height:])]
    f_other = to_core(features)
    f_mate_other = [to_core(half) for half in f_mate]
    f_far = [relay_out(half) for half in f_mate]
    w_near = to_panel(gate(pick(weight_in), f_mate[0]))
    w_far = to_core(w_near)

    dense = build(codes, adj_tiles, rows)
    p_own, p_mate, p_far, p_swap, *p_cross = pull(cotangent, dense)
    p_mate, p_far = swap_sum(
        p_mate, p_far, [to_core(gate(half, f_mate[1])) for half in p_cross]
    )
    p_swap = to_core(p_swap)

    total = spread_near(dense, features, f_other, f_mate, p_far[0])
    f_far = [gate(half, total) for half in f_far]
    p_come = [relay_back(gate(far, *f_far)) for far in p_far]
    f_far_other = [to_core(half) for half in f_far]
    own = spread_far(dense, total, f_far, f_mate_other, f_far_other)
    theirs = to_panel(own)
    q_come = [
        to_mate((mine + come.astype(F32)).astype(BF16)) for mine, come in zip(p_mate, p_come)
    ]
    pre_hidden, hid, mixed = zip(
        *[
            hidden_step(number, (own, theirs), weight_in, w_near, w_far, weight_out, dense)
            for number in range(2)
        ]
    )

    t_mate = [to_mate(half) for half in mixed]
    t_own = jnp.concatenate(mixed, axis=0)
    t_other = to_core(t_own)
    t_mate_other = [to_core(half) for half in t_mate]
    t_far = [relay_out(half) for half in t_mate]
    t_far_other = [to_core(jnp.concatenate(t_far, axis=0))]

    pulled, kept, given = zip(
        *[
            mix_step(number, p_own, p_swap, come, weight_out, dense)
            for number, come in enumerate(q_come)
        ]
    )
    come = [to_panel(half) for half in given]
    out_keep, out_near, out_far = grad_call(
        out_grad_body, "out_grad", [*hid, *pulled], 2 * width, width
    )
    in_keep, in_near, in_far = grad_call(
        in_grad_body,
        "in_grad",
        [own, theirs, *pre_hidden, *kept, *come],
        2 * width,
        width,
        [pltpu.VMEM((height, width), BF16)] * 2,
        (dense, t_mate[1][:8, :128]),
    )
    far = far_sum(out_keep, to_core(out_far), in_keep, to_core(in_far))
    out_own, in_own, terms = mate_sum(
        out_keep, to_core(out_near), in_keep, to_core(in_near), to_mate(far)
    )
    terms = [to_group(terms[distance - 1], distance) for distance in range(len(terms), 0, -1)]

    total = spread_near(dense, t_own, t_other, t_mate)
    layer_output = spread_far(dense, total, t_far, t_mate_other, t_far_other)
    grad_weight_out, grad_weight_in = group_sum(out_own, in_own, terms)
    return (layer_output, grad_weight_in, grad_weight_out)


def solution(mesh):
    return jax.shard_map(
        shards,
        mesh=mesh,
        in_specs=(
            P("blk", "feat"),
            P(None, "feat"),
            P(None, "feat"),
            P("blk", None, None, None, None),
            P("blk", None, None),
            P("blk", None, None),
            P("blk", None),
            P("blk", "feat"),
        ),
        out_specs=(P("blk", "feat"), P("blk", "feat"), P("blk", "feat")),
        check_vma=False,
    )
```

```python
import functools

import jax
import jax.numpy as jnp
from jax import lax
from jax.experimental import pallas as pl
from jax.experimental.pallas import tpu as pltpu
from jax.sharding import PartitionSpec as P

BF16 = jnp.bfloat16
F32 = jnp.float32
VMEM = pl.BlockSpec(memory_space=pltpu.VMEM)
SMEM = pl.BlockSpec(memory_space=pltpu.SMEM)
ANY = pl.BlockSpec(memory_space=pl.ANY)


def params(limit_mib=12):
    return pltpu.CompilerParams(vmem_limit_bytes=limit_mib * 1024 * 1024)


def cost(microseconds=0):
    return pl.CostEstimate(
        flops=1024, bytes_accessed=1024 + 3_600_000 * microseconds, transcendentals=0
    )


def gate_body(*refs):
    del refs


def gate(value, *after, microseconds=0):
    return pl.pallas_call(
        gate_body,
        out_shape=jax.ShapeDtypeStruct(value.shape, value.dtype),
        in_specs=[ANY] * (1 + len(after)),
        out_specs=ANY,
        input_output_aliases={0: 0},
        compiler_params=params(1),
        cost_estimate=cost(microseconds),
        name="gate",
    )(value, *after)


def coordinates():
    block = lax.axis_index("blk")
    return block & 1, (block >> 1) & 1, lax.axis_index("feat")


def coordinates():
    block = lax.axis_index("blk")
    return block & 1, (block >> 1) & 1, lax.axis_index("feat")


def copy_all(pairs, semaphores):
    copies = [
        pltpu.make_async_copy(source, target, semaphores.at[number])
        for number, (source, target) in enumerate(pairs)
    ]
    for copy in copies:
        copy.start()
    for copy in copies:
        copy.wait()


def coordinates():
    block = lax.axis_index("blk")
    return block & 1, (block >> 1) & 1, lax.axis_index("feat")


def blk_pairs(target):
    count = lax.axis_size("blk")
    return [(source, target(source) % count) for source in range(count)]


def to_core(value):
    return lax.ppermute(value, "blk", blk_pairs(lambda b: b ^ 1))


def to_mate(value):
    return lax.ppermute(value, "blk", blk_pairs(lambda b: b ^ 2))


def relay_out(value):
    return lax.ppermute(value, "blk", blk_pairs(lambda b: b - 4 if b & 2 else b + 4))


def relay_back(value):
    return lax.ppermute(value, "blk", blk_pairs(lambda b: b + 4 if b & 2 else b - 4))


def to_group(value, distance):
    return lax.ppermute(value, "blk", blk_pairs(lambda b: b ^ (4 * distance)))


def to_panel(value):
    return lax.ppermute(value, "feat", [(0, 1), (1, 0)])


def pick_body(w_in, send, semaphore):
    half = send.shape[0]
    core, _, panel = coordinates()
    start = pl.multiple_of(((1 - panel) ^ core) * half, half)
    copy = pltpu.make_async_copy(w_in.at[pl.ds(start, half), :], send, semaphore)
    copy.start()
    copy.wait()


def pick(w_in):
    width = w_in.shape[1]
    return pl.pallas_call(
        pick_body,
        out_shape=jax.ShapeDtypeStruct((width, width), BF16),
        in_specs=[ANY],
        out_specs=VMEM,
        scratch_shapes=[pltpu.SemaphoreType.DMA],
        compiler_params=params(4),
        cost_estimate=cost(),
        name="pick",
    )(w_in)


def build_body(codes, tiles, dense):
    _, steps, cap, tile, _ = tiles.shape
    radius = (steps - 1) // 2
    block_tiles = dense.shape[0] // tile
    core, mate, _ = coordinates()
    dense[...] = jnp.zeros_like(dense)

    def place(entry, carry):
        step, slot = entry // cap, entry % cap
        shifted = step - radius + core + 2
        chip = shifted // 2 - 1
        position = (shifted % 2) ^ core
        ahead = jnp.where(mate == 0, 1, -1)
        outside = jnp.where(position == 1, 4, jnp.where(chip == ahead, 2, 3))
        segment = jnp.where(chip == 0, position, outside)
        code = codes[step, 0, slot]
        row = code // block_tiles
        col = segment * block_tiles + code % block_tiles

        @pl.when(code >= 0)
        def _():
            dense[
                pl.ds(pl.multiple_of(row * tile, tile), tile),
                pl.ds(pl.multiple_of(col * tile, tile), tile),
            ] = tiles[0, step, slot]

        return carry

    lax.fori_loop(0, steps * cap, place, 0)


def build(codes, tiles, rows):
    return pl.pallas_call(
        build_body,
        out_shape=jax.ShapeDtypeStruct((rows, 5 * rows), BF16),
        in_specs=[SMEM, VMEM],
        out_specs=VMEM,
        compiler_params=params(),
        cost_estimate=cost(),
        name="build_dense",
    )(codes, tiles)


def sum_products(result, dense, first, refs):
    for ref in refs:
        height = ref.shape[0]
        product = jnp.dot(
            dense[:, first : first + height], ref[...], preferred_element_type=F32
        )
        result = product if result is None else result + product
        first += height
    return result


def spread_near_body(dense, s0, s1, s2, s3, *refs):
    refs[-1][...] = sum_products(None, dense, 0, (s0, s1, s2, s3))


def spread_near(dense, own, other, mate, *after):
    rows, cols = own.shape
    block = rows // 2
    whole = pl.BlockSpec((rows, cols), lambda i: (0, 0))
    half = pl.BlockSpec((block, cols), lambda i: (0, 0))
    return pl.pallas_call(
        spread_near_body,
        grid=(2,),
        out_shape=jax.ShapeDtypeStruct((rows, cols), F32),
        in_specs=[
            pl.BlockSpec((block, 3 * rows), lambda i: (i, 0)),
            whole,
            whole,
            half,
            half,
            *[ANY] * len(after),
        ],
        out_specs=pl.BlockSpec((block, cols), lambda i: (i, 0)),
        compiler_params=params(),
        cost_estimate=cost(),
        name="spread_near",
    )(dense, own, other, *mate, *after)


def spread_far_body(dense, total, f0, f1, m0, m1, *refs):
    *far_other, out = refs
    height = f0.shape[0]
    core, mate, _ = coordinates()

    def add_up(*cross):
        out[...] = sum_products(total[...], dense, 6 * height, (f0, f1, *cross)).astype(BF16)

    pl.when(core == mate)(lambda: add_up(*far_other))
    pl.when(core != mate)(lambda: add_up(m0, m1))


def spread_far(dense, total, far, mate_other, far_other):
    return pl.pallas_call(
        spread_far_body,
        out_shape=jax.ShapeDtypeStruct(total.shape, BF16),
        in_specs=[VMEM] * (6 + len(far_other)),
        out_specs=VMEM,
        compiler_params=params(),
        cost_estimate=cost(),
        name="spread_far",
    )(dense, total, *far, *mate_other, *far_other)


def pull_body(cot, dense, own, mate, far, swap_own, cross_0, cross_1):
    rows = dense.shape[0]
    turned = cot[...].T
    terms = [
        jnp.dot(
            turned, dense[:, index * rows : (index + 1) * rows], preferred_element_type=F32
        )
        for index in range(5)
    ]
    own[...], mate[...], far[...] = terms[0], terms[2], terms[3]
    swap_own[...] = terms[1].astype(BF16)
    half = cross_0.shape[1]
    cross_0[...], cross_1[...] = terms[4][:, :half].astype(BF16), terms[4][:, half:].astype(BF16)


def pull(cot, dense):
    rows, cols = cot.shape
    return pl.pallas_call(
        pull_body,
        out_shape=[jax.ShapeDtypeStruct((cols, rows), F32)] * 3
        + [jax.ShapeDtypeStruct((cols, rows), BF16)]
        + [jax.ShapeDtypeStruct((cols, rows // 2), BF16)] * 2,
        in_specs=[VMEM] * 2,
        out_specs=[VMEM] * 6,
        compiler_params=params(),
        cost_estimate=cost(),
        name="pull",
    )(cot, dense)


def swap_sum_body(mate_term, far_term, cross_0, cross_1, mate_0, mate_1, far_0, far_1):
    half = far_0.shape[1]
    core, mate, _ = coordinates()
    cross = jnp.concatenate([cross_0[...], cross_1[...]], axis=1).astype(F32)
    cross_mate = jnp.where(core == mate, cross, 0.0)
    far = (far_term[...] + (cross - cross_mate)).astype(BF16)
    near = mate_term[...] + cross_mate
    mate_0[...], mate_1[...] = near[:, :half], near[:, half:]
    far_0[...], far_1[...] = far[:, :half], far[:, half:]


def swap_sum(mate_term, far_term, cross):
    cols, rows = far_term.shape
    shape = (cols, rows // 2)
    out = pl.pallas_call(
        swap_sum_body,
        out_shape=[jax.ShapeDtypeStruct(shape, F32)] * 2
        + [jax.ShapeDtypeStruct(shape, BF16)] * 2,
        in_specs=[VMEM] * 4,
        out_specs=[VMEM] * 4,
        compiler_params=params(),
        cost_estimate=cost(),
        name="swap_sum",
    )(mate_term, far_term, *cross)
    return out[:2], out[2:]


def hidden_body(s0, s1, w_mine, w_near, w_far, w_out, *refs, number):
    pre, hid, mixed = refs[-3:]
    height, width = pre.shape
    span = slice(number * height, (number + 1) * height)
    core, _, panel = coordinates()

    def rows_of(side):
        return pl.ds(pl.multiple_of((panel ^ side) * width, width), width)

    def run(w_theirs):
        mine, theirs = 0.0, 0.0
        for side, ref in enumerate((s0, s1)):
            taken = ref[span, :]
            mine += jnp.dot(taken, w_mine[rows_of(side), :], preferred_element_type=F32)
            theirs += jnp.dot(taken, w_theirs[side][...], preferred_element_type=F32)
        pre[...] = mine
        hid[:, :width] = (mine * jax.nn.sigmoid(mine)).astype(BF16)
        hid[:, width:] = (theirs * jax.nn.sigmoid(theirs)).astype(BF16)

    pl.when(core == 0)(lambda: run((w_near, w_far)))
    pl.when(core == 1)(lambda: run((w_far, w_near)))
    result = 0.0
    for side in range(2):
        value = hid[:, side * width : (side + 1) * width]
        result += jnp.dot(value, w_out[rows_of(side), :], preferred_element_type=F32)
    mixed[...] = result.astype(BF16)


def hidden_step(number, pieces, w_mine, w_near, w_far, w_out, *after):
    rows, width = pieces[0].shape
    height = rows // 2
    return pl.pallas_call(
        functools.partial(hidden_body, number=number),
        out_shape=[
            jax.ShapeDtypeStruct((height, width), F32),
            jax.ShapeDtypeStruct((height, 2 * width), BF16),
            jax.ShapeDtypeStruct((height, width), BF16),
        ],
        in_specs=[VMEM] * 6 + [ANY] * len(after),
        out_specs=[VMEM] * 3,
        compiler_params=params(),
        cost_estimate=cost(),
        name="hidden",
    )(*pieces, w_mine, w_near, w_far, w_out, *after)


def mix_body(own, swap, come, w_out, *refs, number):
    pulled, keep, give = refs[-3:]
    height, half = keep.shape
    _, _, panel = coordinates()
    span = slice(number * height, (number + 1) * height)
    total = own[:, span] + swap[:, span].astype(F32) + come[...].astype(F32)
    pulled[...] = total.astype(BF16).T
    contract = (((1,), (1,)), ((), ()))
    theirs = w_out[pl.ds(pl.multiple_of((1 - panel) * half, half), half), :]
    give[...] = lax.dot_general(
        pulled[...], theirs, contract, preferred_element_type=F32
    ).astype(BF16)
    mine = w_out[pl.ds(pl.multiple_of(panel * half, half), half), :]
    keep[...] = lax.dot_general(pulled[...], mine, contract, preferred_element_type=F32)


def mix_step(number, own, swap, come, w_out, *after):
    cols, height = come.shape
    half = w_out.shape[0] // 2
    return pl.pallas_call(
        functools.partial(mix_body, number=number),
        out_shape=[
            jax.ShapeDtypeStruct((height, cols), BF16),
            jax.ShapeDtypeStruct((height, half), F32),
            jax.ShapeDtypeStruct((height, half), BF16),
        ],
        in_specs=[VMEM] * 4 + [ANY] * len(after),
        out_specs=[VMEM] * 3,
        compiler_params=params(),
        cost_estimate=cost(),
        name="mix_back",
    )(own, swap, come, w_out, *after)


def split_term(total, keep, give_near, give_far, scratch, blocks):
    core, mate, _ = coordinates()
    share = total.shape[0] // blocks
    groups = blocks // 4
    for group in range(groups):
        for side in range(2):
            owner = 4 * group + 2 * (mate ^ side)
            target = pl.ds((side * groups + group) * share, share)
            source = pl.multiple_of((owner + core) * share, share)
            keep[target, :] = total[pl.ds(source, share), :]
            source = pl.multiple_of((owner + 1 - core) * share, share)
            scratch[target, :] = total[pl.ds(source, share), :]
    half = give_near.shape[0]
    give_near[...] = scratch[:half].astype(BF16)
    give_far[...] = scratch[half:].astype(BF16)


def grad_into(total, pieces, rights):
    _, _, panel = coordinates()
    contract = (((0,), (0,)), ((), ()))
    width = rights[0].shape[1]
    half = width // 2
    for side, (refs, first) in enumerate(pieces):
        for number in range(2):
            start = (panel ^ side) * width + number * half
            source = first + number * half
            result = 0.0
            for index, right in enumerate(rights):
                height = right.shape[0]
                if len(refs) == 1:
                    taken = refs[0][index * height : (index + 1) * height, source : source + half]
                else:
                    taken = refs[index][:, source : source + half]
                result += lax.dot_general(
                    taken,
                    right[...],
                    contract,
                    preferred_element_type=F32,
                )
            total[pl.ds(pl.multiple_of(start, half), half), :] = result


def out_grad_body(hid_0, hid_1, pulled_0, pulled_1, *refs, blocks):
    keep, near, far, total, scratch = refs[-5:]
    width = pulled_0.shape[1]
    hid = (hid_0, hid_1)
    grad_into(total, ((hid, 0), (hid, width)), (pulled_0, pulled_1))
    split_term(total, keep, near, far, scratch, blocks)


def in_grad_body(*refs, blocks):
    own, theirs, *refs = refs
    pre, kept, come = [refs[2 * i : 2 * i + 2] for i in range(3)]
    keep, near, far, total, scratch, *back = refs[-7:]
    for half in range(2):
        pre_hidden = pre[half][...]
        gate = jax.nn.sigmoid(pre_hidden)
        back_hidden = kept[half][...] + come[half][...].astype(F32)
        slope = gate * (1.0 + pre_hidden * (1.0 - gate))
        back[half][...] = (back_hidden * slope).astype(BF16)
    grad_into(total, (((own,), 0), ((theirs,), 0)), back)
    split_term(total, keep, near, far, scratch, blocks)


def grad_call(body, name, operands, height, width, scratch=(), after=()):
    blocks = lax.axis_size("blk")
    half = height // 2
    return pl.pallas_call(
        functools.partial(body, blocks=blocks),
        out_shape=[
            jax.ShapeDtypeStruct((half, width), F32),
            jax.ShapeDtypeStruct((half // 2, width), BF16),
            jax.ShapeDtypeStruct((half // 2, width), BF16),
        ],
        in_specs=[VMEM] * len(operands) + [ANY] * len(after),
        out_specs=[VMEM] * 3,
        scratch_shapes=[
            pltpu.VMEM((height, width), F32),
            pltpu.VMEM((half, width), F32),
            *scratch,
        ],
        compiler_params=params(),
        cost_estimate=cost(),
        name=name,
    )(*operands, *after)


def far_sum_body(first, first_come, second, second_come, far):
    half = far.shape[0] // 2
    far[:half] = (first[half:] + first_come[...].astype(F32)).astype(BF16)
    far[half:] = (second[half:] + second_come[...].astype(F32)).astype(BF16)


def far_sum(first, first_come, second, second_come):
    return pl.pallas_call(
        far_sum_body,
        out_shape=jax.ShapeDtypeStruct(first.shape, BF16),
        in_specs=[VMEM] * 4,
        out_specs=VMEM,
        compiler_params=params(),
        cost_estimate=cost(),
        name="far_sum",
    )(first, first_come, second, second_come)


def mate_sum_body(first, first_core, second, second_core, come, *refs):
    own_first, own_second, *terms, sum_first, sum_second = refs
    share = own_first.shape[0]
    group = lax.axis_index("blk") // 4
    half = sum_first.shape[0]
    sum_first[...] = first[:half] + first_core[...].astype(F32) + come[:half].astype(F32)
    sum_second[...] = second[:half] + second_core[...].astype(F32) + come[half:].astype(F32)

    def rows_of(distance):
        start = pl.multiple_of((group ^ distance) * share, share)
        return sum_first[pl.ds(start, share), :], sum_second[pl.ds(start, share), :]

    own_first[...], own_second[...] = rows_of(0)
    for number, ref in enumerate(terms):
        ref[...] = jnp.concatenate(rows_of(number + 1), axis=0).astype(BF16)


def mate_sum(first, first_core, second, second_core, come):
    height, width = first_core.shape
    groups = lax.axis_size("blk") // 4
    share = height // groups
    own = jax.ShapeDtypeStruct((share, width), F32)
    term = jax.ShapeDtypeStruct((2 * share, width), BF16)
    own_first, own_second, *terms = pl.pallas_call(
        mate_sum_body,
        out_shape=[own] * 2 + [term] * (groups - 1),
        in_specs=[VMEM] * 5,
        out_specs=[VMEM] * (1 + groups),
        scratch_shapes=[pltpu.VMEM((height, width), F32)] * 2,
        compiler_params=params(),
        cost_estimate=cost(),
        name="mate_sum",
    )(first, first_core, second, second_core, come)
    return own_first, own_second, terms


def group_sum_body(own_first, own_second, *refs):
    *terms, out_first, out_second = refs
    share = own_first.shape[0]
    total_first, total_second = own_first[...], own_second[...]
    for ref in terms:
        term = ref[...].astype(F32)
        total_first += term[:share]
        total_second += term[share:]
    out_first[...] = total_first
    out_second[...] = total_second


def group_sum(own_first, own_second, terms):
    return pl.pallas_call(
        group_sum_body,
        out_shape=[jax.ShapeDtypeStruct(own_first.shape, F32)] * 2,
        in_specs=[VMEM] * (2 + len(terms)),
        out_specs=[VMEM] * 2,
        compiler_params=params(),
        cost_estimate=cost(),
        name="group_sum",
    )(own_first, own_second, *terms)


def shards(
    features, weight_in, weight_out, adj_tiles, tile_rows, tile_cols, tile_counts, cotangent
):
    rows, width = features.shape
    tile_rows, tile_cols = jnp.swapaxes(tile_rows, 0, 1), jnp.swapaxes(tile_cols, 0, 1)
    slots = lax.broadcasted_iota(jnp.int32, tile_rows.shape, 2)
    codes = jnp.where(
        slots < tile_counts[0][:, None, None],
        tile_rows * (rows // adj_tiles.shape[-1]) + tile_cols,
        -1,
    )

    height = rows // 2

    f_mate = [to_mate(features[:height]), to_mate(features[height:])]
    f_other = to_core(features)
    f_mate_other = [to_core(half) for half in f_mate]
    f_far = [relay_out(half) for half in f_mate]
    w_near = to_panel(gate(pick(weight_in), f_mate[0]))
    w_far = to_core(w_near)

    dense = build(codes, adj_tiles, rows)
    p_own, p_mate, p_far, p_swap, *p_cross = pull(cotangent, dense)
    p_mate, p_far = swap_sum(
        p_mate, p_far, [to_core(gate(half, f_mate[1])) for half in p_cross]
    )
    p_swap = to_core(p_swap)

    total = spread_near(dense, features, f_other, f_mate, p_far[0])
    f_far = [gate(half, total) for half in f_far]
    p_come = [relay_back(gate(far, *f_far)) for far in p_far]
    f_far_other = [to_core(half) for half in f_far]
    own = spread_far(dense, total, f_far, f_mate_other, f_far_other)
    theirs = to_panel(own)
    q_come = [
        to_mate((mine + come.astype(F32)).astype(BF16)) for mine, come in zip(p_mate, p_come)
    ]
    pre_hidden, hid, mixed = zip(
        *[
            hidden_step(number, (own, theirs), weight_in, w_near, w_far, weight_out, dense)
            for number in range(2)
        ]
    )

    t_mate = [to_mate(half) for half in mixed]
    t_own = jnp.concatenate(mixed, axis=0)
    t_other = to_core(t_own)
    t_mate_other = [to_core(half) for half in t_mate]
    t_far = [relay_out(half) for half in t_mate]
    t_far_other = [to_core(jnp.concatenate(t_far, axis=0))]

    pulled, kept, given = zip(
        *[
            mix_step(number, p_own, p_swap, come, weight_out, dense)
            for number, come in enumerate(q_come)
        ]
    )
    come = [to_panel(half) for half in given]
    out_keep, out_near, out_far = grad_call(
        out_grad_body, "out_grad", [*hid, *pulled], 2 * width, width
    )
    in_keep, in_near, in_far = grad_call(
        in_grad_body,
        "in_grad",
        [own, theirs, *pre_hidden, *kept, *come],
        2 * width,
        width,
        [pltpu.VMEM((height, width), BF16)] * 2,
        (dense, t_mate[1][:8, :128]),
    )
    far = far_sum(out_keep, to_core(out_far), in_keep, to_core(in_far))
    out_own, in_own, terms = mate_sum(
        out_keep, to_core(out_near), in_keep, to_core(in_near), to_mate(far)
    )
    terms = [to_group(terms[distance - 1], distance) for distance in sorted(range(1, len(terms) + 1), key=lambda d: (d % 2, -d))]

    total = spread_near(dense, t_own, t_other, t_mate)
    layer_output = spread_far(dense, total, t_far, t_mate_other, t_far_other)
    grad_weight_out, grad_weight_in = group_sum(out_own, in_own, terms)
    return (layer_output, grad_weight_in, grad_weight_out)


def solution(mesh):
    return jax.shard_map(
        shards,
        mesh=mesh,
        in_specs=(
            P("blk", "feat"),
            P(None, "feat"),
            P(None, "feat"),
            P("blk", None, None, None, None),
            P("blk", None, None),
            P("blk", None, None),
            P("blk", None),
            P("blk", "feat"),
        ),
        out_specs=(P("blk", "feat"), P("blk", "feat"), P("blk", "feat")),
        check_vma=False,
    )
```

```python
import functools

import jax
import jax.numpy as jnp
from jax import lax
from jax.experimental import pallas as pl
from jax.experimental.pallas import tpu as pltpu
from jax.sharding import PartitionSpec as P

BF16 = jnp.bfloat16
F32 = jnp.float32
VMEM = pl.BlockSpec(memory_space=pltpu.VMEM)
SMEM = pl.BlockSpec(memory_space=pltpu.SMEM)
ANY = pl.BlockSpec(memory_space=pl.ANY)


def params(limit_mib=12):
    return pltpu.CompilerParams(vmem_limit_bytes=limit_mib * 1024 * 1024)


def cost(microseconds=0):
    return pl.CostEstimate(
        flops=1024, bytes_accessed=1024 + 3_600_000 * microseconds, transcendentals=0
    )


def gate_body(*refs):
    del refs


def gate(value, *after, microseconds=0):
    return pl.pallas_call(
        gate_body,
        out_shape=jax.ShapeDtypeStruct(value.shape, value.dtype),
        in_specs=[ANY] * (1 + len(after)),
        out_specs=ANY,
        input_output_aliases={0: 0},
        compiler_params=params(1),
        cost_estimate=cost(microseconds),
        name="gate",
    )(value, *after)


def coordinates():
    block = lax.axis_index("blk")
    return block & 1, (block >> 1) & 1, lax.axis_index("feat")


def coordinates():
    block = lax.axis_index("blk")
    return block & 1, (block >> 1) & 1, lax.axis_index("feat")


def copy_all(pairs, semaphores):
    copies = [
        pltpu.make_async_copy(source, target, semaphores.at[number])
        for number, (source, target) in enumerate(pairs)
    ]
    for copy in copies:
        copy.start()
    for copy in copies:
        copy.wait()


def coordinates():
    block = lax.axis_index("blk")
    return block & 1, (block >> 1) & 1, lax.axis_index("feat")


def blk_pairs(target):
    count = lax.axis_size("blk")
    return [(source, target(source) % count) for source in range(count)]


def to_core(value):
    return lax.ppermute(value, "blk", blk_pairs(lambda b: b ^ 1))


def to_mate(value):
    return lax.ppermute(value, "blk", blk_pairs(lambda b: b ^ 2))


def relay_out(value):
    return lax.ppermute(value, "blk", blk_pairs(lambda b: b - 4 if b & 2 else b + 4))


def relay_back(value):
    return lax.ppermute(value, "blk", blk_pairs(lambda b: b + 4 if b & 2 else b - 4))


def to_group(value, distance):
    return lax.ppermute(value, "blk", blk_pairs(lambda b: b ^ (4 * distance)))


def to_panel(value):
    return lax.ppermute(value, "feat", [(0, 1), (1, 0)])


def pick_body(w_in, send, semaphore):
    half = send.shape[0]
    core, _, panel = coordinates()
    start = pl.multiple_of(((1 - panel) ^ core) * half, half)
    copy = pltpu.make_async_copy(w_in.at[pl.ds(start, half), :], send, semaphore)
    copy.start()
    copy.wait()


def pick(w_in):
    width = w_in.shape[1]
    return pl.pallas_call(
        pick_body,
        out_shape=jax.ShapeDtypeStruct((width, width), BF16),
        in_specs=[ANY],
        out_specs=VMEM,
        scratch_shapes=[pltpu.SemaphoreType.DMA],
        compiler_params=params(4),
        cost_estimate=cost(),
        name="pick",
    )(w_in)


def build_body(codes, tiles, dense):
    _, steps, cap, tile, _ = tiles.shape
    radius = (steps - 1) // 2
    block_tiles = dense.shape[0] // tile
    core, mate, _ = coordinates()
    dense[...] = jnp.zeros_like(dense)

    def place(entry, carry):
        step, slot = entry // cap, entry % cap
        shifted = step - radius + core + 2
        chip = shifted // 2 - 1
        position = (shifted % 2) ^ core
        ahead = jnp.where(mate == 0, 1, -1)
        outside = jnp.where(position == 1, 4, jnp.where(chip == ahead, 2, 3))
        segment = jnp.where(chip == 0, position, outside)
        code = codes[step, 0, slot]
        row = code // block_tiles
        col = segment * block_tiles + code % block_tiles

        @pl.when(code >= 0)
        def _():
            dense[
                pl.ds(pl.multiple_of(row * tile, tile), tile),
                pl.ds(pl.multiple_of(col * tile, tile), tile),
            ] = tiles[0, step, slot]

        return carry

    lax.fori_loop(0, steps * cap, place, 0)


def build(codes, tiles, rows):
    return pl.pallas_call(
        build_body,
        out_shape=jax.ShapeDtypeStruct((rows, 5 * rows), BF16),
        in_specs=[SMEM, VMEM],
        out_specs=VMEM,
        compiler_params=params(),
        cost_estimate=cost(),
        name="build_dense",
    )(codes, tiles)


def sum_products(result, dense, first, refs):
    for ref in refs:
        height = ref.shape[0]
        product = jnp.dot(
            dense[:, first : first + height], ref[...], preferred_element_type=F32
        )
        result = product if result is None else result + product
        first += height
    return result


def spread_near_body(dense, s0, s1, s2, s3, *refs):
    refs[-1][...] = sum_products(None, dense, 0, (s0, s1, s2, s3))


def spread_near(dense, own, other, mate, *after):
    rows, cols = own.shape
    block = rows // 2
    whole = pl.BlockSpec((rows, cols), lambda i: (0, 0))
    half = pl.BlockSpec((block, cols), lambda i: (0, 0))
    return pl.pallas_call(
        spread_near_body,
        grid=(2,),
        out_shape=jax.ShapeDtypeStruct((rows, cols), F32),
        in_specs=[
            pl.BlockSpec((block, 3 * rows), lambda i: (i, 0)),
            whole,
            whole,
            half,
            half,
            *[ANY] * len(after),
        ],
        out_specs=pl.BlockSpec((block, cols), lambda i: (i, 0)),
        compiler_params=params(),
        cost_estimate=cost(),
        name="spread_near",
    )(dense, own, other, *mate, *after)


def spread_far_body(dense, total, f0, f1, m0, m1, *refs):
    *far_other, out = refs
    height = f0.shape[0]
    core, mate, _ = coordinates()

    def add_up(*cross):
        out[...] = sum_products(total[...], dense, 6 * height, (f0, f1, *cross)).astype(BF16)

    pl.when(core == mate)(lambda: add_up(*far_other))
    pl.when(core != mate)(lambda: add_up(m0, m1))


def spread_far(dense, total, far, mate_other, far_other):
    return pl.pallas_call(
        spread_far_body,
        out_shape=jax.ShapeDtypeStruct(total.shape, BF16),
        in_specs=[VMEM] * (6 + len(far_other)),
        out_specs=VMEM,
        compiler_params=params(),
        cost_estimate=cost(),
        name="spread_far",
    )(dense, total, *far, *mate_other, *far_other)


def pull_body(cot, dense, own, mate, far, swap_own, cross_0, cross_1):
    rows = dense.shape[0]
    turned = cot[...].T
    terms = [
        jnp.dot(
            turned, dense[:, index * rows : (index + 1) * rows], preferred_element_type=F32
        )
        for index in range(5)
    ]
    own[...], mate[...], far[...] = terms[0], terms[2], terms[3]
    swap_own[...] = terms[1].astype(BF16)
    half = cross_0.shape[1]
    cross_0[...], cross_1[...] = terms[4][:, :half].astype(BF16), terms[4][:, half:].astype(BF16)


def pull(cot, dense):
    rows, cols = cot.shape
    return pl.pallas_call(
        pull_body,
        out_shape=[jax.ShapeDtypeStruct((cols, rows), F32)] * 3
        + [jax.ShapeDtypeStruct((cols, rows), BF16)]
        + [jax.ShapeDtypeStruct((cols, rows // 2), BF16)] * 2,
        in_specs=[VMEM] * 2,
        out_specs=[VMEM] * 6,
        compiler_params=params(),
        cost_estimate=cost(),
        name="pull",
    )(cot, dense)


def swap_sum_body(mate_term, far_term, cross_0, cross_1, mate_0, mate_1, far_0, far_1):
    half = far_0.shape[1]
    core, mate, _ = coordinates()
    cross = jnp.concatenate([cross_0[...], cross_1[...]], axis=1).astype(F32)
    cross_mate = jnp.where(core == mate, cross, 0.0)
    far = (far_term[...] + (cross - cross_mate)).astype(BF16)
    near = mate_term[...] + cross_mate
    mate_0[...], mate_1[...] = near[:, :half], near[:, half:]
    far_0[...], far_1[...] = far[:, :half], far[:, half:]


def swap_sum(mate_term, far_term, cross):
    cols, rows = far_term.shape
    shape = (cols, rows // 2)
    out = pl.pallas_call(
        swap_sum_body,
        out_shape=[jax.ShapeDtypeStruct(shape, F32)] * 2
        + [jax.ShapeDtypeStruct(shape, BF16)] * 2,
        in_specs=[VMEM] * 4,
        out_specs=[VMEM] * 4,
        compiler_params=params(),
        cost_estimate=cost(),
        name="swap_sum",
    )(mate_term, far_term, *cross)
    return out[:2], out[2:]


def hidden_body(s0, s1, w_mine, w_near, w_far, w_out, *refs, number):
    pre, hid, mixed = refs[-3:]
    height, width = pre.shape
    span = slice(number * height, (number + 1) * height)
    core, _, panel = coordinates()

    def rows_of(side):
        return pl.ds(pl.multiple_of((panel ^ side) * width, width), width)

    def run(w_theirs):
        mine, theirs = 0.0, 0.0
        for side, ref in enumerate((s0, s1)):
            taken = ref[span, :]
            mine += jnp.dot(taken, w_mine[rows_of(side), :], preferred_element_type=F32)
            theirs += jnp.dot(taken, w_theirs[side][...], preferred_element_type=F32)
        pre[...] = mine
        hid[:, :width] = (mine * jax.nn.sigmoid(mine)).astype(BF16)
        hid[:, width:] = (theirs * jax.nn.sigmoid(theirs)).astype(BF16)

    pl.when(core == 0)(lambda: run((w_near, w_far)))
    pl.when(core == 1)(lambda: run((w_far, w_near)))
    result = 0.0
    for side in range(2):
        value = hid[:, side * width : (side + 1) * width]
        result += jnp.dot(value, w_out[rows_of(side), :], preferred_element_type=F32)
    mixed[...] = result.astype(BF16)


def hidden_step(number, pieces, w_mine, w_near, w_far, w_out, *after):
    rows, width = pieces[0].shape
    height = rows // 2
    return pl.pallas_call(
        functools.partial(hidden_body, number=number),
        out_shape=[
            jax.ShapeDtypeStruct((height, width), F32),
            jax.ShapeDtypeStruct((height, 2 * width), BF16),
            jax.ShapeDtypeStruct((height, width), BF16),
        ],
        in_specs=[VMEM] * 6 + [ANY] * len(after),
        out_specs=[VMEM] * 3,
        compiler_params=params(),
        cost_estimate=cost(),
        name="hidden",
    )(*pieces, w_mine, w_near, w_far, w_out, *after)


def mix_body(own, swap, come, w_out, *refs, number):
    pulled, keep, give = refs[-3:]
    height, half = keep.shape
    _, _, panel = coordinates()
    span = slice(number * height, (number + 1) * height)
    total = own[:, span] + swap[:, span].astype(F32) + come[...].astype(F32)
    pulled[...] = total.astype(BF16).T
    contract = (((1,), (1,)), ((), ()))
    theirs = w_out[pl.ds(pl.multiple_of((1 - panel) * half, half), half), :]
    give[...] = lax.dot_general(
        pulled[...], theirs, contract, preferred_element_type=F32
    ).astype(BF16)
    mine = w_out[pl.ds(pl.multiple_of(panel * half, half), half), :]
    keep[...] = lax.dot_general(pulled[...], mine, contract, preferred_element_type=F32)


def mix_step(number, own, swap, come, w_out, *after):
    cols, height = come.shape
    half = w_out.shape[0] // 2
    return pl.pallas_call(
        functools.partial(mix_body, number=number),
        out_shape=[
            jax.ShapeDtypeStruct((height, cols), BF16),
            jax.ShapeDtypeStruct((height, half), F32),
            jax.ShapeDtypeStruct((height, half), BF16),
        ],
        in_specs=[VMEM] * 4 + [ANY] * len(after),
        out_specs=[VMEM] * 3,
        compiler_params=params(),
        cost_estimate=cost(),
        name="mix_back",
    )(own, swap, come, w_out, *after)


def split_term(total, keep, give_near, give_far, scratch, blocks):
    core, mate, _ = coordinates()
    share = total.shape[0] // blocks
    groups = blocks // 4
    for group in range(groups):
        for side in range(2):
            owner = 4 * group + 2 * (mate ^ side)
            target = pl.ds((side * groups + group) * share, share)
            source = pl.multiple_of((owner + core) * share, share)
            keep[target, :] = total[pl.ds(source, share), :]
            source = pl.multiple_of((owner + 1 - core) * share, share)
            scratch[target, :] = total[pl.ds(source, share), :]
    half = give_near.shape[0]
    give_near[...] = scratch[:half].astype(BF16)
    give_far[...] = scratch[half:].astype(BF16)


def grad_into(total, pieces, rights):
    _, _, panel = coordinates()
    contract = (((0,), (0,)), ((), ()))
    width = rights[0].shape[1]
    half = width // 2
    for side, (refs, first) in enumerate(pieces):
        for number in range(2):
            start = (panel ^ side) * width + number * half
            source = first + number * half
            result = 0.0
            for index, right in enumerate(rights):
                height = right.shape[0]
                if len(refs) == 1:
                    taken = refs[0][index * height : (index + 1) * height, source : source + half]
                else:
                    taken = refs[index][:, source : source + half]
                result += lax.dot_general(
                    taken,
                    right[...],
                    contract,
                    preferred_element_type=F32,
                )
            total[pl.ds(pl.multiple_of(start, half), half), :] = result


def out_grad_body(hid_0, hid_1, pulled_0, pulled_1, *refs, blocks):
    keep, near, far, total, scratch = refs[-5:]
    width = pulled_0.shape[1]
    hid = (hid_0, hid_1)
    grad_into(total, ((hid, 0), (hid, width)), (pulled_0, pulled_1))
    split_term(total, keep, near, far, scratch, blocks)


def in_grad_body(*refs, blocks):
    own, theirs, *refs = refs
    pre, kept, come = [refs[2 * i : 2 * i + 2] for i in range(3)]
    keep, near, far, total, scratch, *back = refs[-7:]
    for half in range(2):
        pre_hidden = pre[half][...]
        gate = jax.nn.sigmoid(pre_hidden)
        back_hidden = kept[half][...] + come[half][...].astype(F32)
        slope = gate * (1.0 + pre_hidden * (1.0 - gate))
        back[half][...] = (back_hidden * slope).astype(BF16)
    grad_into(total, (((own,), 0), ((theirs,), 0)), back)
    split_term(total, keep, near, far, scratch, blocks)


def grad_call(body, name, operands, height, width, scratch=(), after=()):
    blocks = lax.axis_size("blk")
    half = height // 2
    return pl.pallas_call(
        functools.partial(body, blocks=blocks),
        out_shape=[
            jax.ShapeDtypeStruct((half, width), F32),
            jax.ShapeDtypeStruct((half // 2, width), BF16),
            jax.ShapeDtypeStruct((half // 2, width), BF16),
        ],
        in_specs=[VMEM] * len(operands) + [ANY] * len(after),
        out_specs=[VMEM] * 3,
        scratch_shapes=[
            pltpu.VMEM((height, width), F32),
            pltpu.VMEM((half, width), F32),
            *scratch,
        ],
        compiler_params=params(),
        cost_estimate=cost(),
        name=name,
    )(*operands, *after)


def far_sum_body(first, first_come, second, second_come, far):
    half = far.shape[0] // 2
    far[:half] = (first[half:] + first_come[...].astype(F32)).astype(BF16)
    far[half:] = (second[half:] + second_come[...].astype(F32)).astype(BF16)


def far_sum(first, first_come, second, second_come):
    return pl.pallas_call(
        far_sum_body,
        out_shape=jax.ShapeDtypeStruct(first.shape, BF16),
        in_specs=[VMEM] * 4,
        out_specs=VMEM,
        compiler_params=params(),
        cost_estimate=cost(),
        name="far_sum",
    )(first, first_come, second, second_come)


def mate_sum_body(first, first_core, second, second_core, come, *refs):
    own_first, own_second, *terms, sum_first, sum_second = refs
    share = own_first.shape[0]
    group = lax.axis_index("blk") // 4
    half = sum_first.shape[0]
    sum_first[...] = first[:half] + first_core[...].astype(F32) + come[:half].astype(F32)
    sum_second[...] = second[:half] + second_core[...].astype(F32) + come[half:].astype(F32)

    def rows_of(distance):
        start = pl.multiple_of((group ^ distance) * share, share)
        return sum_first[pl.ds(start, share), :], sum_second[pl.ds(start, share), :]

    own_first[...], own_second[...] = rows_of(0)
    for number, ref in enumerate(terms):
        ref[...] = jnp.concatenate(rows_of(number + 1), axis=0).astype(BF16)


def mate_sum(first, first_core, second, second_core, come):
    height, width = first_core.shape
    groups = lax.axis_size("blk") // 4
    share = height // groups
    own = jax.ShapeDtypeStruct((share, width), F32)
    term = jax.ShapeDtypeStruct((2 * share, width), BF16)
    own_first, own_second, *terms = pl.pallas_call(
        mate_sum_body,
        out_shape=[own] * 2 + [term] * (groups - 1),
        in_specs=[VMEM] * 5,
        out_specs=[VMEM] * (1 + groups),
        scratch_shapes=[pltpu.VMEM((height, width), F32)] * 2,
        compiler_params=params(),
        cost_estimate=cost(),
        name="mate_sum",
    )(first, first_core, second, second_core, come)
    return own_first, own_second, terms


def group_sum_body(own_first, own_second, *refs):
    *terms, out_first, out_second = refs
    share = own_first.shape[0]
    total_first, total_second = own_first[...], own_second[...]
    for ref in terms:
        term = ref[...].astype(F32)
        total_first += term[:share]
        total_second += term[share:]
    out_first[...] = total_first
    out_second[...] = total_second


def group_sum(own_first, own_second, terms):
    return pl.pallas_call(
        group_sum_body,
        out_shape=[jax.ShapeDtypeStruct(own_first.shape, F32)] * 2,
        in_specs=[VMEM] * (2 + len(terms)),
        out_specs=[VMEM] * 2,
        compiler_params=params(),
        cost_estimate=cost(),
        name="group_sum",
    )(own_first, own_second, *terms)


def shards(
    features, weight_in, weight_out, adj_tiles, tile_rows, tile_cols, tile_counts, cotangent
):
    rows, width = features.shape
    tile_rows, tile_cols = jnp.swapaxes(tile_rows, 0, 1), jnp.swapaxes(tile_cols, 0, 1)
    slots = lax.broadcasted_iota(jnp.int32, tile_rows.shape, 2)
    codes = jnp.where(
        slots < tile_counts[0][:, None, None],
        tile_rows * (rows // adj_tiles.shape[-1]) + tile_cols,
        -1,
    )

    height = rows // 2

    f_mate = [to_mate(features[:height]), to_mate(features[height:])]
    f_other = to_core(features)
    f_mate_other = [to_core(half) for half in f_mate]
    f_far = [relay_out(half) for half in f_mate]
    w_near = to_panel(gate(pick(weight_in), f_mate[0]))
    w_far = to_core(w_near)

    dense = build(codes, adj_tiles, rows)
    p_own, p_mate, p_far, p_swap, *p_cross = pull(cotangent, dense)
    p_mate, p_far = swap_sum(
        p_mate, p_far, [to_core(gate(half, f_mate[1])) for half in p_cross]
    )
    p_swap = to_core(p_swap)

    total = spread_near(dense, features, f_other, f_mate, p_far[0])
    f_far = [gate(half, total) for half in f_far]
    p_come = [relay_back(gate(far, *f_far)) for far in p_far]
    f_far_other = [to_core(half) for half in f_far]
    own = spread_far(dense, total, f_far, f_mate_other, f_far_other)
    theirs = to_panel(own)
    q_come = [
        to_mate((mine + come.astype(F32)).astype(BF16)) for mine, come in zip(p_mate, p_come)
    ]
    pre_hidden, hid, mixed = zip(
        *[
            hidden_step(number, (own, theirs), weight_in, w_near, w_far, weight_out, dense)
            for number in range(2)
        ]
    )

    t_mate = [to_mate(half) for half in mixed]
    t_own = jnp.concatenate(mixed, axis=0)
    t_other = to_core(t_own)
    t_mate_other = [to_core(half) for half in t_mate]
    t_far = [relay_out(half) for half in t_mate]
    t_far_other = [to_core(jnp.concatenate(t_far, axis=0))]

    pulled, kept, given = zip(
        *[
            mix_step(number, p_own, p_swap, come, weight_out, dense)
            for number, come in enumerate(q_come)
        ]
    )
    come = [to_panel(half) for half in given]
    out_keep, out_near, out_far = grad_call(
        out_grad_body, "out_grad", [*hid, *pulled], 2 * width, width
    )
    in_keep, in_near, in_far = grad_call(
        in_grad_body,
        "in_grad",
        [own, theirs, *pre_hidden, *kept, *come],
        2 * width,
        width,
        [pltpu.VMEM((height, width), BF16)] * 2,
        (dense, t_mate[1][:8, :128]),
    )
    far = far_sum(out_keep, to_core(out_far), in_keep, to_core(in_far))
    out_own, in_own, terms = mate_sum(
        out_keep, to_core(out_near), in_keep, to_core(in_near), to_mate(far)
    )
    terms = [to_group(terms[distance - 1], distance) for distance in sorted(range(1, len(terms) + 1), key=lambda d: (d % 2, d))]

    total = spread_near(dense, t_own, t_other, t_mate)
    layer_output = spread_far(dense, total, t_far, t_mate_other, t_far_other)
    grad_weight_out, grad_weight_in = group_sum(out_own, in_own, terms)
    return (layer_output, grad_weight_in, grad_weight_out)


def solution(mesh):
    return jax.shard_map(
        shards,
        mesh=mesh,
        in_specs=(
            P("blk", "feat"),
            P(None, "feat"),
            P(None, "feat"),
            P("blk", None, None, None, None),
            P("blk", None, None),
            P("blk", None, None),
            P("blk", None),
            P("blk", "feat"),
        ),
        out_specs=(P("blk", "feat"), P("blk", "feat"), P("blk", "feat")),
        check_vma=False,
    )
```
